32 devices in a mesh: groups: 2 (over x), row: 8 (over z, y), chan: 2 (over core).
Axes of the slice: x: 2, y: 2, z: 4, core: 2. Of those that a mesh axis runs over, the one named last changes fastest.
Arguments:
- pair: bfloat16 [512, 256, 128], P(('groups', 'row'), 'chan'), parts along dimension 0, may hold values from -6 to 6
- pair_mask: int32 [512, 256], P(('groups', 'row'), 'chan'), parts along dimension 0, may hold values 0 or 1
- in_gain: float32 [128], replicated, may hold values from 0.1 to 1.9
- proj_weight: bfloat16 [128, 512], replicated, may hold values from -0.5 to 0.5
- gate_weight: bfloat16 [128, 128], replicated, may hold values from -0.5 to 0.5
- out_gain: float32 [128], replicated, may hold values from 0.1 to 1.9
- out_weight: bfloat16 [128, 128], replicated, may hold values from -0.5 to 0.5
Outputs:
- update: bfloat16 [512, 256, 128], P(('groups', 'row'), 'chan'), parts along dimension 0
The draws below stay inside these ranges and needn't reach their ends.
There are 2 independent parts, one for each index of `groups`. The reference program is written for one: setup_inputs(seed, part) draws one part's arguments, and reference() takes and returns one part's arrays. A program takes and returns all parts, laid end to end along the dimension named above; an argument that names none is the same for every part. Nothing has to cross between parts.
All inputs are finite; a program needn't handle non-finite values. No bound on the sum of `pair_mask` on one device may be relied on, other than what follows from the above.
Results may differ from the reference program's by a relative error of at most 0.0083.
Values may be sent and summed in bfloat16 or wider, within the bound.
No kernel may reach another device: no remote copies, remote signals or barrier semaphores. Data moves between devices by JAX's collectives and lax.ppermute only.
A program may use at most 64 MiB of HBM per device.

```python
import jax
import jax.numpy as jnp
from jax import lax

CHANNELS = 128
HIDDEN_SIZE = 128
TOKENS = 256


def plant(values, own_key, smallest, largest):
    shape = values.shape
    place = [jax.random.randint(jax.random.fold_in(own_key, axis), (), 0, shape[axis]) for axis in range(len(shape))]
    values = values.at[tuple(place)].set(smallest)
    longest = shape.index(max(shape))
    place[longest] = (place[longest] + 1) % shape[longest]
    return values.at[tuple(place)].set(largest)


def block_scale(rng, extent, cuts, low, largest):
    factor_of, own = 1.0, jax.random.fold_in(rng, 6)
    for axis_at, blocks in cuts:
        heights = jnp.exp(jax.random.uniform(jax.random.fold_in(own, axis_at), (blocks,), jnp.float32, low / len(cuts), largest / len(cuts)))
        factor_of = factor_of * jnp.repeat(heights, extent[axis_at] // blocks).reshape([-1 if axis == axis_at else 1 for axis in range(len(extent))])
    return factor_of


def gaussian(rng, shape, spread, reach, pieces=(), held_as=jnp.bfloat16):
    level = block_scale(rng, shape, pieces, -0.22, 0.18) if pieces else 1.0
    values = jax.random.normal(rng, shape, jnp.float32) * spread * level
    return jnp.minimum(jnp.maximum(values, -reach), reach).astype(held_as)


def setup_inputs(seed: int = 0, part: int = 0) -> dict:
    key_list = jax.random.split(jax.random.key(seed), 8)
    part_keys = jax.random.split(jax.random.fold_in(key_list[7], part), 8)
    return {
        "pair": gaussian(part_keys[0], (TOKENS, TOKENS, CHANNELS), 1.0, 6.0, ((0, 8), (1, 2))),
        "pair_mask": plant((jax.random.randint(part_keys[1], (TOKENS, TOKENS), 0, 5) < 4).astype(jnp.int32), jax.random.fold_in(part_keys[1], 1), 0, 1),
        "in_gain": jnp.clip(1.0 + 0.18 * jax.random.normal(key_list[2], (CHANNELS,), jnp.float32), 0.1, 1.9),
        "proj_weight": gaussian(key_list[3], (CHANNELS, 4 * HIDDEN_SIZE), CHANNELS ** -0.5, 0.5),
        "gate_weight": gaussian(key_list[4], (CHANNELS, CHANNELS), CHANNELS ** -0.5, 0.5),
        "out_gain": jnp.clip(1.0 + 0.18 * jax.random.normal(key_list[5], (HIDDEN_SIZE,), jnp.float32), 0.1, 1.9),
        "out_weight": gaussian(key_list[6], (HIDDEN_SIZE, CHANNELS), HIDDEN_SIZE ** -0.5, 0.5),
    }


def layer_norm(values, gain):
    mean = lax.optimization_barrier(jnp.mean(values, axis=-1, keepdims=True))
    centered = values - mean
    var = lax.optimization_barrier(jnp.mean(centered * centered, axis=-1, keepdims=True))
    return centered * jax.lax.rsqrt(var + 1e-05) * gain

def reference(pair, pair_mask, in_gain, proj_weight, gate_weight, out_gain, out_weight):
    normed = layer_norm(pair.astype(jnp.float32), in_gain).astype(jnp.bfloat16)
    flat = normed.reshape(TOKENS * TOKENS, CHANNELS)
    proj = jnp.dot(flat, proj_weight, preferred_element_type=jnp.float32).reshape(TOKENS, TOKENS, 4 * HIDDEN_SIZE)
    valid = pair_mask.astype(jnp.float32)[:, :, None]
    left = (valid * jax.nn.sigmoid(proj[:, :, :HIDDEN_SIZE]) * proj[:, :, HIDDEN_SIZE:2 * HIDDEN_SIZE]).astype(jnp.bfloat16)
    right = (valid * jax.nn.sigmoid(proj[:, :, 2 * HIDDEN_SIZE:3 * HIDDEN_SIZE]) * proj[:, :, 3 * HIDDEN_SIZE:]).astype(jnp.bfloat16)
    gate = jax.nn.sigmoid(jnp.dot(flat, gate_weight, preferred_element_type=jnp.float32))
    product = jnp.einsum('ikc,jkc->ijc', left.astype(jnp.float32), right.astype(jnp.float32)).astype(jnp.bfloat16)
    pnorm = layer_norm(product.astype(jnp.float32), out_gain).astype(jnp.bfloat16)
    mapped = jnp.dot(pnorm.reshape(TOKENS * TOKENS, HIDDEN_SIZE), out_weight, preferred_element_type=jnp.float32)
    return (gate * mapped).astype(jnp.bfloat16).reshape(TOKENS, TOKENS, CHANNELS)
```

```python
import functools

import jax
import jax.numpy as jnp
from jax import lax
from jax.experimental import pallas as pl
from jax.experimental.pallas import tpu as pltpu
from jax.sharding import PartitionSpec as P

F32, BF16 = jnp.float32, jnp.bfloat16
PIECES = 4
LANES = 128
LIMIT = 40 * 1024 * 1024


def sigmoid(x):
    return 0.5 * jnp.tanh(0.5 * x) + 0.5


def normalise(x, gain):
    mean = jnp.mean(x, axis=-1, keepdims=True)
    centered = x - mean
    var = jnp.mean(centered * centered, axis=-1, keepdims=True)
    return (centered * lax.rsqrt(var + 1e-05) * gain).astype(BF16)


def operands_kernel(where, pair, mask, gain, weight, *rest):
    lefts, rights = rest[:PIECES], rest[PIECES : 2 * PIECES]
    left_all, right_all, turned = rest[2 * PIECES :]
    rows, toks, _ = pair.shape
    hidden = weight.shape[1] // 4
    part = hidden // PIECES
    turned[...] = weight[...].T
    group = 4

    @pl.loop(0, rows // group)
    def _(at):
        first = at * group
        x = pair[pl.ds(first, group)].astype(F32).reshape(group * toks, -1)
        normed = normalise(x, gain[...])
        proj = lax.dot_general(
            turned[...], normed, (((1,), (1,)), ((), ())), preferred_element_type=F32
        )
        for g in range(group):
            valid = mask[pl.ds(first + g, 1), :].astype(F32)
            mine = proj[:, g * toks : (g + 1) * toks]
            blocks = [mine[n * hidden : (n + 1) * hidden] for n in range(4)]
            spot = pl.ds(first + g, hidden, stride=rows)
            left = valid * sigmoid(blocks[0]) * blocks[1]
            right = valid * sigmoid(blocks[2]) * blocks[3]
            for n in range(toks // LANES):
                left_all[n, spot, :] = left[:, n * LANES : (n + 1) * LANES]
                right_all[n, spot, :] = right[:, n * LANES : (n + 1) * LANES]

    for r in range(PIECES):
        span = part * rows
        spot = pl.ds(pl.multiple_of((where[0] ^ r) * span, span), span)
        for n in range(toks // LANES):
            lanes = slice(n * LANES, (n + 1) * LANES)
            rights[r][:, :, lanes] = right_all[n, spot, :].astype(BF16).reshape(part, rows, LANES)
            lefts[r][:, :, lanes] = left_all[n, spot, :].astype(BF16).reshape(part, rows, LANES)


def gate_kernel(pair, gain, weight, out):
    rows, toks, _ = pair.shape
    group = 4

    @pl.loop(0, rows // group)
    def _(at):
        spot = pl.ds(at * group, group)
        x = pair[spot].astype(F32).reshape(group * toks, -1)
        logits = jnp.dot(normalise(x, gain[...]), weight[...], preferred_element_type=F32)
        out[spot] = sigmoid(logits).reshape(group, toks, -1)


def product_kernel(n_left, n_right, places, *rest):
    lefts = [rest[n * PIECES : (n + 1) * PIECES] for n in range(n_left)]
    rest = rest[n_left * PIECES :]
    rights = [rest[n * PIECES : (n + 1) * PIECES] for n in range(n_right)]
    rest = rest[n_right * PIECES :]
    outs, held = rest[: 2 * n_left], rest[2 * n_left]
    part, rows, toks = lefts[0][0].shape
    flip = places[0]
    for s in range(n_right):
        for r in range(PIECES):
            start = places[1 + s] * (2 * rows) + ((r // 2) ^ flip) * rows
            spot = pl.ds(pl.multiple_of(start, rows), rows)
            held[:, spot, (r % 2) * toks : (r % 2 + 1) * toks] = rights[s][r][...]
    for c in range(part):
        left = jnp.concatenate(
            [
                jnp.concatenate([lefts[n][2 * ry][c], lefts[n][2 * ry + 1][c]], axis=1)
                for n in range(n_left)
                for ry in range(2)
            ],
            axis=0,
        )
        out = lax.dot_general(
            left, held[c], (((1,), (1,)), ((), ())), preferred_element_type=F32
        ).astype(BF16)
        for n in range(2 * n_left):
            outs[n][c] = out[n * rows : (n + 1) * rows]


def update_kernel(where, gain, weight, gate, *rest):
    sets = [rest[n * PIECES : (n + 1) * PIECES] for n in range(3)]
    out, pieces, turned, sems = rest[3 * PIECES :]
    part, rows, toks = sets[0][0].shape
    hidden = part * PIECES
    for n in range(3):

        @pl.when(where[1] == n)
        def _():
            copies = [
                pltpu.make_async_copy(sets[n][r], pieces.at[r], sems.at[r]) for r in range(PIECES)
            ]
            for copy in copies:
                copy.start()
            for copy in copies:
                copy.wait()

    for r in range(PIECES):
        base = (where[0] ^ r) * part
        for c in range(part):
            piece = pieces[r, c].astype(F32)
            for n in range(toks // LANES):
                lanes = slice(n * LANES, (n + 1) * LANES)
                turned[n, pl.ds(base + c, rows, stride=hidden), :] = piece[:, lanes]
    scale = jnp.broadcast_to(gain[...], (hidden, toks))

    @pl.loop(0, rows)
    def _(i):
        spot = pl.ds(pl.multiple_of(i * hidden, hidden), hidden)
        x = jnp.concatenate([turned[n, spot, :] for n in range(toks // LANES)], axis=1)
        mean = jnp.mean(x, axis=0, keepdims=True)
        centered = x - mean
        var = jnp.mean(centered * centered, axis=0, keepdims=True)
        pnorm = (centered * lax.rsqrt(var + 1e-05) * scale).astype(BF16)
        mapped = lax.dot_general(
            pnorm, weight[...], (((0,), (0,)), ((), ())), preferred_element_type=F32
        )
        out[i] = (gate[i] * mapped).astype(BF16)


SMEM = pl.BlockSpec(memory_space=pltpu.SMEM)
VMEM = pl.BlockSpec(memory_space=pltpu.VMEM)
ANY = pl.BlockSpec(memory_space=pl.ANY)
PARAMS = pltpu.CompilerParams(vmem_limit_bytes=LIMIT)


def local(pair, pair_mask, in_gain, proj_weight, gate_weight, out_gain, out_weight, *, n_row):
    rows, toks, channels = pair.shape
    hidden = proj_weight.shape[1] // 4
    part = hidden // PIECES
    planes = n_row // 2
    half = planes // 2
    row, core = lax.axis_index("row"), lax.axis_index("chan")
    z, y = row // 2, row % 2
    quarter = 2 * y + core
    own_half = z // half
    at_end = (z == 0) | (z == planes - 1)
    mode = jnp.where(core == own_half, 0, jnp.where(at_end, 2, 1))
    where = jnp.stack([quarter, mode]).astype(jnp.int32)

    def send(x, target):
        pairs = []
        for source in range(2 * n_row):
            to = target(source // 4, source // 2 % 2, source % 2)
            if to is not None:
                pairs.append((source, 4 * to[0] + 2 * to[1] + to[2]))
        return lax.ppermute(x, ("row", "chan"), pairs)

    def is_end(p):
        return p == 0 or p == planes - 1

    def inward(p):
        return 1 if p == 0 else planes - 2

    def outward(p):
        return p - 1 if p < half else p + 1

    def in_plane(r):
        return lambda p, b, k: (p, b ^ (r // 2), k ^ (r % 2))

    def shifted(s):
        def target(p, b, k):
            base = p // half * half
            return (base + (p - base + s) % half, b, k)

        return target

    def mirrored(p, b, k):
        return None if is_end(p) else (planes - 1 - p, b, k)

    def to_inner(p, b, k):
        return (inward(p), b, k) if is_end(p) else None

    def back_own(r):
        def target(p, b, k):
            return (p, b ^ (r // 2), k ^ (r % 2)) if k ^ (r % 2) == p // half else None

        return target

    def back_other(r):
        def target(p, b, k):
            if is_end(p) or k ^ (r % 2) == p // half:
                return None
            return (p, b ^ (r // 2), k ^ (r % 2))

        return target

    def back_end(r):
        def target(p, b, k):
            if is_end(p) or not is_end(outward(p)) or k ^ (r % 2) == p // half:
                return None
            return (outward(p), b ^ (r // 2), k ^ (r % 2))

        return target

    piece = jax.ShapeDtypeStruct((part, rows, toks), BF16)
    made = pl.pallas_call(
        operands_kernel,
        out_shape=[piece] * (2 * PIECES),
        in_specs=[SMEM, VMEM, VMEM, VMEM, VMEM],
        out_specs=[VMEM] * (2 * PIECES),
        scratch_shapes=[
            pltpu.VMEM((toks // LANES, hidden * rows, LANES), F32),
            pltpu.VMEM((toks // LANES, hidden * rows, LANES), F32),
            pltpu.VMEM((4 * hidden, channels), BF16),
        ],
        compiler_params=PARAMS,
        name="operands",
    )(where, pair, pair_mask, in_gain.reshape(1, -1), proj_weight)
    lefts, rights = made[:PIECES], made[PIECES:]
    rights = [rights[0]] + [send(rights[r], in_plane(r)) for r in range(1, PIECES)]
    lefts = [lefts[0]] + [send(lefts[r], in_plane(r)) for r in range(1, PIECES)]
    own = [rights] + [[send(x, shifted(s)) for x in rights] for s in range(1, half)]
    other = [[send(x, mirrored) for x in own[s]] for s in range(half)]
    outer = [send(x, to_inner) for x in lefts]

    gate = pl.pallas_call(
        gate_kernel,
        out_shape=jax.ShapeDtypeStruct((rows, toks, channels), F32),
        in_specs=[VMEM] * 3,
        out_specs=VMEM,
        compiler_params=PARAMS,
        name="gate",
    )(pair, in_gain.reshape(1, -1), gate_weight)

    def products(sides, planes_right, places, name):
        count, depth = len(sides), len(planes_right)
        return pl.pallas_call(
            functools.partial(product_kernel, count, depth),
            out_shape=[jax.ShapeDtypeStruct((part, rows, 2 * rows * depth), BF16)] * (2 * count),
            in_specs=[SMEM] + [VMEM] * (PIECES * (count + depth)),
            out_specs=[VMEM] * (2 * count),
            scratch_shapes=[pltpu.VMEM((part, 2 * rows * depth, 2 * toks), BF16)],
            compiler_params=PARAMS,
            name=name,
        )(places, *[x for side in sides for x in side], *[x for side in planes_right for x in side])

    inner = z - own_half * half
    far = planes - 1 - z
    far_inner = far - far // half * half
    steps = jnp.arange(half)
    places_own = jnp.concatenate([y[None], (inner - steps) % half]).astype(jnp.int32)
    places_far = jnp.concatenate([y[None], (far_inner - steps) % half]).astype(jnp.int32)
    near = products([lefts], own, places_own, "near")
    away = products([lefts, outer], other, places_far, "away")

    own_set = [near[0]] + [send(near[r // 2], back_own(r)) for r in range(1, PIECES)]
    end_set = [send(away[2 + r // 2], back_end(r)) for r in range(PIECES)]
    far_set = [away[0]] + [send(away[r // 2], back_other(r)) for r in range(1, PIECES)]

    return pl.pallas_call(
        update_kernel,
        out_shape=jax.ShapeDtypeStruct((rows, toks, channels), BF16),
        in_specs=[SMEM, VMEM, VMEM, VMEM] + [ANY] * (3 * PIECES),
        out_specs=VMEM,
        scratch_shapes=[
            pltpu.VMEM((PIECES, part, rows, toks), BF16),
            pltpu.VMEM((toks // LANES, rows * hidden, LANES), F32),
            pltpu.SemaphoreType.DMA((PIECES,)),
        ],
        compiler_params=PARAMS,
        name="update",
    )(where, out_gain.reshape(-1, 1), out_weight, gate, *own_set, *far_set, *end_set)


def solution(mesh):
    placed = (
        P(("groups", "row"), "chan", None),
        P(("groups", "row"), "chan"),
        P(),
        P(),
        P(),
        P(),
        P(),
    )
    return jax.shard_map(
        functools.partial(local, n_row=mesh.shape["row"]),
        mesh=mesh,
        in_specs=placed,
        out_specs=P(("groups", "row"), "chan", None),
        check_vma=False,
    )
```

```python
import functools

import jax
import jax.numpy as jnp
from jax import lax
from jax.experimental import pallas as pl
from jax.experimental.pallas import tpu as pltpu
from jax.sharding import PartitionSpec as P

F32, BF16 = jnp.float32, jnp.bfloat16
LANES = 128
LIMIT = 40 * 1024 * 1024
NT = (((1,), (1,)), ((), ()))
TN = (((0,), (0,)), ((), ()))
SMEM = pl.BlockSpec(memory_space=pltpu.SMEM)
VMEM = pl.BlockSpec(memory_space=pltpu.VMEM)
PARAMS = pltpu.CompilerParams(vmem_limit_bytes=LIMIT)


def normalise(x, gain):
    mean = jnp.mean(x, axis=-1, keepdims=True)
    centered = x - mean
    var = jnp.mean(centered * centered, axis=-1, keepdims=True)
    return (centered * lax.rsqrt(var + 1e-05) * gain).astype(BF16)


def operands_kernel(merge, where, pair, mask, gain, weight, *rest):
    before = rest[:4] if merge else ()
    rest = rest[len(before) :]
    outs, held, turned, chosen = rest[:4], rest[4:6], rest[6], rest[7]
    rows, toks, _ = pair.shape
    hidden = weight.shape[1] // 4
    part = hidden // 4
    pitch = rows + 1
    turned[...] = weight[...].T
    for n in range(4):
        for p in range(2):
            start = pl.multiple_of(n * hidden + (where[0] ^ (2 * p)) * part, part)
            half = 0.5 if n % 2 == 0 else 1.0
            chosen[(2 * n + p) * part : (2 * n + p + 1) * part, :] = turned[pl.ds(start, part), :] * half
    group = 4

    @pl.loop(0, rows // group)
    def _(at):
        first = at * group
        x = pair[pl.ds(first, group)].astype(F32).reshape(group * toks, -1)
        normed = normalise(x, gain[...])
        proj = lax.dot_general(chosen[...], normed, NT, preferred_element_type=F32)
        for g in range(group):
            valid = mask[pl.ds(first + g, 1), :].astype(F32) * 0.5
            mine = proj[:, g * toks : (g + 1) * toks]
            blocks = [mine[n * 2 * part : (n + 1) * 2 * part] for n in range(4)]
            spot = pl.ds(first + g, 2 * part, stride=pitch)
            for n in range(2):
                value = (jnp.tanh(blocks[2 * n]) + 1.0) * (valid * blocks[2 * n + 1])
                for m in range(toks // LANES):
                    held[n][m, spot, :] = value[:, m * LANES : (m + 1) * LANES]

    base = toks if merge else 0
    for n in range(2):
        for p in range(2):
            out = outs[2 * n + p]
            if merge:
                out[:, :, :toks] = before[2 * n + p][...]
            for m in range(toks // LANES):
                lanes = slice(base + m * LANES, base + (m + 1) * LANES)
                for c in range(part):
                    row = (p * part + c) * pitch
                    out[c, :, lanes] = held[n][m, row : row + rows, :].astype(BF16)


def gate_kernel(pair, gain, weight, out):
    rows, toks, _ = pair.shape
    group = 4

    @pl.loop(0, rows // group)
    def _(at):
        spot = pl.ds(at * group, group)
        x = pair[spot].astype(F32).reshape(group * toks, -1)
        logits = jnp.dot(normalise(x, gain[...]), weight[...], preferred_element_type=F32)
        out[spot] = (0.5 * jnp.tanh(0.5 * logits) + 0.5).reshape(group, toks, -1)


def product_kernel(n_left, n_right, places, *rest):
    lefts = [rest[2 * n : 2 * n + 2] for n in range(n_left)]
    rest = rest[2 * n_left :]
    rights = [rest[2 * n : 2 * n + 2] for n in range(n_right)]
    rest = rest[2 * n_right :]
    outs, held = rest[: 2 * n_left], rest[2 * n_left]
    part, rows, _ = outs[0].shape
    for s in range(n_right):
        for p in range(2):
            start = places[1 + s] * (2 * rows) + (places[0] ^ p) * rows
            held[:, pl.ds(pl.multiple_of(start, rows), rows), :] = rights[s][p][...]
    for c in range(part):
        left = jnp.concatenate([x[c] for side in lefts for x in side], axis=0)
        out = lax.dot_general(left, held[c], NT, preferred_element_type=F32).astype(BF16)
        for n in range(2 * n_left):
            outs[n][c] = out[n * rows : (n + 1) * rows]


def hand_out_kernel(where, near0, near1, far0, far1, end0, end1, *outs):
    near, far, end = (near0, near1), (far0, far1), (end0, end1)
    for r in range(4):
        source = where[2] ^ (r % 2)

        @pl.when(source == 0)
        def _():
            outs[r][...] = near[r // 2][...]

        @pl.when((source == 1) & (where[1] == 0))
        def _():
            outs[r][...] = far[r // 2][...]

        @pl.when((source == 1) & (where[1] == 1))
        def _():
            outs[r][...] = end[r // 2][...]


def update_kernel(where, gain, weight, gate, *rest):
    pieces, out, turned = rest[:-2], rest[-2], rest[-1]
    part = sum(x.shape[0] for x in pieces[::4])
    _, rows, toks = pieces[0].shape
    hidden = 4 * part
    pitch = hidden + 1
    for r in range(4):
        base = (where[0] ^ r) * part
        for piece in pieces[r::4]:
            for c in range(piece.shape[0]):
                value = piece[c].astype(F32)
                for m in range(toks // LANES):
                    turned[m, pl.ds(base + c, rows, stride=pitch), :] = value[
                        :, m * LANES : (m + 1) * LANES
                    ]
            base = base + piece.shape[0]
    scale = jnp.broadcast_to(gain[...], (hidden, toks))

    @pl.loop(0, rows, unroll=8)
    def _(i):
        x = jnp.concatenate(
            [turned[m, pl.ds(i * pitch, hidden), :] for m in range(toks // LANES)], axis=1
        )
        mean = jnp.mean(x, axis=0, keepdims=True)
        centered = x - mean
        var = jnp.mean(centered * centered, axis=0, keepdims=True)
        pnorm = (centered * lax.rsqrt(var + 1e-05) * scale).astype(BF16)
        mapped = lax.dot_general(pnorm, weight[...], TN, preferred_element_type=F32)
        out[i] = (gate[i] * mapped).astype(BF16)


def local(pair, pair_mask, in_gain, proj_weight, gate_weight, out_gain, out_weight, *, n_row):
    rows, toks, channels = pair.shape
    hidden = proj_weight.shape[1] // 4
    part = hidden // 4
    planes = n_row // 2
    half = planes // 2
    row, core = lax.axis_index("row"), lax.axis_index("chan")
    z, y = row // 2, row % 2
    own_half = z // half
    at_end = (z == 0) | (z == planes - 1)
    where = jnp.stack([2 * y + core, at_end, core ^ own_half]).astype(jnp.int32)

    def send(x, target):
        pairs = []
        for source in range(2 * n_row):
            to = target(source // 4, source // 2 % 2, source % 2)
            pairs.append((source, 4 * to[0] + 2 * to[1] + to[2]))
        return lax.ppermute(x, ("row", "chan"), pairs)

    def after(x, *earlier):
        return lax.optimization_barrier((x, *earlier))[0]

    def in_plane(r):
        return lambda p, b, k: (p, b ^ (r // 2), k ^ (r % 2))

    def shifted(s):
        return lambda p, b, k: (p // half * half + (p + s) % half, b, k)

    def mirrored(p, b, k):
        return (p if p in (0, planes - 1) else planes - 1 - p, b, k)

    def edge(p, b, k):
        swap = {0: 1, 1: 0, planes - 1: planes - 2, planes - 2: planes - 1}
        return (swap.get(p, p), b, k)

    gains = in_gain.reshape(1, -1)
    twin, twin_mask = send(pair, in_plane(1)), send(pair_mask, in_plane(1))

    def operands(x, mask, before):
        depth = toks * (2 if before else 1)
        return pl.pallas_call(
            functools.partial(operands_kernel, bool(before)),
            out_shape=[jax.ShapeDtypeStruct((part, rows, depth), BF16)] * 4,
            in_specs=[SMEM] + [VMEM] * (4 + len(before)),
            out_specs=[VMEM] * 4,
            scratch_shapes=[pltpu.VMEM((toks // LANES, 2 * part * (rows + 1), LANES), F32)] * 2
            + [pltpu.VMEM((4 * hidden, channels), BF16), pltpu.VMEM((8 * part, channels), BF16)],
            compiler_params=PARAMS,
            name="operands_b" if before else "operands_a",
        )(where, x, mask, gains, proj_weight, *before)

    mine = operands(pair, pair_mask, [])
    left0, left1, right0, right1 = operands(twin, twin_mask, mine)

    shifts = range(1, half)
    near0 = [right0] + [send(right0, shifted(s)) for s in shifts]
    right1 = send(right1, in_plane(2))
    far0 = [send(right0, mirrored)]
    left1 = send(after(left1, right1), in_plane(2))
    far0 += [send(x, mirrored) for x in near0[1:]]
    outer0 = send(after(left0, near0[-1]), edge)
    near1 = [right1] + [send(right1, shifted(s)) for s in shifts]
    far1 = [send(x, mirrored) for x in near1]
    outer1 = send(left1, edge)

    gate = pl.pallas_call(
        gate_kernel,
        out_shape=jax.ShapeDtypeStruct((rows, toks, channels), F32),
        in_specs=[VMEM] * 3,
        out_specs=VMEM,
        compiler_params=PARAMS,
        name="gate",
    )(pair, gains, gate_weight)

    def products(lefts, rights, places, name):
        span = 2 * rows * len(rights)
        return pl.pallas_call(
            functools.partial(product_kernel, len(lefts), len(rights)),
            out_shape=[jax.ShapeDtypeStruct((part, rows, span), BF16)] * (2 * len(lefts)),
            in_specs=[SMEM] + [VMEM] * (2 * (len(lefts) + len(rights))),
            out_specs=[VMEM] * (2 * len(lefts)),
            scratch_shapes=[pltpu.VMEM((part, span, 2 * toks), BF16)],
            compiler_params=PARAMS,
            name=name,
        )(places, *[x for side in (*lefts, *rights) for x in side])

    steps = jnp.arange(half)
    inner = z % half
    far_inner = (planes - 1 - z) % half
    places_near = jnp.concatenate([y[None], (inner - steps) % half]).astype(jnp.int32)
    places_far = jnp.concatenate([y[None], (far_inner - steps) % half]).astype(jnp.int32)
    near = products([(left0, left1)], list(zip(near0, near1)), places_near, "near")
    away = products(
        [(after(left0, near[0], gate), left1), (outer0, outer1)], list(zip(far0, far1)), places_far, "away"
    )
    ends = [send(x, edge) for x in away[2:]]
    handed = pl.pallas_call(
        hand_out_kernel,
        out_shape=[jax.ShapeDtypeStruct((part, rows, toks), BF16)] * 4,
        in_specs=[SMEM] + [VMEM] * 6,
        out_specs=[VMEM] * 4,
        compiler_params=PARAMS,
        name="hand_out",
    )(where, *near, *away[:2], *ends)
    pieces = [handed[0]] + [send(handed[r], in_plane(r)) for r in range(1, 4)]

    return pl.pallas_call(
        update_kernel,
        out_shape=jax.ShapeDtypeStruct((rows, toks, channels), BF16),
        in_specs=[SMEM] + [VMEM] * (3 + len(pieces)),
        out_specs=VMEM,
        scratch_shapes=[pltpu.VMEM((toks // LANES, rows * (hidden + 1), LANES), F32)],
        compiler_params=PARAMS,
        name="update",
    )(where, out_gain.reshape(-1, 1), out_weight, gate, *pieces)


def solution(mesh):
    placed = (
        P(("groups", "row"), "chan", None),
        P(("groups", "row"), "chan"),
        P(),
        P(),
        P(),
        P(),
        P(),
    )
    return jax.shard_map(
        functools.partial(local, n_row=mesh.shape["row"]),
        mesh=mesh,
        in_specs=placed,
        out_specs=P(("groups", "row"), "chan", None),
        check_vma=False,
    )
```

```python
import functools

import jax
import jax.numpy as jnp
from jax import lax
from jax.experimental import pallas as pl
from jax.experimental.pallas import tpu as pltpu
from jax.sharding import PartitionSpec as P

F32, BF16 = jnp.float32, jnp.bfloat16
LANES = 128
LIMIT = 40 * 1024 * 1024
SHARES = (2, 2)
NT = (((1,), (1,)), ((), ()))
TN = (((0,), (0,)), ((), ()))
SMEM = pl.BlockSpec(memory_space=pltpu.SMEM)
VMEM = pl.BlockSpec(memory_space=pltpu.VMEM)
HBM = pl.BlockSpec(memory_space=pltpu.HBM)
PARAMS = pltpu.CompilerParams(vmem_limit_bytes=LIMIT)
GROUP = 4


def normalise(x, gain):
    mean = jnp.mean(x, axis=-1, keepdims=True)
    centered = x - mean
    var = jnp.mean(centered * centered, axis=-1, keepdims=True)
    return (centered * lax.rsqrt(var + 1e-05) * gain).astype(BF16)


def gated(normed, chosen, mask, first, held):
    toks = mask.shape[1]
    wide = chosen.shape[0] // 2
    rows = mask.shape[0]
    proj = lax.dot_general(chosen[...], normed, NT, preferred_element_type=F32)
    for g in range(normed.shape[0] // toks):
        valid = mask[pl.ds(first + g, 1), :].astype(F32) * 0.5
        mine = proj[:, g * toks : (g + 1) * toks]
        value = (jnp.tanh(mine[:wide]) + 1.0) * (valid * mine[wide:])
        for m in range(toks // LANES):
            spot = pl.ds(first + g, wide, stride=rows + 1)
            held[m, spot, :] = value[:, m * LANES : (m + 1) * LANES]


def write_pieces(outs, held, base):
    row = 0
    for out in outs:
        count, rows, _ = out.shape
        for c in range(count):
            for m in range(held.shape[0]):
                lanes = slice(base + m * LANES, base + (m + 1) * LANES)
                out[c, :, lanes] = held[m, row : row + rows, :].astype(BF16)
            row += rows + 1


def right_own_kernel(where, pair, mask, gain, weight, *rest):
    outs, (normed_out, chosen_right, chosen_left) = rest[:-11], rest[-11:-8]
    pair_v, mask_v, gain_v, weight_v, turned, held, sem, pair_sem = rest[-8:]
    rows, toks, _ = pair_v.shape
    hidden = weight_v.shape[1] // 4
    part = hidden // 4
    parts = pair_sem.shape[0]
    each = rows // parts
    small = [
        pltpu.make_async_copy(a, b, sem.at[n])
        for n, (a, b) in enumerate(((weight, weight_v), (mask, mask_v), (gain, gain_v)))
    ]
    large = [
        pltpu.make_async_copy(
            pair.at[pl.ds(n * each, each)], pair_v.at[pl.ds(n * each, each)], pair_sem.at[n]
        )
        for n in range(parts)
    ]
    for copy in small + large:
        copy.start()
    for copy in small:
        copy.wait()
    turned[...] = weight_v[...].T
    for n in range(4):
        chosen = chosen_left if n < 2 else chosen_right
        half = 0.5 if n % 2 == 0 else 1.0
        for p in range(2):
            start = pl.multiple_of(n * hidden + (where[0] ^ (2 * p)) * part, part)
            at = (2 * (n % 2) + p) * part
            chosen[at : at + part, :] = turned[pl.ds(start, part), :] * half
    for n in range(parts):
        large[n].wait()

        @pl.loop(0, each // GROUP)
        def _(at):
            first = n * each + at * GROUP
            x = pair_v[pl.ds(first, GROUP)].astype(F32).reshape(GROUP * toks, -1)
            normed = normalise(x, gain_v[...])
            normed_out[pl.ds(first * toks, GROUP * toks), :] = normed
            gated(normed, chosen_right, mask_v, first, held)

    write_pieces(outs, held, 0)


def right_twin_kernel(pair, mask, gain, chosen, *rest):
    count = (len(rest) - 2) // 2
    before, outs, normed_out, held = rest[:count], rest[count:-2], rest[-2], rest[-1]
    rows, toks, _ = pair.shape
    for x, out in zip(before, outs):
        out[:, :, :toks] = x[...]

    @pl.loop(0, rows // GROUP)
    def _(at):
        first = at * GROUP
        x = pair[pl.ds(first, GROUP)].astype(F32).reshape(GROUP * toks, -1)
        normed = normalise(x, gain[...])
        normed_out[pl.ds(first * toks, GROUP * toks), :] = normed
        gated(normed, chosen, mask, first, held)

    write_pieces(outs, held, toks)


def left_kernel(normed0, normed1, mask0, mask1, chosen, *rest):
    outs, held = rest[:-1], rest[-1]
    rows, toks = mask0.shape
    for n, (normed, mask) in enumerate(((normed0, mask0), (normed1, mask1))):

        @pl.loop(0, rows // GROUP)
        def _(at):
            first = at * GROUP
            gated(normed[pl.ds(first * toks, GROUP * toks), :], chosen, mask, first, held)

        write_pieces(outs, held, n * toks)


def gate_kernel(normed, weight, out):
    rows, toks, _ = out.shape

    @pl.loop(0, rows // GROUP)
    def _(at):
        x = normed[pl.ds(at * GROUP * toks, GROUP * toks), :]
        logits = jnp.dot(x, weight[...], preferred_element_type=F32)
        out[pl.ds(at * GROUP, GROUP)] = (0.5 * jnp.tanh(0.5 * logits) + 0.5).reshape(GROUP, toks, -1)


def merge_kernel(start, own, neighbour, out):
    rows = own.shape[1]
    own_at = pl.multiple_of(start[0] * rows, rows)
    out[:, pl.ds(own_at, rows), :] = own[...]
    out[:, pl.ds(rows - own_at, rows), :] = neighbour[...]


def product_kernel(n_left, n_right, places, *rest):
    lefts, rights = rest[:n_left], rest[n_left : n_left + n_right]
    outs, held = rest[n_left + n_right : -1], rest[-1]
    count, span, _ = lefts[0].shape
    for s in range(n_right):
        held[:, pl.ds(pl.multiple_of(places[s] * span, span), span), :] = rights[s][...]
    for c in range(count):
        left = jnp.concatenate([x[c] for x in lefts], axis=0)
        out = lax.dot_general(left, held[c], NT, preferred_element_type=F32).astype(BF16)
        for n in range(n_left):
            outs[n][c] = out[n * span : (n + 1) * span]


def hand_out_kernel(where, near, far, end, *outs):
    rows = outs[0].shape[1]
    for r in range(4):
        source = where[2] ^ (r % 2)
        span = slice((r // 2) * rows, (r // 2 + 1) * rows)

        @pl.when(source == 0)
        def _():
            outs[r][...] = near[:, span, :]

        @pl.when((source == 1) & (where[1] == 0))
        def _():
            outs[r][...] = far[:, span, :]

        @pl.when((source == 1) & (where[1] == 1))
        def _():
            outs[r][...] = end[:, span, :]


def update_kernel(where, gain, weight, gate, *rest):
    pieces, out, turned = rest[:-2], rest[-2], rest[-1]
    part = sum(x.shape[0] for x in pieces[::4])
    _, rows, toks = pieces[0].shape
    hidden = 4 * part
    pitch = hidden + 1
    for r in range(4):
        base = (where[0] ^ r) * part
        for piece in pieces[r::4]:
            for c in range(piece.shape[0]):
                value = piece[c].astype(F32)
                for m in range(toks // LANES):
                    turned[m, pl.ds(base + c, rows, stride=pitch), :] = value[
                        :, m * LANES : (m + 1) * LANES
                    ]
            base = base + piece.shape[0]
    scale = jnp.broadcast_to(gain[...], (hidden, toks))

    @pl.loop(0, rows, unroll=8)
    def _(i):
        x = jnp.concatenate(
            [turned[m, pl.ds(i * pitch, hidden), :] for m in range(toks // LANES)], axis=1
        )
        mean = jnp.mean(x, axis=0, keepdims=True)
        centered = x - mean
        var = jnp.mean(centered * centered, axis=0, keepdims=True)
        pnorm = (centered * lax.rsqrt(var + 1e-05) * scale).astype(BF16)
        mapped = lax.dot_general(pnorm, weight[...], TN, preferred_element_type=F32)
        out[i] = (gate[i] * mapped).astype(BF16)


def kernel(body, name, out_shape, in_specs, scratch=()):
    outs = jax.tree.map(lambda _: VMEM, out_shape)
    return pl.pallas_call(
        body,
        out_shape=out_shape,
        in_specs=in_specs,
        out_specs=outs,
        scratch_shapes=list(scratch),
        compiler_params=PARAMS,
        name=name,
    )


def local(pair, pair_mask, in_gain, proj_weight, gate_weight, out_gain, out_weight, *, n_row):
    rows, toks, channels = pair.shape
    hidden = proj_weight.shape[1] // 4
    part = hidden // 4
    planes = n_row // 2
    half = planes // 2
    counts = [part * share // sum(SHARES) for share in SHARES]
    groups = range(len(counts))
    row, core = lax.axis_index("row"), lax.axis_index("chan")
    z, y = row // 2, row % 2
    own_half = z // half
    at_end = (z == 0) | (z == planes - 1)
    where = jnp.stack([2 * y + core, at_end, core ^ own_half]).astype(jnp.int32)
    start = y[None].astype(jnp.int32)
    zero = jnp.zeros((1,), jnp.int32)

    def send(x, target):
        pairs = []
        for source in range(2 * n_row):
            to = target(source // 4, source // 2 % 2, source % 2)
            pairs.append((source, 4 * to[0] + 2 * to[1] + to[2]))
        return lax.ppermute(x, ("row", "chan"), pairs)

    def after(x, *earlier):
        return lax.optimization_barrier((x, *earlier))[0]

    def in_plane(r):
        return lambda p, b, k: (p, b ^ (r // 2), k ^ (r % 2))

    def shifted(s):
        return lambda p, b, k: (p // half * half + (p + s) % half, b, k)

    def mirrored(p, b, k):
        return (p if p in (0, planes - 1) else planes - 1 - p, b, k)

    def edge(p, b, k):
        swap = {0: 1, 1: 0, planes - 1: planes - 2, planes - 2: planes - 1}
        return (swap.get(p, p), b, k)

    gains = in_gain.reshape(1, -1)
    twin, twin_mask = send(pair, in_plane(1)), send(pair_mask, in_plane(1))

    def piece(count, height, depth):
        return jax.ShapeDtypeStruct((count, height, depth), BF16)

    held = pltpu.VMEM((toks // LANES, 2 * part * (rows + 1), LANES), F32)
    rows_all = jax.ShapeDtypeStruct((rows * toks, channels), BF16)
    weights = jax.ShapeDtypeStruct((4 * part, channels), BF16)
    copies = 4
    *mine, normed0, chosen_right, chosen_left = kernel(
        right_own_kernel,
        "right_own",
        [piece(count, rows, toks) for _ in range(2) for count in counts] + [rows_all, weights, weights],
        [SMEM] + [HBM] * 4,
        [
            pltpu.VMEM(pair.shape, BF16),
            pltpu.VMEM(pair_mask.shape, pair_mask.dtype),
            pltpu.VMEM(gains.shape, F32),
            pltpu.VMEM(proj_weight.shape, BF16),
            pltpu.VMEM((4 * hidden, channels), BF16),
            held,
            pltpu.SemaphoreType.DMA((3,)),
            pltpu.SemaphoreType.DMA((copies,)),
        ],
    )(where, pair, pair_mask, gains, proj_weight)
    whole = [piece(count, rows, 2 * toks) for _ in range(2) for count in counts]
    *right, normed1 = kernel(
        right_twin_kernel, "right_twin", whole + [rows_all], [VMEM] * (4 + len(mine)), [held]
    )(twin, twin_mask, gains, chosen_right, *mine)
    right0, right1 = list(right[: len(counts)]), list(right[len(counts) :])
    right1[0] = send(right1[0], in_plane(2))
    left = kernel(left_kernel, "left", whole, [VMEM] * 5, [held])(
        normed0, normed1, pair_mask, twin_mask, chosen_left
    )
    left0, left1 = list(left[: len(counts)]), list(left[len(counts) :])
    gate = kernel(
        gate_kernel, "gate", jax.ShapeDtypeStruct((rows, toks, channels), F32), [VMEM] * 2
    )(normed0, gate_weight)

    def merge(own, neighbour, at, name):
        shape = piece(own.shape[0], 2 * rows, 2 * toks)
        return kernel(merge_kernel, name, shape, [SMEM, VMEM, VMEM])(at, own, neighbour)

    def products(lefts, rights, places, name):
        span = 2 * rows * len(rights)
        count = lefts[0].shape[0]
        return kernel(
            functools.partial(product_kernel, len(lefts), len(rights)),
            name,
            [piece(count, 2 * rows, span)] * len(lefts),
            [SMEM] + [VMEM] * (len(lefts) + len(rights)),
            [pltpu.VMEM((count, span, 2 * toks), BF16)],
        )(places, *lefts, *rights)

    steps = jnp.arange(half)
    places_near = ((z - steps) % half).astype(jnp.int32)
    places_far = ((planes - 1 - z - steps) % half).astype(jnp.int32)
    done_y, done_z, done = [right1[0]], [], [gate]
    pieces = []
    for g in groups:
        if g:
            right1[g] = send(after(right1[g], *done_y), in_plane(2))
            done_y = [right1[g]]
        left1[g] = send(after(left1[g], *done_y), in_plane(2))
        done_y = [left1[g]]
        own = merge(right0[g], right1[g], start, "merge_right")
        own = after(own, *done_z)
        far = [send(own, mirrored)]
        near = [own] + [send(own, shifted(s)) for s in range(1, half)]
        far += [send(x, mirrored) for x in near[1:]]
        left = merge(left0[g], left1[g], zero, "merge_left")
        done_z = [far[0], near[-1], left]
        outer = send(after(left, near[-1]), edge)
        (close,) = products([left], near, places_near, "near")
        away, ends = products([after(left, close, *done), outer], far, places_far, "away")
        ends = send(ends, edge)
        handed = kernel(
            hand_out_kernel,
            "hand_out",
            [piece(counts[g], rows, toks)] * 4,
            [SMEM] + [VMEM] * 3,
        )(where, close, away, ends)
        done = [handed[0]] + [send(handed[r], in_plane(r)) for r in range(1, 4)]
        pieces += done

    return kernel(
        update_kernel,
        "update",
        jax.ShapeDtypeStruct((rows, toks, channels), BF16),
        [SMEM] + [VMEM] * (3 + len(pieces)),
        [pltpu.VMEM((toks // LANES, rows * (hidden + 1), LANES), F32)],
    )(where, out_gain.reshape(-1, 1), out_weight, gate, *pieces)


def solution(mesh):
    placed = (
        P(("groups", "row"), "chan", None),
        P(("groups", "row"), "chan"),
        P(),
        P(),
        P(),
        P(),
        P(),
    )
    return jax.shard_map(
        functools.partial(local, n_row=mesh.shape["row"]),
        mesh=mesh,
        in_specs=placed,
        out_specs=P(("groups", "row"), "chan", None),
        check_vma=False,
    )
```

```python
import functools

import jax
import jax.numpy as jnp
from jax import lax
from jax.experimental import pallas as pl
from jax.experimental.pallas import tpu as pltpu
from jax.sharding import PartitionSpec as P

F32, BF16 = jnp.float32, jnp.bfloat16
LANES = 128
LIMIT = 40 * 1024 * 1024
SHARES = (5, 3)
NT = (((1,), (1,)), ((), ()))
TN = (((0,), (0,)), ((), ()))
SMEM = pl.BlockSpec(memory_space=pltpu.SMEM)
VMEM = pl.BlockSpec(memory_space=pltpu.VMEM)
HBM = pl.BlockSpec(memory_space=pltpu.HBM)
PARAMS = pltpu.CompilerParams(vmem_limit_bytes=LIMIT)
GROUP = 4


def normalise(x, gain):
    mean = jnp.mean(x, axis=-1, keepdims=True)
    centered = x - mean
    var = jnp.mean(centered * centered, axis=-1, keepdims=True)
    return (centered * lax.rsqrt(var + 1e-05) * gain).astype(BF16)


def gated(normed, chosen, mask, first, held):
    toks = mask.shape[1]
    wide = chosen.shape[0] // 2
    rows = mask.shape[0]
    proj = lax.dot_general(chosen[...], normed, NT, preferred_element_type=F32)
    for g in range(normed.shape[0] // toks):
        valid = mask[pl.ds(first + g, 1), :].astype(F32) * 0.5
        mine = proj[:, g * toks : (g + 1) * toks]
        value = (jnp.tanh(mine[:wide]) + 1.0) * (valid * mine[wide:])
        for m in range(toks // LANES):
            spot = pl.ds(first + g, wide, stride=rows + 1)
            held[m, spot, :] = value[:, m * LANES : (m + 1) * LANES]


def write_pieces(outs, held, base):
    row = 0
    for out in outs:
        count, rows, _ = out.shape
        for c in range(count):
            for m in range(held.shape[0]):
                lanes = slice(base + m * LANES, base + (m + 1) * LANES)
                out[c, :, lanes] = held[m, row : row + rows, :].astype(BF16)
            row += rows + 1


def right_own_kernel(where, pair, mask, gain, weight, *rest):
    outs, (normed_out, chosen_right, chosen_left) = rest[:-11], rest[-11:-8]
    pair_v, mask_v, gain_v, weight_v, turned, held, sem, pair_sem = rest[-8:]
    rows, toks, _ = pair_v.shape
    hidden = weight_v.shape[1] // 4
    part = hidden // 4
    parts = pair_sem.shape[0]
    each = rows // parts
    small = [
        pltpu.make_async_copy(a, b, sem.at[n])
        for n, (a, b) in enumerate(((weight, weight_v), (mask, mask_v), (gain, gain_v)))
    ]
    large = [
        pltpu.make_async_copy(
            pair.at[pl.ds(n * each, each)], pair_v.at[pl.ds(n * each, each)], pair_sem.at[n]
        )
        for n in range(parts)
    ]
    for copy in small + large:
        copy.start()
    for copy in small:
        copy.wait()
    turned[...] = weight_v[...].T
    for n in range(4):
        chosen = chosen_left if n < 2 else chosen_right
        half = 0.5 if n % 2 == 0 else 1.0
        for p in range(2):
            start = pl.multiple_of(n * hidden + (where[0] ^ (2 * p)) * part, part)
            at = (2 * (n % 2) + p) * part
            chosen[at : at + part, :] = turned[pl.ds(start, part), :] * half
    for n in range(parts):
        large[n].wait()

        @pl.loop(0, each // GROUP)
        def _(at):
            first = n * each + at * GROUP
            x = pair_v[pl.ds(first, GROUP)].astype(F32).reshape(GROUP * toks, -1)
            normed = normalise(x, gain_v[...])
            normed_out[pl.ds(first * toks, GROUP * toks), :] = normed
            gated(normed, chosen_right, mask_v, first, held)

    write_pieces(outs, held, 0)


def right_twin_kernel(pair, mask, gain, chosen, *rest):
    count = (len(rest) - 2) // 2
    before, outs, normed_out, held = rest[:count], rest[count:-2], rest[-2], rest[-1]
    rows, toks, _ = pair.shape
    for x, out in zip(before, outs):
        out[:, :, :toks] = x[...]

    @pl.loop(0, rows // GROUP)
    def _(at):
        first = at * GROUP
        x = pair[pl.ds(first, GROUP)].astype(F32).reshape(GROUP * toks, -1)
        normed = normalise(x, gain[...])
        normed_out[pl.ds(first * toks, GROUP * toks), :] = normed
        gated(normed, chosen, mask, first, held)

    write_pieces(outs, held, toks)


def left_kernel(normed0, normed1, mask0, mask1, chosen, *rest):
    outs, held = rest[:-1], rest[-1]
    rows, toks = mask0.shape
    for n, (normed, mask) in enumerate(((normed0, mask0), (normed1, mask1))):

        @pl.loop(0, rows // GROUP)
        def _(at):
            first = at * GROUP
            gated(normed[pl.ds(first * toks, GROUP * toks), :], chosen, mask, first, held)

        write_pieces(outs, held, n * toks)


def gate_kernel(normed, weight, out):
    rows, toks, _ = out.shape

    @pl.loop(0, rows // GROUP)
    def _(at):
        x = normed[pl.ds(at * GROUP * toks, GROUP * toks), :]
        logits = jnp.dot(x, weight[...], preferred_element_type=F32)
        out[pl.ds(at * GROUP, GROUP)] = (0.5 * jnp.tanh(0.5 * logits) + 0.5).reshape(GROUP, toks, -1)


def product_kernel(first, n_left, n_right, places, *rest):
    lefts = [rest[2 * n : 2 * n + 2] for n in range(n_left)]
    rest = rest[2 * n_left :]
    rights = [rest[2 * n : 2 * n + 2] for n in range(n_right)]
    outs, held = rest[2 * n_right : -1], rest[-1]
    count, span, _ = outs[0].shape
    rows = span // 2
    for s in range(n_right):
        for p in range(2):
            start = pl.multiple_of(places[1 + s] * span + (places[0] ^ p) * rows, rows)
            part = rights[s][p][...] if p else rights[s][p][first : first + count]
            held[:, pl.ds(start, rows), :] = part
    for c in range(count):
        left = jnp.concatenate([x for own, other in lefts for x in (own[first + c], other[c])], axis=0)
        out = lax.dot_general(left, held[c], NT, preferred_element_type=F32).astype(BF16)
        for n in range(n_left):
            outs[n][c] = out[n * span : (n + 1) * span]


def hand_out_kernel(where, near, far, end, *outs):
    rows = outs[0].shape[1]
    for r in range(4):
        source = where[2] ^ (r % 2)
        span = slice((r // 2) * rows, (r // 2 + 1) * rows)

        @pl.when(source == 0)
        def _():
            outs[r][...] = near[:, span, :]

        @pl.when((source == 1) & (where[1] == 0))
        def _():
            outs[r][...] = far[:, span, :]

        @pl.when((source == 1) & (where[1] == 1))
        def _():
            outs[r][...] = end[:, span, :]


def update_kernel(where, gain, weight, gate, *rest):
    pieces, out, turned = rest[:-2], rest[-2], rest[-1]
    part = sum(x.shape[0] for x in pieces[::4])
    _, rows, toks = pieces[0].shape
    hidden = 4 * part
    pitch = hidden + 1
    for r in range(4):
        base = (where[0] ^ r) * part
        for piece in pieces[r::4]:
            for c in range(piece.shape[0]):
                value = piece[c].astype(F32)
                for m in range(toks // LANES):
                    turned[m, pl.ds(base + c, rows, stride=pitch), :] = value[
                        :, m * LANES : (m + 1) * LANES
                    ]
            base = base + piece.shape[0]
    scale = jnp.broadcast_to(gain[...], (hidden, toks))

    @pl.loop(0, rows, unroll=8)
    def _(i):
        x = jnp.concatenate(
            [turned[m, pl.ds(i * pitch, hidden), :] for m in range(toks // LANES)], axis=1
        )
        mean = jnp.mean(x, axis=0, keepdims=True)
        centered = x - mean
        var = jnp.mean(centered * centered, axis=0, keepdims=True)
        pnorm = (centered * lax.rsqrt(var + 1e-05) * scale).astype(BF16)
        mapped = lax.dot_general(pnorm, weight[...], TN, preferred_element_type=F32)
        out[i] = (gate[i] * mapped).astype(BF16)


def kernel(body, name, out_shape, in_specs, scratch=()):
    outs = jax.tree.map(lambda _: VMEM, out_shape)
    return pl.pallas_call(
        body,
        out_shape=out_shape,
        in_specs=in_specs,
        out_specs=outs,
        scratch_shapes=list(scratch),
        compiler_params=PARAMS,
        name=name,
    )


def local(pair, pair_mask, in_gain, proj_weight, gate_weight, out_gain, out_weight, *, n_row):
    rows, toks, channels = pair.shape
    hidden = proj_weight.shape[1] // 4
    part = hidden // 4
    planes = n_row // 2
    half = planes // 2
    counts = [part * share // sum(SHARES) for share in SHARES]
    groups = range(len(counts))
    row, core = lax.axis_index("row"), lax.axis_index("chan")
    z, y = row // 2, row % 2
    own_half = z // half
    at_end = (z == 0) | (z == planes - 1)
    where = jnp.stack([2 * y + core, at_end, core ^ own_half]).astype(jnp.int32)

    def send(x, target):
        pairs = []
        for source in range(2 * n_row):
            to = target(source // 4, source // 2 % 2, source % 2)
            pairs.append((source, 4 * to[0] + 2 * to[1] + to[2]))
        return lax.ppermute(x, ("row", "chan"), pairs)

    def after(x, *earlier):
        return lax.optimization_barrier((x, *earlier))[0]

    def in_plane(r):
        return lambda p, b, k: (p, b ^ (r // 2), k ^ (r % 2))

    def shifted(s):
        return lambda p, b, k: (p // half * half + (p + s) % half, b, k)

    def mirrored(p, b, k):
        return (p, b, 1 - k) if p in (0, planes - 1) else (planes - 1 - p, b, k)

    def edge(p, b, k):
        swap = {0: 1, 1: 0, planes - 1: planes - 2, planes - 2: planes - 1}
        return (swap[p], b, k) if p in swap else (p, b, 1 - k)

    gains = in_gain.reshape(1, -1)
    twin, twin_mask = send(pair, in_plane(1)), send(pair_mask, in_plane(1))

    def piece(count, height, depth):
        return jax.ShapeDtypeStruct((count, height, depth), BF16)

    held = pltpu.VMEM((toks // LANES, 2 * part * (rows + 1), LANES), F32)
    rows_all = jax.ShapeDtypeStruct((rows * toks, channels), BF16)
    weights = jax.ShapeDtypeStruct((4 * part, channels), BF16)
    copies = 4
    *mine, normed0, chosen_right, chosen_left = kernel(
        right_own_kernel,
        "right_own",
        [piece(count, rows, toks) for count in (part, *counts)] + [rows_all, weights, weights],
        [SMEM] + [HBM] * 4,
        [
            pltpu.VMEM(pair.shape, BF16),
            pltpu.VMEM(pair_mask.shape, pair_mask.dtype),
            pltpu.VMEM(gains.shape, F32),
            pltpu.VMEM(proj_weight.shape, BF16),
            pltpu.VMEM((4 * hidden, channels), BF16),
            held,
            pltpu.SemaphoreType.DMA((3,)),
            pltpu.SemaphoreType.DMA((copies,)),
        ],
    )(where, pair, pair_mask, gains, proj_weight)
    whole = [piece(count, rows, 2 * toks) for count in (part, *counts)]
    *right, normed1 = kernel(
        right_twin_kernel, "right_twin", whole + [rows_all], [VMEM] * (4 + len(mine)), [held]
    )(twin, twin_mask, gains, chosen_right, *mine)
    right0, right1 = right[0], list(right[1:])
    queues = {"y": [], "end": [], "mid": []}

    def queued(link, x, target, window=2, also=()):
        done = queues[link]
        early = done[len(done) - window :][:1] if len(done) >= window else []
        done.append(send(after(x, *early, *also), target))
        return done[-1]

    def shift_all(x, link, target):
        return [x] + [queued(link, x, target(s)) for s in range(1, half)]

    far0 = [queued("mid", right0, mirrored)]
    near0 = shift_all(right0, "end", shifted)
    right1[0] = queued("y", right1[0], in_plane(2), 1)
    left = kernel(left_kernel, "left", whole, [VMEM] * 5, [held])(
        normed0, normed1, pair_mask, twin_mask, chosen_left
    )
    left0, left1 = left[0], list(left[1:])
    far0 += [queued("mid", x, mirrored) for x in near0[1:]]
    outer0 = queued("end", left0, edge)
    left1[0] = queued("y", left1[0], in_plane(2), 1)
    for g in groups[1:]:
        right1[g] = queued("y", right1[g], in_plane(2), 1)
        left1[g] = queued("y", left1[g], in_plane(2), 1)
    gate = kernel(
        gate_kernel, "gate", jax.ShapeDtypeStruct((rows, toks, channels), F32), [VMEM] * 2
    )(normed0, gate_weight)

    def products(first, lefts, rights, places, name):
        span = 2 * rows * len(rights)
        count = lefts[0][1].shape[0]
        return kernel(
            functools.partial(product_kernel, first, len(lefts), len(rights)),
            name,
            [piece(count, 2 * rows, span)] * len(lefts),
            [SMEM] + [VMEM] * (2 * (len(lefts) + len(rights))),
            [pltpu.VMEM((count, span, 2 * toks), BF16)],
        )(places, *[x for pairs in (*lefts, *rights) for x in pairs])

    steps = jnp.arange(half)
    places_near = jnp.concatenate([y[None], (z - steps) % half]).astype(jnp.int32)
    places_far = jnp.concatenate([y[None], (planes - 1 - z - steps) % half]).astype(jnp.int32)
    near1, far1, outer1 = [], [], []
    for g in groups:
        far = [queued("mid", right1[g], mirrored)]
        near1.append(shift_all(right1[g], "end", shifted))
        far1.append(far + [queued("mid", x, mirrored) for x in near1[g][1:]])
        outer1.append(queued("end", left1[g], edge))
    done, pieces, first = [gate], [], 0
    for g in groups:
        crossed = [x[g + 1] for x in (right1, left1) if g < groups[-1]]
        moved = [x[g + 1][n] for x, n in ((far1, 0), (near1, -1)) if g < groups[-1]]
        mine = (left0, after(left1[g], *crossed))
        (close,) = products(first, [mine], list(zip(near0, near1[g])), places_near, "near")
        mine = (left0, after(left1[g], close, *done))
        away, ends = products(
            first, [mine, (outer0, outer1[g])], list(zip(far0, far1[g])), places_far, "away"
        )
        ends = after(send(ends, edge), *moved)
        handed = kernel(
            hand_out_kernel,
            "hand_out",
            [piece(counts[g], rows, toks)] * 4,
            [SMEM] + [VMEM] * 3,
        )(where, close, away, ends)
        done = [handed[0]] + [send(handed[r], in_plane(r)) for r in range(1, 4)]
        pieces += done
        first += counts[g]

    return kernel(
        update_kernel,
        "update",
        jax.ShapeDtypeStruct((rows, toks, channels), BF16),
        [SMEM] + [VMEM] * (3 + len(pieces)),
        [pltpu.VMEM((toks // LANES, rows * (hidden + 1), LANES), F32)],
    )(where, out_gain.reshape(-1, 1), out_weight, gate, *pieces)


def solution(mesh):
    placed = (
        P(("groups", "row"), "chan", None),
        P(("groups", "row"), "chan"),
        P(),
        P(),
        P(),
        P(),
        P(),
    )
    return jax.shard_map(
        functools.partial(local, n_row=mesh.shape["row"]),
        mesh=mesh,
        in_specs=placed,
        out_specs=P(("groups", "row"), "chan", None),
        check_vma=False,
    )
```

```python
import functools
import math

import jax
import jax.numpy as jnp
from jax import lax
from jax.experimental import pallas as pl
from jax.experimental.pallas import tpu as pltpu
from jax.sharding import PartitionSpec as P

F32, BF16 = jnp.float32, jnp.bfloat16
LANES = 128
SPARE = 6 * 1024 * 1024
SHARES = (4, 4)
NT = (((1,), (1,)), ((), ()))
TN = (((0,), (0,)), ((), ()))
SMEM = pl.BlockSpec(memory_space=pltpu.SMEM)
VMEM = pl.BlockSpec(memory_space=pltpu.VMEM)
GROUP = 4
UNROLL = 2


def normalise(x, gain):
    mean = jnp.mean(x, axis=-1, keepdims=True)
    centered = x - mean
    var = jnp.mean(centered * centered, axis=-1, keepdims=True)
    return (centered * lax.rsqrt(var + 1e-05) * gain).astype(BF16)


def gated(normed, chosen, valid, first, held):
    toks = valid.shape[1]
    wide = chosen.shape[0] // 2
    rows = valid.shape[0]
    proj = lax.dot_general(chosen[...], normed, NT, preferred_element_type=F32)
    for g in range(normed.shape[0] // toks):
        mine = proj[:, g * toks : (g + 1) * toks]
        value = (jnp.tanh(mine[:wide]) + 1.0) * (valid[pl.ds(first + g, 1), :] * mine[wide:])
        for m in range(toks // LANES):
            spot = pl.ds(first + g, wide, stride=rows + 1)
            held[m, spot, :] = value[:, m * LANES : (m + 1) * LANES]


def write_pieces(outs, held, base):
    row = 0
    for out in outs:
        count, rows, _ = out.shape
        for c in range(count):
            for m in range(held.shape[0]):
                lanes = slice(base + m * LANES, base + (m + 1) * LANES)
                out[c, :, lanes] = held[m, row : row + rows, :].astype(BF16)
            row += rows + 1


def right_rows(pair, valid, gain, chosen, normed_out, held):
    rows, toks, _ = pair.shape

    @pl.loop(0, rows // GROUP, unroll=UNROLL)
    def _(at):
        first = at * GROUP
        x = pair[pl.ds(first, GROUP)].astype(F32).reshape(GROUP * toks, -1)
        normed = normalise(x, gain[0:1, :])
        normed_out[pl.ds(first * toks, GROUP * toks), :] = normed
        gated(normed, chosen, valid, first, held)


def right_own_kernel(where, pair, valid, gain, weight, *rest):
    *outs, normed_out, chosen_right, chosen_left, turned, held = rest
    hidden = weight.shape[1] // 4
    part = hidden // 4
    turned[...] = weight[...].T
    for n in range(4):
        chosen = chosen_left if n < 2 else chosen_right
        for p in range(2):
            start = pl.multiple_of(n * hidden + (where[0] ^ (2 * p)) * part, part)
            at = (2 * (n % 2) + p) * part
            chosen[at : at + part, :] = turned[pl.ds(start, part), :]
    right_rows(pair, valid, gain, chosen_right, normed_out, held)
    write_pieces(outs, held, 0)


def right_twin_kernel(pair, valid, gain, chosen, *rest):
    count = (len(rest) - 2) // 2
    before, outs, normed_out, held = rest[:count], rest[count:-2], rest[-2], rest[-1]
    for x, out in zip(before, outs):
        out[:, :, : x.shape[2]] = x[...]
    right_rows(pair, valid, gain, chosen, normed_out, held)
    write_pieces(outs, held, pair.shape[1])


def left_kernel(normed0, normed1, valid0, valid1, chosen, *rest):
    outs, held = rest[:-1], rest[-1]
    rows, toks = valid0.shape
    for n, (normed, valid) in enumerate(((normed0, valid0), (normed1, valid1))):

        @pl.loop(0, rows // GROUP, unroll=UNROLL)
        def _(at):
            first = at * GROUP
            gated(normed[pl.ds(first * toks, GROUP * toks), :], chosen, valid, first, held)

        write_pieces(outs, held, n * toks)


def gate_kernel(normed, weight, out):
    rows, toks, _ = out.shape

    @pl.loop(0, rows // GROUP, unroll=UNROLL)
    def _(at):
        x = normed[pl.ds(at * GROUP * toks, GROUP * toks), :]
        logits = jnp.dot(x, weight[...], preferred_element_type=F32)
        out[pl.ds(at * GROUP, GROUP)] = (0.5 * jnp.tanh(0.5 * logits) + 0.5).reshape(GROUP, toks, -1)


def product_kernel(first, n_left, n_right, places, *rest):
    lefts = [rest[2 * n : 2 * n + 2] for n in range(n_left)]
    rest = rest[2 * n_left :]
    rights = [rest[2 * n : 2 * n + 2] for n in range(n_right)]
    outs, held = rest[2 * n_right : -1], rest[-1]
    count, span, _ = outs[0].shape
    rows = span // 2
    for s in range(n_right):
        for p in range(2):
            start = pl.multiple_of(places[1 + s] * span + (places[0] ^ p) * rows, rows)
            held[:, pl.ds(start, rows), :] = rights[s][p][first : first + count]
    for c in range(count):
        left = jnp.concatenate([x[first + c] for side in lefts for x in side], axis=0)
        out = lax.dot_general(left, held[c], NT, preferred_element_type=F32).astype(BF16)
        for n in range(n_left):
            outs[n][c] = out[n * span : (n + 1) * span]


def hand_out_kernel(first, where, near, far, end, *outs):
    count, rows, _ = outs[0].shape
    for r in range(4):
        source = where[2] ^ (r % 2)
        span = slice((r // 2) * rows, (r // 2 + 1) * rows)

        @pl.when(source == 0)
        def _():
            outs[r][...] = near[first : first + count, span, :]

        @pl.when((source == 1) & (where[1] == 0))
        def _():
            outs[r][...] = far[:, span, :]

        @pl.when((source == 1) & (where[1] == 1))
        def _():
            outs[r][...] = end[:, span, :]


def update_kernel(where, scale, weight, gate, *rest):
    pieces, out, turned = rest[:-2], rest[-2], rest[-1]
    part = sum(x.shape[0] for x in pieces[::4])
    _, rows, toks = pieces[0].shape
    hidden = 4 * part
    pitch = hidden + 1
    for r in range(4):
        base = (where[0] ^ r) * part
        for piece in pieces[r::4]:
            for c in range(piece.shape[0]):
                value = piece[c].astype(F32)
                for m in range(toks // LANES):
                    turned[m, pl.ds(base + c, rows, stride=pitch), :] = value[
                        :, m * LANES : (m + 1) * LANES
                    ]
            base = base + piece.shape[0]

    @pl.loop(0, rows, unroll=8)
    def _(i):
        x = jnp.concatenate(
            [turned[m, pl.ds(i * pitch, hidden), :] for m in range(toks // LANES)], axis=1
        )
        mean = jnp.mean(x, axis=0, keepdims=True)
        centered = x - mean
        var = jnp.mean(centered * centered, axis=0, keepdims=True)
        pnorm = (centered * lax.rsqrt(var + 1e-05) * scale[...]).astype(BF16)
        mapped = lax.dot_general(pnorm, weight[...], TN, preferred_element_type=F32)
        out[i] = (gate[i] * mapped).astype(BF16)


def kernel(body, name, out_shape, in_specs, scratch=()):
    outs = jax.tree.map(lambda _: VMEM, out_shape)

    def call(*args):
        arrays = [*args, *jax.tree.leaves(out_shape), *scratch]
        size = sum(x.dtype.itemsize * math.prod(x.shape) for x in arrays)
        return pl.pallas_call(
            body,
            out_shape=out_shape,
            in_specs=in_specs,
            out_specs=outs,
            scratch_shapes=list(scratch),
            compiler_params=pltpu.CompilerParams(vmem_limit_bytes=size + SPARE),
            name=name,
        )(*args)

    return call


def local(pair, pair_mask, in_gain, proj_weight, gate_weight, out_gain, out_weight, *, n_row):
    rows, toks, channels = pair.shape
    hidden = proj_weight.shape[1] // 4
    part = hidden // 4
    planes = n_row // 2
    half = planes // 2
    counts = [part * share // sum(SHARES) for share in SHARES]
    groups = range(len(counts))
    row, core = lax.axis_index("row"), lax.axis_index("chan")
    z, y = row // 2, row % 2
    own_half = z // half
    at_end = (z == 0) | (z == planes - 1)
    where = jnp.stack([2 * y + core, at_end, core ^ own_half]).astype(jnp.int32)

    def send(x, target, name):
        pairs = []
        for source in range(2 * n_row):
            to = target(source // 4, source // 2 % 2, source % 2)
            pairs.append((source, 4 * to[0] + 2 * to[1] + to[2]))
        with jax.named_scope(name):
            return lax.ppermute(x, ("row", "chan"), pairs)

    def after(x, *earlier):
        return lax.optimization_barrier((x, *earlier))[0]

    def in_plane(r):
        return lambda p, b, k: (p, b ^ (r // 2), k ^ (r % 2))

    def shifted(s):
        return lambda p, b, k: (p // half * half + (p + s) % half, b, k)

    def mirrored(p, b, k):
        return (p, b, 1 - k) if p in (0, planes - 1) else (planes - 1 - p, b, k)

    def edge(p, b, k):
        swap = {0: 1, 1: 0, planes - 1: planes - 2, planes - 2: planes - 1}
        return (swap[p], b, k) if p in swap else (p, b, 1 - k)

    gains = jnp.broadcast_to(in_gain, (8, channels))
    scales = jnp.broadcast_to(out_gain[:, None], (hidden, toks))
    halves = jnp.where(jnp.arange(4 * hidden) // hidden % 2 == 0, 0.5, 1.0).astype(BF16)
    weight = proj_weight * halves
    valid = pair_mask.astype(F32) * 0.5
    twin, twin_valid = send(pair, in_plane(1), "pair"), send(valid, in_plane(1), "valid")

    def piece(count, height, depth):
        return jax.ShapeDtypeStruct((count, height, depth), BF16)

    held = pltpu.VMEM((toks // LANES, 2 * part * (rows + 1), LANES), F32)
    rows_all = jax.ShapeDtypeStruct((rows * toks, channels), BF16)
    weights = jax.ShapeDtypeStruct((4 * part, channels), BF16)
    *mine, normed0, chosen_right, chosen_left = kernel(
        right_own_kernel,
        "right_own",
        [piece(part, rows, toks) for _ in range(2)] + [rows_all, weights, weights],
        [SMEM] + [VMEM] * 4,
        [pltpu.VMEM((4 * hidden, channels), BF16), held],
    )(where, pair, valid, gains, weight)
    whole = [piece(part, rows, 2 * toks) for _ in range(2)]
    *right, normed1 = kernel(
        right_twin_kernel, "right_twin", whole + [rows_all], [VMEM] * (4 + len(mine)), [held]
    )(twin, twin_valid, gains, chosen_right, *mine)
    queues = {"mid": [], "end": []}

    def queued(link, name, x, target):
        done = queues[link]
        done.append(send(after(x, *done[:-1][-1:]), target, name))
        return done[-1]

    def near_far(x, name):
        near = [x] + [queued("end", f"end_{name}", x, shifted(s)) for s in range(1, half)]
        return near, [queued("mid", f"mid_{name}", x, mirrored)]

    right0, right1 = right
    near0, far0 = near_far(right0, "right_0")
    right1 = send(right1, in_plane(2), "cross_right")
    left0, left1 = kernel(left_kernel, "left", whole, [VMEM] * 5, [held])(
        normed0, normed1, valid, twin_valid, chosen_left
    )
    near1, far1 = near_far(after(right1, left0), "right_1")
    left1 = send(after(left1, right1), in_plane(2), "cross_left")
    gate = kernel(
        gate_kernel, "gate", jax.ShapeDtypeStruct((rows, toks, channels), F32), [VMEM] * 2
    )(normed0, gate_weight)
    far0 += [queued("mid", "mid_next_0", x, mirrored) for x in near0[1:]]
    outer0 = queued("end", "end_left_0", after(left0, gate), edge)
    far1 += [queued("mid", "mid_next_1", x, mirrored) for x in near1[1:]]
    outer1 = queued("end", "end_left_1", left1, edge)

    def products(first, count, lefts, rights, places, name):
        span = 2 * rows * len(rights)
        return kernel(
            functools.partial(product_kernel, first, len(lefts), len(rights)),
            name,
            [piece(count, 2 * rows, span)] * len(lefts),
            [SMEM] + [VMEM] * (2 * (len(lefts) + len(rights))),
            [pltpu.VMEM((count, span, 2 * toks), BF16)],
        )(places, *[x for pairs in (*lefts, *rights) for x in pairs])

    steps = jnp.arange(half)
    places_near = jnp.concatenate([y[None], (z - steps) % half]).astype(jnp.int32)
    places_far = jnp.concatenate([y[None], (planes - 1 - z - steps) % half]).astype(jnp.int32)
    (near,) = products(0, part, [(left0, left1)], list(zip(near0, near1)), places_near, "near")
    starts = [sum(counts[:g]) for g in groups]
    done, far, ends = [near], [], []
    for g in groups:
        sides = [(after(left0, *done), left1), (outer0, outer1)]
        away, end = products(starts[g], counts[g], sides, list(zip(far0, far1)), places_far, "away")
        ends.append(send(end, edge, f"products_back_{g}"))
        far.append(away)
        done = [away]
    pieces = []
    for g in groups:
        handed = kernel(
            functools.partial(hand_out_kernel, starts[g]),
            "hand_out",
            [piece(counts[g], rows, toks)] * 4,
            [SMEM] + [VMEM] * 3,
        )(where, near, far[g], ends[g])
        pieces += [handed[0]] + [
            send(handed[r], in_plane(r), f"return_{g}{r}") for r in range(1, 4)
        ]

    return kernel(
        update_kernel,
        "update",
        jax.ShapeDtypeStruct((rows, toks, channels), BF16),
        [SMEM] + [VMEM] * (3 + len(pieces)),
        [pltpu.VMEM((toks // LANES, rows * (hidden + 1), LANES), F32)],
    )(where, scales, out_weight, gate, *pieces)


def solution(mesh):
    placed = (
        P(("groups", "row"), "chan", None),
        P(("groups", "row"), "chan"),
        P(),
        P(),
        P(),
        P(),
        P(),
    )
    return jax.shard_map(
        functools.partial(local, n_row=mesh.shape["row"]),
        mesh=mesh,
        in_specs=placed,
        out_specs=P(("groups", "row"), "chan", None),
        check_vma=False,
    )
```

```python
import functools
import math

import jax
import jax.numpy as jnp
from jax import lax
from jax.experimental import pallas as pl
from jax.experimental.pallas import tpu as pltpu
from jax.sharding import PartitionSpec as P

F32, BF16 = jnp.float32, jnp.bfloat16
LANES = 128
SPARE = 6 * 1024 * 1024
SHARES = (4, 4)
NT = (((1,), (1,)), ((), ()))
TN = (((0,), (0,)), ((), ()))
SMEM = pl.BlockSpec(memory_space=pltpu.SMEM)
VMEM = pl.BlockSpec(memory_space=pltpu.VMEM)
GROUP = 4
UNROLL = 2


def normalise(x, gain):
    mean = jnp.mean(x, axis=-1, keepdims=True)
    centered = x - mean
    var = jnp.mean(centered * centered, axis=-1, keepdims=True)
    return (centered * lax.rsqrt(var + 1e-05) * gain).astype(BF16)


def gated(normed, chosen, valid, first, held):
    _, rows, toks = valid.shape
    wide = chosen.shape[0] // 2
    proj = lax.dot_general(chosen[...], normed, NT, preferred_element_type=F32)
    for g in range(normed.shape[0] // toks):
        mine = proj[:, g * toks : (g + 1) * toks]
        value = (jnp.tanh(mine[:wide]) + 1.0) * (valid[0, pl.ds(first + g, 1), :] * mine[wide:])
        for m in range(toks // LANES):
            spot = pl.ds(first + g, wide, stride=rows + 1)
            held[m, spot, :] = value[:, m * LANES : (m + 1) * LANES]


def write_pieces(outs, held, base):
    row = 0
    for out in outs:
        count, rows, _ = out.shape
        for c in range(count):
            for m in range(held.shape[0]):
                lanes = slice(base + m * LANES, base + (m + 1) * LANES)
                out[c, :, lanes] = held[m, row : row + rows, :].astype(BF16)
            row += rows + 1


def right_rows(pair, valid, gain, chosen, normed_out, held):
    rows, toks, _ = pair.shape

    @pl.loop(0, rows // GROUP, unroll=UNROLL)
    def _(at):
        first = at * GROUP
        x = pair[pl.ds(first, GROUP)].astype(F32).reshape(GROUP * toks, -1)
        normed = normalise(x, gain[0:1, :])
        normed_out[pl.ds(first * toks, GROUP * toks), :] = normed
        gated(normed, chosen, valid, first, held)


def right_own_kernel(where, pair, packed, *rest):
    *outs, normed_out, chosen_right, chosen_left, valid, gain, turned, held = rest
    rows, toks, channels = pair.shape
    hidden = packed.shape[1] // 4
    part = hidden // 4
    turned[...] = packed[:channels, :].astype(BF16).T
    valid[0] = packed[channels : channels + rows, :toks] * 0.5
    gain[...] = packed[channels + rows :, :channels]
    for n in range(4):
        chosen = chosen_left if n < 2 else chosen_right
        half = 0.5 if n % 2 == 0 else 1.0
        for p in range(2):
            start = pl.multiple_of(n * hidden + (where[0] ^ (2 * p)) * part, part)
            at = (2 * (n % 2) + p) * part
            chosen[at : at + part, :] = turned[pl.ds(start, part), :] * half
    right_rows(pair, valid, gain, chosen_right, normed_out, held)
    write_pieces(outs, held, 0)


def right_twin_kernel(pair, mask, gain, chosen, *rest):
    count = (len(rest) - 3) // 2
    before, (*outs, normed_out, valid, held) = rest[:count], rest[count:]
    for x, out in zip(before, outs):
        out[:, :, : x.shape[2]] = x[...]
    valid[0] = mask[...].astype(F32) * 0.5
    right_rows(pair, valid, gain, chosen, normed_out, held)
    write_pieces(outs, held, pair.shape[1])


def left_kernel(normed0, normed1, valid0, valid1, chosen, *rest):
    outs, held = rest[:-1], rest[-1]
    _, rows, toks = valid0.shape
    for n, (normed, valid) in enumerate(((normed0, valid0), (normed1, valid1))):

        @pl.loop(0, rows // GROUP, unroll=UNROLL)
        def _(at):
            first = at * GROUP
            gated(normed[pl.ds(first * toks, GROUP * toks), :], chosen, valid, first, held)

        write_pieces(outs, held, n * toks)


def gate_kernel(normed, weight, out):
    rows, toks, _ = out.shape

    @pl.loop(0, rows // GROUP, unroll=UNROLL)
    def _(at):
        x = normed[pl.ds(at * GROUP * toks, GROUP * toks), :]
        logits = jnp.dot(x, weight[...], preferred_element_type=F32)
        out[pl.ds(at * GROUP, GROUP)] = (0.5 * jnp.tanh(0.5 * logits) + 0.5).reshape(GROUP, toks, -1)


def product_kernel(first, n_left, n_right, places, *rest):
    lefts = [rest[2 * n : 2 * n + 2] for n in range(n_left)]
    rest = rest[2 * n_left :]
    rights = [rest[2 * n : 2 * n + 2] for n in range(n_right)]
    outs, held = rest[2 * n_right : -1], rest[-1]
    count, span, _ = outs[0].shape
    rows = span // 2
    for s in range(n_right):
        for p in range(2):
            start = pl.multiple_of(places[1 + s] * span + (places[0] ^ p) * rows, rows)
            part = rights[s][p][...] if p else rights[s][p][first : first + count]
            held[:, pl.ds(start, rows), :] = part
    for c in range(count):
        left = jnp.concatenate([x for own, other in lefts for x in (own[first + c], other[c])], axis=0)
        out = lax.dot_general(left, held[c], NT, preferred_element_type=F32).astype(BF16)
        for n in range(n_left):
            outs[n][c] = out[n * span : (n + 1) * span]


def hand_out_kernel(where, near, far, end, *outs):
    rows = outs[0].shape[1]
    for r in range(4):
        source = where[2] ^ (r % 2)
        span = slice((r // 2) * rows, (r // 2 + 1) * rows)

        @pl.when(source == 0)
        def _():
            outs[r][...] = near[:, span, :]

        @pl.when((source == 1) & (where[1] == 0))
        def _():
            outs[r][...] = far[:, span, :]

        @pl.when((source == 1) & (where[1] == 1))
        def _():
            outs[r][...] = end[:, span, :]


def update_kernel(where, scale, weight, gate, *rest):
    pieces, out, turned = rest[:-2], rest[-2], rest[-1]
    part = sum(x.shape[0] for x in pieces[::4])
    _, rows, toks = pieces[0].shape
    hidden = 4 * part
    pitch = hidden + 1
    for r in range(4):
        base = (where[0] ^ r) * part
        for piece in pieces[r::4]:
            for c in range(piece.shape[0]):
                value = piece[c].astype(F32)
                for m in range(toks // LANES):
                    turned[m, pl.ds(base + c, rows, stride=pitch), :] = value[
                        :, m * LANES : (m + 1) * LANES
                    ]
            base = base + piece.shape[0]

    @pl.loop(0, rows, unroll=8)
    def _(i):
        x = jnp.concatenate(
            [turned[m, pl.ds(i * pitch, hidden), :] for m in range(toks // LANES)], axis=1
        )
        mean = jnp.mean(x, axis=0, keepdims=True)
        centered = x - mean
        var = jnp.mean(centered * centered, axis=0, keepdims=True)
        pnorm = (centered * lax.rsqrt(var + 1e-05) * scale[...]).astype(BF16)
        mapped = lax.dot_general(pnorm, weight[...], TN, preferred_element_type=F32)
        out[i] = (gate[i] * mapped).astype(BF16)


def kernel(body, name, out_shape, in_specs, scratch=()):
    outs = jax.tree.map(lambda _: VMEM, out_shape)

    def call(*args):
        arrays = [*args, *jax.tree.leaves(out_shape), *scratch]
        size = sum(x.dtype.itemsize * math.prod(x.shape) for x in arrays)
        return pl.pallas_call(
            body,
            out_shape=out_shape,
            in_specs=in_specs,
            out_specs=outs,
            scratch_shapes=list(scratch),
            compiler_params=pltpu.CompilerParams(vmem_limit_bytes=size + SPARE),
            name=name,
        )(*args)

    return call


def local(pair, pair_mask, in_gain, proj_weight, gate_weight, out_gain, out_weight, *, n_row):
    rows, toks, channels = pair.shape
    hidden = proj_weight.shape[1] // 4
    part = hidden // 4
    planes = n_row // 2
    half = planes // 2
    counts = [part * share // sum(SHARES) for share in SHARES]
    groups = range(len(counts))
    row, core = lax.axis_index("row"), lax.axis_index("chan")
    z, y = row // 2, row % 2
    own_half = z // half
    at_end = (z == 0) | (z == planes - 1)
    where = jnp.stack([2 * y + core, at_end, core ^ own_half]).astype(jnp.int32)

    def send(x, target, name):
        pairs = []
        for source in range(2 * n_row):
            to = target(source // 4, source // 2 % 2, source % 2)
            pairs.append((source, 4 * to[0] + 2 * to[1] + to[2]))
        with jax.named_scope(name):
            return lax.ppermute(x, ("row", "chan"), pairs)

    def after(x, *earlier):
        return lax.optimization_barrier((x, *earlier))[0]

    def in_plane(r):
        return lambda p, b, k: (p, b ^ (r // 2), k ^ (r % 2))

    def shifted(s):
        return lambda p, b, k: (p // half * half + (p + s) % half, b, k)

    def mirrored(p, b, k):
        return (p, b, 1 - k) if p in (0, planes - 1) else (planes - 1 - p, b, k)

    def edge(p, b, k):
        swap = {0: 1, 1: 0, planes - 1: planes - 2, planes - 2: planes - 1}
        return (swap[p], b, k) if p in swap else (p, b, 1 - k)

    scales = jnp.broadcast_to(out_gain[:, None], (hidden, toks))
    wide = 4 * hidden
    packed = (
        jnp.pad(proj_weight.astype(F32), ((0, rows + 8), (0, 0)))
        + jnp.pad(pair_mask.astype(F32), ((channels, 8), (0, wide - toks)))
        + jnp.pad(in_gain[None], ((channels + rows, 7), (0, wide - channels)))
    )
    twin, twin_mask = send(pair, in_plane(1), "pair"), send(pair_mask, in_plane(1), "mask")

    def piece(count, height, depth):
        return jax.ShapeDtypeStruct((count, height, depth), BF16)

    held = pltpu.VMEM((toks // LANES, 2 * part * (rows + 1), LANES), F32)
    rows_all = jax.ShapeDtypeStruct((rows * toks, channels), BF16)
    weights = jax.ShapeDtypeStruct((4 * part, channels), BF16)
    valid_shape = jax.ShapeDtypeStruct((1, rows, toks), F32)
    gain_shape = jax.ShapeDtypeStruct((8, channels), F32)
    *mine, normed0, chosen_right, chosen_left, valid, gain = kernel(
        right_own_kernel,
        "right_own",
        [piece(count, rows, toks) for count in (part, *counts)]
        + [rows_all, weights, weights, valid_shape, gain_shape],
        [SMEM, VMEM, VMEM],
        [pltpu.VMEM((4 * hidden, channels), BF16), held],
    )(where, pair, packed)
    whole = [piece(count, rows, 2 * toks) for count in (part, *counts)]
    *right, normed1, twin_valid = kernel(
        right_twin_kernel,
        "right_twin",
        whole + [rows_all, valid_shape],
        [VMEM] * (4 + len(mine)),
        [held],
    )(twin, twin_mask, gain, chosen_right, *mine)
    right0, right1 = right[0], list(right[1:])
    queues = {"y": [], "end": [], "mid": []}

    def queued(link, name, x, target, window=3, also=()):
        done = queues[link]
        early = done[len(done) - window :][:1] if len(done) >= window else []
        done.append(send(after(x, *early, *also), target, name))
        return done[-1]

    def shift_all(x, name):
        return [x] + [queued("end", name, x, shifted(s)) for s in range(1, half)]

    far0 = [queued("mid", "mid_own_0", right0, mirrored)]
    near0 = shift_all(right0, "end_right_0")
    right1[0] = queued("y", "cross_right_0", right1[0], in_plane(2), 1)
    left = kernel(left_kernel, "left", whole, [VMEM] * 5, [held])(
        normed0, normed1, valid, twin_valid, chosen_left
    )
    left0, left1 = left[0], list(left[1:])
    for g in groups[1:]:
        right1[g] = queued("y", f"cross_right_{g}", after(right1[g], left0), in_plane(2), 1)
    for g in groups:
        left1[g] = queued("y", f"cross_left_{g}", left1[g], in_plane(2), 1)
    far1, near1 = [], []
    for g in groups:
        far1.append([queued("mid", f"mid_own_1{g}", right1[g], mirrored)])
        near1.append(shift_all(right1[g], f"end_right_1{g}"))
    far0 += [queued("mid", "mid_next_0", x, mirrored) for x in near0[1:]]
    outer0 = queued("end", "end_left_0", left0, edge)
    gate = kernel(
        gate_kernel, "gate", jax.ShapeDtypeStruct((rows, toks, channels), F32), [VMEM] * 2
    )(normed0, gate_weight)
    def products(first, lefts, rights, places, name):
        span = 2 * rows * len(rights)
        count = lefts[0][1].shape[0]
        return kernel(
            functools.partial(product_kernel, first, len(lefts), len(rights)),
            name,
            [piece(count, 2 * rows, span)] * len(lefts),
            [SMEM] + [VMEM] * (2 * (len(lefts) + len(rights))),
            [pltpu.VMEM((count, span, 2 * toks), BF16)],
        )(places, *[x for pairs in (*lefts, *rights) for x in pairs])

    steps = jnp.arange(half)
    places_near = jnp.concatenate([y[None], (z - steps) % half]).astype(jnp.int32)
    places_far = jnp.concatenate([y[None], (planes - 1 - z - steps) % half]).astype(jnp.int32)
    outer1, close, first = [], [], 0
    for g in groups:
        far1[g] += [queued("mid", f"mid_next_1{g}", x, mirrored) for x in near1[g][1:]]
        outer1.append(queued("end", f"end_left_1{g}", left1[g], edge))
        close += products(
            first,
            [(after(left0, gate), left1[g])],
            list(zip(near0, near1[g])),
            places_near,
            "near",
        )
        first += counts[g]
    done, pieces, first = close, [], 0
    for g in groups:
        mine = (left0, after(left1[g], *done))
        away, ends = products(
            first, [mine, (outer0, outer1[g])], list(zip(far0, far1[g])), places_far, "away"
        )
        ends = send(ends, edge, f"products_back_{g}")
        handed = kernel(
            hand_out_kernel,
            "hand_out",
            [piece(counts[g], rows, toks)] * 4,
            [SMEM] + [VMEM] * 3,
        )(where, close[g], away, ends)
        done = [away]
        pieces += [handed[0]] + [
            send(handed[r], in_plane(r), f"return_{g}{r}") for r in range(1, 4)
        ]
        first += counts[g]

    return kernel(
        update_kernel,
        "update",
        jax.ShapeDtypeStruct((rows, toks, channels), BF16),
        [SMEM] + [VMEM] * (3 + len(pieces)),
        [pltpu.VMEM((toks // LANES, rows * (hidden + 1), LANES), F32)],
    )(where, scales, out_weight, gate, *pieces)


def solution(mesh):
    placed = (
        P(("groups", "row"), "chan", None),
        P(("groups", "row"), "chan"),
        P(),
        P(),
        P(),
        P(),
        P(),
    )
    return jax.shard_map(
        functools.partial(local, n_row=mesh.shape["row"]),
        mesh=mesh,
        in_specs=placed,
        out_specs=P(("groups", "row"), "chan", None),
        check_vma=False,
    )
```

```python
import functools
import math

import jax
import jax.numpy as jnp
from jax import lax
from jax.experimental import pallas as pl
from jax.experimental.pallas import tpu as pltpu
from jax.sharding import PartitionSpec as P

F32, BF16 = jnp.float32, jnp.bfloat16
LANES = 128
SPARE = 6 * 1024 * 1024
SHARES = (5, 3)
NT = (((1,), (1,)), ((), ()))
TN = (((0,), (0,)), ((), ()))
VMEM = pl.BlockSpec(memory_space=pltpu.VMEM)
GROUP = 4
UNROLL = 2


def place():
    row = lax.axis_index("row")
    return row // 2, row % 2, lax.axis_index("chan")


def normalise(x, gain):
    mean = jnp.mean(x, axis=-1, keepdims=True)
    centered = x - mean
    var = jnp.mean(centered * centered, axis=-1, keepdims=True)
    return (centered * lax.rsqrt(var + 1e-05) * gain).astype(BF16)


def gated(normed, chosen, valid, first, held):
    _, rows, toks = valid.shape
    wide = chosen.shape[0] // 2
    proj = lax.dot_general(chosen[...], normed, NT, preferred_element_type=F32)
    for g in range(normed.shape[0] // toks):
        mine = proj[:, g * toks : (g + 1) * toks]
        value = (jnp.tanh(mine[:wide]) + 1.0) * (valid[0, pl.ds(first + g, 1), :] * mine[wide:])
        for m in range(toks // LANES):
            spot = pl.ds(first + g, wide, stride=rows + 1)
            held[m, spot, :] = value[:, m * LANES : (m + 1) * LANES]


def write_pieces(outs, held, base):
    row = 0
    for out in outs:
        count, rows, _ = out.shape
        for c in range(count):
            for m in range(held.shape[0]):
                lanes = slice(base + m * LANES, base + (m + 1) * LANES)
                out[c, :, lanes] = held[m, row : row + rows, :].astype(BF16)
            row += rows + 1


def right_rows(pair, valid, gain, chosen, normed_out, held):
    rows, toks, _ = pair.shape

    @pl.loop(0, rows // GROUP, unroll=UNROLL)
    def _(at):
        first = at * GROUP
        x = pair[pl.ds(first, GROUP)].astype(F32).reshape(GROUP * toks, -1)
        normed = normalise(x, gain[...])
        normed_out[pl.ds(first * toks, GROUP * toks), :] = normed
        gated(normed, chosen, valid, first, held)


def right_own_kernel(pair, mask, gain, weight, *rest):
    *outs, normed_out, chosen_right, chosen_left, valid, turned, held = rest
    hidden = weight.shape[1] // 4
    part = hidden // 4
    _, y, core = place()
    turned[...] = weight[...].T
    valid[0] = mask[...].astype(F32) * 0.5
    for n in range(4):
        chosen = chosen_left if n < 2 else chosen_right
        half = 0.5 if n % 2 == 0 else 1.0
        for p in range(2):
            start = pl.multiple_of(n * hidden + ((2 * y + core) ^ (2 * p)) * part, part)
            at = (2 * (n % 2) + p) * part
            chosen[at : at + part, :] = turned[pl.ds(start, part), :] * half
    right_rows(pair, valid, gain, chosen_right, normed_out, held)
    write_pieces(outs, held, 0)


def right_twin_kernel(pair, mask, gain, chosen, *rest):
    count = (len(rest) - 3) // 2
    before, (*outs, normed_out, valid, held) = rest[:count], rest[count:]
    for x, out in zip(before, outs):
        out[:, :, : x.shape[2]] = x[...]
    valid[0] = mask[...].astype(F32) * 0.5
    right_rows(pair, valid, gain, chosen, normed_out, held)
    write_pieces(outs, held, pair.shape[1])


def left_kernel(normed0, normed1, valid0, valid1, chosen, *rest):
    outs, held = rest[:-1], rest[-1]
    _, rows, toks = valid0.shape
    for n, (normed, valid) in enumerate(((normed0, valid0), (normed1, valid1))):

        @pl.loop(0, rows // GROUP, unroll=UNROLL)
        def _(at):
            first = at * GROUP
            gated(normed[pl.ds(first * toks, GROUP * toks), :], chosen, valid, first, held)

        write_pieces(outs, held, n * toks)


def gate_kernel(normed, weight, out):
    rows, toks, _ = out.shape

    @pl.loop(0, rows // GROUP, unroll=UNROLL)
    def _(at):
        x = normed[pl.ds(at * GROUP * toks, GROUP * toks), :]
        logits = jnp.dot(x, weight[...], preferred_element_type=F32)
        out[pl.ds(at * GROUP, GROUP)] = (0.5 * jnp.tanh(0.5 * logits) + 0.5).reshape(GROUP, toks, -1)


def merge_kernel(own, neighbour, out):
    rows = own.shape[1]
    out[:, :rows, :] = own[...]
    out[:, rows:, :] = neighbour[...]


def product_kernel(mirror, lefts, rights, *rest):
    count, span, width = rest[sum(lefts) + sum(rights)].shape
    rows = span // 2
    refs = iter(rest)

    def plane(arrays):
        if arrays == 1:
            both = next(refs)
            return [both.at[:, :rows, :], both.at[:, rows:, :]]
        return [next(refs), next(refs)]

    lefts, rights = [plane(n) for n in lefts], [plane(n) for n in rights]
    *outs, held = refs
    half = len(rights)
    z, y, _ = place()
    z = 2 * half - 1 - z if mirror else z
    for s in range(half):
        for p in range(2):
            start = pl.multiple_of((z + half - s) % half * span + (y ^ p) * rows, rows)
            held[:, pl.ds(start, rows), :] = rights[s][p][...]
    for c in range(count):
        left = jnp.concatenate([x[c] for side in lefts for x in side], axis=0)
        out = lax.dot_general(left, held[c], NT, preferred_element_type=F32).astype(BF16)
        for n in range(len(lefts)):
            outs[n][c] = out[n * span : (n + 1) * span]


def hand_out_kernel(planes, near, far, end, *outs):
    _, rows, _ = outs[0].shape
    z, _, core = place()
    at_end = (z == 0) | (z == planes - 1)
    for r in range(4):
        is_near = (core ^ (r % 2)) == z // (planes // 2)
        span = slice((r // 2) * rows, (r // 2 + 1) * rows)

        @pl.when(is_near)
        def _():
            outs[r][...] = near[:, span, :]

        @pl.when(jnp.logical_not(is_near | at_end))
        def _():
            outs[r][...] = far[:, span, :]

        @pl.when(jnp.logical_not(is_near) & at_end)
        def _():
            outs[r][...] = end[:, span, :]


def update_kernel(gain, weight, gate, *rest):
    pieces, out, turned = rest[:-2], rest[-2], rest[-1]
    part = sum(x.shape[0] for x in pieces[::4])
    _, rows, toks = pieces[0].shape
    hidden = 4 * part
    pitch = hidden + 1
    _, y, core = place()
    scale = jnp.broadcast_to(gain[...], (toks, hidden)).T
    for r in range(4):
        base = ((2 * y + core) ^ r) * part
        for piece in pieces[r::4]:
            for c in range(piece.shape[0]):
                value = piece[c].astype(F32)
                for m in range(toks // LANES):
                    turned[m, pl.ds(base + c, rows, stride=pitch), :] = value[
                        :, m * LANES : (m + 1) * LANES
                    ]
            base = base + piece.shape[0]

    @pl.loop(0, rows, unroll=8)
    def _(i):
        x = jnp.concatenate(
            [turned[m, pl.ds(i * pitch, hidden), :] for m in range(toks // LANES)], axis=1
        )
        mean = jnp.mean(x, axis=0, keepdims=True)
        centered = x - mean
        var = jnp.mean(centered * centered, axis=0, keepdims=True)
        pnorm = (centered * lax.rsqrt(var + 1e-05) * scale).astype(BF16)
        mapped = lax.dot_general(pnorm, weight[...], TN, preferred_element_type=F32)
        out[i] = (gate[i] * mapped).astype(BF16)


def kernel(body, name, out_shape, in_specs, scratch=()):
    outs = jax.tree.map(lambda _: VMEM, out_shape)

    def call(*args):
        arrays = [*args, *jax.tree.leaves(out_shape), *scratch]
        size = sum(x.dtype.itemsize * math.prod(x.shape) for x in arrays)
        return pl.pallas_call(
            body,
            out_shape=out_shape,
            in_specs=in_specs,
            out_specs=outs,
            scratch_shapes=list(scratch),
            compiler_params=pltpu.CompilerParams(vmem_limit_bytes=size + SPARE),
            name=name,
        )(*args)

    return call


def local(pair, pair_mask, in_gain, proj_weight, gate_weight, out_gain, out_weight, *, n_row):
    rows, toks, channels = pair.shape
    hidden = proj_weight.shape[1] // 4
    part = hidden // 4
    planes = n_row // 2
    half = planes // 2
    counts = [part * share // sum(SHARES) for share in SHARES]
    groups = range(len(counts))
    def send(x, target, name):
        pairs = []
        for source in range(2 * n_row):
            to = target(source // 4, source // 2 % 2, source % 2)
            if to is not None:
                pairs.append((source, 4 * to[0] + 2 * to[1] + to[2]))
        with jax.named_scope(name):
            return lax.ppermute(x, ("row", "chan"), pairs)

    def after(x, *earlier):
        return lax.optimization_barrier((x, *earlier))[0]

    def in_plane(r):
        return lambda p, b, k: (p, b ^ (r // 2), k ^ (r % 2))

    def shifted(s):
        return lambda p, b, k: (p // half * half + (p + s) % half, b, k)

    def mirrored(p, b, k):
        return (p, b, 1 - k) if p in (0, planes - 1) else (planes - 1 - p, b, k)

    def edge(p, b, k):
        swap = {0: 1, 1: 0, planes - 1: planes - 2, planes - 2: planes - 1}
        return (swap[p], b, k) if p in swap else (p, b, 1 - k)

    def outward(p, b, k):
        return {1: (0, b, k), planes - 2: (planes - 1, b, k)}.get(p)

    gains = in_gain.reshape(1, -1)
    twin, twin_mask = send(pair, in_plane(1), "pair"), send(pair_mask, in_plane(1), "mask")

    def piece(count, height, depth):
        return jax.ShapeDtypeStruct((count, height, depth), BF16)

    held = pltpu.VMEM((toks // LANES, 2 * part * (rows + 1), LANES), F32)
    rows_all = jax.ShapeDtypeStruct((rows * toks, channels), BF16)
    weights = jax.ShapeDtypeStruct((4 * part, channels), BF16)
    valid_shape = jax.ShapeDtypeStruct((1, rows, toks), F32)
    *mine, normed0, chosen_right, chosen_left, valid = kernel(
        right_own_kernel,
        "right_own",
        [piece(count, rows, toks) for count in (*counts, *counts)]
        + [rows_all, weights, weights, valid_shape],
        [VMEM] * 4,
        [pltpu.VMEM((4 * hidden, channels), BF16), held],
    )(pair, pair_mask, gains, proj_weight)
    whole = [piece(count, rows, 2 * toks) for count in (*counts, *counts)]
    *right, normed1, twin_valid = kernel(
        right_twin_kernel,
        "right_twin",
        whole + [rows_all, valid_shape],
        [VMEM] * (4 + len(mine)),
        [held],
    )(twin, twin_mask, gains, chosen_right, *mine)
    right0, right1 = list(right[: len(counts)]), list(right[len(counts) :])
    queues = {"y": [], "end": [], "mid": []}

    def queued(link, name, x, target, window=2, also=()):
        done = queues[link]
        early = done[len(done) - window :][:1] if len(done) >= window else []
        done.append(send(after(x, *early, *also), target, name))
        return done[-1]

    def hops(name, right, left):
        far = [queued("mid", f"mid_own_{name}", right, mirrored)]
        near = [right] + [
            queued("end", f"end_right_{name}", right, shifted(s)) for s in range(1, half)
        ]
        return near, far, left

    def last_hops(name, near, far, left):
        far = far + [queued("mid", f"mid_next_{name}", x, mirrored) for x in near[1:]]
        return near, far, left, queued("end", f"end_left_{name}", left, edge)

    def cross(name, x):
        return queued("y", f"cross_{name}", x, in_plane(2), 1)

    def merge(own, neighbour, name):
        shape = piece(own.shape[0], 2 * rows, 2 * toks)
        return kernel(merge_kernel, name, shape, [VMEM, VMEM])(own, neighbour)

    first0 = hops("00", right0[0], None)
    right1[0] = cross("right_0", right1[0])
    left = kernel(left_kernel, "left", whole, [VMEM] * 5, [held])(
        normed0, normed1, valid, twin_valid, chosen_left
    )
    left0, left1 = list(left[: len(counts)]), list(left[len(counts) :])
    first1 = hops("01", after(right1[0], left0[0]), None)
    left1[0] = cross("left_0", after(left1[0], first0[0][-1], first0[1][0]))
    begun = [[("00", *first0[:2], left0[0]), ("01", *first1[:2], left1[0])]]
    moved = [[last_hops(*begun[0][0])]]
    for g in groups[1:]:
        right1[g] = cross(f"right_{g}", right1[g])
        left1[g] = cross(f"left_{g}", left1[g])
        right = merge(right0[g], right1[g], "merge_right")
        left = merge(left0[g], left1[g], "merge_left")
        begun.append([(f"{g}", *hops(f"{g}", right, left))])
    moved[0].append(last_hops(*begun[0][1]))
    moved += [[last_hops(*x) for x in begun[g]] for g in groups[1:]]
    gate = kernel(
        gate_kernel, "gate", jax.ShapeDtypeStruct((rows, toks, channels), F32), [VMEM] * 2
    )(normed0, gate_weight)

    def products(mirror, lefts, rights, name):
        span = 2 * rows * len(rights)
        count = lefts[0][0].shape[0]
        args = [x for arrays in (*lefts, *rights) for x in arrays]
        return kernel(
            functools.partial(
                product_kernel, mirror, [len(x) for x in lefts], [len(x) for x in rights]
            ),
            name,
            [piece(count, 2 * rows, span)] * len(lefts),
            [VMEM] * len(args),
            [pltpu.VMEM((count, span, 2 * toks), BF16)],
        )(*args)

    done, pieces = [], []
    for g in groups:
        near, far, left, outer = zip(*moved[g])
        (close,) = products(False, [left], list(zip(*near)), "near")
        left = (after(left[0], *done), *left[1:])
        away, ends = products(True, [left, outer], list(zip(*far)), "away")
        ends = send(ends, edge if g == groups[-1] else outward, f"products_back_{g}")
        handed = kernel(
            functools.partial(hand_out_kernel, planes),
            "hand_out",
            [piece(counts[g], rows, toks)] * 4,
            [VMEM] * 3,
        )(close, away, ends)
        got = [handed[0]] + [send(handed[r], in_plane(r), f"return_{g}{r}") for r in range(1, 4)]
        done = got[:2]
        pieces += got

    return kernel(
        update_kernel,
        "update",
        jax.ShapeDtypeStruct((rows, toks, channels), BF16),
        [VMEM] * (3 + len(pieces)),
        [pltpu.VMEM((toks // LANES, rows * (hidden + 1), LANES), F32)],
    )(out_gain.reshape(1, -1), out_weight, gate, *pieces)


def solution(mesh):
    placed = (
        P(("groups", "row"), "chan", None),
        P(("groups", "row"), "chan"),
        P(),
        P(),
        P(),
        P(),
        P(),
    )
    return jax.shard_map(
        functools.partial(local, n_row=mesh.shape["row"]),
        mesh=mesh,
        in_specs=placed,
        out_specs=P(("groups", "row"), "chan", None),
        check_vma=False,
    )
```

```python
import functools
import math

import jax
import jax.numpy as jnp
from jax import lax
from jax.experimental import pallas as pl
from jax.experimental.pallas import tpu as pltpu
from jax.sharding import PartitionSpec as P

F32, BF16 = jnp.float32, jnp.bfloat16
LANES = 128
SPARE = 6 * 1024 * 1024
SHARES = (5, 3)
NT = (((1,), (1,)), ((), ()))
TN = (((0,), (0,)), ((), ()))
VMEM = pl.BlockSpec(memory_space=pltpu.VMEM)
GROUP = 4
UNROLL = 2


def place():
    row = lax.axis_index("row")
    return row // 2, row % 2, lax.axis_index("chan")


def normalise(x, gain):
    mean = jnp.mean(x, axis=-1, keepdims=True)
    centered = x - mean
    var = jnp.mean(centered * centered, axis=-1, keepdims=True)
    return (centered * lax.rsqrt(var + 1e-05) * gain).astype(BF16)


def gated(normed, chosen, valid, first, held):
    _, rows, toks = valid.shape
    wide = chosen.shape[0] // 2
    proj = lax.dot_general(chosen[...], normed, NT, preferred_element_type=F32)
    for g in range(normed.shape[0] // toks):
        mine = proj[:, g * toks : (g + 1) * toks]
        value = (jnp.tanh(mine[:wide]) + 1.0) * (valid[0, pl.ds(first + g, 1), :] * mine[wide:])
        for m in range(toks // LANES):
            spot = pl.ds(first + g, wide, stride=rows + 1)
            held[m, spot, :] = value[:, m * LANES : (m + 1) * LANES]


def write_pieces(outs, held, base):
    row = 0
    for out in outs:
        count, rows, _ = out.shape
        for c in range(count):
            for m in range(held.shape[0]):
                lanes = slice(base + m * LANES, base + (m + 1) * LANES)
                out[c, :, lanes] = held[m, row : row + rows, :].astype(BF16)
            row += rows + 1


def right_rows(pair, valid, gain, chosen, normed_out, held):
    rows, toks, _ = pair.shape

    @pl.loop(0, rows // GROUP, unroll=UNROLL)
    def _(at):
        first = at * GROUP
        x = pair[pl.ds(first, GROUP)].astype(F32).reshape(GROUP * toks, -1)
        normed = normalise(x, gain[...])
        normed_out[pl.ds(first * toks, GROUP * toks), :] = normed
        gated(normed, chosen, valid, first, held)


def right_own_kernel(pair, mask, gain, weight, *rest):
    *outs, normed_out, chosen_right, chosen_left, valid, gain_out, turned, held = rest
    gain_out[...] = gain[...]
    hidden = weight.shape[1] // 4
    part = hidden // 4
    _, y, core = place()
    turned[...] = weight[...].T
    valid[0] = mask[...].astype(F32) * 0.5
    for n in range(4):
        chosen = chosen_left if n < 2 else chosen_right
        half = 0.5 if n % 2 == 0 else 1.0
        for p in range(2):
            start = pl.multiple_of(n * hidden + ((2 * y + core) ^ (2 * p)) * part, part)
            at = (2 * (n % 2) + p) * part
            chosen[at : at + part, :] = turned[pl.ds(start, part), :] * half
    right_rows(pair, valid, gain, chosen_right, normed_out, held)
    write_pieces(outs, held, 0)


def right_twin_kernel(pair, mask, gain, chosen, *rest):
    count = (len(rest) - 3) // 2
    before, (*outs, normed_out, valid, held) = rest[:count], rest[count:]
    for x, out in zip(before, outs):
        out[:, :, : x.shape[2]] = x[...]
    valid[0] = mask[...].astype(F32) * 0.5
    right_rows(pair, valid, gain, chosen, normed_out, held)
    write_pieces(outs, held, pair.shape[1])


def left_kernel(normed0, normed1, valid0, valid1, chosen, *rest):
    outs, held = rest[:-1], rest[-1]
    _, rows, toks = valid0.shape
    for n, (normed, valid) in enumerate(((normed0, valid0), (normed1, valid1))):

        @pl.loop(0, rows // GROUP, unroll=UNROLL)
        def _(at):
            first = at * GROUP
            gated(normed[pl.ds(first * toks, GROUP * toks), :], chosen, valid, first, held)

        write_pieces(outs, held, n * toks)


def gate_kernel(normed, weight, out):
    rows, toks, _ = out.shape

    @pl.loop(0, rows // GROUP, unroll=UNROLL)
    def _(at):
        x = normed[pl.ds(at * GROUP * toks, GROUP * toks), :]
        logits = jnp.dot(x, weight[...], preferred_element_type=F32)
        out[pl.ds(at * GROUP, GROUP)] = (0.5 * jnp.tanh(0.5 * logits) + 0.5).reshape(GROUP, toks, -1)


def merge_kernel(own, neighbour, out):
    rows = own.shape[1]
    out[:, :rows, :] = own[...]
    out[:, rows:, :] = neighbour[...]


def product_kernel(mirror, lefts, rights, *rest):
    count, span, width = rest[sum(lefts) + sum(rights)].shape
    rows = span // 2
    refs = iter(rest)

    def plane(arrays):
        if arrays == 1:
            both = next(refs)
            return [both.at[:, :rows, :], both.at[:, rows:, :]]
        return [next(refs), next(refs)]

    lefts, rights = [plane(n) for n in lefts], [plane(n) for n in rights]
    *outs, held = refs
    half = len(rights)
    z, y, _ = place()
    z = 2 * half - 1 - z if mirror else z
    for s in range(half):
        for p in range(2):
            start = pl.multiple_of((z + half - s) % half * span + (y ^ p) * rows, rows)
            held[:, pl.ds(start, rows), :] = rights[s][p][...]
    for c in range(count):
        left = jnp.concatenate([x[c] for side in lefts for x in side], axis=0)
        out = lax.dot_general(left, held[c], NT, preferred_element_type=F32).astype(BF16)
        for n in range(len(lefts)):
            outs[n][c] = out[n * span : (n + 1) * span]


def hand_out_kernel(planes, near, far, end, *outs):
    _, rows, _ = outs[0].shape
    z, _, core = place()
    at_end = (z == 0) | (z == planes - 1)
    for r in range(4):
        is_near = (core ^ (r % 2)) == z // (planes // 2)
        span = slice((r // 2) * rows, (r // 2 + 1) * rows)

        @pl.when(is_near)
        def _():
            outs[r][...] = near[:, span, :]

        @pl.when(jnp.logical_not(is_near | at_end))
        def _():
            outs[r][...] = far[:, span, :]

        @pl.when(jnp.logical_not(is_near) & at_end)
        def _():
            outs[r][...] = end[:, span, :]


def update_kernel(gain, weight, gate, *rest):
    pieces, out, turned = rest[:-2], rest[-2], rest[-1]
    part = sum(x.shape[0] for x in pieces[::4])
    _, rows, toks = pieces[0].shape
    hidden = 4 * part
    pitch = hidden + 1
    _, y, core = place()
    scale = jnp.broadcast_to(gain[...], (toks, hidden)).T
    for r in range(4):
        base = ((2 * y + core) ^ r) * part
        for piece in pieces[r::4]:
            for c in range(piece.shape[0]):
                value = piece[c].astype(F32)
                for m in range(toks // LANES):
                    turned[m, pl.ds(base + c, rows, stride=pitch), :] = value[
                        :, m * LANES : (m + 1) * LANES
                    ]
            base = base + piece.shape[0]

    @pl.loop(0, rows, unroll=8)
    def _(i):
        x = jnp.concatenate(
            [turned[m, pl.ds(i * pitch, hidden), :] for m in range(toks // LANES)], axis=1
        )
        mean = jnp.mean(x, axis=0, keepdims=True)
        centered = x - mean
        var = jnp.mean(centered * centered, axis=0, keepdims=True)
        pnorm = (centered * lax.rsqrt(var + 1e-05) * scale).astype(BF16)
        mapped = lax.dot_general(pnorm, weight[...], TN, preferred_element_type=F32)
        out[i] = (gate[i] * mapped).astype(BF16)


def kernel(body, name, out_shape, in_specs, scratch=()):
    outs = jax.tree.map(lambda _: VMEM, out_shape)

    def call(*args):
        arrays = [*args, *jax.tree.leaves(out_shape), *scratch]
        size = sum(x.dtype.itemsize * math.prod(x.shape) for x in arrays)
        return pl.pallas_call(
            body,
            out_shape=out_shape,
            in_specs=in_specs,
            out_specs=outs,
            scratch_shapes=list(scratch),
            compiler_params=pltpu.CompilerParams(vmem_limit_bytes=size + SPARE),
            name=name,
        )(*args)

    return call


def local(pair, pair_mask, in_gain, proj_weight, gate_weight, out_gain, out_weight, *, n_row):
    rows, toks, channels = pair.shape
    hidden = proj_weight.shape[1] // 4
    part = hidden // 4
    planes = n_row // 2
    half = planes // 2
    counts = [part * share // sum(SHARES) for share in SHARES]
    groups = range(len(counts))
    def send(x, target, name):
        pairs = []
        for source in range(2 * n_row):
            to = target(source // 4, source // 2 % 2, source % 2)
            if to is not None:
                pairs.append((source, 4 * to[0] + 2 * to[1] + to[2]))
        with jax.named_scope(name):
            return lax.ppermute(x, ("row", "chan"), pairs)

    def after(x, *earlier):
        return lax.optimization_barrier((x, *earlier))[0]

    def in_plane(r):
        return lambda p, b, k: (p, b ^ (r // 2), k ^ (r % 2))

    def shifted(s):
        return lambda p, b, k: (p // half * half + (p + s) % half, b, k)

    def mirrored(p, b, k):
        return (p, b, 1 - k) if p in (0, planes - 1) else (planes - 1 - p, b, k)

    def edge(p, b, k):
        swap = {0: 1, 1: 0, planes - 1: planes - 2, planes - 2: planes - 1}
        return (swap[p], b, k) if p in swap else (p, b, 1 - k)

    def outward(p, b, k):
        return {1: (0, b, k), planes - 2: (planes - 1, b, k)}.get(p)

    gains = in_gain.reshape(1, -1)
    twin, twin_mask = send(pair, in_plane(1), "pair"), send(pair_mask, in_plane(1), "mask")

    def piece(count, height, depth):
        return jax.ShapeDtypeStruct((count, height, depth), BF16)

    held = pltpu.VMEM((toks // LANES, 2 * part * (rows + 1), LANES), F32)
    rows_all = jax.ShapeDtypeStruct((rows * toks, channels), BF16)
    weights = jax.ShapeDtypeStruct((4 * part, channels), BF16)
    valid_shape = jax.ShapeDtypeStruct((1, rows, toks), F32)
    *mine, normed0, chosen_right, chosen_left, valid, gains = kernel(
        right_own_kernel,
        "right_own",
        [piece(count, rows, toks) for count in (*counts, *counts)]
        + [rows_all, weights, weights, valid_shape, gains],
        [VMEM] * 4,
        [pltpu.VMEM((4 * hidden, channels), BF16), held],
    )(pair, pair_mask, gains, proj_weight)
    whole = [piece(count, rows, 2 * toks) for count in (*counts, *counts)]
    *right, normed1, twin_valid = kernel(
        right_twin_kernel,
        "right_twin",
        whole + [rows_all, valid_shape],
        [VMEM] * (4 + len(mine)),
        [held],
    )(twin, twin_mask, gains, chosen_right, *mine)
    right0, right1 = list(right[: len(counts)]), list(right[len(counts) :])

    def mid(name, x, *earlier):
        return send(after(x, *earlier), mirrored, f"mid_{name}")

    def end_right(name, x, *earlier):
        x = after(x, *earlier)
        return [send(x, shifted(s), f"end_right_{name}") for s in range(1, half)]

    def end_left(name, x, *earlier):
        return send(after(x, *earlier), edge, f"end_left_{name}")

    def cross(name, x, *earlier):
        return send(after(x, *earlier), in_plane(2), f"cross_{name}")

    def merge(own, neighbour, name):
        shape = piece(own.shape[0], 2 * rows, 2 * toks)
        return kernel(merge_kernel, name, shape, [VMEM, VMEM])(own, neighbour)

    crossed = cross("right_0", right1[0])
    own0 = mid("own_00", right0[0])
    near0 = end_right("00", right0[0])
    left = kernel(left_kernel, "left", whole, [VMEM] * 5, [held])(
        normed0, normed1, valid, twin_valid, chosen_left
    )
    left0, left1 = list(left[: len(counts)]), list(left[len(counts) :])
    right1[0] = after(crossed, left0[0])
    own1 = mid("own_01", right1[0])
    near1 = end_right("01", right1[0])
    left1[0] = cross("left_0", left1[0], crossed, own0)
    next0 = [mid("next_00", x, own0) for x in near0]
    outer0 = end_left("00", left0[0], near0[-1])
    right1[1] = cross("right_1", right1[1], left1[0], own1)
    next1 = [mid("next_01", x, own1) for x in near1]
    outer1 = end_left("01", left1[0], near1[-1])
    left1[1] = cross("left_1", left1[1], right1[1], next0[-1])
    right = merge(right0[1], right1[1], "merge_right")
    own2 = mid("own_1", right, own1)
    near2 = end_right("1", right, near1[-1])
    left = merge(left0[1], left1[1], "merge_left")
    next2 = [mid("next_1", x, next1[-1]) for x in near2]
    outer2 = end_left("1", left, outer1, own2)
    moved = [
        [
            ([right0[0], *near0], [own0, *next0], left0[0], outer0),
            ([right1[0], *near1], [own1, *next1], left1[0], outer1),
        ],
        [([right, *near2], [own2, *next2], left, outer2)],
    ]
    gate = kernel(
        gate_kernel, "gate", jax.ShapeDtypeStruct((rows, toks, channels), F32), [VMEM] * 2
    )(normed0, gate_weight)

    def products(mirror, lefts, rights, name):
        span = 2 * rows * len(rights)
        count = lefts[0][0].shape[0]
        args = [x for arrays in (*lefts, *rights) for x in arrays]
        return kernel(
            functools.partial(
                product_kernel, mirror, [len(x) for x in lefts], [len(x) for x in rights]
            ),
            name,
            [piece(count, 2 * rows, span)] * len(lefts),
            [VMEM] * len(args),
            [pltpu.VMEM((count, span, 2 * toks), BF16)],
        )(*args)

    done, pieces = [], []
    for g in groups:
        near, far, left, outer = zip(*moved[g])
        (close,) = products(False, [left], list(zip(*near)), "near")
        left = (after(left[0], *done), *left[1:])
        away, ends = products(True, [left, outer], list(zip(*far)), "away")
        ends = send(ends, edge if g == groups[-1] else outward, f"products_back_{g}")
        handed = kernel(
            functools.partial(hand_out_kernel, planes),
            "hand_out",
            [piece(counts[g], rows, toks)] * 4,
            [VMEM] * 3,
        )(close, away, ends)
        got = [handed[0]] + [
            send(handed[r], in_plane(r), f"return_{g}{r}") for r in range(1, 4)
        ]
        done = got
        pieces += got

    return kernel(
        update_kernel,
        "update",
        jax.ShapeDtypeStruct((rows, toks, channels), BF16),
        [VMEM] * (3 + len(pieces)),
        [pltpu.VMEM((toks // LANES, rows * (hidden + 1), LANES), F32)],
    )(out_gain.reshape(1, -1), out_weight, gate, *pieces)


def solution(mesh):
    placed = (
        P(("groups", "row"), "chan", None),
        P(("groups", "row"), "chan"),
        P(),
        P(),
        P(),
        P(),
        P(),
    )
    return jax.shard_map(
        functools.partial(local, n_row=mesh.shape["row"]),
        mesh=mesh,
        in_specs=placed,
        out_specs=P(("groups", "row"), "chan", None),
        check_vma=False,
    )
```

```python
import functools
import math

import jax
import jax.numpy as jnp
from jax import lax
from jax.experimental import pallas as pl
from jax.experimental.pallas import tpu as pltpu
from jax.sharding import PartitionSpec as P

F32, BF16 = jnp.float32, jnp.bfloat16
LANES = 128
SPARE = 6 * 1024 * 1024
SHARES = (4, 4)
NT = (((1,), (1,)), ((), ()))
TN = (((0,), (0,)), ((), ()))
VMEM = pl.BlockSpec(memory_space=pltpu.VMEM)
GROUP = 4
UNROLL = 2


def place():
    row = lax.axis_index("row")
    return row // 2, row % 2, lax.axis_index("chan")


def normalise(x, gain):
    mean = jnp.mean(x, axis=-1, keepdims=True)
    centered = x - mean
    var = jnp.mean(centered * centered, axis=-1, keepdims=True)
    return (centered * lax.rsqrt(var + 1e-05) * gain).astype(BF16)


def gated(normed, chosen, valid, first, held):
    _, rows, toks = valid.shape
    wide = chosen.shape[0] // 2
    proj = lax.dot_general(chosen[...], normed, NT, preferred_element_type=F32)
    for g in range(normed.shape[0] // toks):
        mine = proj[:, g * toks : (g + 1) * toks]
        value = (jnp.tanh(mine[:wide]) + 1.0) * (valid[0, pl.ds(first + g, 1), :] * mine[wide:])
        for m in range(toks // LANES):
            spot = pl.ds(first + g, wide, stride=rows + 1)
            held[m, spot, :] = value[:, m * LANES : (m + 1) * LANES]


def write_pieces(outs, held, base):
    row = 0
    for out in outs:
        count, rows, _ = out.shape
        for c in range(count):
            for m in range(held.shape[0]):
                lanes = slice(base + m * LANES, base + (m + 1) * LANES)
                out[c, :, lanes] = held[m, row : row + rows, :].astype(BF16)
            row += rows + 1


def right_rows(pair, valid, gain, chosen, normed_out, held):
    rows, toks, _ = pair.shape

    @pl.loop(0, rows // GROUP, unroll=UNROLL)
    def _(at):
        first = at * GROUP
        x = pair[pl.ds(first, GROUP)].astype(F32).reshape(GROUP * toks, -1)
        normed = normalise(x, gain[...])
        normed_out[pl.ds(first * toks, GROUP * toks), :] = normed
        gated(normed, chosen, valid, first, held)


def right_own_kernel(pair, mask, gain, weight, *rest):
    *outs, normed_out, chosen_right, chosen_left, valid, gain_out, turned, held = rest
    gain_out[...] = gain[...]
    hidden = weight.shape[1] // 4
    part = hidden // 4
    _, y, core = place()
    turned[...] = weight[...].T
    valid[0] = mask[...].astype(F32) * 0.5
    for n in range(4):
        chosen = chosen_left if n < 2 else chosen_right
        half = 0.5 if n % 2 == 0 else 1.0
        for p in range(2):
            start = pl.multiple_of(n * hidden + ((2 * y + core) ^ (2 * p)) * part, part)
            at = (2 * (n % 2) + p) * part
            chosen[at : at + part, :] = turned[pl.ds(start, part), :] * half
    right_rows(pair, valid, gain, chosen_right, normed_out, held)
    write_pieces(outs, held, 0)


def right_twin_kernel(pair, mask, gain, chosen, *rest):
    count = (len(rest) - 3) // 2
    before, (*outs, normed_out, valid, held) = rest[:count], rest[count:]
    for x, out in zip(before, outs):
        out[:, :, : x.shape[2]] = x[...]
    valid[0] = mask[...].astype(F32) * 0.5
    right_rows(pair, valid, gain, chosen, normed_out, held)
    write_pieces(outs, held, pair.shape[1])


def left_kernel(normed0, normed1, valid0, valid1, chosen, *rest):
    outs, held = rest[:-1], rest[-1]
    _, rows, toks = valid0.shape
    for n, (normed, valid) in enumerate(((normed0, valid0), (normed1, valid1))):

        @pl.loop(0, rows // GROUP, unroll=UNROLL)
        def _(at):
            first = at * GROUP
            gated(normed[pl.ds(first * toks, GROUP * toks), :], chosen, valid, first, held)

        write_pieces(outs, held, n * toks)


def gate_kernel(normed, weight, out):
    rows, toks, _ = out.shape

    @pl.loop(0, rows // GROUP, unroll=UNROLL)
    def _(at):
        x = normed[pl.ds(at * GROUP * toks, GROUP * toks), :]
        logits = jnp.dot(x, weight[...], preferred_element_type=F32)
        out[pl.ds(at * GROUP, GROUP)] = (0.5 * jnp.tanh(0.5 * logits) + 0.5).reshape(GROUP, toks, -1)


def product_kernel(mirror, first, n_left, n_right, *rest):
    *refs, held = rest
    planes = [refs[2 * n : 2 * n + 2] for n in range(n_left + n_right)]
    lefts, rights = planes[:n_left], planes[n_left:]
    outs = refs[2 * (n_left + n_right) :]
    count, span, _ = outs[0].shape
    rows = span // 2
    z, y, _ = place()
    z = 2 * n_right - 1 - z if mirror else z
    for s in range(n_right):
        for p in range(2):
            start = pl.multiple_of((z + n_right - s) % n_right * span + (y ^ p) * rows, rows)
            at = 0 if p else first
            held[:, pl.ds(start, rows), :] = rights[s][p][at : at + count]
    for c in range(count):
        left = jnp.concatenate([x for own, other in lefts for x in (own[first + c], other[c])], axis=0)
        out = lax.dot_general(left, held[c], NT, preferred_element_type=F32).astype(BF16)
        for n in range(n_left):
            outs[n][c] = out[n * span : (n + 1) * span]


def hand_out_kernel(planes, near, far, end, *outs):
    _, rows, _ = outs[0].shape
    z, _, core = place()
    at_end = (z == 0) | (z == planes - 1)
    for r in range(4):
        is_near = (core ^ (r % 2)) == z // (planes // 2)
        span = slice((r // 2) * rows, (r // 2 + 1) * rows)

        @pl.when(is_near)
        def _():
            outs[r][...] = near[:, span, :]

        @pl.when(jnp.logical_not(is_near | at_end))
        def _():
            outs[r][...] = far[:, span, :]

        @pl.when(jnp.logical_not(is_near) & at_end)
        def _():
            outs[r][...] = end[:, span, :]


def update_kernel(gain, weight, gate, *rest):
    pieces, out, turned = rest[:-2], rest[-2], rest[-1]
    part = sum(x.shape[0] for x in pieces[::4])
    _, rows, toks = pieces[0].shape
    hidden = 4 * part
    pitch = hidden + 1
    _, y, core = place()
    scale = jnp.broadcast_to(gain[...], (toks, hidden)).T
    for r in range(4):
        base = ((2 * y + core) ^ r) * part
        for piece in pieces[r::4]:
            for c in range(piece.shape[0]):
                value = piece[c].astype(F32)
                for m in range(toks // LANES):
                    turned[m, pl.ds(base + c, rows, stride=pitch), :] = value[
                        :, m * LANES : (m + 1) * LANES
                    ]
            base = base + piece.shape[0]

    @pl.loop(0, rows, unroll=8)
    def _(i):
        x = jnp.concatenate(
            [turned[m, pl.ds(i * pitch, hidden), :] for m in range(toks // LANES)], axis=1
        )
        mean = jnp.mean(x, axis=0, keepdims=True)
        centered = x - mean
        var = jnp.mean(centered * centered, axis=0, keepdims=True)
        pnorm = (centered * lax.rsqrt(var + 1e-05) * scale).astype(BF16)
        mapped = lax.dot_general(pnorm, weight[...], TN, preferred_element_type=F32)
        out[i] = (gate[i] * mapped).astype(BF16)


def kernel(body, name, out_shape, in_specs, scratch=()):
    outs = jax.tree.map(lambda _: VMEM, out_shape)

    def call(*args):
        arrays = [*args, *jax.tree.leaves(out_shape), *scratch]
        size = sum(x.dtype.itemsize * math.prod(x.shape) for x in arrays)
        return pl.pallas_call(
            body,
            out_shape=out_shape,
            in_specs=in_specs,
            out_specs=outs,
            scratch_shapes=list(scratch),
            compiler_params=pltpu.CompilerParams(vmem_limit_bytes=size + SPARE),
            name=name,
        )(*args)

    return call


def local(pair, pair_mask, in_gain, proj_weight, gate_weight, out_gain, out_weight, *, n_row):
    rows, toks, channels = pair.shape
    hidden = proj_weight.shape[1] // 4
    part = hidden // 4
    planes = n_row // 2
    half = planes // 2
    counts = [part * share // sum(SHARES) for share in SHARES]
    groups = range(len(counts))
    def send(x, target, name):
        pairs = []
        for source in range(2 * n_row):
            to = target(source // 4, source // 2 % 2, source % 2)
            if to is not None:
                pairs.append((source, 4 * to[0] + 2 * to[1] + to[2]))
        with jax.named_scope(name):
            return lax.ppermute(x, ("row", "chan"), pairs)

    def after(x, *earlier):
        return lax.optimization_barrier((x, *earlier))[0]

    def in_plane(r):
        return lambda p, b, k: (p, b ^ (r // 2), k ^ (r % 2))

    def shifted(s):
        return lambda p, b, k: (p // half * half + (p + s) % half, b, k)

    def mirrored(p, b, k):
        return (p, b, 1 - k) if p in (0, planes - 1) else (planes - 1 - p, b, k)

    def edge(p, b, k):
        swap = {0: 1, 1: 0, planes - 1: planes - 2, planes - 2: planes - 1}
        return (swap[p], b, k) if p in swap else (p, b, 1 - k)

    def outward(p, b, k):
        return {1: (0, b, k), planes - 2: (planes - 1, b, k)}.get(p)

    gains = in_gain.reshape(1, -1)
    twin, twin_mask = send(pair, in_plane(1), "pair"), send(pair_mask, in_plane(1), "mask")

    def piece(count, height, depth):
        return jax.ShapeDtypeStruct((count, height, depth), BF16)

    held = pltpu.VMEM((toks // LANES, 2 * part * (rows + 1), LANES), F32)
    rows_all = jax.ShapeDtypeStruct((rows * toks, channels), BF16)
    weights = jax.ShapeDtypeStruct((4 * part, channels), BF16)
    valid_shape = jax.ShapeDtypeStruct((1, rows, toks), F32)
    *mine, normed0, chosen_right, chosen_left, valid, gains = kernel(
        right_own_kernel,
        "right_own",
        [piece(count, rows, toks) for count in (part, *counts)]
        + [rows_all, weights, weights, valid_shape, gains],
        [VMEM] * 4,
        [pltpu.VMEM((4 * hidden, channels), BF16), held],
    )(pair, pair_mask, gains, proj_weight)
    whole = [piece(count, rows, 2 * toks) for count in (part, *counts)]
    *right, normed1, twin_valid = kernel(
        right_twin_kernel,
        "right_twin",
        whole + [rows_all, valid_shape],
        [VMEM] * (4 + len(mine)),
        [held],
    )(twin, twin_mask, gains, chosen_right, *mine)
    right0, right1 = right[0], list(right[1:])

    def mid(name, x, *earlier):
        return send(after(x, *earlier), mirrored, f"mid_{name}")

    def end_right(name, x, *earlier):
        x = after(x, *earlier)
        return [send(x, shifted(s), f"end_right_{name}") for s in range(1, half)]

    def end_left(name, x, *earlier):
        return send(after(x, *earlier), edge, f"end_left_{name}")

    def cross(name, x, *earlier):
        return send(after(x, *earlier), in_plane(2), f"cross_{name}")

    own0 = mid("own_0", right0)
    crossed = cross("right_0", right1[0])
    near0 = end_right("0", right0)
    left = kernel(left_kernel, "left", whole, [VMEM] * 5, [held])(
        normed0, normed1, valid, twin_valid, chosen_left
    )
    left0, left1 = left[0], list(left[1:])
    gate = kernel(
        gate_kernel, "gate", jax.ShapeDtypeStruct((rows, toks, channels), F32), [VMEM] * 2
    )(normed0, gate_weight)
    right1[0] = after(crossed, left0)
    right1[1] = cross("right_1", right1[1], right1[0])
    own1 = [mid(f"own_1{g}", right1[g]) for g in groups]
    near1 = [end_right(f"1{g}", right1[g]) for g in groups]
    left1[0] = cross("left_0", left1[0], right1[1])
    next0 = [mid("next_0", x, own0) for x in near0]
    outer0 = end_left("0", left0, own0, crossed)
    left1[1] = cross("left_1", left1[1], left1[0], own1[0])
    next1 = [[mid("next_10", x, own1[0], gate) for x in near1[0]]]
    outer1 = [end_left("10", left1[0], near1[0][-1])]
    next1.append([mid("next_11", x, own1[1], next0[-1]) for x in near1[1]])
    outer1.append(end_left("11", left1[1], near1[1][-1], outer0))

    def products(mirror, first, lefts, rights, name):
        span = 2 * rows * len(rights)
        count = lefts[0][1].shape[0]
        args = [x for arrays in (*lefts, *rights) for x in arrays]
        return kernel(
            functools.partial(product_kernel, mirror, first, len(lefts), len(rights)),
            name,
            [piece(count, 2 * rows, span)] * len(lefts),
            [VMEM] * len(args),
            [pltpu.VMEM((count, span, 2 * toks), BF16)],
        )(*args)

    done, pieces, first = [], [], 0
    for g in groups:
        mine = (left0, left1[g])
        near = list(zip([right0, *near0], [right1[g], *near1[g]]))
        far = list(zip([own0, *next0], [own1[g], *next1[g]]))
        (close,) = products(False, first, [mine], near, "near")
        mine = (after(left0, *done), left1[g])
        away, ends = products(True, first, [mine, (outer0, outer1[g])], far, "away")
        ends = send(ends, edge if g == groups[-1] else outward, f"products_back_{g}")
        handed = kernel(
            functools.partial(hand_out_kernel, planes),
            "hand_out",
            [piece(counts[g], rows, toks)] * 4,
            [VMEM] * 3,
        )(close, away, ends)
        done = [away]
        pieces += [handed[0]] + [
            send(handed[r], in_plane(r), f"return_{g}{r}") for r in range(1, 4)
        ]
        first += counts[g]

    return kernel(
        update_kernel,
        "update",
        jax.ShapeDtypeStruct((rows, toks, channels), BF16),
        [VMEM] * (3 + len(pieces)),
        [pltpu.VMEM((toks // LANES, rows * (hidden + 1), LANES), F32)],
    )(out_gain.reshape(1, -1), out_weight, gate, *pieces)


def solution(mesh):
    placed = (
        P(("groups", "row"), "chan", None),
        P(("groups", "row"), "chan"),
        P(),
        P(),
        P(),
        P(),
        P(),
    )
    return jax.shard_map(
        functools.partial(local, n_row=mesh.shape["row"]),
        mesh=mesh,
        in_specs=placed,
        out_specs=P(("groups", "row"), "chan", None),
        check_vma=False,
    )
```

```python
import functools
import math

import jax
import jax.numpy as jnp
from jax import lax
from jax.experimental import pallas as pl
from jax.experimental.pallas import tpu as pltpu
from jax.sharding import PartitionSpec as P

F32, BF16 = jnp.float32, jnp.bfloat16
LANES = 128
SPARE = 6 * 1024 * 1024
SHARES = (5, 3)
NT = (((1,), (1,)), ((), ()))
TN = (((0,), (0,)), ((), ()))
VMEM = pl.BlockSpec(memory_space=pltpu.VMEM)
GROUP = 4
UNROLL = 2


def place():
    row = lax.axis_index("row")
    return row // 2, row % 2, lax.axis_index("chan")


def normalise(x, gain):
    mean = jnp.mean(x, axis=-1, keepdims=True)
    centered = x - mean
    var = jnp.mean(centered * centered, axis=-1, keepdims=True)
    return (centered * lax.rsqrt(var + 1e-05) * gain).astype(BF16)


def gated(normed, chosen, valid, first, held):
    _, rows, toks = valid.shape
    wide = chosen.shape[0] // 2
    proj = lax.dot_general(chosen[...], normed, NT, preferred_element_type=F32)
    for g in range(normed.shape[0] // toks):
        mine = proj[:, g * toks : (g + 1) * toks]
        value = (jnp.tanh(mine[:wide]) + 1.0) * (valid[0, pl.ds(first + g, 1), :] * mine[wide:])
        for m in range(toks // LANES):
            spot = pl.ds(first + g, wide, stride=rows + 1)
            held[m, spot, :] = value[:, m * LANES : (m + 1) * LANES]


def write_pieces(outs, held, base):
    row = 0
    for out in outs:
        count, rows, _ = out.shape
        for c in range(count):
            for m in range(held.shape[0]):
                lanes = slice(base + m * LANES, base + (m + 1) * LANES)
                out[c, :, lanes] = held[m, row : row + rows, :].astype(BF16)
            row += rows + 1


def right_rows(pair, valid, gain, chosen, normed_out, held):
    rows, toks, _ = pair.shape

    @pl.loop(0, rows // GROUP, unroll=UNROLL)
    def _(at):
        first = at * GROUP
        x = pair[pl.ds(first, GROUP)].astype(F32).reshape(GROUP * toks, -1)
        normed = normalise(x, gain[...])
        normed_out[pl.ds(first * toks, GROUP * toks), :] = normed
        gated(normed, chosen, valid, first, held)


def right_own_kernel(pair, mask, gain, weight, *rest):
    *outs, normed_out, chosen_right, chosen_left, valid, gain_out, turned, held = rest
    gain_out[...] = gain[...]
    hidden = weight.shape[1] // 4
    part = hidden // 4
    _, y, core = place()
    turned[...] = weight[...].T
    valid[0] = mask[...].astype(F32) * 0.5
    for n in range(4):
        chosen = chosen_left if n < 2 else chosen_right
        half = 0.5 if n % 2 == 0 else 1.0
        for p in range(2):
            start = pl.multiple_of(n * hidden + ((2 * y + core) ^ (2 * p)) * part, part)
            at = (2 * (n % 2) + p) * part
            chosen[at : at + part, :] = turned[pl.ds(start, part), :] * half
    right_rows(pair, valid, gain, chosen_right, normed_out, held)
    write_pieces(outs, held, 0)


def right_twin_kernel(pair, mask, gain, chosen, *rest):
    count = (len(rest) - 3) // 2
    before, (*outs, normed_out, valid, held) = rest[:count], rest[count:]
    for x, out in zip(before, outs):
        out[:, :, : x.shape[2]] = x[...]
    valid[0] = mask[...].astype(F32) * 0.5
    right_rows(pair, valid, gain, chosen, normed_out, held)
    write_pieces(outs, held, pair.shape[1])


def left_kernel(normed0, normed1, valid0, valid1, chosen, *rest):
    outs, held = rest[:-1], rest[-1]
    _, rows, toks = valid0.shape
    for n, (normed, valid) in enumerate(((normed0, valid0), (normed1, valid1))):

        @pl.loop(0, rows // GROUP, unroll=UNROLL)
        def _(at):
            first = at * GROUP
            gated(normed[pl.ds(first * toks, GROUP * toks), :], chosen, valid, first, held)

        write_pieces(outs, held, n * toks)


def gate_kernel(normed, weight, out):
    rows, toks, _ = out.shape

    @pl.loop(0, rows // GROUP, unroll=UNROLL)
    def _(at):
        x = normed[pl.ds(at * GROUP * toks, GROUP * toks), :]
        logits = jnp.dot(x, weight[...], preferred_element_type=F32)
        out[pl.ds(at * GROUP, GROUP)] = (0.5 * jnp.tanh(0.5 * logits) + 0.5).reshape(GROUP, toks, -1)


def product_kernel(mirror, first, n_left, n_right, *rest):
    *refs, held = rest
    planes = [refs[2 * n : 2 * n + 2] for n in range(n_left + n_right)]
    lefts, rights = planes[:n_left], planes[n_left:]
    outs = refs[2 * (n_left + n_right) :]
    count, span, _ = outs[0].shape
    rows = span // 2
    z, y, _ = place()
    z = 2 * n_right - 1 - z if mirror else z
    for s in range(n_right):
        for p in range(2):
            start = pl.multiple_of((z + n_right - s) % n_right * span + (y ^ p) * rows, rows)
            at = 0 if p else first
            held[:, pl.ds(start, rows), :] = rights[s][p][at : at + count]
    for c in range(count):
        left = jnp.concatenate([x for own, other in lefts for x in (own[first + c], other[c])], axis=0)
        out = lax.dot_general(left, held[c], NT, preferred_element_type=F32).astype(BF16)
        for n in range(n_left):
            outs[n][c] = out[n * span : (n + 1) * span]


def hand_out_kernel(planes, near, far, end, *outs):
    _, rows, _ = outs[0].shape
    z, _, core = place()
    at_end = (z == 0) | (z == planes - 1)
    for r in range(4):
        is_near = (core ^ (r % 2)) == z // (planes // 2)
        span = slice((r // 2) * rows, (r // 2 + 1) * rows)

        @pl.when(is_near)
        def _():
            outs[r][...] = near[:, span, :]

        @pl.when(jnp.logical_not(is_near | at_end))
        def _():
            outs[r][...] = far[:, span, :]

        @pl.when(jnp.logical_not(is_near) & at_end)
        def _():
            outs[r][...] = end[:, span, :]


def update_kernel(gain, weight, gate, *rest):
    pieces, out, turned = rest[:-2], rest[-2], rest[-1]
    part = sum(x.shape[0] for x in pieces[::4])
    _, rows, toks = pieces[0].shape
    hidden = 4 * part
    pitch = hidden + 1
    _, y, core = place()
    scale = jnp.broadcast_to(gain[...], (toks, hidden)).T
    for r in range(4):
        base = ((2 * y + core) ^ r) * part
        for piece in pieces[r::4]:
            for c in range(piece.shape[0]):
                value = piece[c].astype(F32)
                for m in range(toks // LANES):
                    turned[m, pl.ds(base + c, rows, stride=pitch), :] = value[
                        :, m * LANES : (m + 1) * LANES
                    ]
            base = base + piece.shape[0]

    @pl.loop(0, rows, unroll=8)
    def _(i):
        x = jnp.concatenate(
            [turned[m, pl.ds(i * pitch, hidden), :] for m in range(toks // LANES)], axis=1
        )
        mean = jnp.mean(x, axis=0, keepdims=True)
        centered = x - mean
        var = jnp.mean(centered * centered, axis=0, keepdims=True)
        pnorm = (centered * lax.rsqrt(var + 1e-05) * scale).astype(BF16)
        mapped = lax.dot_general(pnorm, weight[...], TN, preferred_element_type=F32)
        out[i] = (gate[i] * mapped).astype(BF16)


def kernel(body, name, out_shape, in_specs, scratch=()):
    outs = jax.tree.map(lambda _: VMEM, out_shape)

    def call(*args):
        arrays = [*args, *jax.tree.leaves(out_shape), *scratch]
        size = sum(x.dtype.itemsize * math.prod(x.shape) for x in arrays)
        return pl.pallas_call(
            body,
            out_shape=out_shape,
            in_specs=in_specs,
            out_specs=outs,
            scratch_shapes=list(scratch),
            compiler_params=pltpu.CompilerParams(vmem_limit_bytes=size + SPARE),
            name=name,
        )(*args)

    return call


def local(pair, pair_mask, in_gain, proj_weight, gate_weight, out_gain, out_weight, *, n_row):
    rows, toks, channels = pair.shape
    hidden = proj_weight.shape[1] // 4
    part = hidden // 4
    planes = n_row // 2
    half = planes // 2
    counts = [part * share // sum(SHARES) for share in SHARES]
    groups = range(len(counts))
    def send(x, target, name):
        pairs = []
        for source in range(2 * n_row):
            to = target(source // 4, source // 2 % 2, source % 2)
            if to is not None:
                pairs.append((source, 4 * to[0] + 2 * to[1] + to[2]))
        with jax.named_scope(name):
            return lax.ppermute(x, ("row", "chan"), pairs)

    def after(x, *earlier):
        return lax.optimization_barrier((x, *earlier))[0]

    def in_plane(r):
        return lambda p, b, k: (p, b ^ (r // 2), k ^ (r % 2))

    def shifted(s):
        return lambda p, b, k: (p // half * half + (p + s) % half, b, k)

    def mirrored(p, b, k):
        return (p, b, 1 - k) if p in (0, planes - 1) else (planes - 1 - p, b, k)

    def edge(p, b, k):
        swap = {0: 1, 1: 0, planes - 1: planes - 2, planes - 2: planes - 1}
        return (swap[p], b, k) if p in swap else (p, b, 1 - k)

    def outward(p, b, k):
        return {1: (0, b, k), planes - 2: (planes - 1, b, k)}.get(p)

    gains = in_gain.reshape(1, -1)
    twin, twin_mask = send(pair, in_plane(1), "pair"), send(pair_mask, in_plane(1), "mask")

    def piece(count, height, depth):
        return jax.ShapeDtypeStruct((count, height, depth), BF16)

    held = pltpu.VMEM((toks // LANES, 2 * part * (rows + 1), LANES), F32)
    rows_all = jax.ShapeDtypeStruct((rows * toks, channels), BF16)
    weights = jax.ShapeDtypeStruct((4 * part, channels), BF16)
    valid_shape = jax.ShapeDtypeStruct((1, rows, toks), F32)
    *mine, normed0, chosen_right, chosen_left, valid, gains = kernel(
        right_own_kernel,
        "right_own",
        [piece(count, rows, toks) for count in (part, *counts)]
        + [rows_all, weights, weights, valid_shape, gains],
        [VMEM] * 4,
        [pltpu.VMEM((4 * hidden, channels), BF16), held],
    )(pair, pair_mask, gains, proj_weight)
    whole = [piece(count, rows, 2 * toks) for count in (part, *counts)]
    *right, normed1, twin_valid = kernel(
        right_twin_kernel,
        "right_twin",
        whole + [rows_all, valid_shape],
        [VMEM] * (4 + len(mine)),
        [held],
    )(twin, twin_mask, gains, chosen_right, *mine)
    right0, right1 = right[0], list(right[1:])

    def mid(name, x, *earlier):
        return send(after(x, *earlier), mirrored, f"mid_{name}")

    def end_right(name, x, *earlier):
        x = after(x, *earlier)
        return [send(x, shifted(s), f"end_right_{name}") for s in range(1, half)]

    def end_left(name, x, *earlier):
        return send(after(x, *earlier), edge, f"end_left_{name}")

    def cross(name, x, *earlier):
        return send(after(x, *earlier), in_plane(2), f"cross_{name}")

    own0 = mid("own_0", right0)
    crossed = cross("right_0", right1[0])
    near0 = end_right("0", right0)
    left = kernel(left_kernel, "left", whole, [VMEM] * 5, [held])(
        normed0, normed1, valid, twin_valid, chosen_left
    )
    left0, left1 = left[0], list(left[1:])
    gate = kernel(
        gate_kernel, "gate", jax.ShapeDtypeStruct((rows, toks, channels), F32), [VMEM] * 2
    )(normed0, gate_weight)
    right1[0] = after(crossed, left0)
    own1 = [mid("own_10", right1[0])]
    near1 = [end_right("10", right1[0])]
    left1[0] = cross("left_0", left1[0], crossed, own0)
    next0 = [mid("next_0", x, own0) for x in near0]
    outer0 = end_left("0", left0, own0)
    right1[1] = cross("right_1", right1[1], left1[0], own1[0])
    next1 = [[mid("next_10", x, own1[0], gate) for x in near1[0]]]
    outer1 = [end_left("10", left1[0], near1[0][-1])]
    left1[1] = cross("left_1", left1[1], right1[1], next0[-1])
    own1.append(mid("own_11", right1[1], own1[0]))
    near1.append(end_right("11", right1[1], outer0))
    next1.append([mid("next_11", x, next1[0][-1], own1[1]) for x in near1[1]])
    outer1.append(end_left("11", left1[1], outer1[0], own1[1]))

    def products(mirror, first, lefts, rights, name):
        span = 2 * rows * len(rights)
        count = lefts[0][1].shape[0]
        args = [x for arrays in (*lefts, *rights) for x in arrays]
        return kernel(
            functools.partial(product_kernel, mirror, first, len(lefts), len(rights)),
            name,
            [piece(count, 2 * rows, span)] * len(lefts),
            [VMEM] * len(args),
            [pltpu.VMEM((count, span, 2 * toks), BF16)],
        )(*args)

    done, pieces, first = [], [], 0
    for g in groups:
        mine = (left0, left1[g])
        near = list(zip([right0, *near0], [right1[g], *near1[g]]))
        far = list(zip([own0, *next0], [own1[g], *next1[g]]))
        (close,) = products(False, first, [mine], near, "near")
        mine = (after(left0, *done), left1[g])
        away, ends = products(True, first, [mine, (outer0, outer1[g])], far, "away")
        ends = send(ends, edge if g == groups[-1] else outward, f"products_back_{g}")
        handed = kernel(
            functools.partial(hand_out_kernel, planes),
            "hand_out",
            [piece(counts[g], rows, toks)] * 4,
            [VMEM] * 3,
        )(close, away, ends)
        done = [away]
        pieces += [handed[0]] + [
            send(handed[r], in_plane(r), f"return_{g}{r}") for r in range(1, 4)
        ]
        first += counts[g]

    return kernel(
        update_kernel,
        "update",
        jax.ShapeDtypeStruct((rows, toks, channels), BF16),
        [VMEM] * (3 + len(pieces)),
        [pltpu.VMEM((toks // LANES, rows * (hidden + 1), LANES), F32)],
    )(out_gain.reshape(1, -1), out_weight, gate, *pieces)


def solution(mesh):
    placed = (
        P(("groups", "row"), "chan", None),
        P(("groups", "row"), "chan"),
        P(),
        P(),
        P(),
        P(),
        P(),
    )
    return jax.shard_map(
        functools.partial(local, n_row=mesh.shape["row"]),
        mesh=mesh,
        in_specs=placed,
        out_specs=P(("groups", "row"), "chan", None),
        check_vma=False,
    )
```

```python
import functools
import math

import jax
import jax.numpy as jnp
from jax import lax
from jax.experimental import pallas as pl
from jax.experimental.pallas import tpu as pltpu
from jax.sharding import PartitionSpec as P

F32, BF16 = jnp.float32, jnp.bfloat16
LANES = 128
SPARE = 6 * 1024 * 1024
SHARES = (4, 4)
NT = (((1,), (1,)), ((), ()))
TN = (((0,), (0,)), ((), ()))
VMEM = pl.BlockSpec(memory_space=pltpu.VMEM)
GROUP = 4
UNROLL = 2


def place():
    row = lax.axis_index("row")
    return row // 2, row % 2, lax.axis_index("chan")


def normalise(x, gain):
    mean = jnp.mean(x, axis=-1, keepdims=True)
    centered = x - mean
    var = jnp.mean(centered * centered, axis=-1, keepdims=True)
    return (centered * lax.rsqrt(var + 1e-05) * gain).astype(BF16)


def gated(normed, chosen, valid, first, held):
    _, rows, toks = valid.shape
    wide = chosen.shape[0] // 2
    proj = lax.dot_general(chosen[...], normed, NT, preferred_element_type=F32)
    for g in range(normed.shape[0] // toks):
        mine = proj[:, g * toks : (g + 1) * toks]
        value = (jnp.tanh(mine[:wide]) + 1.0) * (valid[0, pl.ds(first + g, 1), :] * mine[wide:])
        for m in range(toks // LANES):
            spot = pl.ds(first + g, wide, stride=rows + 1)
            held[m, spot, :] = value[:, m * LANES : (m + 1) * LANES]


def write_pieces(outs, held, base):
    row = 0
    for out in outs:
        count, rows, _ = out.shape
        for c in range(count):
            for m in range(held.shape[0]):
                lanes = slice(base + m * LANES, base + (m + 1) * LANES)
                out[c, :, lanes] = held[m, row : row + rows, :].astype(BF16)
            row += rows + 1


def right_rows(pair, valid, gain, chosen, normed_out, held):
    rows, toks, _ = pair.shape

    @pl.loop(0, rows // GROUP, unroll=UNROLL)
    def _(at):
        first = at * GROUP
        x = pair[pl.ds(first, GROUP)].astype(F32).reshape(GROUP * toks, -1)
        normed = normalise(x, gain[...])
        normed_out[pl.ds(first * toks, GROUP * toks), :] = normed
        gated(normed, chosen, valid, first, held)


def right_own_kernel(pair, mask, gain, weight, *rest):
    *outs, normed_out, chosen_right, chosen_left, valid, gain_out, turned, held = rest
    gain_out[...] = gain[...]
    hidden = weight.shape[1] // 4
    part = hidden // 4
    _, y, core = place()
    turned[...] = weight[...].T
    valid[0] = mask[...].astype(F32) * 0.5
    for n in range(4):
        chosen = chosen_left if n < 2 else chosen_right
        half = 0.5 if n % 2 == 0 else 1.0
        for p in range(2):
            start = pl.multiple_of(n * hidden + ((2 * y + core) ^ (2 * p)) * part, part)
            at = (2 * (n % 2) + p) * part
            chosen[at : at + part, :] = turned[pl.ds(start, part), :] * half
    right_rows(pair, valid, gain, chosen_right, normed_out, held)
    write_pieces(outs, held, 0)


def right_twin_kernel(pair, mask, gain, chosen, *rest):
    count = (len(rest) - 3) // 2
    before, (*outs, normed_out, valid, held) = rest[:count], rest[count:]
    for x, out in zip(before, outs):
        out[:, :, : x.shape[2]] = x[...]
    valid[0] = mask[...].astype(F32) * 0.5
    right_rows(pair, valid, gain, chosen, normed_out, held)
    write_pieces(outs, held, pair.shape[1])


def left_kernel(normed0, normed1, valid0, valid1, chosen, *rest):
    outs, held = rest[:-1], rest[-1]
    _, rows, toks = valid0.shape
    for n, (normed, valid) in enumerate(((normed0, valid0), (normed1, valid1))):

        @pl.loop(0, rows // GROUP, unroll=UNROLL)
        def _(at):
            first = at * GROUP
            gated(normed[pl.ds(first * toks, GROUP * toks), :], chosen, valid, first, held)

        write_pieces(outs, held, n * toks)


def gate_kernel(normed, weight, out):
    rows, toks, _ = out.shape

    @pl.loop(0, rows // GROUP, unroll=UNROLL)
    def _(at):
        x = normed[pl.ds(at * GROUP * toks, GROUP * toks), :]
        logits = jnp.dot(x, weight[...], preferred_element_type=F32)
        out[pl.ds(at * GROUP, GROUP)] = (0.5 * jnp.tanh(0.5 * logits) + 0.5).reshape(GROUP, toks, -1)


def product_kernel(mirror, instead, first, n_left, n_right, *rest):
    *refs, held = rest
    planes = [refs[2 * n : 2 * n + 2] for n in range(n_left + n_right)]
    lefts, rights = planes[:n_left], planes[n_left:]
    refs = refs[2 * (n_left + n_right) :]
    other, outs = refs[0], refs[1 if instead else 0 :]
    count, span, toks = outs[0].shape
    rows = span // 2
    z, y, _ = place()
    at_end = (z == 0) | (z == 2 * n_right - 1)
    z = 2 * n_right - 1 - z if mirror else z
    for s in range(n_right):
        for p in range(2):
            start = pl.multiple_of((z + n_right - s) % n_right * span + (y ^ p) * rows, rows)
            at = 0 if p else first
            held[:, pl.ds(start, rows), :] = rights[s][p][at : at + count]
    for c in range(count):
        left = jnp.concatenate([x for own, other in lefts for x in (own[first + c], other[c])], axis=0)
        out = lax.dot_general(left, held[c], NT, preferred_element_type=F32).astype(BF16)
        outs[0][c] = out[:span]
        if n_left == 2:
            outs[1][c, :, :toks] = out[span : span + rows]
            outs[1][c, :, toks:] = out[span + rows :]
    if instead:

        @pl.when(at_end)
        def _():
            outs[1][...] = other[...]


def hand_out_kernel(planes, near, far, end, *outs):
    _, rows, toks = outs[0].shape
    z, _, core = place()
    at_end = (z == 0) | (z == planes - 1)
    for r in range(4):
        is_near = (core ^ (r % 2)) == z // (planes // 2)
        span = slice((r // 2) * rows, (r // 2 + 1) * rows)
        lanes = slice((r // 2) * toks, (r // 2 + 1) * toks)

        @pl.when(is_near)
        def _():
            outs[r][...] = near[:, span, :]

        @pl.when(jnp.logical_not(is_near | at_end))
        def _():
            outs[r][...] = far[:, span, :]

        @pl.when(jnp.logical_not(is_near) & at_end)
        def _():
            outs[r][...] = end[:, :, lanes]


def update_kernel(gain, weight, gate, *rest):
    pieces, out, turned = rest[:-2], rest[-2], rest[-1]
    part = sum(x.shape[0] for x in pieces[::4])
    _, rows, toks = pieces[0].shape
    hidden = 4 * part
    pitch = hidden + 1
    _, y, core = place()
    scale = jnp.broadcast_to(gain[...], (toks, hidden)).T
    for r in range(4):
        base = ((2 * y + core) ^ r) * part
        for piece in pieces[r::4]:
            for c in range(piece.shape[0]):
                value = piece[c].astype(F32)
                for m in range(toks // LANES):
                    turned[m, pl.ds(base + c, rows, stride=pitch), :] = value[
                        :, m * LANES : (m + 1) * LANES
                    ]
            base = base + piece.shape[0]

    @pl.loop(0, rows, unroll=8)
    def _(i):
        x = jnp.concatenate(
            [turned[m, pl.ds(i * pitch, hidden), :] for m in range(toks // LANES)], axis=1
        )
        mean = jnp.mean(x, axis=0, keepdims=True)
        centered = x - mean
        var = jnp.mean(centered * centered, axis=0, keepdims=True)
        pnorm = (centered * lax.rsqrt(var + 1e-05) * scale).astype(BF16)
        mapped = lax.dot_general(pnorm, weight[...], TN, preferred_element_type=F32)
        out[i] = (gate[i] * mapped).astype(BF16)


def kernel(body, name, out_shape, in_specs, scratch=()):
    outs = jax.tree.map(lambda _: VMEM, out_shape)

    def call(*args):
        arrays = [*args, *jax.tree.leaves(out_shape), *scratch]
        size = sum(x.dtype.itemsize * math.prod(x.shape) for x in arrays)
        return pl.pallas_call(
            body,
            out_shape=out_shape,
            in_specs=in_specs,
            out_specs=outs,
            scratch_shapes=list(scratch),
            compiler_params=pltpu.CompilerParams(vmem_limit_bytes=size + SPARE),
            name=name,
        )(*args)

    return call


def local(pair, pair_mask, in_gain, proj_weight, gate_weight, out_gain, out_weight, *, n_row):
    rows, toks, channels = pair.shape
    hidden = proj_weight.shape[1] // 4
    part = hidden // 4
    planes = n_row // 2
    half = planes // 2
    counts = [part * share // sum(SHARES) for share in SHARES]
    groups = range(len(counts))
    def send(x, target, name):
        pairs = []
        for source in range(2 * n_row):
            to = target(source // 4, source // 2 % 2, source % 2)
            if to is not None:
                pairs.append((source, 4 * to[0] + 2 * to[1] + to[2]))
        with jax.named_scope(name):
            return lax.ppermute(x, ("row", "chan"), pairs)

    def after(x, *earlier):
        return lax.optimization_barrier((x, *earlier))[0]

    def in_plane(r):
        return lambda p, b, k: (p, b ^ (r // 2), k ^ (r % 2))

    def shifted(s):
        return lambda p, b, k: (p // half * half + (p + s) % half, b, k)

    def mirrored(p, b, k):
        return (p, b, 1 - k) if p in (0, planes - 1) else (planes - 1 - p, b, k)

    def edge(p, b, k):
        swap = {0: 1, 1: 0, planes - 1: planes - 2, planes - 2: planes - 1}
        return (swap[p], b, k) if p in swap else (p, b, 1 - k)

    def outward(p, b, k):
        return {1: (0, b, k), planes - 2: (planes - 1, b, k)}.get(p)

    gains = in_gain.reshape(1, -1)
    twin, twin_mask = send(pair, in_plane(1), "pair"), send(pair_mask, in_plane(1), "mask")

    def piece(count, height, depth):
        return jax.ShapeDtypeStruct((count, height, depth), BF16)

    held = pltpu.VMEM((toks // LANES, 2 * part * (rows + 1), LANES), F32)
    rows_all = jax.ShapeDtypeStruct((rows * toks, channels), BF16)
    weights = jax.ShapeDtypeStruct((4 * part, channels), BF16)
    valid_shape = jax.ShapeDtypeStruct((1, rows, toks), F32)
    *mine, normed0, chosen_right, chosen_left, valid, gains = kernel(
        right_own_kernel,
        "right_own",
        [piece(count, rows, toks) for count in (part, *counts)]
        + [rows_all, weights, weights, valid_shape, gains],
        [VMEM] * 4,
        [pltpu.VMEM((4 * hidden, channels), BF16), held],
    )(pair, pair_mask, gains, proj_weight)
    whole = [piece(count, rows, 2 * toks) for count in (part, *counts)]
    *right, normed1, twin_valid = kernel(
        right_twin_kernel,
        "right_twin",
        whole + [rows_all, valid_shape],
        [VMEM] * (4 + len(mine)),
        [held],
    )(twin, twin_mask, gains, chosen_right, *mine)
    right0, right1 = right[0], list(right[1:])

    def mid(name, x, *earlier):
        return send(after(x, *earlier), mirrored, f"mid_{name}")

    def end_right(name, x, *earlier):
        x = after(x, *earlier)
        return [send(x, shifted(s), f"end_right_{name}") for s in range(1, half)]

    def end_left(name, x, *earlier):
        return send(after(x, *earlier), edge, f"end_left_{name}")

    def cross(name, x, *earlier):
        return send(after(x, *earlier), in_plane(2), f"cross_{name}")

    own0 = mid("own_0", right0)
    crossed = cross("right_0", right1[0])
    near0 = end_right("0", right0)
    left = kernel(left_kernel, "left", whole, [VMEM] * 5, [held])(
        normed0, normed1, valid, twin_valid, chosen_left
    )
    left0, left1 = left[0], list(left[1:])
    gate = kernel(
        gate_kernel, "gate", jax.ShapeDtypeStruct((rows, toks, channels), F32), [VMEM] * 2
    )(normed0, gate_weight)
    right1[0] = after(crossed, left0)
    own1 = [mid("own_10", right1[0])]
    near1 = [end_right("10", right1[0])]
    left1[0] = cross("left_0", left1[0], crossed, own0)
    next0 = [mid("next_0", x, own0) for x in near0]
    outer0 = end_left("0", left0, own0)
    right1[1] = cross("right_1", right1[1], left1[0], own1[0])
    next1 = [[mid("next_10", x, own1[0], gate) for x in near1[0]]]
    outer1 = [end_left("10", left1[0], near1[0][-1])]
    left1[1] = cross("left_1", left1[1], right1[1], next0[-1])
    own1.append(mid("own_11", right1[1], own1[0]))
    near1.append(end_right("11", right1[1], outer0))
    def products(mirror, first, lefts, rights, name, instead=()):
        span = 2 * rows * len(rights)
        count = lefts[0][1].shape[0]
        args = [x for arrays in (*lefts, *rights) for x in arrays] + [*instead]
        shapes = [piece(count, 2 * rows, span), piece(count, rows, 2 * span)]
        return kernel(
            functools.partial(
                product_kernel, mirror, bool(instead), first, len(lefts), len(rights)
            ),
            name,
            shapes[: len(lefts)],
            [VMEM] * len(args),
            [pltpu.VMEM((count, span, 2 * toks), BF16)],
        )(*args)

    def near_planes(g):
        return list(zip([right0, *near0], [right1[g], *near1[g]]))

    def far_planes(g):
        return list(zip([own0, *next0], [own1[g], *next1[g]]))

    def hand_out(g, close, away, ends):
        handed = kernel(
            functools.partial(hand_out_kernel, planes),
            "hand_out",
            [piece(counts[g], rows, toks)] * 4,
            [VMEM] * 3,
        )(close, away, ends)
        return [handed[0]] + [
            send(handed[r], in_plane(r), f"return_{g}{r}") for r in range(1, 4)
        ]

    close, mine, first = [], [(left0, x) for x in left1], [0, counts[0]]
    for g in groups:
        close += products(False, first[g], [mine[g]], near_planes(g), "near")
    sides = [mine[0], (outer0, outer1[0])]
    away0, swapped = products(True, first[0], sides, far_planes(0), "away", [left1[1]])
    next1.append([mid("next_11", x, next1[0][-1], own1[1], away0) for x in near1[1]])
    swapped = send(swapped, edge, "left_11_and_products_back_0")
    pieces = hand_out(0, close[0], away0, swapped)
    sides = [(after(left0, pieces[0]), left1[1]), (outer0, swapped)]
    away1, ends = products(True, first[1], sides, far_planes(1), "away")
    ends = send(ends, edge, "products_back_1")
    pieces += hand_out(1, close[1], away1, ends)

    return kernel(
        update_kernel,
        "update",
        jax.ShapeDtypeStruct((rows, toks, channels), BF16),
        [VMEM] * (3 + len(pieces)),
        [pltpu.VMEM((toks // LANES, rows * (hidden + 1), LANES), F32)],
    )(out_gain.reshape(1, -1), out_weight, gate, *pieces)


def solution(mesh):
    placed = (
        P(("groups", "row"), "chan", None),
        P(("groups", "row"), "chan"),
        P(),
        P(),
        P(),
        P(),
        P(),
    )
    return jax.shard_map(
        functools.partial(local, n_row=mesh.shape["row"]),
        mesh=mesh,
        in_specs=placed,
        out_specs=P(("groups", "row"), "chan", None),
        check_vma=False,
    )
```

```python
import functools
import math

import jax
import jax.numpy as jnp
from jax import lax
from jax.experimental import pallas as pl
from jax.experimental.pallas import tpu as pltpu
from jax.sharding import PartitionSpec as P

F32, BF16 = jnp.float32, jnp.bfloat16
LANES = 128
SPARE = 6 * 1024 * 1024
SHARES = (4, 4)
NT = (((1,), (1,)), ((), ()))
TN = (((0,), (0,)), ((), ()))
VMEM = pl.BlockSpec(memory_space=pltpu.VMEM)
GROUP = 4
UNROLL = 2


def place():
    row = lax.axis_index("row")
    return row // 2, row % 2, lax.axis_index("chan")


def normalise(x, gain):
    mean = jnp.mean(x, axis=-1, keepdims=True)
    centered = x - mean
    var = jnp.mean(centered * centered, axis=-1, keepdims=True)
    return (centered * lax.rsqrt(var + 1e-05) * gain).astype(BF16)


def gated(normed, chosen, valid, first, held):
    _, rows, toks = valid.shape
    wide = chosen.shape[0] // 2
    proj = lax.dot_general(chosen[...], normed, NT, preferred_element_type=F32)
    for g in range(normed.shape[0] // toks):
        mine = proj[:, g * toks : (g + 1) * toks]
        value = (jnp.tanh(mine[:wide]) + 1.0) * (valid[0, pl.ds(first + g, 1), :] * mine[wide:])
        for m in range(toks // LANES):
            spot = pl.ds(first + g, wide, stride=rows + 1)
            held[m, spot, :] = value[:, m * LANES : (m + 1) * LANES]


def write_pieces(outs, held, base):
    row = 0
    for out in outs:
        count, rows, _ = out.shape
        for c in range(count):
            for m in range(held.shape[0]):
                lanes = slice(base + m * LANES, base + (m + 1) * LANES)
                out[c, :, lanes] = held[m, row : row + rows, :].astype(BF16)
            row += rows + 1


def right_rows(pair, valid, gain, chosen, normed_out, held):
    rows, toks, _ = pair.shape

    @pl.loop(0, rows // GROUP, unroll=UNROLL)
    def _(at):
        first = at * GROUP
        x = pair[pl.ds(first, GROUP)].astype(F32).reshape(GROUP * toks, -1)
        normed = normalise(x, gain[...])
        normed_out[pl.ds(first * toks, GROUP * toks), :] = normed
        gated(normed, chosen, valid, first, held)


def right_own_kernel(pair, mask, gain, weight, *rest):
    *outs, normed_out, chosen_right, chosen_left, valid, gain_out, turned, held = rest
    gain_out[...] = gain[...]
    hidden = weight.shape[1] // 4
    part = hidden // 4
    _, y, core = place()
    turned[...] = weight[...].T
    valid[0] = mask[...].astype(F32) * 0.5
    for n in range(4):
        chosen = chosen_left if n < 2 else chosen_right
        half = 0.5 if n % 2 == 0 else 1.0
        for p in range(2):
            start = pl.multiple_of(n * hidden + ((2 * y + core) ^ (2 * p)) * part, part)
            at = (2 * (n % 2) + p) * part
            chosen[at : at + part, :] = turned[pl.ds(start, part), :] * half
    right_rows(pair, valid, gain, chosen_right, normed_out, held)
    write_pieces(outs, held, 0)


def right_twin_kernel(pair, mask, gain, chosen, *rest):
    count = (len(rest) - 3) // 2
    before, (*outs, normed_out, valid, held) = rest[:count], rest[count:]
    for x, out in zip(before, outs):
        out[:, :, : x.shape[2]] = x[...]
    valid[0] = mask[...].astype(F32) * 0.5
    right_rows(pair, valid, gain, chosen, normed_out, held)
    write_pieces(outs, held, pair.shape[1])


def left_kernel(normed0, normed1, valid0, valid1, chosen, *rest):
    outs, held = rest[:-1], rest[-1]
    _, rows, toks = valid0.shape
    for n, (normed, valid) in enumerate(((normed0, valid0), (normed1, valid1))):

        @pl.loop(0, rows // GROUP, unroll=UNROLL)
        def _(at):
            first = at * GROUP
            gated(normed[pl.ds(first * toks, GROUP * toks), :], chosen, valid, first, held)

        write_pieces(outs, held, n * toks)


def gate_kernel(normed, weight, out):
    rows, toks, _ = out.shape

    @pl.loop(0, rows // GROUP, unroll=UNROLL)
    def _(at):
        x = normed[pl.ds(at * GROUP * toks, GROUP * toks), :]
        logits = jnp.dot(x, weight[...], preferred_element_type=F32)
        out[pl.ds(at * GROUP, GROUP)] = (0.5 * jnp.tanh(0.5 * logits) + 0.5).reshape(GROUP, toks, -1)


def product_kernel(mirror, instead, first, n_left, n_right, *rest):
    *refs, held = rest
    planes = [refs[2 * n : 2 * n + 2] for n in range(n_left + n_right)]
    lefts, rights = planes[:n_left], planes[n_left:]
    refs = refs[2 * (n_left + n_right) :]
    other, outs = refs[0], refs[1 if instead else 0 :]
    count, span, toks = outs[0].shape
    rows = span // 2
    z, y, _ = place()
    at_end = (z == 0) | (z == 2 * n_right - 1)
    z = 2 * n_right - 1 - z if mirror else z
    for s in range(n_right):
        for p in range(2):
            start = pl.multiple_of((z + n_right - s) % n_right * span + (y ^ p) * rows, rows)
            at = 0 if p else first
            held[:, pl.ds(start, rows), :] = rights[s][p][at : at + count]
    for c in range(count):
        left = jnp.concatenate([x for own, other in lefts for x in (own[first + c], other[c])], axis=0)
        out = lax.dot_general(left, held[c], NT, preferred_element_type=F32).astype(BF16)
        outs[0][c] = out[:span]
        if n_left == 2:
            outs[1][c, :, :toks] = out[span : span + rows]
            outs[1][c, :, toks:] = out[span + rows :]
    if instead:

        @pl.when(at_end)
        def _():
            outs[1][...] = other[...]


def hand_out_kernel(planes, near, far, end, *outs):
    _, rows, toks = outs[0].shape
    z, _, core = place()
    at_end = (z == 0) | (z == planes - 1)
    for r in range(4):
        is_near = (core ^ (r % 2)) == z // (planes // 2)
        span = slice((r // 2) * rows, (r // 2 + 1) * rows)
        lanes = slice((r // 2) * toks, (r // 2 + 1) * toks)

        @pl.when(is_near)
        def _():
            outs[r][...] = near[:, span, :]

        @pl.when(jnp.logical_not(is_near | at_end))
        def _():
            outs[r][...] = far[:, span, :]

        @pl.when(jnp.logical_not(is_near) & at_end)
        def _():
            outs[r][...] = end[:, :, lanes]


def update_kernel(gain, weight, gate, *rest):
    pieces, out, turned = rest[:-2], rest[-2], rest[-1]
    part = sum(x.shape[0] for x in pieces[::4])
    _, rows, toks = pieces[0].shape
    hidden = 4 * part
    pitch = hidden + 1
    _, y, core = place()
    scale = jnp.broadcast_to(gain[...], (toks, hidden)).T
    for r in range(4):
        base = ((2 * y + core) ^ r) * part
        for piece in pieces[r::4]:
            for c in range(piece.shape[0]):
                value = piece[c].astype(F32)
                for m in range(toks // LANES):
                    turned[m, pl.ds(base + c, rows, stride=pitch), :] = value[
                        :, m * LANES : (m + 1) * LANES
                    ]
            base = base + piece.shape[0]

    @pl.loop(0, rows, unroll=8)
    def _(i):
        x = jnp.concatenate(
            [turned[m, pl.ds(i * pitch, hidden), :] for m in range(toks // LANES)], axis=1
        )
        mean = jnp.mean(x, axis=0, keepdims=True)
        centered = x - mean
        var = jnp.mean(centered * centered, axis=0, keepdims=True)
        pnorm = (centered * lax.rsqrt(var + 1e-05) * scale).astype(BF16)
        mapped = lax.dot_general(pnorm, weight[...], TN, preferred_element_type=F32)
        out[i] = (gate[i] * mapped).astype(BF16)


def kernel(body, name, out_shape, in_specs, scratch=()):
    outs = jax.tree.map(lambda _: VMEM, out_shape)

    def call(*args):
        arrays = [*args, *jax.tree.leaves(out_shape), *scratch]
        size = sum(x.dtype.itemsize * math.prod(x.shape) for x in arrays)
        return pl.pallas_call(
            body,
            out_shape=out_shape,
            in_specs=in_specs,
            out_specs=outs,
            scratch_shapes=list(scratch),
            compiler_params=pltpu.CompilerParams(vmem_limit_bytes=size + SPARE),
            name=name,
        )(*args)

    return call


def local(pair, pair_mask, in_gain, proj_weight, gate_weight, out_gain, out_weight, *, n_row):
    rows, toks, channels = pair.shape
    hidden = proj_weight.shape[1] // 4
    part = hidden // 4
    planes = n_row // 2
    half = planes // 2
    counts = [part * share // sum(SHARES) for share in SHARES]
    groups = range(len(counts))
    def send(x, target, name):
        pairs = []
        for source in range(2 * n_row):
            to = target(source // 4, source // 2 % 2, source % 2)
            if to is not None:
                pairs.append((source, 4 * to[0] + 2 * to[1] + to[2]))
        with jax.named_scope(name):
            return lax.ppermute(x, ("row", "chan"), pairs)

    def after(x, *earlier):
        return lax.optimization_barrier((x, *earlier))[0]

    def in_plane(r):
        return lambda p, b, k: (p, b ^ (r // 2), k ^ (r % 2))

    def shifted(s):
        return lambda p, b, k: (p // half * half + (p + s) % half, b, k)

    def mirrored(p, b, k):
        return (p, b, 1 - k) if p in (0, planes - 1) else (planes - 1 - p, b, k)

    def edge(p, b, k):
        swap = {0: 1, 1: 0, planes - 1: planes - 2, planes - 2: planes - 1}
        return (swap[p], b, k) if p in swap else (p, b, 1 - k)

    def outward(p, b, k):
        return {1: (0, b, k), planes - 2: (planes - 1, b, k)}.get(p)

    gains = in_gain.reshape(1, -1)
    twin, twin_mask = send(pair, in_plane(1), "pair"), send(pair_mask, in_plane(1), "mask")

    def piece(count, height, depth):
        return jax.ShapeDtypeStruct((count, height, depth), BF16)

    held = pltpu.VMEM((toks // LANES, 2 * part * (rows + 1), LANES), F32)
    rows_all = jax.ShapeDtypeStruct((rows * toks, channels), BF16)
    weights = jax.ShapeDtypeStruct((4 * part, channels), BF16)
    valid_shape = jax.ShapeDtypeStruct((1, rows, toks), F32)
    *mine, normed0, chosen_right, chosen_left, valid, gains = kernel(
        right_own_kernel,
        "right_own",
        [piece(count, rows, toks) for count in (part, *counts)]
        + [rows_all, weights, weights, valid_shape, gains],
        [VMEM] * 4,
        [pltpu.VMEM((4 * hidden, channels), BF16), held],
    )(pair, pair_mask, gains, proj_weight)
    whole = [piece(count, rows, 2 * toks) for count in (part, *counts)]
    *right, normed1, twin_valid = kernel(
        right_twin_kernel,
        "right_twin",
        whole + [rows_all, valid_shape],
        [VMEM] * (4 + len(mine)),
        [held],
    )(twin, twin_mask, gains, chosen_right, *mine)
    right0, right1 = right[0], list(right[1:])

    def mid(name, x, *earlier):
        return send(after(x, *earlier), mirrored, f"mid_{name}")

    def end_right(name, x, *earlier):
        x = after(x, *earlier)
        return [send(x, shifted(s), f"end_right_{name}") for s in range(1, half)]

    def end_left(name, x, *earlier):
        return send(after(x, *earlier), edge, f"end_left_{name}")

    def cross(name, x, *earlier):
        return send(after(x, *earlier), in_plane(2), f"cross_{name}")

    own0 = mid("own_0", right0)
    crossed = cross("right_0", right1[0])
    near0 = end_right("0", right0)
    left = kernel(left_kernel, "left", whole, [VMEM] * 5, [held])(
        normed0, normed1, valid, twin_valid, chosen_left
    )
    left0, left1 = left[0], list(left[1:])
    gate = kernel(
        gate_kernel, "gate", jax.ShapeDtypeStruct((rows, toks, channels), F32), [VMEM] * 2
    )(normed0, gate_weight)
    right1[0] = after(crossed, left0)
    own1 = [mid("own_10", right1[0])]
    near1 = [end_right("10", right1[0])]
    left1[0] = cross("left_0", left1[0], crossed, own0)
    next0 = [mid("next_0", x, own0) for x in near0]
    outer0 = end_left("0", left0, own0)
    right1[1] = cross("right_1", right1[1], left1[0], own1[0], near1[0][-1])
    next1 = [[mid("next_10", x, own1[0], gate) for x in near1[0]]]
    outer1 = [end_left("10", left1[0], near1[0][-1])]
    left1[1] = cross("left_1", left1[1], right1[1], next0[-1])
    own1.append(mid("own_11", right1[1], own1[0]))
    near1.append(end_right("11", right1[1], outer0))
    def products(mirror, first, lefts, rights, name, instead=()):
        span = 2 * rows * len(rights)
        count = lefts[0][1].shape[0]
        args = [x for arrays in (*lefts, *rights) for x in arrays] + [*instead]
        shapes = [piece(count, 2 * rows, span), piece(count, rows, 2 * span)]
        return kernel(
            functools.partial(
                product_kernel, mirror, bool(instead), first, len(lefts), len(rights)
            ),
            name,
            shapes[: len(lefts)],
            [VMEM] * len(args),
            [pltpu.VMEM((count, span, 2 * toks), BF16)],
        )(*args)

    def near_planes(g):
        return list(zip([right0, *near0], [right1[g], *near1[g]]))

    def far_planes(g):
        return list(zip([own0, *next0], [own1[g], *next1[g]]))

    def hand_out(g, close, away, ends):
        handed = kernel(
            functools.partial(hand_out_kernel, planes),
            "hand_out",
            [piece(counts[g], rows, toks)] * 4,
            [VMEM] * 3,
        )(close, away, ends)
        return [handed[0]] + [
            send(handed[r], in_plane(r), f"return_{g}{r}") for r in range(1, 4)
        ]

    close, mine, first = [], [(left0, x) for x in left1], [0, counts[0]]
    for g in groups:
        close += products(False, first[g], [mine[g]], near_planes(g), "near")
    sides = [mine[0], (outer0, outer1[0])]
    away0, swapped = products(True, first[0], sides, far_planes(0), "away", [left1[1]])
    next1.append([mid("next_11", x, next1[0][-1], own1[1], away0) for x in near1[1]])
    swapped = send(swapped, edge, "left_11_and_products_back_0")
    pieces = hand_out(0, close[0], away0, swapped)
    sides = [(after(left0, pieces[0]), left1[1]), (outer0, swapped)]
    away1, ends = products(True, first[1], sides, far_planes(1), "away")
    ends = send(ends, edge, "products_back_1")
    pieces += hand_out(1, close[1], away1, ends)

    return kernel(
        update_kernel,
        "update",
        jax.ShapeDtypeStruct((rows, toks, channels), BF16),
        [VMEM] * (3 + len(pieces)),
        [pltpu.VMEM((toks // LANES, rows * (hidden + 1), LANES), F32)],
    )(out_gain.reshape(1, -1), out_weight, gate, *pieces)


def solution(mesh):
    placed = (
        P(("groups", "row"), "chan", None),
        P(("groups", "row"), "chan"),
        P(),
        P(),
        P(),
        P(),
        P(),
    )
    return jax.shard_map(
        functools.partial(local, n_row=mesh.shape["row"]),
        mesh=mesh,
        in_specs=placed,
        out_specs=P(("groups", "row"), "chan", None),
        check_vma=False,
    )
```

```python
import functools
import math

import jax
import jax.numpy as jnp
from jax import lax
from jax.experimental import pallas as pl
from jax.experimental.pallas import tpu as pltpu
from jax.sharding import PartitionSpec as P

F32, BF16 = jnp.float32, jnp.bfloat16
LANES = 128
SPARE = 6 * 1024 * 1024
SHARES = (4, 4)
NT = (((1,), (1,)), ((), ()))
TN = (((0,), (0,)), ((), ()))
VMEM = pl.BlockSpec(memory_space=pltpu.VMEM)
GROUP = 4
UNROLL = 2


def place():
    row = lax.axis_index("row")
    return row // 2, row % 2, lax.axis_index("chan")


def normalise(x, gain):
    width = x.shape[1]
    ones = jnp.full((width, width), 1.0 / width, BF16)
    mean = jnp.dot(x, ones, preferred_element_type=F32)
    centered = x.astype(F32) - mean
    squares = centered * centered
    high = squares.astype(BF16)
    low = (squares - high.astype(F32)).astype(BF16)
    both = jnp.concatenate([high, low], axis=1)
    var = jnp.dot(both, jnp.concatenate([ones, ones]), preferred_element_type=F32)
    return (centered * lax.rsqrt(var + 1e-05) * gain).astype(BF16)


def gated(normed, chosen, valid, first, held):
    _, rows, toks = valid.shape
    wide = chosen.shape[0] // 2
    proj = lax.dot_general(chosen[...], normed, NT, preferred_element_type=F32)
    for g in range(normed.shape[0] // toks):
        mine = proj[:, g * toks : (g + 1) * toks]
        value = (jnp.tanh(mine[:wide]) + 1.0) * (valid[0, pl.ds(first + g, 1), :] * mine[wide:])
        for m in range(toks // LANES):
            spot = pl.ds(first + g, wide, stride=rows + 1)
            held[m, spot, :] = value[:, m * LANES : (m + 1) * LANES]


def write_pieces(outs, held, base):
    row = 0
    for out in outs:
        count, rows, _ = out.shape
        for c in range(count):
            for m in range(held.shape[0]):
                lanes = slice(base + m * LANES, base + (m + 1) * LANES)
                out[c, :, lanes] = held[m, row : row + rows, :].astype(BF16)
            row += rows + 1


def right_rows(pair, valid, gain, chosen, normed_out, held):
    rows, toks, _ = pair.shape

    @pl.loop(0, rows // GROUP, unroll=UNROLL)
    def _(at):
        first = at * GROUP
        x = pair[pl.ds(first, GROUP)].reshape(GROUP * toks, -1)
        normed = normalise(x, gain[...])
        normed_out[pl.ds(first * toks, GROUP * toks), :] = normed
        gated(normed, chosen, valid, first, held)


def right_own_kernel(pair, mask, gain, weight, *rest):
    *outs, normed_out, chosen_right, chosen_left, valid, gain_out, turned, held = rest
    gain_out[...] = gain[...]
    hidden = weight.shape[1] // 4
    part = hidden // 4
    _, y, core = place()
    turned[...] = weight[...].T
    valid[0] = mask[...].astype(F32) * 0.5
    for n in range(4):
        chosen = chosen_left if n < 2 else chosen_right
        half = 0.5 if n % 2 == 0 else 1.0
        for p in range(2):
            start = pl.multiple_of(n * hidden + ((2 * y + core) ^ (2 * p)) * part, part)
            at = (2 * (n % 2) + p) * part
            chosen[at : at + part, :] = turned[pl.ds(start, part), :] * half
    right_rows(pair, valid, gain, chosen_right, normed_out, held)
    write_pieces(outs, held, 0)


def right_twin_kernel(pair, mask, gain, chosen, *rest):
    count = (len(rest) - 3) // 2
    before, (*outs, normed_out, valid, held) = rest[:count], rest[count:]
    for x, out in zip(before, outs):
        out[:, :, : x.shape[2]] = x[...]
    valid[0] = mask[...].astype(F32) * 0.5
    right_rows(pair, valid, gain, chosen, normed_out, held)
    write_pieces(outs, held, pair.shape[1])


def left_kernel(normed0, normed1, valid0, valid1, chosen, *rest):
    outs, held = rest[:-1], rest[-1]
    _, rows, toks = valid0.shape
    for n, (normed, valid) in enumerate(((normed0, valid0), (normed1, valid1))):

        @pl.loop(0, rows // GROUP, unroll=UNROLL)
        def _(at):
            first = at * GROUP
            gated(normed[pl.ds(first * toks, GROUP * toks), :], chosen, valid, first, held)

        write_pieces(outs, held, n * toks)


def gate_kernel(normed, weight, out):
    rows, toks, _ = out.shape

    @pl.loop(0, rows // GROUP, unroll=UNROLL)
    def _(at):
        x = normed[pl.ds(at * GROUP * toks, GROUP * toks), :]
        logits = jnp.dot(x, weight[...], preferred_element_type=F32)
        out[pl.ds(at * GROUP, GROUP)] = (0.5 * jnp.tanh(0.5 * logits) + 0.5).reshape(GROUP, toks, -1)


def product_kernel(mirror, instead, first, n_left, n_right, *rest):
    *refs, held = rest
    planes = [refs[2 * n : 2 * n + 2] for n in range(n_left + n_right)]
    lefts, rights = planes[:n_left], planes[n_left:]
    refs = refs[2 * (n_left + n_right) :]
    other, outs = refs[0], refs[1 if instead else 0 :]
    count, span, toks = outs[0].shape
    rows = span // 2
    z, y, _ = place()
    at_end = (z == 0) | (z == 2 * n_right - 1)
    z = 2 * n_right - 1 - z if mirror else z
    for s in range(n_right):
        for p in range(2):
            start = pl.multiple_of((z + n_right - s) % n_right * span + (y ^ p) * rows, rows)
            at = 0 if p else first
            held[:, pl.ds(start, rows), :] = rights[s][p][at : at + count]
    for c in range(count):
        left = jnp.concatenate([x for own, other in lefts for x in (own[first + c], other[c])], axis=0)
        out = lax.dot_general(left, held[c], NT, preferred_element_type=F32).astype(BF16)
        outs[0][c] = out[:span]
        if n_left == 2:
            outs[1][c, :, :toks] = out[span : span + rows]
            outs[1][c, :, toks:] = out[span + rows :]
    if instead:

        @pl.when(at_end)
        def _():
            outs[1][...] = other[...]


def hand_out_kernel(planes, near, far, end, *outs):
    _, rows, toks = outs[0].shape
    z, _, core = place()
    at_end = (z == 0) | (z == planes - 1)
    for r in range(4):
        is_near = (core ^ (r % 2)) == z // (planes // 2)
        span = slice((r // 2) * rows, (r // 2 + 1) * rows)
        lanes = slice((r // 2) * toks, (r // 2 + 1) * toks)

        @pl.when(is_near)
        def _():
            outs[r][...] = near[:, span, :]

        @pl.when(jnp.logical_not(is_near | at_end))
        def _():
            outs[r][...] = far[:, span, :]

        @pl.when(jnp.logical_not(is_near) & at_end)
        def _():
            outs[r][...] = end[:, :, lanes]


def update_kernel(gain, weight, gate, *rest):
    pieces, out, turned = rest[:-2], rest[-2], rest[-1]
    part = sum(x.shape[0] for x in pieces[::4])
    _, rows, toks = pieces[0].shape
    hidden = 4 * part
    pitch = hidden + 1
    _, y, core = place()
    scale = jnp.broadcast_to(gain[...], (toks, hidden)).T
    for r in range(4):
        base = ((2 * y + core) ^ r) * part
        for piece in pieces[r::4]:
            for c in range(piece.shape[0]):
                value = piece[c].astype(F32)
                for m in range(toks // LANES):
                    turned[m, pl.ds(base + c, rows, stride=pitch), :] = value[
                        :, m * LANES : (m + 1) * LANES
                    ]
            base = base + piece.shape[0]

    @pl.loop(0, rows, unroll=8)
    def _(i):
        x = jnp.concatenate(
            [turned[m, pl.ds(i * pitch, hidden), :] for m in range(toks // LANES)], axis=1
        )
        mean = jnp.mean(x, axis=0, keepdims=True)
        centered = x - mean
        var = jnp.mean(centered * centered, axis=0, keepdims=True)
        pnorm = (centered * lax.rsqrt(var + 1e-05) * scale).astype(BF16)
        mapped = lax.dot_general(pnorm, weight[...], TN, preferred_element_type=F32)
        out[i] = (gate[i] * mapped).astype(BF16)


def kernel(body, name, out_shape, in_specs, scratch=()):
    outs = jax.tree.map(lambda _: VMEM, out_shape)

    def call(*args):
        arrays = [*args, *jax.tree.leaves(out_shape), *scratch]
        size = sum(x.dtype.itemsize * math.prod(x.shape) for x in arrays)
        return pl.pallas_call(
            body,
            out_shape=out_shape,
            in_specs=in_specs,
            out_specs=outs,
            scratch_shapes=list(scratch),
            compiler_params=pltpu.CompilerParams(vmem_limit_bytes=size + SPARE),
            name=name,
        )(*args)

    return call


def local(pair, pair_mask, in_gain, proj_weight, gate_weight, out_gain, out_weight, *, n_row):
    rows, toks, channels = pair.shape
    hidden = proj_weight.shape[1] // 4
    part = hidden // 4
    planes = n_row // 2
    half = planes // 2
    counts = [part * share // sum(SHARES) for share in SHARES]
    groups = range(len(counts))
    def send(x, target, name):
        pairs = []
        for source in range(2 * n_row):
            to = target(source // 4, source // 2 % 2, source % 2)
            if to is not None:
                pairs.append((source, 4 * to[0] + 2 * to[1] + to[2]))
        with jax.named_scope(name):
            return lax.ppermute(x, ("row", "chan"), pairs)

    def after(x, *earlier):
        return lax.optimization_barrier((x, *earlier))[0]

    def in_plane(r):
        return lambda p, b, k: (p, b ^ (r // 2), k ^ (r % 2))

    def shifted(s):
        return lambda p, b, k: (p // half * half + (p + s) % half, b, k)

    def mirrored(p, b, k):
        return (p, b, 1 - k) if p in (0, planes - 1) else (planes - 1 - p, b, k)

    def edge(p, b, k):
        swap = {0: 1, 1: 0, planes - 1: planes - 2, planes - 2: planes - 1}
        return (swap[p], b, k) if p in swap else (p, b, 1 - k)

    def outward(p, b, k):
        return {1: (0, b, k), planes - 2: (planes - 1, b, k)}.get(p)

    gains = in_gain.reshape(1, -1)
    other = in_plane(1)
    weight, gains = send(proj_weight, other, "weights"), send(gains, other, "gain")
    twin_mask, twin = send(pair_mask, other, "mask"), send(after(pair, weight, gains), other, "pair")

    def piece(count, height, depth):
        return jax.ShapeDtypeStruct((count, height, depth), BF16)

    held = pltpu.VMEM((toks // LANES, 2 * part * (rows + 1), LANES), F32)
    rows_all = jax.ShapeDtypeStruct((rows * toks, channels), BF16)
    weights = jax.ShapeDtypeStruct((4 * part, channels), BF16)
    valid_shape = jax.ShapeDtypeStruct((1, rows, toks), F32)
    *mine, normed0, chosen_right, chosen_left, valid, gains = kernel(
        right_own_kernel,
        "right_own",
        [piece(count, rows, toks) for count in (part, *counts)]
        + [rows_all, weights, weights, valid_shape, gains],
        [VMEM] * 4,
        [pltpu.VMEM((4 * hidden, channels), BF16), held],
    )(pair, pair_mask, gains, weight)
    whole = [piece(count, rows, 2 * toks) for count in (part, *counts)]
    *right, normed1, twin_valid = kernel(
        right_twin_kernel,
        "right_twin",
        whole + [rows_all, valid_shape],
        [VMEM] * (4 + len(mine)),
        [held],
    )(twin, twin_mask, gains, chosen_right, *mine)
    right0, right1 = right[0], list(right[1:])

    def mid(name, x, *earlier):
        return send(after(x, *earlier), mirrored, f"mid_{name}")

    def end_right(name, x, *earlier):
        x = after(x, *earlier)
        return [send(x, shifted(s), f"end_right_{name}") for s in range(1, half)]

    def end_left(name, x, *earlier):
        return send(after(x, *earlier), edge, f"end_left_{name}")

    def cross(name, x, *earlier):
        return send(after(x, *earlier), in_plane(2), f"cross_{name}")

    own0 = mid("own_0", right0)
    crossed = cross("right_0", right1[0])
    near0 = end_right("0", right0)
    left = kernel(left_kernel, "left", whole, [VMEM] * 5, [held])(
        normed0, normed1, valid, twin_valid, chosen_left
    )
    left0, left1 = left[0], list(left[1:])
    gate = kernel(
        gate_kernel, "gate", jax.ShapeDtypeStruct((rows, toks, channels), F32), [VMEM] * 2
    )(normed0, gate_weight)
    right1[0] = after(crossed, left0)
    own1 = [mid("own_10", right1[0])]
    near1 = [end_right("10", right1[0])]
    left1[0] = cross("left_0", left1[0], crossed, own0)
    next0 = [mid("next_0", x, own0) for x in near0]
    outer0 = end_left("0", left0, own0)
    right1[1] = cross("right_1", right1[1], left1[0], own1[0], near1[0][-1])
    next1 = [[mid("next_10", x, own1[0], gate) for x in near1[0]]]
    outer1 = [end_left("10", left1[0], near1[0][-1])]
    left1[1] = cross("left_1", left1[1], right1[1], next0[-1])
    own1.append(mid("own_11", right1[1], own1[0]))
    near1.append(end_right("11", right1[1], outer0))
    def products(mirror, first, lefts, rights, name, instead=()):
        span = 2 * rows * len(rights)
        count = lefts[0][1].shape[0]
        args = [x for arrays in (*lefts, *rights) for x in arrays] + [*instead]
        shapes = [piece(count, 2 * rows, span), piece(count, rows, 2 * span)]
        return kernel(
            functools.partial(
                product_kernel, mirror, bool(instead), first, len(lefts), len(rights)
            ),
            name,
            shapes[: len(lefts)],
            [VMEM] * len(args),
            [pltpu.VMEM((count, span, 2 * toks), BF16)],
        )(*args)

    def near_planes(g):
        return list(zip([right0, *near0], [right1[g], *near1[g]]))

    def far_planes(g):
        return list(zip([own0, *next0], [own1[g], *next1[g]]))

    def hand_out(g, close, away, ends):
        handed = kernel(
            functools.partial(hand_out_kernel, planes),
            "hand_out",
            [piece(counts[g], rows, toks)] * 4,
            [VMEM] * 3,
        )(close, away, ends)
        return [handed[0]] + [
            send(handed[r], in_plane(r), f"return_{g}{r}") for r in range(1, 4)
        ]

    close, mine, first = [], [(left0, x) for x in left1], [0, counts[0]]
    for g in groups:
        close += products(False, first[g], [mine[g]], near_planes(g), "near")
    sides = [mine[0], (outer0, outer1[0])]
    away0, swapped = products(True, first[0], sides, far_planes(0), "away", [left1[1]])
    next1.append([mid("next_11", x, next1[0][-1], own1[1], away0) for x in near1[1]])
    swapped = send(swapped, edge, "left_11_and_products_back_0")
    pieces = hand_out(0, close[0], away0, swapped)
    sides = [(after(left0, pieces[0], close[1]), left1[1]), (outer0, swapped)]
    away1, ends = products(True, first[1], sides, far_planes(1), "away")
    ends = send(ends, edge, "products_back_1")
    pieces += hand_out(1, close[1], away1, ends)

    return kernel(
        update_kernel,
        "update",
        jax.ShapeDtypeStruct((rows, toks, channels), BF16),
        [VMEM] * (3 + len(pieces)),
        [pltpu.VMEM((toks // LANES, rows * (hidden + 1), LANES), F32)],
    )(out_gain.reshape(1, -1), out_weight, gate, *pieces)


def solution(mesh):
    placed = (
        P(("groups", "row"), "chan", None),
        P(("groups", "row"), "chan"),
        P(),
        P(),
        P(),
        P(),
        P(),
    )
    return jax.shard_map(
        functools.partial(local, n_row=mesh.shape["row"]),
        mesh=mesh,
        in_specs=placed,
        out_specs=P(("groups", "row"), "chan", None),
        check_vma=False,
    )
```

```python
import functools
import math

import jax
import jax.numpy as jnp
from jax import lax
from jax.experimental import pallas as pl
from jax.experimental.pallas import tpu as pltpu
from jax.sharding import PartitionSpec as P

F32, BF16 = jnp.float32, jnp.bfloat16
LANES = 128
SPARE = 6 * 1024 * 1024
SHARES = (4, 4)
NT = (((1,), (1,)), ((), ()))
TN = (((0,), (0,)), ((), ()))
VMEM = pl.BlockSpec(memory_space=pltpu.VMEM)
GROUP = 4
UNROLL = 4


def place():
    row = lax.axis_index("row")
    return row // 2, row % 2, lax.axis_index("chan")


def normalise(x, gain):
    mean = jnp.mean(x, axis=-1, keepdims=True)
    centered = x - mean
    var = jnp.mean(centered * centered, axis=-1, keepdims=True)
    return (centered * lax.rsqrt(var + 1e-05) * gain).astype(BF16)


def gated(normed, chosen, valid, first, held):
    _, rows, toks = valid.shape
    wide = chosen.shape[0] // 2
    proj = lax.dot_general(chosen[...], normed, NT, preferred_element_type=F32)
    for g in range(normed.shape[0] // toks):
        mine = proj[:, g * toks : (g + 1) * toks]
        value = (jnp.tanh(mine[:wide]) + 1.0) * (valid[0, pl.ds(first + g, 1), :] * mine[wide:])
        for m in range(toks // LANES):
            spot = pl.ds(first + g, wide, stride=rows + 1)
            held[m, spot, :] = value[:, m * LANES : (m + 1) * LANES]


def write_pieces(outs, held, base):
    row = 0
    for out in outs:
        count, rows, _ = out.shape
        for c in range(count):
            for m in range(held.shape[0]):
                lanes = slice(base + m * LANES, base + (m + 1) * LANES)
                out[c, :, lanes] = held[m, row : row + rows, :].astype(BF16)
            row += rows + 1


def right_rows(pair, valid, gain, chosen, normed_out, held):
    rows, toks, _ = pair.shape

    @pl.loop(0, rows // GROUP, unroll=UNROLL)
    def _(at):
        first = at * GROUP
        x = pair[pl.ds(first, GROUP)].astype(F32).reshape(GROUP * toks, -1)
        normed = normalise(x, gain[...])
        normed_out[pl.ds(first * toks, GROUP * toks), :] = normed
        gated(normed, chosen, valid, first, held)


def right_own_kernel(pair, mask, gain, weight, *rest):
    *outs, normed_out, chosen_right, chosen_left, valid, gain_out, turned, held = rest
    gain_out[...] = gain[...]
    hidden = weight.shape[1] // 4
    part = hidden // 4
    _, y, core = place()
    turned[...] = weight[...].T
    valid[0] = mask[...].astype(F32) * 0.5
    for n in range(4):
        chosen = chosen_left if n < 2 else chosen_right
        half = 0.5 if n % 2 == 0 else 1.0
        for p in range(2):
            start = pl.multiple_of(n * hidden + ((2 * y + core) ^ (2 * p)) * part, part)
            at = (2 * (n % 2) + p) * part
            chosen[at : at + part, :] = turned[pl.ds(start, part), :] * half
    right_rows(pair, valid, gain, chosen_right, normed_out, held)
    write_pieces(outs, held, 0)


def right_twin_kernel(pair, mask, gain, chosen, *rest):
    count = (len(rest) - 3) // 2
    before, (*outs, normed_out, valid, held) = rest[:count], rest[count:]
    for x, out in zip(before, outs):
        out[:, :, : x.shape[2]] = x[...]
    valid[0] = mask[...].astype(F32) * 0.5
    right_rows(pair, valid, gain, chosen, normed_out, held)
    write_pieces(outs, held, pair.shape[1])


def left_kernel(normed0, normed1, valid0, valid1, chosen, *rest):
    outs, held = rest[:-1], rest[-1]
    _, rows, toks = valid0.shape
    for n, (normed, valid) in enumerate(((normed0, valid0), (normed1, valid1))):

        @pl.loop(0, rows // GROUP, unroll=UNROLL)
        def _(at):
            first = at * GROUP
            gated(normed[pl.ds(first * toks, GROUP * toks), :], chosen, valid, first, held)

        write_pieces(outs, held, n * toks)


def gate_kernel(normed, weight, out):
    rows, toks, _ = out.shape

    @pl.loop(0, rows // GROUP, unroll=UNROLL)
    def _(at):
        x = normed[pl.ds(at * GROUP * toks, GROUP * toks), :]
        logits = jnp.dot(x, weight[...], preferred_element_type=F32)
        out[pl.ds(at * GROUP, GROUP)] = (0.5 * jnp.tanh(0.5 * logits) + 0.5).reshape(GROUP, toks, -1)


def product_kernel(mirror, instead, first, n_left, n_right, *rest):
    *refs, held = rest
    planes = [refs[2 * n : 2 * n + 2] for n in range(n_left + n_right)]
    lefts, rights = planes[:n_left], planes[n_left:]
    refs = refs[2 * (n_left + n_right) :]
    other, outs = refs[0], refs[1 if instead else 0 :]
    count, span, toks = outs[0].shape
    rows = span // 2
    z, y, _ = place()
    at_end = (z == 0) | (z == 2 * n_right - 1)
    z = 2 * n_right - 1 - z if mirror else z
    for s in range(n_right):
        for p in range(2):
            start = pl.multiple_of((z + n_right - s) % n_right * span + (y ^ p) * rows, rows)
            at = 0 if p else first
            held[:, pl.ds(start, rows), :] = rights[s][p][at : at + count]
    for c in range(count):
        left = jnp.concatenate([x for own, other in lefts for x in (own[first + c], other[c])], axis=0)
        out = lax.dot_general(left, held[c], NT, preferred_element_type=F32).astype(BF16)
        outs[0][c] = out[:span]
        if n_left == 2:
            outs[1][c, :, :toks] = out[span : span + rows]
            outs[1][c, :, toks:] = out[span + rows :]
    if instead:

        @pl.when(at_end)
        def _():
            outs[1][...] = other[...]


def hand_out_kernel(planes, near, far, end, *outs):
    _, rows, toks = outs[0].shape
    z, _, core = place()
    at_end = (z == 0) | (z == planes - 1)
    for r in range(4):
        is_near = (core ^ (r % 2)) == z // (planes // 2)
        span = slice((r // 2) * rows, (r // 2 + 1) * rows)
        lanes = slice((r // 2) * toks, (r // 2 + 1) * toks)

        @pl.when(is_near)
        def _():
            outs[r][...] = near[:, span, :]

        @pl.when(jnp.logical_not(is_near | at_end))
        def _():
            outs[r][...] = far[:, span, :]

        @pl.when(jnp.logical_not(is_near) & at_end)
        def _():
            outs[r][...] = end[:, :, lanes]


def update_kernel(gain, weight, gate, *rest):
    pieces, out, turned = rest[:-2], rest[-2], rest[-1]
    part = sum(x.shape[0] for x in pieces[::4])
    _, rows, toks = pieces[0].shape
    hidden = 4 * part
    pitch = hidden + 1
    _, y, core = place()
    scale = jnp.broadcast_to(gain[...], (toks, hidden)).T
    for r in range(4):
        base = ((2 * y + core) ^ r) * part
        for piece in pieces[r::4]:
            for c in range(piece.shape[0]):
                value = piece[c].astype(F32)
                for m in range(toks // LANES):
                    turned[m, pl.ds(base + c, rows, stride=pitch), :] = value[
                        :, m * LANES : (m + 1) * LANES
                    ]
            base = base + piece.shape[0]

    @pl.loop(0, rows, unroll=16)
    def _(i):
        x = jnp.concatenate(
            [turned[m, pl.ds(i * pitch, hidden), :] for m in range(toks // LANES)], axis=1
        )
        mean = jnp.mean(x, axis=0, keepdims=True)
        centered = x - mean
        var = jnp.mean(centered * centered, axis=0, keepdims=True)
        pnorm = (centered * lax.rsqrt(var + 1e-05) * scale).astype(BF16)
        mapped = lax.dot_general(pnorm, weight[...], TN, preferred_element_type=F32)
        out[i] = (gate[i] * mapped).astype(BF16)


def kernel(body, name, out_shape, in_specs, scratch=()):
    outs = jax.tree.map(lambda _: VMEM, out_shape)

    def call(*args):
        arrays = [*args, *jax.tree.leaves(out_shape), *scratch]
        size = sum(x.dtype.itemsize * math.prod(x.shape) for x in arrays)
        return pl.pallas_call(
            body,
            out_shape=out_shape,
            in_specs=in_specs,
            out_specs=outs,
            scratch_shapes=list(scratch),
            compiler_params=pltpu.CompilerParams(vmem_limit_bytes=size + SPARE),
            name=name,
        )(*args)

    return call


def local(pair, pair_mask, in_gain, proj_weight, gate_weight, out_gain, out_weight, *, n_row):
    rows, toks, channels = pair.shape
    hidden = proj_weight.shape[1] // 4
    part = hidden // 4
    planes = n_row // 2
    half = planes // 2
    counts = [part * share // sum(SHARES) for share in SHARES]
    groups = range(len(counts))
    def send(x, target, name):
        pairs = []
        for source in range(2 * n_row):
            to = target(source // 4, source // 2 % 2, source % 2)
            if to is not None:
                pairs.append((source, 4 * to[0] + 2 * to[1] + to[2]))
        with jax.named_scope(name):
            return lax.ppermute(x, ("row", "chan"), pairs)

    def after(x, *earlier):
        return lax.optimization_barrier((x, *earlier))[0]

    def in_plane(r):
        return lambda p, b, k: (p, b ^ (r // 2), k ^ (r % 2))

    def shifted(s):
        return lambda p, b, k: (p // half * half + (p + s) % half, b, k)

    def mirrored(p, b, k):
        return (p, b, 1 - k) if p in (0, planes - 1) else (planes - 1 - p, b, k)

    def edge(p, b, k):
        swap = {0: 1, 1: 0, planes - 1: planes - 2, planes - 2: planes - 1}
        return (swap[p], b, k) if p in swap else (p, b, 1 - k)

    def outward(p, b, k):
        return {1: (0, b, k), planes - 2: (planes - 1, b, k)}.get(p)

    gains = in_gain.reshape(1, -1)
    twin, twin_mask = send(pair, in_plane(1), "pair"), send(pair_mask, in_plane(1), "mask")

    def piece(count, height, depth):
        return jax.ShapeDtypeStruct((count, height, depth), BF16)

    held = pltpu.VMEM((toks // LANES, 2 * part * (rows + 1), LANES), F32)
    rows_all = jax.ShapeDtypeStruct((rows * toks, channels), BF16)
    weights = jax.ShapeDtypeStruct((4 * part, channels), BF16)
    valid_shape = jax.ShapeDtypeStruct((1, rows, toks), F32)
    *mine, normed0, chosen_right, chosen_left, valid, gains = kernel(
        right_own_kernel,
        "right_own",
        [piece(count, rows, toks) for count in (part, *counts)]
        + [rows_all, weights, weights, valid_shape, gains],
        [VMEM] * 4,
        [pltpu.VMEM((4 * hidden, channels), BF16), held],
    )(pair, pair_mask, gains, proj_weight)
    whole = [piece(count, rows, 2 * toks) for count in (part, *counts)]
    *right, normed1, twin_valid = kernel(
        right_twin_kernel,
        "right_twin",
        whole + [rows_all, valid_shape],
        [VMEM] * (4 + len(mine)),
        [held],
    )(twin, twin_mask, gains, chosen_right, *mine)
    right0, right1 = right[0], list(right[1:])

    def mid(name, x, *earlier):
        return send(after(x, *earlier), mirrored, f"mid_{name}")

    def end_right(name, x, *earlier):
        x = after(x, *earlier)
        return [send(x, shifted(s), f"end_right_{name}") for s in range(1, half)]

    def end_left(name, x, *earlier):
        return send(after(x, *earlier), edge, f"end_left_{name}")

    def cross(name, x, *earlier):
        return send(after(x, *earlier), in_plane(2), f"cross_{name}")

    own0 = mid("own_0", right0)
    crossed = cross("right_0", right1[0])
    near0 = end_right("0", right0)
    left = kernel(left_kernel, "left", whole, [VMEM] * 5, [held])(
        normed0, normed1, valid, twin_valid, chosen_left
    )
    left0, left1 = left[0], list(left[1:])
    gate = kernel(
        gate_kernel, "gate", jax.ShapeDtypeStruct((rows, toks, channels), F32), [VMEM] * 2
    )(normed0, gate_weight)
    right1[0] = after(crossed, left0)
    own1 = [mid("own_10", right1[0])]
    near1 = [end_right("10", right1[0])]
    left1[0] = cross("left_0", left1[0], crossed, own0)
    next0 = [mid("next_0", x, own0) for x in near0]
    outer0 = end_left("0", left0, own0)
    right1[1] = cross("right_1", right1[1], left1[0], own1[0], near1[0][-1])
    next1 = [[mid("next_10", x, own1[0], gate) for x in near1[0]]]
    outer1 = [end_left("10", left1[0], near1[0][-1])]
    left1[1] = cross("left_1", left1[1], right1[1], next0[-1])
    own1.append(mid("own_11", right1[1], own1[0]))
    near1.append(end_right("11", right1[1], outer0))
    def products(mirror, first, lefts, rights, name, instead=()):
        span = 2 * rows * len(rights)
        count = lefts[0][1].shape[0]
        args = [x for arrays in (*lefts, *rights) for x in arrays] + [*instead]
        shapes = [piece(count, 2 * rows, span), piece(count, rows, 2 * span)]
        return kernel(
            functools.partial(
                product_kernel, mirror, bool(instead), first, len(lefts), len(rights)
            ),
            name,
            shapes[: len(lefts)],
            [VMEM] * len(args),
            [pltpu.VMEM((count, span, 2 * toks), BF16)],
        )(*args)

    def near_planes(g):
        return list(zip([right0, *near0], [right1[g], *near1[g]]))

    def far_planes(g):
        return list(zip([own0, *next0], [own1[g], *next1[g]]))

    def hand_out(g, close, away, ends):
        handed = kernel(
            functools.partial(hand_out_kernel, planes),
            "hand_out",
            [piece(counts[g], rows, toks)] * 4,
            [VMEM] * 3,
        )(close, away, ends)
        return [handed[0]] + [
            send(handed[r], in_plane(r), f"return_{g}{r}") for r in range(1, 4)
        ]

    close, mine, first = [], [(left0, x) for x in left1], [0, counts[0]]
    for g in groups:
        close += products(False, first[g], [mine[g]], near_planes(g), "near")
    sides = [mine[0], (outer0, outer1[0])]
    away0, swapped = products(True, first[0], sides, far_planes(0), "away", [left1[1]])
    next1.append([mid("next_11", x, next1[0][-1], own1[1], away0) for x in near1[1]])
    swapped = send(swapped, edge, "left_11_and_products_back_0")
    pieces = hand_out(0, close[0], away0, swapped)
    sides = [(after(left0, pieces[0], close[1]), left1[1]), (outer0, swapped)]
    away1, ends = products(True, first[1], sides, far_planes(1), "away")
    ends = send(ends, edge, "products_back_1")
    pieces += hand_out(1, close[1], away1, ends)

    return kernel(
        update_kernel,
        "update",
        jax.ShapeDtypeStruct((rows, toks, channels), BF16),
        [VMEM] * (3 + len(pieces)),
        [pltpu.VMEM((toks // LANES, rows * (hidden + 1), LANES), F32)],
    )(out_gain.reshape(1, -1), out_weight, gate, *pieces)


def solution(mesh):
    placed = (
        P(("groups", "row"), "chan", None),
        P(("groups", "row"), "chan"),
        P(),
        P(),
        P(),
        P(),
        P(),
    )
    return jax.shard_map(
        functools.partial(local, n_row=mesh.shape["row"]),
        mesh=mesh,
        in_specs=placed,
        out_specs=P(("groups", "row"), "chan", None),
        check_vma=False,
    )
```

```python
import functools
import math

import jax
import jax.numpy as jnp
from jax import lax
from jax.experimental import pallas as pl
from jax.experimental.pallas import tpu as pltpu
from jax.sharding import PartitionSpec as P

F32, BF16 = jnp.float32, jnp.bfloat16
LANES = 128
SPARE = 6 * 1024 * 1024
SHARES = (4, 4)
NT = (((1,), (1,)), ((), ()))
TN = (((0,), (0,)), ((), ()))
VMEM = pl.BlockSpec(memory_space=pltpu.VMEM)
GROUP = 4
UNROLL = 8


def place():
    row = lax.axis_index("row")
    return row // 2, row % 2, lax.axis_index("chan")


def normalise(x, gain):
    mean = jnp.mean(x, axis=-1, keepdims=True)
    centered = x - mean
    var = jnp.mean(centered * centered, axis=-1, keepdims=True)
    return (centered * lax.rsqrt(var + 1e-05) * gain).astype(BF16)


def gated(normed, chosen, valid, first, held):
    _, rows, toks = valid.shape
    wide = chosen.shape[0] // 2
    proj = lax.dot_general(chosen[...], normed, NT, preferred_element_type=F32)
    for g in range(normed.shape[0] // toks):
        mine = proj[:, g * toks : (g + 1) * toks]
        value = (jnp.tanh(mine[:wide]) + 1.0) * (valid[0, pl.ds(first + g, 1), :] * mine[wide:])
        for m in range(toks // LANES):
            spot = pl.ds(first + g, wide, stride=rows + 1)
            held[m, spot, :] = value[:, m * LANES : (m + 1) * LANES]


def write_pieces(outs, held, base):
    row = 0
    for out in outs:
        count, rows, _ = out.shape
        for c in range(count):
            for m in range(held.shape[0]):
                lanes = slice(base + m * LANES, base + (m + 1) * LANES)
                out[c, :, lanes] = held[m, row : row + rows, :].astype(BF16)
            row += rows + 1


def right_rows(pair, valid, gain, chosen, normed_out, held):
    rows, toks, _ = pair.shape

    @pl.loop(0, rows // GROUP, unroll=UNROLL)
    def _(at):
        first = at * GROUP
        x = pair[pl.ds(first, GROUP)].astype(F32).reshape(GROUP * toks, -1)
        normed = normalise(x, gain[...])
        normed_out[pl.ds(first * toks, GROUP * toks), :] = normed
        gated(normed, chosen, valid, first, held)


def right_own_kernel(pair, mask, gain, weight, *rest):
    out, normed_out, first, second, chosen_left, valid, gain_out, turned, held = rest
    gain_out[...] = gain[...]
    hidden = weight.shape[1] // 4
    part = hidden // 4
    _, y, core = place()
    turned[...] = weight[...].T
    valid[0] = mask[...].astype(F32) * 0.5
    for n in range(4):
        half = 0.5 if n % 2 == 0 else 1.0
        for p in range(2):
            start = pl.multiple_of(n * hidden + ((2 * y + core) ^ (2 * p)) * part, part)
            columns = turned[pl.ds(start, part), :] * half
            if n < 2:
                at = (2 * n + p) * part
                chosen_left[at : at + part, :] = columns
            else:
                chosen = second if p else first
                chosen[(n - 2) * part : (n - 1) * part, :] = columns
    right_rows(pair, valid, gain, first, normed_out, held)
    write_pieces([out], held, 0)


def right_twin_kernel(pair, mask, gain, chosen, before, out, normed_out, valid, held):
    out[:, :, : before.shape[2]] = before[...]
    valid[0] = mask[...].astype(F32) * 0.5
    right_rows(pair, valid, gain, chosen, normed_out, held)
    write_pieces([out], held, pair.shape[1])


def rows_kernel(normed0, normed1, valid0, valid1, chosen, *rest):
    *outs, held = rest
    _, rows, toks = valid0.shape
    for n, (normed, valid) in enumerate(((normed0, valid0), (normed1, valid1))):

        @pl.loop(0, rows // GROUP, unroll=UNROLL)
        def _(at):
            first = at * GROUP
            gated(normed[pl.ds(first * toks, GROUP * toks), :], chosen, valid, first, held)

        write_pieces(outs, held, n * toks)


def gate_kernel(normed, weight, out):
    rows, toks, _ = out.shape

    @pl.loop(0, rows // GROUP, unroll=UNROLL)
    def _(at):
        x = normed[pl.ds(at * GROUP * toks, GROUP * toks), :]
        logits = jnp.dot(x, weight[...], preferred_element_type=F32)
        out[pl.ds(at * GROUP, GROUP)] = (0.5 * jnp.tanh(0.5 * logits) + 0.5).reshape(GROUP, toks, -1)


def product_kernel(mirror, instead, first, n_left, n_right, *rest):
    *refs, held = rest
    planes = [refs[2 * n : 2 * n + 2] for n in range(n_left + n_right)]
    lefts, rights = planes[:n_left], planes[n_left:]
    refs = refs[2 * (n_left + n_right) :]
    other, outs = refs[0], refs[1 if instead else 0 :]
    count, span, toks = outs[0].shape
    rows = span // 2
    z, y, _ = place()
    at_end = (z == 0) | (z == 2 * n_right - 1)
    z = 2 * n_right - 1 - z if mirror else z
    for s in range(n_right):
        for p in range(2):
            start = pl.multiple_of((z + n_right - s) % n_right * span + (y ^ p) * rows, rows)
            at = 0 if p else first
            held[:, pl.ds(start, rows), :] = rights[s][p][at : at + count]
    for c in range(count):
        left = jnp.concatenate([x for own, other in lefts for x in (own[first + c], other[c])], axis=0)
        out = lax.dot_general(left, held[c], NT, preferred_element_type=F32).astype(BF16)
        outs[0][c] = out[:span]
        if n_left == 2:
            outs[1][c, :, :toks] = out[span : span + rows]
            outs[1][c, :, toks:] = out[span + rows :]
    if instead:

        @pl.when(at_end)
        def _():
            outs[1][...] = other[...]


def hand_out_kernel(planes, near, far, end, *outs):
    _, rows, toks = outs[0].shape
    z, _, core = place()
    at_end = (z == 0) | (z == planes - 1)
    for r in range(4):
        is_near = (core ^ (r % 2)) == z // (planes // 2)
        span = slice((r // 2) * rows, (r // 2 + 1) * rows)
        lanes = slice((r // 2) * toks, (r // 2 + 1) * toks)

        @pl.when(is_near)
        def _():
            outs[r][...] = near[:, span, :]

        @pl.when(jnp.logical_not(is_near | at_end))
        def _():
            outs[r][...] = far[:, span, :]

        @pl.when(jnp.logical_not(is_near) & at_end)
        def _():
            outs[r][...] = end[:, :, lanes]


def update_kernel(gain, weight, gate, *rest):
    pieces, out, turned = rest[:-2], rest[-2], rest[-1]
    part = sum(x.shape[0] for x in pieces[::4])
    _, rows, toks = pieces[0].shape
    hidden = 4 * part
    pitch = hidden + 1
    _, y, core = place()
    scale = jnp.broadcast_to(gain[...], (toks, hidden)).T
    for r in range(4):
        base = ((2 * y + core) ^ r) * part
        for piece in pieces[r::4]:
            for c in range(piece.shape[0]):
                value = piece[c].astype(F32)
                for m in range(toks // LANES):
                    turned[m, pl.ds(base + c, rows, stride=pitch), :] = value[
                        :, m * LANES : (m + 1) * LANES
                    ]
            base = base + piece.shape[0]

    @pl.loop(0, rows, unroll=32)
    def _(i):
        x = jnp.concatenate(
            [turned[m, pl.ds(i * pitch, hidden), :] for m in range(toks // LANES)], axis=1
        )
        mean = jnp.mean(x, axis=0, keepdims=True)
        centered = x - mean
        var = jnp.mean(centered * centered, axis=0, keepdims=True)
        pnorm = (centered * lax.rsqrt(var + 1e-05) * scale).astype(BF16)
        mapped = lax.dot_general(pnorm, weight[...], TN, preferred_element_type=F32)
        out[i] = (gate[i] * mapped).astype(BF16)


def kernel(body, name, out_shape, in_specs, scratch=()):
    outs = jax.tree.map(lambda _: VMEM, out_shape)

    def call(*args):
        arrays = [*args, *jax.tree.leaves(out_shape), *scratch]
        size = sum(x.dtype.itemsize * math.prod(x.shape) for x in arrays)
        return pl.pallas_call(
            body,
            out_shape=out_shape,
            in_specs=in_specs,
            out_specs=outs,
            scratch_shapes=list(scratch),
            compiler_params=pltpu.CompilerParams(vmem_limit_bytes=size + SPARE),
            name=name,
        )(*args)

    return call


def local(pair, pair_mask, in_gain, proj_weight, gate_weight, out_gain, out_weight, *, n_row):
    rows, toks, channels = pair.shape
    hidden = proj_weight.shape[1] // 4
    part = hidden // 4
    planes = n_row // 2
    half = planes // 2
    counts = [part * share // sum(SHARES) for share in SHARES]
    groups = range(len(counts))
    def send(x, target, name):
        pairs = []
        for source in range(2 * n_row):
            to = target(source // 4, source // 2 % 2, source % 2)
            if to is not None:
                pairs.append((source, 4 * to[0] + 2 * to[1] + to[2]))
        with jax.named_scope(name):
            return lax.ppermute(x, ("row", "chan"), pairs)

    def after(x, *earlier):
        return lax.optimization_barrier((x, *earlier))[0]

    def in_plane(r):
        return lambda p, b, k: (p, b ^ (r // 2), k ^ (r % 2))

    def shifted(s):
        return lambda p, b, k: (p // half * half + (p + s) % half, b, k)

    def mirrored(p, b, k):
        return (p, b, 1 - k) if p in (0, planes - 1) else (planes - 1 - p, b, k)

    def edge(p, b, k):
        swap = {0: 1, 1: 0, planes - 1: planes - 2, planes - 2: planes - 1}
        return (swap[p], b, k) if p in swap else (p, b, 1 - k)

    def outward(p, b, k):
        return {1: (0, b, k), planes - 2: (planes - 1, b, k)}.get(p)

    gains = in_gain.reshape(1, -1)
    twin, twin_mask = send(pair, in_plane(1), "pair"), send(pair_mask, in_plane(1), "mask")

    def piece(count, height, depth):
        return jax.ShapeDtypeStruct((count, height, depth), BF16)

    def columns(count):
        return pltpu.VMEM((toks // LANES, count * (rows + 1), LANES), F32)

    rows_all = jax.ShapeDtypeStruct((rows * toks, channels), BF16)
    valid_shape = jax.ShapeDtypeStruct((1, rows, toks), F32)
    weights = [jax.ShapeDtypeStruct((n * part, channels), BF16) for n in (2, 2, 4)]
    before, normed0, first, second, chosen_left, valid, gains = kernel(
        right_own_kernel,
        "right_own",
        [piece(part, rows, toks), rows_all, *weights, valid_shape, gains],
        [VMEM] * 4,
        [pltpu.VMEM((4 * hidden, channels), BF16), columns(part)],
    )(pair, pair_mask, gains, proj_weight)
    right0, normed1, twin_valid = kernel(
        right_twin_kernel,
        "right_twin",
        [piece(part, rows, 2 * toks), rows_all, valid_shape],
        [VMEM] * 5,
        [columns(part)],
    )(twin, twin_mask, gains, first, before)

    def operand(chosen, shares, name):
        return kernel(
            rows_kernel,
            name,
            [piece(count, rows, 2 * toks) for count in shares],
            [VMEM] * 5,
            [columns(sum(shares))],
        )(normed0, normed1, valid, twin_valid, chosen)

    right1 = list(operand(second, counts, "right_neighbour"))

    def mid(name, x, *earlier):
        return send(after(x, *earlier), mirrored, f"mid_{name}")

    def end_right(name, x, *earlier):
        x = after(x, *earlier)
        return [send(x, shifted(s), f"end_right_{name}") for s in range(1, half)]

    def end_left(name, x, *earlier):
        return send(after(x, *earlier), edge, f"end_left_{name}")

    def cross(name, x, *earlier):
        return send(after(x, *earlier), in_plane(2), f"cross_{name}")

    own0 = mid("own_0", right0)
    crossed = cross("right_0", right1[0])
    near0 = end_right("0", right0)
    left0, *left1 = operand(chosen_left, (part, *counts), "left")
    gate = kernel(
        gate_kernel, "gate", jax.ShapeDtypeStruct((rows, toks, channels), F32), [VMEM] * 2
    )(normed0, gate_weight)
    right1[0] = after(crossed, left0)
    own1 = [mid("own_10", right1[0])]
    near1 = [end_right("10", right1[0])]
    left1[0] = cross("left_0", left1[0], crossed, own0)
    next0 = [mid("next_0", x, own0) for x in near0]
    outer0 = end_left("0", left0, own0)
    right1[1] = cross("right_1", right1[1], left1[0], own1[0], near1[0][-1])
    next1 = [[mid("next_10", x, own1[0], gate) for x in near1[0]]]
    outer1 = [end_left("10", left1[0], near1[0][-1])]
    left1[1] = cross("left_1", left1[1], right1[1], next0[-1])
    own1.append(mid("own_11", right1[1], own1[0]))
    near1.append(end_right("11", right1[1], outer0))
    def products(mirror, first, lefts, rights, name, instead=()):
        span = 2 * rows * len(rights)
        count = lefts[0][1].shape[0]
        args = [x for arrays in (*lefts, *rights) for x in arrays] + [*instead]
        shapes = [piece(count, 2 * rows, span), piece(count, rows, 2 * span)]
        return kernel(
            functools.partial(
                product_kernel, mirror, bool(instead), first, len(lefts), len(rights)
            ),
            name,
            shapes[: len(lefts)],
            [VMEM] * len(args),
            [pltpu.VMEM((count, span, 2 * toks), BF16)],
        )(*args)

    def near_planes(g):
        return list(zip([right0, *near0], [right1[g], *near1[g]]))

    def far_planes(g):
        return list(zip([own0, *next0], [own1[g], *next1[g]]))

    def hand_out(g, close, away, ends):
        handed = kernel(
            functools.partial(hand_out_kernel, planes),
            "hand_out",
            [piece(counts[g], rows, toks)] * 4,
            [VMEM] * 3,
        )(close, away, ends)
        return [handed[0]] + [
            send(handed[r], in_plane(r), f"return_{g}{r}") for r in range(1, 4)
        ]

    close, mine, first = [], [(left0, x) for x in left1], [0, counts[0]]
    for g in groups:
        close += products(False, first[g], [mine[g]], near_planes(g), "near")
    sides = [mine[0], (outer0, outer1[0])]
    away0, swapped = products(True, first[0], sides, far_planes(0), "away", [left1[1]])
    next1.append([mid("next_11", x, next1[0][-1], own1[1], away0) for x in near1[1]])
    swapped = send(swapped, edge, "left_11_and_products_back_0")
    pieces = hand_out(0, close[0], away0, swapped)
    sides = [(after(left0, pieces[0], close[1]), left1[1]), (outer0, swapped)]
    away1, ends = products(True, first[1], sides, far_planes(1), "away")
    ends = send(ends, edge, "products_back_1")
    pieces += hand_out(1, close[1], away1, ends)

    return kernel(
        update_kernel,
        "update",
        jax.ShapeDtypeStruct((rows, toks, channels), BF16),
        [VMEM] * (3 + len(pieces)),
        [pltpu.VMEM((toks // LANES, rows * (hidden + 1), LANES), F32)],
    )(out_gain.reshape(1, -1), out_weight, gate, *pieces)


def solution(mesh):
    placed = (
        P(("groups", "row"), "chan", None),
        P(("groups", "row"), "chan"),
        P(),
        P(),
        P(),
        P(),
        P(),
    )
    return jax.shard_map(
        functools.partial(local, n_row=mesh.shape["row"]),
        mesh=mesh,
        in_specs=placed,
        out_specs=P(("groups", "row"), "chan", None),
        check_vma=False,
    )
```

```python
import functools
import math

import jax
import jax.numpy as jnp
from jax import lax
from jax.experimental import pallas as pl
from jax.experimental.pallas import tpu as pltpu
from jax.sharding import PartitionSpec as P

F32, BF16 = jnp.float32, jnp.bfloat16
LANES = 128
SPARE = 6 * 1024 * 1024
SHARES = (4, 4)
NT = (((1,), (1,)), ((), ()))
TN = (((0,), (0,)), ((), ()))
VMEM = pl.BlockSpec(memory_space=pltpu.VMEM)
GROUP = 4
UNROLL = 8


def place():
    row = lax.axis_index("row")
    return row // 2, row % 2, lax.axis_index("chan")


def normalise(x, gain):
    mean = jnp.mean(x, axis=-1, keepdims=True)
    centered = x - mean
    var = jnp.mean(centered * centered, axis=-1, keepdims=True)
    return (centered * lax.rsqrt(var + 1e-05) * gain).astype(BF16)


def gated(normed, chosen, valid, first, held):
    _, rows, toks = valid.shape
    wide = chosen.shape[0] // 2
    proj = lax.dot_general(chosen[...], normed, NT, preferred_element_type=F32)
    for g in range(normed.shape[0] // toks):
        mine = proj[:, g * toks : (g + 1) * toks]
        value = (jnp.tanh(mine[:wide]) + 1.0) * (valid[0, pl.ds(first + g, 1), :] * mine[wide:])
        for m in range(toks // LANES):
            spot = pl.ds(first + g, wide, stride=rows + 1)
            held[m, spot, :] = value[:, m * LANES : (m + 1) * LANES]


def write_pieces(outs, held, base):
    row = 0
    for out in outs:
        count, rows, _ = out.shape
        for c in range(count):
            for m in range(held.shape[0]):
                lanes = slice(base + m * LANES, base + (m + 1) * LANES)
                out[c, :, lanes] = held[m, row : row + rows, :].astype(BF16)
            row += rows + 1


def right_rows(pair, valid, gain, chosen, normed_out, held):
    rows, toks, _ = pair.shape

    @pl.loop(0, rows // GROUP, unroll=UNROLL)
    def _(at):
        first = at * GROUP
        x = pair[pl.ds(first, GROUP)].astype(F32).reshape(GROUP * toks, -1)
        normed = normalise(x, gain[...])
        normed_out[pl.ds(first * toks, GROUP * toks), :] = normed
        gated(normed, chosen, valid, first, held)


def right_own_kernel(pair, mask, gain, weight, *rest):
    out, normed_out, first, second, chosen_left, valid, gain_out, turned, held = rest
    gain_out[...] = gain[...]
    hidden = weight.shape[1] // 4
    part = hidden // 4
    _, y, core = place()
    turned[...] = weight[...].T
    valid[0] = mask[...].astype(F32) * 0.5
    for n in range(4):
        half = 0.5 if n % 2 == 0 else 1.0
        for p in range(2):
            start = pl.multiple_of(n * hidden + ((2 * y + core) ^ (2 * p)) * part, part)
            columns = turned[pl.ds(start, part), :] * half
            if n < 2:
                at = (2 * n + p) * part
                chosen_left[at : at + part, :] = columns
            else:
                chosen = second if p else first
                chosen[(n - 2) * part : (n - 1) * part, :] = columns
    right_rows(pair, valid, gain, first, normed_out, held)
    write_pieces([out], held, 0)


def right_twin_kernel(pair, mask, gain, chosen, before, out, normed_out, valid, held):
    out[:, :, : before.shape[2]] = before[...]
    valid[0] = mask[...].astype(F32) * 0.5
    right_rows(pair, valid, gain, chosen, normed_out, held)
    write_pieces([out], held, pair.shape[1])


def rows_kernel(normed0, normed1, valid0, valid1, chosen, *rest):
    *outs, held = rest
    _, rows, toks = valid0.shape
    for n, (normed, valid) in enumerate(((normed0, valid0), (normed1, valid1))):

        @pl.loop(0, rows // GROUP, unroll=UNROLL)
        def _(at):
            first = at * GROUP
            gated(normed[pl.ds(first * toks, GROUP * toks), :], chosen, valid, first, held)

        write_pieces(outs, held, n * toks)


def gate_kernel(normed, weight, out):
    rows, toks, _ = out.shape

    @pl.loop(0, rows // GROUP, unroll=UNROLL)
    def _(at):
        x = normed[pl.ds(at * GROUP * toks, GROUP * toks), :]
        logits = jnp.dot(x, weight[...], preferred_element_type=F32)
        out[pl.ds(at * GROUP, GROUP)] = (0.5 * jnp.tanh(0.5 * logits) + 0.5).reshape(GROUP, toks, -1)


def product_kernel(mirror, instead, first, n_left, n_right, *rest):
    *refs, held = rest
    planes = [refs[2 * n : 2 * n + 2] for n in range(n_left + n_right)]
    lefts, rights = planes[:n_left], planes[n_left:]
    refs = refs[2 * (n_left + n_right) :]
    other, outs = refs[0], refs[1 if instead else 0 :]
    count, span, toks = outs[0].shape
    rows = span // 2
    z, y, _ = place()
    at_end = (z == 0) | (z == 2 * n_right - 1)
    z = 2 * n_right - 1 - z if mirror else z
    for s in range(n_right):
        for p in range(2):
            start = pl.multiple_of((z + n_right - s) % n_right * span + (y ^ p) * rows, rows)
            at = 0 if p else first
            held[:, pl.ds(start, rows), :] = rights[s][p][at : at + count]
    for c in range(count):
        left = jnp.concatenate([x for own, other in lefts for x in (own[first + c], other[c])], axis=0)
        out = lax.dot_general(left, held[c], NT, preferred_element_type=F32).astype(BF16)
        outs[0][c] = out[:span]
        if n_left == 2:
            outs[1][c, :, :toks] = out[span : span + rows]
            outs[1][c, :, toks:] = out[span + rows :]
    if instead:

        @pl.when(at_end)
        def _():
            outs[1][...] = other[...]


def hand_out_kernel(planes, near, far, end, *outs):
    _, rows, toks = outs[0].shape
    z, _, core = place()
    at_end = (z == 0) | (z == planes - 1)
    for r in range(4):
        is_near = (core ^ (r % 2)) == z // (planes // 2)
        span = slice((r // 2) * rows, (r // 2 + 1) * rows)
        lanes = slice((r // 2) * toks, (r // 2 + 1) * toks)

        @pl.when(is_near)
        def _():
            outs[r][...] = near[:, span, :]

        @pl.when(jnp.logical_not(is_near | at_end))
        def _():
            outs[r][...] = far[:, span, :]

        @pl.when(jnp.logical_not(is_near) & at_end)
        def _():
            outs[r][...] = end[:, :, lanes]


def update_kernel(gain, weight, gate, *rest):
    pieces, out, turned = rest[:-2], rest[-2], rest[-1]
    part = sum(x.shape[0] for x in pieces[::4])
    _, rows, toks = pieces[0].shape
    hidden = 4 * part
    pitch = hidden + 1
    _, y, core = place()
    scale = jnp.broadcast_to(gain[...], (toks, hidden)).T
    for r in range(4):
        base = ((2 * y + core) ^ r) * part
        for piece in pieces[r::4]:
            for c in range(piece.shape[0]):
                value = piece[c].astype(F32)
                for m in range(toks // LANES):
                    turned[m, pl.ds(base + c, rows, stride=pitch), :] = value[
                        :, m * LANES : (m + 1) * LANES
                    ]
            base = base + piece.shape[0]

    @pl.loop(0, rows, unroll=32)
    def _(i):
        x = jnp.concatenate(
            [turned[m, pl.ds(i * pitch, hidden), :] for m in range(toks // LANES)], axis=1
        )
        mean = jnp.mean(x, axis=0, keepdims=True)
        centered = x - mean
        var = jnp.mean(centered * centered, axis=0, keepdims=True)
        pnorm = (centered * lax.rsqrt(var + 1e-05) * scale).astype(BF16)
        mapped = lax.dot_general(pnorm, weight[...], TN, preferred_element_type=F32)
        out[i] = (gate[i] * mapped).astype(BF16)


def kernel(body, name, out_shape, in_specs, scratch=()):
    outs = jax.tree.map(lambda _: VMEM, out_shape)

    def call(*args):
        arrays = [*args, *jax.tree.leaves(out_shape), *scratch]
        size = sum(x.dtype.itemsize * math.prod(x.shape) for x in arrays)
        return pl.pallas_call(
            body,
            out_shape=out_shape,
            in_specs=in_specs,
            out_specs=outs,
            scratch_shapes=list(scratch),
            compiler_params=pltpu.CompilerParams(
                vmem_limit_bytes=size + SPARE, fuse_transposed_lhs_in_matmul=True
            ),
            name=name,
        )(*args)

    return call


def local(pair, pair_mask, in_gain, proj_weight, gate_weight, out_gain, out_weight, *, n_row):
    rows, toks, channels = pair.shape
    hidden = proj_weight.shape[1] // 4
    part = hidden // 4
    planes = n_row // 2
    half = planes // 2
    counts = [part * share // sum(SHARES) for share in SHARES]
    groups = range(len(counts))
    def send(x, target, name):
        pairs = []
        for source in range(2 * n_row):
            to = target(source // 4, source // 2 % 2, source % 2)
            if to is not None:
                pairs.append((source, 4 * to[0] + 2 * to[1] + to[2]))
        with jax.named_scope(name):
            return lax.ppermute(x, ("row", "chan"), pairs)

    def after(x, *earlier):
        return lax.optimization_barrier((x, *earlier))[0]

    def in_plane(r):
        return lambda p, b, k: (p, b ^ (r // 2), k ^ (r % 2))

    def shifted(s):
        return lambda p, b, k: (p // half * half + (p + s) % half, b, k)

    def mirrored(p, b, k):
        return (p, b, 1 - k) if p in (0, planes - 1) else (planes - 1 - p, b, k)

    def edge(p, b, k):
        swap = {0: 1, 1: 0, planes - 1: planes - 2, planes - 2: planes - 1}
        return (swap[p], b, k) if p in swap else (p, b, 1 - k)

    def outward(p, b, k):
        return {1: (0, b, k), planes - 2: (planes - 1, b, k)}.get(p)

    gains = in_gain.reshape(1, -1)
    twin, twin_mask = send(pair, in_plane(1), "pair"), send(pair_mask, in_plane(1), "mask")

    def piece(count, height, depth):
        return jax.ShapeDtypeStruct((count, height, depth), BF16)

    def columns(count):
        return pltpu.VMEM((toks // LANES, count * (rows + 1), LANES), F32)

    rows_all = jax.ShapeDtypeStruct((rows * toks, channels), BF16)
    valid_shape = jax.ShapeDtypeStruct((1, rows, toks), F32)
    weights = [jax.ShapeDtypeStruct((n * part, channels), BF16) for n in (2, 2, 4)]
    before, normed0, first, second, chosen_left, valid, gains = kernel(
        right_own_kernel,
        "right_own",
        [piece(part, rows, toks), rows_all, *weights, valid_shape, gains],
        [VMEM] * 4,
        [pltpu.VMEM((4 * hidden, channels), BF16), columns(part)],
    )(pair, pair_mask, gains, proj_weight)
    right0, normed1, twin_valid = kernel(
        right_twin_kernel,
        "right_twin",
        [piece(part, rows, 2 * toks), rows_all, valid_shape],
        [VMEM] * 5,
        [columns(part)],
    )(twin, twin_mask, gains, first, before)

    def operand(chosen, shares, name):
        return kernel(
            rows_kernel,
            name,
            [piece(count, rows, 2 * toks) for count in shares],
            [VMEM] * 5,
            [columns(sum(shares))],
        )(normed0, normed1, valid, twin_valid, chosen)

    right1 = list(operand(second, counts, "right_neighbour"))

    def mid(name, x, *earlier):
        return send(after(x, *earlier), mirrored, f"mid_{name}")

    def end_right(name, x, *earlier):
        x = after(x, *earlier)
        return [send(x, shifted(s), f"end_right_{name}") for s in range(1, half)]

    def end_left(name, x, *earlier):
        return send(after(x, *earlier), edge, f"end_left_{name}")

    def cross(name, x, *earlier):
        return send(after(x, *earlier), in_plane(2), f"cross_{name}")

    own0 = mid("own_0", right0)
    crossed = cross("right_0", right1[0])
    near0 = end_right("0", right0)
    left0, *left1 = operand(chosen_left, (part, *counts), "left")
    gate = kernel(
        gate_kernel, "gate", jax.ShapeDtypeStruct((rows, toks, channels), F32), [VMEM] * 2
    )(normed0, gate_weight)
    right1[0] = after(crossed, left0)
    own1 = [mid("own_10", right1[0])]
    near1 = [end_right("10", right1[0])]
    left1[0] = cross("left_0", left1[0], crossed, near0[-1])
    next0 = [mid("next_0", x, own0) for x in near0]
    outer0 = end_left("0", left0, own0)
    right1[1] = cross("right_1", right1[1], left1[0], own1[0], near1[0][-1])
    next1 = [[mid("next_10", x, own1[0], gate) for x in near1[0]]]
    outer1 = [end_left("10", left1[0], near1[0][-1])]
    left1[1] = cross("left_1", left1[1], right1[1], next0[-1])
    own1.append(mid("own_11", right1[1], own1[0]))
    near1.append(end_right("11", right1[1], outer0))
    def products(mirror, first, lefts, rights, name, instead=()):
        span = 2 * rows * len(rights)
        count = lefts[0][1].shape[0]
        args = [x for arrays in (*lefts, *rights) for x in arrays] + [*instead]
        shapes = [piece(count, 2 * rows, span), piece(count, rows, 2 * span)]
        return kernel(
            functools.partial(
                product_kernel, mirror, bool(instead), first, len(lefts), len(rights)
            ),
            name,
            shapes[: len(lefts)],
            [VMEM] * len(args),
            [pltpu.VMEM((count, span, 2 * toks), BF16)],
        )(*args)

    def near_planes(g):
        return list(zip([right0, *near0], [right1[g], *near1[g]]))

    def far_planes(g):
        return list(zip([own0, *next0], [own1[g], *next1[g]]))

    def hand_out(g, close, away, ends):
        handed = kernel(
            functools.partial(hand_out_kernel, planes),
            "hand_out",
            [piece(counts[g], rows, toks)] * 4,
            [VMEM] * 3,
        )(close, away, ends)
        return [handed[0]] + [
            send(handed[r], in_plane(r), f"return_{g}{r}") for r in range(1, 4)
        ]

    close, mine, first = [], [(left0, x) for x in left1], [0, counts[0]]
    for g in groups:
        close += products(False, first[g], [mine[g]], near_planes(g), "near")
    sides = [mine[0], (outer0, outer1[0])]
    away0, swapped = products(True, first[0], sides, far_planes(0), "away", [left1[1]])
    next1.append([mid("next_11", x, next1[0][-1], own1[1], away0) for x in near1[1]])
    swapped = send(swapped, edge, "left_11_and_products_back_0")
    pieces = hand_out(0, close[0], away0, swapped)
    sides = [(after(left0, pieces[0], close[1]), left1[1]), (outer0, swapped)]
    away1, ends = products(True, first[1], sides, far_planes(1), "away")
    ends = send(ends, edge, "products_back_1")
    pieces += hand_out(1, close[1], away1, ends)

    return kernel(
        update_kernel,
        "update",
        jax.ShapeDtypeStruct((rows, toks, channels), BF16),
        [VMEM] * (3 + len(pieces)),
        [pltpu.VMEM((toks // LANES, rows * (hidden + 1), LANES), F32)],
    )(out_gain.reshape(1, -1), out_weight, gate, *pieces)


def solution(mesh):
    placed = (
        P(("groups", "row"), "chan", None),
        P(("groups", "row"), "chan"),
        P(),
        P(),
        P(),
        P(),
        P(),
    )
    return jax.shard_map(
        functools.partial(local, n_row=mesh.shape["row"]),
        mesh=mesh,
        in_specs=placed,
        out_specs=P(("groups", "row"), "chan", None),
        check_vma=False,
    )
```

```python
import functools
import math

import jax
import jax.numpy as jnp
from jax import lax
from jax.experimental import pallas as pl
from jax.experimental.pallas import tpu as pltpu
from jax.sharding import PartitionSpec as P

F32, BF16 = jnp.float32, jnp.bfloat16
LANES = 128
SPARE = 6 * 1024 * 1024
SHARES = (9, 7)
NT = (((1,), (1,)), ((), ()))
TN = (((0,), (0,)), ((), ()))
VMEM = pl.BlockSpec(memory_space=pltpu.VMEM)
GROUP = 4
UNROLL = 8


def place():
    row = lax.axis_index("row")
    return row // 2, row % 2, lax.axis_index("chan")


def normalise(x, gain):
    mean = jnp.mean(x, axis=-1, keepdims=True)
    centered = x - mean
    var = jnp.mean(centered * centered, axis=-1, keepdims=True)
    return (centered * lax.rsqrt(var + 1e-05) * gain).astype(BF16)


def gated(normed, chosen, valid, first, held):
    _, rows, toks = valid.shape
    wide = chosen.shape[0] // 2
    proj = lax.dot_general(chosen[...], normed, NT, preferred_element_type=F32)
    for g in range(normed.shape[0] // toks):
        mine = proj[:, g * toks : (g + 1) * toks]
        value = (jnp.tanh(mine[:wide]) + 1.0) * (valid[0, pl.ds(first + g, 1), :] * mine[wide:])
        for m in range(toks // LANES):
            spot = pl.ds(first + g, wide, stride=rows + 1)
            held[m, spot, :] = value[:, m * LANES : (m + 1) * LANES]


def write_pieces(outs, held, base):
    row = 0
    for out in outs:
        count, rows, _ = out.shape
        for c in range(count):
            for m in range(held.shape[0]):
                lanes = slice(base + m * LANES, base + (m + 1) * LANES)
                out[c, :, lanes] = held[m, row : row + rows, :].astype(BF16)
            row += rows + 1


def right_rows(pair, valid, gain, chosen, normed_out, held):
    rows, toks, _ = pair.shape

    @pl.loop(0, rows // GROUP, unroll=UNROLL)
    def _(at):
        first = at * GROUP
        x = pair[pl.ds(first, GROUP)].astype(F32).reshape(GROUP * toks, -1)
        normed = normalise(x, gain[...])
        normed_out[pl.ds(first * toks, GROUP * toks), :] = normed
        gated(normed, chosen, valid, first, held)


def right_own_kernel(pair, mask, gain, weight, *rest):
    out, normed_out, first, second, chosen_left, valid, gain_out, turned, held = rest
    gain_out[...] = gain[...]
    hidden = weight.shape[1] // 4
    part = hidden // 4
    _, y, core = place()
    turned[...] = weight[...].T
    valid[0] = mask[...].astype(F32) * 0.5
    for n in range(4):
        half = 0.5 if n % 2 == 0 else 1.0
        for p in range(2):
            start = pl.multiple_of(n * hidden + ((2 * y + core) ^ (2 * p)) * part, part)
            columns = turned[pl.ds(start, part), :] * half
            if n < 2:
                at = (2 * n + p) * part
                chosen_left[at : at + part, :] = columns
            else:
                chosen = second if p else first
                chosen[(n - 2) * part : (n - 1) * part, :] = columns
    right_rows(pair, valid, gain, first, normed_out, held)
    write_pieces([out], held, 0)


def right_twin_kernel(pair, mask, gain, chosen, before, out, normed_out, valid, held):
    out[:, :, : before.shape[2]] = before[...]
    valid[0] = mask[...].astype(F32) * 0.5
    right_rows(pair, valid, gain, chosen, normed_out, held)
    write_pieces([out], held, pair.shape[1])


def rows_kernel(normed0, normed1, valid0, valid1, chosen, *rest):
    *outs, held = rest
    _, rows, toks = valid0.shape
    for n, (normed, valid) in enumerate(((normed0, valid0), (normed1, valid1))):

        @pl.loop(0, rows // GROUP, unroll=UNROLL)
        def _(at):
            first = at * GROUP
            gated(normed[pl.ds(first * toks, GROUP * toks), :], chosen, valid, first, held)

        write_pieces(outs, held, n * toks)


def gate_kernel(normed, weight, out):
    rows, toks, _ = out.shape

    @pl.loop(0, rows // GROUP, unroll=UNROLL)
    def _(at):
        x = normed[pl.ds(at * GROUP * toks, GROUP * toks), :]
        logits = jnp.dot(x, weight[...], preferred_element_type=F32)
        out[pl.ds(at * GROUP, GROUP)] = (0.5 * jnp.tanh(0.5 * logits) + 0.5).reshape(GROUP, toks, -1)


def product_kernel(mirror, instead, first, n_left, n_right, *rest):
    *refs, held = rest
    planes = [refs[2 * n : 2 * n + 2] for n in range(n_left + n_right)]
    lefts, rights = planes[:n_left], planes[n_left:]
    refs = refs[2 * (n_left + n_right) :]
    other, outs = refs[0], refs[1 if instead else 0 :]
    count, span, toks = outs[0].shape
    rows = span // 2
    z, y, _ = place()
    at_end = (z == 0) | (z == 2 * n_right - 1)
    z = 2 * n_right - 1 - z if mirror else z
    for s in range(n_right):
        for p in range(2):
            start = pl.multiple_of((z + n_right - s) % n_right * span + (y ^ p) * rows, rows)
            at = 0 if p else first
            held[:, pl.ds(start, rows), :] = rights[s][p][at : at + count]
    for c in range(count):
        left = jnp.concatenate([x for own, other in lefts for x in (own[first + c], other[c])], axis=0)
        out = lax.dot_general(left, held[c], NT, preferred_element_type=F32).astype(BF16)
        outs[0][c] = out[:span]
        if n_left == 2:
            outs[1][c, :, :toks] = out[span : span + rows]
            outs[1][c, :, toks:] = out[span + rows :]
    if instead:

        @pl.when(at_end)
        def _():
            outs[1][: other.shape[0]] = other[...]


def hand_out_kernel(planes, near, far, end, *outs):
    _, rows, toks = outs[0].shape
    z, _, core = place()
    at_end = (z == 0) | (z == planes - 1)
    for r in range(4):
        is_near = (core ^ (r % 2)) == z // (planes // 2)
        span = slice((r // 2) * rows, (r // 2 + 1) * rows)
        lanes = slice((r // 2) * toks, (r // 2 + 1) * toks)

        @pl.when(is_near)
        def _():
            outs[r][...] = near[:, span, :]

        @pl.when(jnp.logical_not(is_near | at_end))
        def _():
            outs[r][...] = far[:, span, :]

        @pl.when(jnp.logical_not(is_near) & at_end)
        def _():
            outs[r][...] = end[:, :, lanes]


def update_kernel(gain, weight, gate, *rest):
    pieces, out, turned = rest[:-2], rest[-2], rest[-1]
    part = sum(x.shape[0] for x in pieces[::4])
    _, rows, toks = pieces[0].shape
    hidden = 4 * part
    pitch = hidden + 1
    _, y, core = place()
    scale = jnp.broadcast_to(gain[...], (toks, hidden)).T
    for r in range(4):
        base = ((2 * y + core) ^ r) * part
        for piece in pieces[r::4]:
            for c in range(piece.shape[0]):
                value = piece[c].astype(F32)
                for m in range(toks // LANES):
                    turned[m, pl.ds(base + c, rows, stride=pitch), :] = value[
                        :, m * LANES : (m + 1) * LANES
                    ]
            base = base + piece.shape[0]

    @pl.loop(0, rows, unroll=32)
    def _(i):
        x = jnp.concatenate(
            [turned[m, pl.ds(i * pitch, hidden), :] for m in range(toks // LANES)], axis=1
        )
        mean = jnp.mean(x, axis=0, keepdims=True)
        centered = x - mean
        var = jnp.mean(centered * centered, axis=0, keepdims=True)
        pnorm = (centered * lax.rsqrt(var + 1e-05) * scale).astype(BF16)
        mapped = lax.dot_general(pnorm, weight[...], TN, preferred_element_type=F32)
        out[i] = (gate[i] * mapped).astype(BF16)


def kernel(body, name, out_shape, in_specs, scratch=()):
    outs = jax.tree.map(lambda _: VMEM, out_shape)

    def call(*args):
        arrays = [*args, *jax.tree.leaves(out_shape), *scratch]
        size = sum(x.dtype.itemsize * math.prod(x.shape) for x in arrays)
        return pl.pallas_call(
            body,
            out_shape=out_shape,
            in_specs=in_specs,
            out_specs=outs,
            scratch_shapes=list(scratch),
            compiler_params=pltpu.CompilerParams(
                vmem_limit_bytes=size + SPARE, fuse_transposed_lhs_in_matmul=True
            ),
            name=name,
        )(*args)

    return call


def local(pair, pair_mask, in_gain, proj_weight, gate_weight, out_gain, out_weight, *, n_row):
    rows, toks, channels = pair.shape
    hidden = proj_weight.shape[1] // 4
    part = hidden // 4
    planes = n_row // 2
    half = planes // 2
    counts = [part * share // sum(SHARES) for share in SHARES]
    groups = range(len(counts))
    def send(x, target, name):
        pairs = []
        for source in range(2 * n_row):
            to = target(source // 4, source // 2 % 2, source % 2)
            if to is not None:
                pairs.append((source, 4 * to[0] + 2 * to[1] + to[2]))
        with jax.named_scope(name):
            return lax.ppermute(x, ("row", "chan"), pairs)

    def after(x, *earlier):
        return lax.optimization_barrier((x, *earlier))[0]

    def in_plane(r):
        return lambda p, b, k: (p, b ^ (r // 2), k ^ (r % 2))

    def shifted(s):
        return lambda p, b, k: (p // half * half + (p + s) % half, b, k)

    def mirrored(p, b, k):
        return (p, b, 1 - k) if p in (0, planes - 1) else (planes - 1 - p, b, k)

    def edge(p, b, k):
        swap = {0: 1, 1: 0, planes - 1: planes - 2, planes - 2: planes - 1}
        return (swap[p], b, k) if p in swap else (p, b, 1 - k)

    def outward(p, b, k):
        return {1: (0, b, k), planes - 2: (planes - 1, b, k)}.get(p)

    gains = in_gain.reshape(1, -1)
    twin, twin_mask = send(pair, in_plane(1), "pair"), send(pair_mask, in_plane(1), "mask")

    def piece(count, height, depth):
        return jax.ShapeDtypeStruct((count, height, depth), BF16)

    def columns(count):
        return pltpu.VMEM((toks // LANES, count * (rows + 1), LANES), F32)

    rows_all = jax.ShapeDtypeStruct((rows * toks, channels), BF16)
    valid_shape = jax.ShapeDtypeStruct((1, rows, toks), F32)
    weights = [jax.ShapeDtypeStruct((n * part, channels), BF16) for n in (2, 2, 4)]
    before, normed0, first, second, chosen_left, valid, gains = kernel(
        right_own_kernel,
        "right_own",
        [piece(part, rows, toks), rows_all, *weights, valid_shape, gains],
        [VMEM] * 4,
        [pltpu.VMEM((4 * hidden, channels), BF16), columns(part)],
    )(pair, pair_mask, gains, proj_weight)
    right0, normed1, twin_valid = kernel(
        right_twin_kernel,
        "right_twin",
        [piece(part, rows, 2 * toks), rows_all, valid_shape],
        [VMEM] * 5,
        [columns(part)],
    )(twin, twin_mask, gains, first, before)

    def operand(chosen, shares, name):
        return kernel(
            rows_kernel,
            name,
            [piece(count, rows, 2 * toks) for count in shares],
            [VMEM] * 5,
            [columns(sum(shares))],
        )(normed0, normed1, valid, twin_valid, chosen)

    right1 = list(operand(second, counts, "right_neighbour"))

    def mid(name, x, *earlier):
        return send(after(x, *earlier), mirrored, f"mid_{name}")

    def end_right(name, x, *earlier):
        x = after(x, *earlier)
        return [send(x, shifted(s), f"end_right_{name}") for s in range(1, half)]

    def end_left(name, x, *earlier):
        return send(after(x, *earlier), edge, f"end_left_{name}")

    def cross(name, x, *earlier):
        return send(after(x, *earlier), in_plane(2), f"cross_{name}")

    own0 = mid("own_0", right0)
    crossed = cross("right_0", right1[0])
    near0 = end_right("0", right0)
    left0, *left1 = operand(chosen_left, (part, *counts), "left")
    gate = kernel(
        gate_kernel, "gate", jax.ShapeDtypeStruct((rows, toks, channels), F32), [VMEM] * 2
    )(normed0, gate_weight)
    right1[0] = after(crossed, left0)
    own1 = [mid("own_10", right1[0])]
    near1 = [end_right("10", right1[0])]
    left1[0] = cross("left_0", left1[0], crossed, near0[-1])
    next0 = [mid("next_0", x, own0) for x in near0]
    outer0 = end_left("0", left0, own0)
    right1[1] = cross("right_1", right1[1], left1[0], own1[0], near1[0][-1])
    next1 = [[mid("next_10", x, own1[0], gate) for x in near1[0]]]
    outer1 = [end_left("10", left1[0], near1[0][-1])]
    left1[1] = cross("left_1", left1[1], right1[1], next0[-1])
    own1.append(mid("own_11", right1[1], own1[0]))
    near1.append(end_right("11", right1[1], outer0))
    def products(mirror, first, lefts, rights, name, instead=()):
        span = 2 * rows * len(rights)
        count = lefts[0][1].shape[0]
        args = [x for arrays in (*lefts, *rights) for x in arrays] + [*instead]
        shapes = [piece(count, 2 * rows, span), piece(count, rows, 2 * span)]
        return kernel(
            functools.partial(
                product_kernel, mirror, bool(instead), first, len(lefts), len(rights)
            ),
            name,
            shapes[: len(lefts)],
            [VMEM] * len(args),
            [pltpu.VMEM((count, span, 2 * toks), BF16)],
        )(*args)

    def near_planes(g):
        return list(zip([right0, *near0], [right1[g], *near1[g]]))

    def far_planes(g):
        return list(zip([own0, *next0], [own1[g], *next1[g]]))

    def hand_out(g, close, away, ends):
        handed = kernel(
            functools.partial(hand_out_kernel, planes),
            "hand_out",
            [piece(counts[g], rows, toks)] * 4,
            [VMEM] * 3,
        )(close, away, ends)
        return [handed[0]] + [
            send(handed[r], in_plane(r), f"return_{g}{r}") for r in range(1, 4)
        ]

    close, mine, first = [], [(left0, x) for x in left1], [0, counts[0]]
    for g in groups:
        close += products(False, first[g], [mine[g]], near_planes(g), "near")
    sides = [mine[0], (outer0, outer1[0])]
    away0, swapped = products(True, first[0], sides, far_planes(0), "away", [left1[1]])
    next1.append([mid("next_11", x, next1[0][-1], own1[1], away0) for x in near1[1]])
    swapped = send(swapped, edge, "left_11_and_products_back_0")
    pieces = hand_out(0, close[0], away0, swapped)
    sides = [(after(left0, pieces[0], close[1]), left1[1]), (outer0, swapped)]
    away1, ends = products(True, first[1], sides, far_planes(1), "away")
    ends = send(ends, edge, "products_back_1")
    pieces += hand_out(1, close[1], away1, ends)

    return kernel(
        update_kernel,
        "update",
        jax.ShapeDtypeStruct((rows, toks, channels), BF16),
        [VMEM] * (3 + len(pieces)),
        [pltpu.VMEM((toks // LANES, rows * (hidden + 1), LANES), F32)],
    )(out_gain.reshape(1, -1), out_weight, gate, *pieces)


def solution(mesh):
    placed = (
        P(("groups", "row"), "chan", None),
        P(("groups", "row"), "chan"),
        P(),
        P(),
        P(),
        P(),
        P(),
    )
    return jax.shard_map(
        functools.partial(local, n_row=mesh.shape["row"]),
        mesh=mesh,
        in_specs=placed,
        out_specs=P(("groups", "row"), "chan", None),
        check_vma=False,
    )
```

```python
import functools
import math

import jax
import jax.numpy as jnp
from jax import lax
from jax.experimental import pallas as pl
from jax.experimental.pallas import tpu as pltpu
from jax.sharding import PartitionSpec as P

F32, BF16 = jnp.float32, jnp.bfloat16
LANES = 128
SPARE = 6 * 1024 * 1024
SHARES = (9, 7)
NT = (((1,), (1,)), ((), ()))
TN = (((0,), (0,)), ((), ()))
VMEM = pl.BlockSpec(memory_space=pltpu.VMEM)
GROUP = 4
UNROLL = 8


def place():
    row = lax.axis_index("row")
    return row // 2, row % 2, lax.axis_index("chan")


def normalise(x, gain):
    mean = jnp.mean(x, axis=-1, keepdims=True)
    centered = x - mean
    var = jnp.mean(centered * centered, axis=-1, keepdims=True)
    return (centered * lax.rsqrt(var + 1e-05) * gain).astype(BF16)


def gated(normed, chosen, valid, first, held):
    _, rows, toks = valid.shape
    wide = chosen.shape[0] // 2
    proj = lax.dot_general(chosen[...], normed, NT, preferred_element_type=F32)
    for g in range(normed.shape[0] // toks):
        mine = proj[:, g * toks : (g + 1) * toks]
        value = (jnp.tanh(mine[:wide]) + 1.0) * (valid[0, pl.ds(first + g, 1), :] * mine[wide:])
        for m in range(toks // LANES):
            spot = pl.ds(first + g, wide, stride=rows + 1)
            held[m, spot, :] = value[:, m * LANES : (m + 1) * LANES]


def write_pieces(outs, held, base):
    row = 0
    for out in outs:
        count, rows, _ = out.shape
        for c in range(count):
            for m in range(held.shape[0]):
                lanes = slice(base + m * LANES, base + (m + 1) * LANES)
                out[c, :, lanes] = held[m, row : row + rows, :].astype(BF16)
            row += rows + 1


def right_rows(pair, valid, gain, chosen, normed_out, held):
    rows, toks, _ = pair.shape

    @pl.loop(0, rows // GROUP, unroll=UNROLL)
    def _(at):
        first = at * GROUP
        x = pair[pl.ds(first, GROUP)].astype(F32).reshape(GROUP * toks, -1)
        normed = normalise(x, gain[...])
        normed_out[pl.ds(first * toks, GROUP * toks), :] = normed
        gated(normed, chosen, valid, first, held)


def right_own_kernel(pair, mask, gain, weight, *rest):
    out, normed_out, first, second, chosen_left, valid, gain_out, turned, held = rest
    gain_out[...] = gain[...]
    hidden = weight.shape[1] // 4
    part = hidden // 4
    _, y, core = place()
    turned[...] = weight[...].T
    valid[0] = mask[...].astype(F32) * 0.5
    for n in range(4):
        half = 0.5 if n % 2 == 0 else 1.0
        for p in range(2):
            start = pl.multiple_of(n * hidden + ((2 * y + core) ^ (2 * p)) * part, part)
            columns = turned[pl.ds(start, part), :] * half
            if n < 2:
                at = (2 * n + p) * part
                chosen_left[at : at + part, :] = columns
            else:
                chosen = second if p else first
                chosen[(n - 2) * part : (n - 1) * part, :] = columns
    right_rows(pair, valid, gain, first, normed_out, held)
    write_pieces([out], held, 0)


def right_twin_kernel(pair, mask, gain, chosen, before, out, normed_out, valid, held):
    out[:, :, : before.shape[2]] = before[...]
    valid[0] = mask[...].astype(F32) * 0.5
    right_rows(pair, valid, gain, chosen, normed_out, held)
    write_pieces([out], held, pair.shape[1])


def rows_kernel(normed0, normed1, valid0, valid1, chosen, *rest):
    *outs, held = rest
    _, rows, toks = valid0.shape
    for n, (normed, valid) in enumerate(((normed0, valid0), (normed1, valid1))):

        @pl.loop(0, rows // GROUP, unroll=UNROLL)
        def _(at):
            first = at * GROUP
            gated(normed[pl.ds(first * toks, GROUP * toks), :], chosen, valid, first, held)

        write_pieces(outs, held, n * toks)


def gate_kernel(normed, weight, out):
    rows, toks, _ = out.shape

    @pl.loop(0, rows // GROUP, unroll=UNROLL)
    def _(at):
        x = normed[pl.ds(at * GROUP * toks, GROUP * toks), :]
        logits = jnp.dot(x, weight[...], preferred_element_type=F32)
        out[pl.ds(at * GROUP, GROUP)] = (0.5 * jnp.tanh(0.5 * logits) + 0.5).reshape(GROUP, toks, -1)


def product_kernel(mirror, instead, first, n_left, n_right, *rest):
    *refs, held = rest
    planes = [refs[2 * n : 2 * n + 2] for n in range(n_left + n_right)]
    lefts, rights = planes[:n_left], planes[n_left:]
    refs = refs[2 * (n_left + n_right) :]
    other, outs = refs[0], refs[1 if instead else 0 :]
    count, span, toks = outs[0].shape
    rows = span // 2
    z, y, _ = place()
    at_end = (z == 0) | (z == 2 * n_right - 1)
    z = 2 * n_right - 1 - z if mirror else z
    for s in range(n_right):
        for p in range(2):
            start = pl.multiple_of((z + n_right - s) % n_right * span + (y ^ p) * rows, rows)
            at = 0 if p else first
            held[:, pl.ds(start, rows), :] = rights[s][p][at : at + count]
    for c in range(count):
        left = jnp.concatenate([x for own, other in lefts for x in (own[first + c], other[c])], axis=0)
        out = lax.dot_general(left, held[c], NT, preferred_element_type=F32).astype(BF16)
        outs[0][c] = out[:span]
        if n_left == 2:
            outs[1][c, :, :toks] = out[span : span + rows]
            outs[1][c, :, toks:] = out[span + rows :]
    if instead:

        @pl.when(at_end)
        def _():
            outs[1][: other.shape[0]] = other[...]


def hand_out_kernel(planes, near, far, end, *outs):
    _, rows, toks = outs[0].shape
    z, _, core = place()
    at_end = (z == 0) | (z == planes - 1)
    for r in range(4):
        is_near = (core ^ (r % 2)) == z // (planes // 2)
        span = slice((r // 2) * rows, (r // 2 + 1) * rows)
        lanes = slice((r // 2) * toks, (r // 2 + 1) * toks)

        @pl.when(is_near)
        def _():
            outs[r][...] = near[:, span, :]

        @pl.when(jnp.logical_not(is_near | at_end))
        def _():
            outs[r][...] = far[:, span, :]

        @pl.when(jnp.logical_not(is_near) & at_end)
        def _():
            outs[r][...] = end[:, :, lanes]


def choose_kernel(planes, at_ends, elsewhere, out):
    z, _, _ = place()
    is_end = (z == 0) | (z == planes - 1)

    @pl.when(is_end)
    def _():
        out[: at_ends.shape[0]] = at_ends[...]

    @pl.when(jnp.logical_not(is_end))
    def _():
        out[: elsewhere.shape[0]] = elsewhere[...]


def last_far_kernel(first, *refs):
    left, outer, next_mid, next_end, last = (refs[2 * n : 2 * n + 2] for n in range(5))
    away, ends, held, padded = refs[10:]
    count, span, _ = away.shape
    rows = span // 2
    z, y, _ = place()
    at_end = (z == 0) | (z == 3)
    at = z // 2 * span
    for p in range(2):
        start = pl.multiple_of(at + (y ^ p) * rows, rows)
        own = slice(first, first + count) if p == 0 else slice(0, count)

        @pl.when(at_end)
        def _():
            held[:, pl.ds(start, rows), :] = next_end[p][own]

        @pl.when(jnp.logical_not(at_end))
        def _():
            held[:, pl.ds(start, rows), :] = next_mid[p][own]

        start = pl.multiple_of(span - at + (y ^ p) * rows, rows)
        held[:, pl.ds(start, rows), :] = last[p][own]
        start = pl.multiple_of(span + (y ^ p) * rows, rows)
        padded[:, pl.ds(start, rows), :] = last[p][own]
    padded[:, :span, :] = jnp.zeros((count, span, padded.shape[2]), BF16)
    padded[:, 2 * span :, :] = jnp.zeros((count, span, padded.shape[2]), BF16)
    for c in range(count):
        mine = jnp.concatenate([left[0][first + c], left[1][c]], axis=0)
        away[c] = lax.dot_general(mine, held[c], NT, preferred_element_type=F32).astype(BF16)
        one = lax.dot_general(
            outer[0][first + c], padded[c, span:, :], NT, preferred_element_type=F32
        )
        two = lax.dot_general(
            outer[1][c], padded[c, : 2 * span, :], NT, preferred_element_type=F32
        )
        ends[c] = (one + two).astype(BF16)


def last_hand_out_kernel(near, far, end, *outs):
    _, rows, toks = outs[0].shape
    z, _, core = place()
    for r in range(4):
        p = r // 2
        is_near = (core ^ (r % 2)) == z // 2
        span = slice(p * rows, (p + 1) * rows)

        @pl.when(is_near)
        def _():
            outs[r][...] = near[:, span, :]

        @pl.when(jnp.logical_not(is_near) & ((z == 1) | (z == 2)))
        def _():
            outs[r][...] = far[:, span, :]

        for plane, upper in ((0, 1), (3, 0)):

            @pl.when(jnp.logical_not(is_near) & (z == plane))
            def _():
                last = end[...].astype(F32)
                if p != upper:
                    last = pltpu.roll(last, toks // 2, 2)
                lane = lax.broadcasted_iota(jnp.int32, last.shape, 2)
                mixed = jnp.where(lane // (toks // 2) == upper, last, far[:, span, :].astype(F32))
                outs[r][...] = mixed.astype(BF16)


def update_kernel(gain, weight, gate, *rest):
    pieces, out, turned = rest[:-2], rest[-2], rest[-1]
    part = sum(x.shape[0] for x in pieces[::4])
    _, rows, toks = pieces[0].shape
    hidden = 4 * part
    pitch = hidden + 1
    _, y, core = place()
    scale = jnp.broadcast_to(gain[...], (toks, hidden)).T
    for r in range(4):
        base = ((2 * y + core) ^ r) * part
        for piece in pieces[r::4]:
            for c in range(piece.shape[0]):
                value = piece[c].astype(F32)
                for m in range(toks // LANES):
                    turned[m, pl.ds(base + c, rows, stride=pitch), :] = value[
                        :, m * LANES : (m + 1) * LANES
                    ]
            base = base + piece.shape[0]

    @pl.loop(0, rows, unroll=32)
    def _(i):
        x = jnp.concatenate(
            [turned[m, pl.ds(i * pitch, hidden), :] for m in range(toks // LANES)], axis=1
        )
        mean = jnp.mean(x, axis=0, keepdims=True)
        centered = x - mean
        var = jnp.mean(centered * centered, axis=0, keepdims=True)
        pnorm = (centered * lax.rsqrt(var + 1e-05) * scale).astype(BF16)
        mapped = lax.dot_general(pnorm, weight[...], TN, preferred_element_type=F32)
        out[i] = (gate[i] * mapped).astype(BF16)


def kernel(body, name, out_shape, in_specs, scratch=()):
    outs = jax.tree.map(lambda _: VMEM, out_shape)

    def call(*args):
        arrays = [*args, *jax.tree.leaves(out_shape), *scratch]
        size = sum(x.dtype.itemsize * math.prod(x.shape) for x in arrays)
        return pl.pallas_call(
            body,
            out_shape=out_shape,
            in_specs=in_specs,
            out_specs=outs,
            scratch_shapes=list(scratch),
            compiler_params=pltpu.CompilerParams(
                vmem_limit_bytes=size + SPARE, fuse_transposed_lhs_in_matmul=True
            ),
            name=name,
        )(*args)

    return call


def local(pair, pair_mask, in_gain, proj_weight, gate_weight, out_gain, out_weight, *, n_row):
    rows, toks, channels = pair.shape
    hidden = proj_weight.shape[1] // 4
    part = hidden // 4
    planes = n_row // 2
    half = planes // 2
    counts = [part * share // sum(SHARES) for share in SHARES]
    groups = range(len(counts))
    def send(x, target, name):
        pairs = []
        for source in range(2 * n_row):
            to = target(source // 4, source // 2 % 2, source % 2)
            if to is not None:
                pairs.append((source, 4 * to[0] + 2 * to[1] + to[2]))
        with jax.named_scope(name):
            return lax.ppermute(x, ("row", "chan"), pairs)

    def after(x, *earlier):
        return lax.optimization_barrier((x, *earlier))[0]

    def in_plane(r):
        return lambda p, b, k: (p, b ^ (r // 2), k ^ (r % 2))

    def shifted(s):
        return lambda p, b, k: (p // half * half + (p + s) % half, b, k)

    def mirrored(p, b, k):
        return (p, b, 1 - k) if p in (0, planes - 1) else (planes - 1 - p, b, k)

    def edge(p, b, k):
        swap = {0: 1, 1: 0, planes - 1: planes - 2, planes - 2: planes - 1}
        return (swap[p], b, k) if p in swap else (p, b, 1 - k)

    def outward(p, b, k):
        return {1: (0, b, k), planes - 2: (planes - 1, b, k)}.get(p)

    gains = in_gain.reshape(1, -1)
    twin, twin_mask = send(pair, in_plane(1), "pair"), send(pair_mask, in_plane(1), "mask")

    def piece(count, height, depth):
        return jax.ShapeDtypeStruct((count, height, depth), BF16)

    def columns(count):
        return pltpu.VMEM((toks // LANES, count * (rows + 1), LANES), F32)

    rows_all = jax.ShapeDtypeStruct((rows * toks, channels), BF16)
    valid_shape = jax.ShapeDtypeStruct((1, rows, toks), F32)
    weights = [jax.ShapeDtypeStruct((n * part, channels), BF16) for n in (2, 2, 4)]
    before, normed0, first, second, chosen_left, valid, gains = kernel(
        right_own_kernel,
        "right_own",
        [piece(part, rows, toks), rows_all, *weights, valid_shape, gains],
        [VMEM] * 4,
        [pltpu.VMEM((4 * hidden, channels), BF16), columns(part)],
    )(pair, pair_mask, gains, proj_weight)
    right0, normed1, twin_valid = kernel(
        right_twin_kernel,
        "right_twin",
        [piece(part, rows, 2 * toks), rows_all, valid_shape],
        [VMEM] * 5,
        [columns(part)],
    )(twin, twin_mask, gains, first, before)

    def operand(chosen, shares, name):
        return kernel(
            rows_kernel,
            name,
            [piece(count, rows, 2 * toks) for count in shares],
            [VMEM] * 5,
            [columns(sum(shares))],
        )(normed0, normed1, valid, twin_valid, chosen)

    right1 = list(operand(second, counts, "right_neighbour"))

    def mid(name, x, *earlier):
        return send(after(x, *earlier), mirrored, f"mid_{name}")

    def end_right(name, x, *earlier):
        x = after(x, *earlier)
        return [send(x, shifted(s), f"end_right_{name}") for s in range(1, half)]

    def end_left(name, x, *earlier):
        return send(after(x, *earlier), edge, f"end_left_{name}")

    def cross(name, x, *earlier):
        return send(after(x, *earlier), in_plane(2), f"cross_{name}")

    own0 = mid("own_0", right0)
    crossed = cross("right_0", right1[0])
    near0 = end_right("0", right0)
    left0, *left1 = operand(chosen_left, (part, *counts), "left")
    gate = kernel(
        gate_kernel, "gate", jax.ShapeDtypeStruct((rows, toks, channels), F32), [VMEM] * 2
    )(normed0, gate_weight)
    split = planes == 4

    def chosen(at_ends, elsewhere):
        if not split:
            return at_ends
        longer = max(at_ends.shape[0], elsewhere.shape[0])
        return kernel(
            functools.partial(choose_kernel, planes),
            "choose",
            piece(longer, rows, 2 * toks),
            [VMEM] * 2,
        )(at_ends, elsewhere)

    right1[0] = after(crossed, left0)
    own1 = [mid("own_10", right1[0])]
    near1 = [end_right("10", right1[0])]
    right1[1] = cross("right_1", right1[1], crossed)
    own1.append(mid("own_11", right1[1]))
    left1[0] = cross("left_0", left1[0], right1[1], near0[-1], near1[0][-1], own1[0])
    next0 = [mid("next_0", x, own0) for x in near0]
    outer0 = end_left("0", chosen(left0, own0), near0[-1])
    next1 = [[mid("next_10", x, own1[0], gate) for x in near1[0]]]
    outer1 = [end_left("10", chosen(left1[0], own1[1]), near1[0][-1])]
    left1[1] = cross("left_1", left1[1], left1[0], own1[1])
    near1.append(end_right("11", right1[1], outer0))

    def products(mirror, first, lefts, rights, name, instead=()):
        span = 2 * rows * len(rights)
        count = lefts[0][1].shape[0]
        args = [x for arrays in (*lefts, *rights) for x in arrays] + [*instead]
        shapes = [piece(count, 2 * rows, span), piece(count, rows, 2 * span)]
        return kernel(
            functools.partial(
                product_kernel, mirror, bool(instead), first, len(lefts), len(rights)
            ),
            name,
            shapes[: len(lefts)],
            [VMEM] * len(args),
            [pltpu.VMEM((count, span, 2 * toks), BF16)],
        )(*args)

    def near_planes(g):
        return list(zip([right0, *near0], [right1[g], *near1[g]]))

    def far_planes(g):
        return list(zip([own0, *next0], [own1[g], *next1[g]]))

    def hand_out(g, body, close, away, ends):
        handed = kernel(
            body,
            "hand_out",
            [piece(counts[g], rows, toks)] * 4,
            [VMEM] * 3,
        )(close, away, ends)
        return [handed[0]] + [
            send(handed[r], in_plane(r), f"return_{g}{r}") for r in range(1, 4)
        ]

    close, mine, first = [], [(left0, x) for x in left1], [0, counts[0]]
    for g in groups:
        close += products(False, first[g], [mine[g]], near_planes(g), "near")
    sides = [mine[0], (outer0, outer1[0])]
    away0, swapped = products(True, first[0], sides, far_planes(0), "away", [left1[1]])
    next1.append([mid("next_11", x, next1[0][-1], own1[1], away0) for x in near1[1]])
    swapped = send(swapped, edge, "left_11_and_products_back_0")
    body = functools.partial(hand_out_kernel, planes)
    pieces = hand_out(0, body, close[0], away0, swapped)
    sides = [(after(left0, pieces[0], close[1]), left1[1]), (outer0, swapped)]
    if split:
        args = [*sides[0], *sides[1], own0, own1[1], outer0, outer1[0], next0[-1], next1[1][-1]]
        away1, ends = kernel(
            functools.partial(last_far_kernel, first[1]),
            "away_last",
            [piece(counts[1], 2 * rows, toks), piece(counts[1], rows, toks)],
            [VMEM] * len(args),
            [pltpu.VMEM((counts[1], n * rows, 2 * toks), BF16) for n in (4, 6)],
        )(*args)
    else:
        away1, ends = products(True, first[1], sides, far_planes(1), "away")
    ends = send(ends, edge, "products_back_1")
    body = last_hand_out_kernel if split else functools.partial(hand_out_kernel, planes)
    pieces += hand_out(1, body, close[1], away1, ends)

    return kernel(
        update_kernel,
        "update",
        jax.ShapeDtypeStruct((rows, toks, channels), BF16),
        [VMEM] * (3 + len(pieces)),
        [pltpu.VMEM((toks // LANES, rows * (hidden + 1), LANES), F32)],
    )(out_gain.reshape(1, -1), out_weight, gate, *pieces)


def solution(mesh):
    placed = (
        P(("groups", "row"), "chan", None),
        P(("groups", "row"), "chan"),
        P(),
        P(),
        P(),
        P(),
        P(),
    )
    return jax.shard_map(
        functools.partial(local, n_row=mesh.shape["row"]),
        mesh=mesh,
        in_specs=placed,
        out_specs=P(("groups", "row"), "chan", None),
        check_vma=False,
    )
```

```python
import functools
import math

import jax
import jax.numpy as jnp
from jax import lax
from jax.experimental import pallas as pl
from jax.experimental.pallas import tpu as pltpu
from jax.sharding import PartitionSpec as P

F32, BF16 = jnp.float32, jnp.bfloat16
LANES = 128
SPARE = 6 * 1024 * 1024
SHARES = (9, 7)
NT = (((1,), (1,)), ((), ()))
TN = (((0,), (0,)), ((), ()))
VMEM = pl.BlockSpec(memory_space=pltpu.VMEM)
GROUP = 4
UNROLL = 8


def place():
    row = lax.axis_index("row")
    return row // 2, row % 2, lax.axis_index("chan")


def normalise(x, gain):
    mean = jnp.mean(x, axis=-1, keepdims=True)
    centered = x - mean
    var = jnp.mean(centered * centered, axis=-1, keepdims=True)
    return (centered * lax.rsqrt(var + 1e-05) * gain).astype(BF16)


def gated(normed, chosen, valid, first, held):
    _, rows, toks = valid.shape
    wide = chosen.shape[0] // 2
    proj = lax.dot_general(chosen[...], normed, NT, preferred_element_type=F32)
    for g in range(normed.shape[0] // toks):
        mine = proj[:, g * toks : (g + 1) * toks]
        value = (jnp.tanh(mine[:wide]) + 1.0) * (valid[0, pl.ds(first + g, 1), :] * mine[wide:])
        for m in range(toks // LANES):
            spot = pl.ds(first + g, wide, stride=rows + 1)
            held[m, spot, :] = value[:, m * LANES : (m + 1) * LANES]


def write_pieces(outs, held, base):
    row = 0
    for out in outs:
        count, rows, _ = out.shape
        for c in range(count):
            for m in range(held.shape[0]):
                lanes = slice(base + m * LANES, base + (m + 1) * LANES)
                out[c, :, lanes] = held[m, row : row + rows, :].astype(BF16)
            row += rows + 1


def right_rows(pair, valid, gain, chosen, normed_out, held):
    rows, toks, _ = pair.shape

    @pl.loop(0, rows // GROUP, unroll=UNROLL)
    def _(at):
        first = at * GROUP
        x = pair[pl.ds(first, GROUP)].astype(F32).reshape(GROUP * toks, -1)
        normed = normalise(x, gain[...])
        normed_out[pl.ds(first * toks, GROUP * toks), :] = normed
        gated(normed, chosen, valid, first, held)


def right_own_kernel(pair, mask, gain, weight, *rest):
    out, normed_out, first, second, chosen_left, valid, gain_out, turned, held = rest
    gain_out[...] = gain[...]
    hidden = weight.shape[1] // 4
    part = hidden // 4
    _, y, core = place()
    turned[...] = weight[...].T
    valid[0] = mask[...].astype(F32) * 0.5
    for n in range(4):
        half = 0.5 if n % 2 == 0 else 1.0
        for p in range(2):
            start = pl.multiple_of(n * hidden + ((2 * y + core) ^ (2 * p)) * part, part)
            columns = turned[pl.ds(start, part), :] * half
            if n < 2:
                at = (2 * n + p) * part
                chosen_left[at : at + part, :] = columns
            else:
                chosen = second if p else first
                chosen[(n - 2) * part : (n - 1) * part, :] = columns
    right_rows(pair, valid, gain, first, normed_out, held)
    write_pieces([out], held, 0)


def right_twin_kernel(pair, mask, gain, chosen, before, out, normed_out, valid, held):
    out[:, :, : before.shape[2]] = before[...]
    valid[0] = mask[...].astype(F32) * 0.5
    right_rows(pair, valid, gain, chosen, normed_out, held)
    write_pieces([out], held, pair.shape[1])


def rows_kernel(normed0, normed1, valid0, valid1, chosen, *rest):
    *outs, held = rest
    _, rows, toks = valid0.shape
    for n, (normed, valid) in enumerate(((normed0, valid0), (normed1, valid1))):

        @pl.loop(0, rows // GROUP, unroll=UNROLL)
        def _(at):
            first = at * GROUP
            gated(normed[pl.ds(first * toks, GROUP * toks), :], chosen, valid, first, held)

        write_pieces(outs, held, n * toks)


def gate_kernel(normed, weight, out):
    rows, toks, _ = out.shape

    @pl.loop(0, rows // GROUP, unroll=UNROLL)
    def _(at):
        x = normed[pl.ds(at * GROUP * toks, GROUP * toks), :]
        logits = jnp.dot(x, weight[...], preferred_element_type=F32)
        out[pl.ds(at * GROUP, GROUP)] = (0.5 * jnp.tanh(0.5 * logits) + 0.5).reshape(GROUP, toks, -1)


def product_kernel(mirror, instead, first, n_left, n_right, *rest):
    *refs, held = rest
    planes = [refs[2 * n : 2 * n + 2] for n in range(n_left + n_right)]
    lefts, rights = planes[:n_left], planes[n_left:]
    refs = refs[2 * (n_left + n_right) :]
    other, outs = refs[0], refs[1 if instead else 0 :]
    count, span, toks = outs[0].shape
    rows = span // 2
    z, y, _ = place()
    at_end = (z == 0) | (z == 2 * n_right - 1)
    z = 2 * n_right - 1 - z if mirror else z
    for s in range(n_right):
        for p in range(2):
            start = pl.multiple_of((z + n_right - s) % n_right * span + (y ^ p) * rows, rows)
            at = 0 if p else first
            held[:, pl.ds(start, rows), :] = rights[s][p][at : at + count]
    for c in range(count):
        left = jnp.concatenate([x for own, other in lefts for x in (own[first + c], other[c])], axis=0)
        out = lax.dot_general(left, held[c], NT, preferred_element_type=F32).astype(BF16)
        outs[0][c] = out[:span]
        if n_left == 2:
            outs[1][c, :, :toks] = out[span : span + rows]
            outs[1][c, :, toks:] = out[span + rows :]
    if instead:

        @pl.when(at_end)
        def _():
            outs[1][: other.shape[0]] = other[...]


def hand_out_kernel(planes, near, far, end, *outs):
    _, rows, toks = outs[0].shape
    z, _, core = place()
    at_end = (z == 0) | (z == planes - 1)
    for r in range(4):
        is_near = (core ^ (r % 2)) == z // (planes // 2)
        span = slice((r // 2) * rows, (r // 2 + 1) * rows)
        lanes = slice((r // 2) * toks, (r // 2 + 1) * toks)

        @pl.when(is_near)
        def _():
            outs[r][...] = near[:, span, :]

        @pl.when(jnp.logical_not(is_near | at_end))
        def _():
            outs[r][...] = far[:, span, :]

        @pl.when(jnp.logical_not(is_near) & at_end)
        def _():
            outs[r][...] = end[:, :, lanes]


def update_kernel(gain, weight, gate, *rest):
    pieces, out, turned = rest[:-2], rest[-2], rest[-1]
    part = sum(x.shape[0] for x in pieces[::4])
    _, rows, toks = pieces[0].shape
    hidden = 4 * part
    pitch = hidden + 1
    _, y, core = place()
    scale = jnp.broadcast_to(gain[...], (toks, hidden)).T
    for r in range(4):
        base = ((2 * y + core) ^ r) * part
        for piece in pieces[r::4]:
            for c in range(piece.shape[0]):
                value = piece[c].astype(F32)
                for m in range(toks // LANES):
                    turned[m, pl.ds(base + c, rows, stride=pitch), :] = value[
                        :, m * LANES : (m + 1) * LANES
                    ]
            base = base + piece.shape[0]

    @pl.loop(0, rows, unroll=32)
    def _(i):
        x = jnp.concatenate(
            [turned[m, pl.ds(i * pitch, hidden), :] for m in range(toks // LANES)], axis=1
        )
        mean = jnp.mean(x, axis=0, keepdims=True)
        centered = x - mean
        var = jnp.mean(centered * centered, axis=0, keepdims=True)
        pnorm = (centered * lax.rsqrt(var + 1e-05) * scale).astype(BF16)
        mapped = lax.dot_general(pnorm, weight[...], TN, preferred_element_type=F32)
        out[i] = (gate[i] * mapped).astype(BF16)


def kernel(body, name, out_shape, in_specs, scratch=()):
    outs = jax.tree.map(lambda _: VMEM, out_shape)

    def call(*args):
        arrays = [*args, *jax.tree.leaves(out_shape), *scratch]
        size = sum(x.dtype.itemsize * math.prod(x.shape) for x in arrays)
        return pl.pallas_call(
            body,
            out_shape=out_shape,
            in_specs=in_specs,
            out_specs=outs,
            scratch_shapes=list(scratch),
            compiler_params=pltpu.CompilerParams(
                vmem_limit_bytes=size + SPARE, fuse_transposed_lhs_in_matmul=True
            ),
            name=name,
        )(*args)

    return call


def local(pair, pair_mask, in_gain, proj_weight, gate_weight, out_gain, out_weight, *, n_row):
    rows, toks, channels = pair.shape
    hidden = proj_weight.shape[1] // 4
    part = hidden // 4
    planes = n_row // 2
    half = planes // 2
    counts = [part * share // sum(SHARES) for share in SHARES]
    groups = range(len(counts))
    def send(x, target, name):
        pairs = []
        for source in range(2 * n_row):
            to = target(source // 4, source // 2 % 2, source % 2)
            if to is not None:
                pairs.append((source, 4 * to[0] + 2 * to[1] + to[2]))
        with jax.named_scope(name):
            return lax.ppermute(x, ("row", "chan"), pairs)

    def after(x, *earlier):
        return lax.optimization_barrier((x, *earlier))[0]

    def in_plane(r):
        return lambda p, b, k: (p, b ^ (r // 2), k ^ (r % 2))

    def shifted(s):
        return lambda p, b, k: (p // half * half + (p + s) % half, b, k)

    def mirrored(p, b, k):
        return (p, b, 1 - k) if p in (0, planes - 1) else (planes - 1 - p, b, k)

    def edge(p, b, k):
        swap = {0: 1, 1: 0, planes - 1: planes - 2, planes - 2: planes - 1}
        return (swap[p], b, k) if p in swap else (p, b, 1 - k)

    def inward(p, b, k):
        return {0: (1, b, k), planes - 1: (planes - 2, b, k)}.get(p)

    gains = in_gain.reshape(1, -1)
    twin, twin_mask = send(pair, in_plane(1), "pair"), send(pair_mask, in_plane(1), "mask")

    def piece(count, height, depth):
        return jax.ShapeDtypeStruct((count, height, depth), BF16)

    def columns(count):
        return pltpu.VMEM((toks // LANES, count * (rows + 1), LANES), F32)

    rows_all = jax.ShapeDtypeStruct((rows * toks, channels), BF16)
    valid_shape = jax.ShapeDtypeStruct((1, rows, toks), F32)
    weights = [jax.ShapeDtypeStruct((n * part, channels), BF16) for n in (2, 2, 4)]
    before, normed0, first, second, chosen_left, valid, gains = kernel(
        right_own_kernel,
        "right_own",
        [piece(part, rows, toks), rows_all, *weights, valid_shape, gains],
        [VMEM] * 4,
        [pltpu.VMEM((4 * hidden, channels), BF16), columns(part)],
    )(pair, pair_mask, gains, proj_weight)
    right0, normed1, twin_valid = kernel(
        right_twin_kernel,
        "right_twin",
        [piece(part, rows, 2 * toks), rows_all, valid_shape],
        [VMEM] * 5,
        [columns(part)],
    )(twin, twin_mask, gains, first, before)

    def operand(chosen, shares, name):
        return kernel(
            rows_kernel,
            name,
            [piece(count, rows, 2 * toks) for count in shares],
            [VMEM] * 5,
            [columns(sum(shares))],
        )(normed0, normed1, valid, twin_valid, chosen)

    right1 = list(operand(second, counts, "right_neighbour"))

    def mid(name, x, *earlier):
        return send(after(x, *earlier), mirrored, f"mid_{name}")

    def end_right(name, x, *earlier):
        x = after(x, *earlier)
        return [send(x, shifted(s), f"end_right_{name}") for s in range(1, half)]

    def end_left(name, x, *earlier):
        return send(after(x, *earlier), inward, f"end_left_{name}")

    def cross(name, x, *earlier):
        return send(after(x, *earlier), in_plane(2), f"cross_{name}")

    own0 = mid("own_0", right0)
    crossed = cross("right_0", right1[0])
    near0 = end_right("0", right0)
    left0, *left1 = operand(chosen_left, (part, *counts), "left")
    gate = kernel(
        gate_kernel, "gate", jax.ShapeDtypeStruct((rows, toks, channels), F32), [VMEM] * 2
    )(normed0, gate_weight)
    right1[0] = after(crossed, left0)
    own1 = [mid("own_10", right1[0])]
    near1 = [end_right("10", right1[0])]
    left1[0] = cross("left_0", left1[0], crossed, near0[-1])
    next0 = [mid("next_0", x, own0) for x in near0]
    outer0 = end_left("0", left0, own0)
    right1[1] = cross("right_1", right1[1], left1[0], own1[0], near1[0][-1])
    next1 = [[mid("next_10", x, own1[0], gate) for x in near1[0]]]
    outer1 = [end_left("10", left1[0], near1[0][-1])]
    left1[1] = cross("left_1", left1[1], right1[1], next0[-1])
    own1.append(mid("own_11", right1[1], own1[0]))
    near1.append(end_right("11", right1[1], outer0))
    def products(mirror, first, lefts, rights, name, instead=()):
        span = 2 * rows * len(rights)
        count = lefts[0][1].shape[0]
        args = [x for arrays in (*lefts, *rights) for x in arrays] + [*instead]
        shapes = [piece(count, 2 * rows, span), piece(count, rows, 2 * span)]
        return kernel(
            functools.partial(
                product_kernel, mirror, bool(instead), first, len(lefts), len(rights)
            ),
            name,
            shapes[: len(lefts)],
            [VMEM] * len(args),
            [pltpu.VMEM((count, span, 2 * toks), BF16)],
        )(*args)

    def near_planes(g):
        return list(zip([right0, *near0], [right1[g], *near1[g]]))

    def far_planes(g):
        return list(zip([own0, *next0], [own1[g], *next1[g]]))

    def hand_out(g, close, away, ends):
        handed = kernel(
            functools.partial(hand_out_kernel, planes),
            "hand_out",
            [piece(counts[g], rows, toks)] * 4,
            [VMEM] * 3,
        )(close, away, ends)
        return [handed[0]] + [
            send(handed[r], in_plane(r), f"return_{g}{r}") for r in range(1, 4)
        ]

    close, mine, first = [], [(left0, x) for x in left1], [0, counts[0]]
    for g in groups:
        close += products(False, first[g], [mine[g]], near_planes(g), "near")
    sides = [mine[0], (outer0, outer1[0])]
    away0, swapped = products(True, first[0], sides, far_planes(0), "away", [left1[1]])
    next1.append([mid("next_11", x, next1[0][-1], own1[1], away0) for x in near1[1]])
    swapped = send(swapped, edge, "left_11_and_products_back_0")
    pieces = hand_out(0, close[0], away0, swapped)
    sides = [(after(left0, pieces[0], close[1]), left1[1]), (outer0, swapped)]
    away1, ends = products(True, first[1], sides, far_planes(1), "away")
    ends = send(ends, edge, "products_back_1")
    pieces += hand_out(1, close[1], away1, ends)

    return kernel(
        update_kernel,
        "update",
        jax.ShapeDtypeStruct((rows, toks, channels), BF16),
        [VMEM] * (3 + len(pieces)),
        [pltpu.VMEM((toks // LANES, rows * (hidden + 1), LANES), F32)],
    )(out_gain.reshape(1, -1), out_weight, gate, *pieces)


def solution(mesh):
    placed = (
        P(("groups", "row"), "chan", None),
        P(("groups", "row"), "chan"),
        P(),
        P(),
        P(),
        P(),
        P(),
    )
    return jax.shard_map(
        functools.partial(local, n_row=mesh.shape["row"]),
        mesh=mesh,
        in_specs=placed,
        out_specs=P(("groups", "row"), "chan", None),
        check_vma=False,
    )
```

```python
import functools
import math

import jax
import jax.numpy as jnp
from jax import lax
from jax.experimental import pallas as pl
from jax.experimental.pallas import tpu as pltpu
from jax.sharding import PartitionSpec as P

F32, BF16 = jnp.float32, jnp.bfloat16
LANES = 128
SPARE = 6 * 1024 * 1024
SHARES = (10, 6)
NT = (((1,), (1,)), ((), ()))
TN = (((0,), (0,)), ((), ()))
VMEM = pl.BlockSpec(memory_space=pltpu.VMEM)
GROUP = 4
UNROLL = 8


def place():
    row = lax.axis_index("row")
    return row // 2, row % 2, lax.axis_index("chan")


def normalise(x, gain):
    mean = jnp.mean(x, axis=-1, keepdims=True)
    centered = x - mean
    var = jnp.mean(centered * centered, axis=-1, keepdims=True)
    return (centered * lax.rsqrt(var + 1e-05) * gain).astype(BF16)


def gated(normed, chosen, valid, first, held):
    _, rows, toks = valid.shape
    wide = chosen.shape[0] // 2
    proj = lax.dot_general(chosen[...], normed, NT, preferred_element_type=F32)
    for g in range(normed.shape[0] // toks):
        mine = proj[:, g * toks : (g + 1) * toks]
        value = (jnp.tanh(mine[:wide]) + 1.0) * (valid[0, pl.ds(first + g, 1), :] * mine[wide:])
        for m in range(toks // LANES):
            spot = pl.ds(first + g, wide, stride=rows + 1)
            held[m, spot, :] = value[:, m * LANES : (m + 1) * LANES]


def write_pieces(outs, held, base):
    row = 0
    for out in outs:
        count, rows, _ = out.shape
        for c in range(count):
            for m in range(held.shape[0]):
                lanes = slice(base + m * LANES, base + (m + 1) * LANES)
                out[c, :, lanes] = held[m, row : row + rows, :].astype(BF16)
            row += rows + 1


def right_rows(pair, valid, gain, chosen, normed_out, held):
    rows, toks, _ = pair.shape

    @pl.loop(0, rows // GROUP, unroll=UNROLL)
    def _(at):
        first = at * GROUP
        x = pair[pl.ds(first, GROUP)].astype(F32).reshape(GROUP * toks, -1)
        normed = normalise(x, gain[...])
        normed_out[pl.ds(first * toks, GROUP * toks), :] = normed
        gated(normed, chosen, valid, first, held)


def right_own_kernel(pair, mask, gain, weight, *rest):
    out, normed_out, first, second, chosen_left, valid, gain_out, turned, held = rest
    gain_out[...] = gain[...]
    hidden = weight.shape[1] // 4
    part = hidden // 4
    _, y, core = place()
    turned[...] = weight[...].T
    valid[0] = mask[...].astype(F32) * 0.5
    for n in range(4):
        half = 0.5 if n % 2 == 0 else 1.0
        for p in range(2):
            start = pl.multiple_of(n * hidden + ((2 * y + core) ^ (2 * p)) * part, part)
            columns = turned[pl.ds(start, part), :] * half
            if n < 2:
                at = (2 * n + p) * part
                chosen_left[at : at + part, :] = columns
            else:
                chosen = second if p else first
                chosen[(n - 2) * part : (n - 1) * part, :] = columns
    right_rows(pair, valid, gain, first, normed_out, held)
    write_pieces([out], held, 0)


def right_twin_kernel(pair, mask, gain, chosen, before, out, normed_out, valid, held):
    out[:, :, : before.shape[2]] = before[...]
    valid[0] = mask[...].astype(F32) * 0.5
    right_rows(pair, valid, gain, chosen, normed_out, held)
    write_pieces([out], held, pair.shape[1])


def rows_kernel(normed0, normed1, valid0, valid1, chosen, *rest):
    *outs, held = rest
    _, rows, toks = valid0.shape
    for n, (normed, valid) in enumerate(((normed0, valid0), (normed1, valid1))):

        @pl.loop(0, rows // GROUP, unroll=UNROLL)
        def _(at):
            first = at * GROUP
            gated(normed[pl.ds(first * toks, GROUP * toks), :], chosen, valid, first, held)

        write_pieces(outs, held, n * toks)


def gate_kernel(normed, weight, out):
    rows, toks, _ = out.shape

    @pl.loop(0, rows // GROUP, unroll=UNROLL)
    def _(at):
        x = normed[pl.ds(at * GROUP * toks, GROUP * toks), :]
        logits = jnp.dot(x, weight[...], preferred_element_type=F32)
        out[pl.ds(at * GROUP, GROUP)] = (0.5 * jnp.tanh(0.5 * logits) + 0.5).reshape(GROUP, toks, -1)


def product_kernel(mirror, instead, first, n_left, n_right, *rest):
    *refs, held = rest
    planes = [refs[2 * n : 2 * n + 2] for n in range(n_left + n_right)]
    lefts, rights = planes[:n_left], planes[n_left:]
    refs = refs[2 * (n_left + n_right) :]
    other, outs = refs[0], refs[1 if instead else 0 :]
    count, span, toks = outs[0].shape
    rows = span // 2
    z, y, _ = place()
    at_end = (z == 0) | (z == 2 * n_right - 1)
    z = 2 * n_right - 1 - z if mirror else z
    for s in range(n_right):
        for p in range(2):
            start = pl.multiple_of((z + n_right - s) % n_right * span + (y ^ p) * rows, rows)
            at = 0 if p else first
            held[:, pl.ds(start, rows), :] = rights[s][p][at : at + count]
    for c in range(count):
        left = jnp.concatenate([x for own, other in lefts for x in (own[first + c], other[c])], axis=0)
        out = lax.dot_general(left, held[c], NT, preferred_element_type=F32).astype(BF16)
        outs[0][c] = out[:span]
        if n_left == 2:
            outs[1][c, :, :toks] = out[span : span + rows]
            outs[1][c, :, toks:] = out[span + rows :]
    if instead:

        @pl.when(at_end)
        def _():
            outs[1][: other.shape[0]] = other[...]


def hand_out_kernel(planes, near, far, end, *outs):
    _, rows, toks = outs[0].shape
    z, _, core = place()
    at_end = (z == 0) | (z == planes - 1)
    for r in range(4):
        is_near = (core ^ (r % 2)) == z // (planes // 2)
        span = slice((r // 2) * rows, (r // 2 + 1) * rows)
        lanes = slice((r // 2) * toks, (r // 2 + 1) * toks)

        @pl.when(is_near)
        def _():
            outs[r][...] = near[:, span, :]

        @pl.when(jnp.logical_not(is_near | at_end))
        def _():
            outs[r][...] = far[:, span, :]

        @pl.when(jnp.logical_not(is_near) & at_end)
        def _():
            outs[r][...] = end[:, :, lanes]


def update_kernel(gain, weight, gate, *rest):
    pieces, out, turned = rest[:-2], rest[-2], rest[-1]
    part = sum(x.shape[0] for x in pieces[::4])
    _, rows, toks = pieces[0].shape
    hidden = 4 * part
    pitch = hidden + 1
    _, y, core = place()
    scale = jnp.broadcast_to(gain[...], (toks, hidden)).T
    for r in range(4):
        base = ((2 * y + core) ^ r) * part
        for piece in pieces[r::4]:
            for c in range(piece.shape[0]):
                value = piece[c].astype(F32)
                for m in range(toks // LANES):
                    turned[m, pl.ds(base + c, rows, stride=pitch), :] = value[
                        :, m * LANES : (m + 1) * LANES
                    ]
            base = base + piece.shape[0]

    @pl.loop(0, rows, unroll=32)
    def _(i):
        x = jnp.concatenate(
            [turned[m, pl.ds(i * pitch, hidden), :] for m in range(toks // LANES)], axis=1
        )
        mean = jnp.mean(x, axis=0, keepdims=True)
        centered = x - mean
        var = jnp.mean(centered * centered, axis=0, keepdims=True)
        pnorm = (centered * lax.rsqrt(var + 1e-05) * scale).astype(BF16)
        mapped = lax.dot_general(pnorm, weight[...], TN, preferred_element_type=F32)
        out[i] = (gate[i] * mapped).astype(BF16)


def kernel(body, name, out_shape, in_specs, scratch=()):
    outs = jax.tree.map(lambda _: VMEM, out_shape)

    def call(*args):
        arrays = [*args, *jax.tree.leaves(out_shape), *scratch]
        size = sum(x.dtype.itemsize * math.prod(x.shape) for x in arrays)
        return pl.pallas_call(
            body,
            out_shape=out_shape,
            in_specs=in_specs,
            out_specs=outs,
            scratch_shapes=list(scratch),
            compiler_params=pltpu.CompilerParams(
                vmem_limit_bytes=size + SPARE, fuse_transposed_lhs_in_matmul=True
            ),
            name=name,
        )(*args)

    return call


def local(pair, pair_mask, in_gain, proj_weight, gate_weight, out_gain, out_weight, *, n_row):
    rows, toks, channels = pair.shape
    hidden = proj_weight.shape[1] // 4
    part = hidden // 4
    planes = n_row // 2
    half = planes // 2
    counts = [part * share // sum(SHARES) for share in SHARES]
    groups = range(len(counts))
    def send(x, target, name):
        pairs = []
        for source in range(2 * n_row):
            to = target(source // 4, source // 2 % 2, source % 2)
            if to is not None:
                pairs.append((source, 4 * to[0] + 2 * to[1] + to[2]))
        with jax.named_scope(name):
            return lax.ppermute(x, ("row", "chan"), pairs)

    def after(x, *earlier):
        return lax.optimization_barrier((x, *earlier))[0]

    def in_plane(r):
        return lambda p, b, k: (p, b ^ (r // 2), k ^ (r % 2))

    def shifted(s):
        return lambda p, b, k: (p // half * half + (p + s) % half, b, k)

    def mirrored(p, b, k):
        return (p, b, 1 - k) if p in (0, planes - 1) else (planes - 1 - p, b, k)

    def edge(p, b, k):
        swap = {0: 1, 1: 0, planes - 1: planes - 2, planes - 2: planes - 1}
        return (swap[p], b, k) if p in swap else (p, b, 1 - k)

    def outward(p, b, k):
        return {1: (0, b, k), planes - 2: (planes - 1, b, k)}.get(p)

    gains = in_gain.reshape(1, -1)
    twin, twin_mask = send(pair, in_plane(1), "pair"), send(pair_mask, in_plane(1), "mask")

    def piece(count, height, depth):
        return jax.ShapeDtypeStruct((count, height, depth), BF16)

    def columns(count):
        return pltpu.VMEM((toks // LANES, count * (rows + 1), LANES), F32)

    rows_all = jax.ShapeDtypeStruct((rows * toks, channels), BF16)
    valid_shape = jax.ShapeDtypeStruct((1, rows, toks), F32)
    weights = [jax.ShapeDtypeStruct((n * part, channels), BF16) for n in (2, 2, 4)]
    before, normed0, first, second, chosen_left, valid, gains = kernel(
        right_own_kernel,
        "right_own",
        [piece(part, rows, toks), rows_all, *weights, valid_shape, gains],
        [VMEM] * 4,
        [pltpu.VMEM((4 * hidden, channels), BF16), columns(part)],
    )(pair, pair_mask, gains, proj_weight)
    right0, normed1, twin_valid = kernel(
        right_twin_kernel,
        "right_twin",
        [piece(part, rows, 2 * toks), rows_all, valid_shape],
        [VMEM] * 5,
        [columns(part)],
    )(twin, twin_mask, gains, first, before)

    def operand(chosen, shares, name):
        return kernel(
            rows_kernel,
            name,
            [piece(count, rows, 2 * toks) for count in shares],
            [VMEM] * 5,
            [columns(sum(shares))],
        )(normed0, normed1, valid, twin_valid, chosen)

    right1 = list(operand(second, counts, "right_neighbour"))

    def mid(name, x, *earlier):
        return send(after(x, *earlier), mirrored, f"mid_{name}")

    def end_right(name, x, *earlier):
        x = after(x, *earlier)
        return [send(x, shifted(s), f"end_right_{name}") for s in range(1, half)]

    def end_left(name, x, *earlier):
        return send(after(x, *earlier), edge, f"end_left_{name}")

    def cross(name, x, *earlier):
        return send(after(x, *earlier), in_plane(2), f"cross_{name}")

    own0 = mid("own_0", right0)
    crossed = cross("right_0", right1[0])
    near0 = end_right("0", right0)
    left0, *left1 = operand(chosen_left, (part, *counts), "left")
    gate = kernel(
        gate_kernel, "gate", jax.ShapeDtypeStruct((rows, toks, channels), F32), [VMEM] * 2
    )(normed0, gate_weight)
    right1[0] = after(crossed, left0)
    own1 = [mid("own_10", right1[0])]
    near1 = [end_right("10", right1[0])]
    left1[0] = cross("left_0", left1[0], crossed, near0[-1])
    next0 = [mid("next_0", x, own0) for x in near0]
    outer0 = end_left("0", left0, own0)
    right1[1] = cross("right_1", right1[1], left1[0], own1[0], near1[0][-1])
    next1 = [[mid("next_10", x, own1[0], gate) for x in near1[0]]]
    outer1 = [end_left("10", left1[0], near1[0][-1])]
    left1[1] = cross("left_1", left1[1], right1[1], next0[-1])
    own1.append(mid("own_11", right1[1], own1[0]))
    near1.append(end_right("11", right1[1], outer0))
    def products(mirror, first, lefts, rights, name, instead=()):
        span = 2 * rows * len(rights)
        count = lefts[0][1].shape[0]
        args = [x for arrays in (*lefts, *rights) for x in arrays] + [*instead]
        shapes = [piece(count, 2 * rows, span), piece(count, rows, 2 * span)]
        return kernel(
            functools.partial(
                product_kernel, mirror, bool(instead), first, len(lefts), len(rights)
            ),
            name,
            shapes[: len(lefts)],
            [VMEM] * len(args),
            [pltpu.VMEM((count, span, 2 * toks), BF16)],
        )(*args)

    def near_planes(g):
        return list(zip([right0, *near0], [right1[g], *near1[g]]))

    def far_planes(g):
        return list(zip([own0, *next0], [own1[g], *next1[g]]))

    def hand_out(g, close, away, ends):
        handed = kernel(
            functools.partial(hand_out_kernel, planes),
            "hand_out",
            [piece(counts[g], rows, toks)] * 4,
            [VMEM] * 3,
        )(close, away, ends)
        return [handed[0]] + [
            send(handed[r], in_plane(r), f"return_{g}{r}") for r in range(1, 4)
        ]

    close, mine, first = [], [(left0, x) for x in left1], [0, counts[0]]
    for g in groups:
        close += products(False, first[g], [mine[g]], near_planes(g), "near")
    sides = [mine[0], (outer0, outer1[0])]
    away0, swapped = products(True, first[0], sides, far_planes(0), "away", [left1[1]])
    next1.append([mid("next_11", x, next1[0][-1], own1[1], away0) for x in near1[1]])
    swapped = send(swapped, edge, "left_11_and_products_back_0")
    pieces = hand_out(0, close[0], away0, swapped)
    sides = [(after(left0, pieces[0], close[1]), left1[1]), (outer0, swapped)]
    away1, ends = products(True, first[1], sides, far_planes(1), "away")
    ends = send(ends, edge, "products_back_1")
    pieces += hand_out(1, close[1], away1, ends)

    return kernel(
        update_kernel,
        "update",
        jax.ShapeDtypeStruct((rows, toks, channels), BF16),
        [VMEM] * (3 + len(pieces)),
        [pltpu.VMEM((toks // LANES, rows * (hidden + 1), LANES), F32)],
    )(out_gain.reshape(1, -1), out_weight, gate, *pieces)


def solution(mesh):
    placed = (
        P(("groups", "row"), "chan", None),
        P(("groups", "row"), "chan"),
        P(),
        P(),
        P(),
        P(),
        P(),
    )
    return jax.shard_map(
        functools.partial(local, n_row=mesh.shape["row"]),
        mesh=mesh,
        in_specs=placed,
        out_specs=P(("groups", "row"), "chan", None),
        check_vma=False,
    )
```

```python
import functools
import math

import jax
import jax.numpy as jnp
from jax import lax
from jax.experimental import pallas as pl
from jax.experimental.pallas import tpu as pltpu
from jax.sharding import PartitionSpec as P

F32, BF16 = jnp.float32, jnp.bfloat16
LANES = 128
SPARE = 6 * 1024 * 1024
GRANT = 52 * 1024 * 1024
SHARES = (9, 7)
NT = (((1,), (1,)), ((), ()))
TN = (((0,), (0,)), ((), ()))
VMEM = pl.BlockSpec(memory_space=pltpu.VMEM)
GROUP = 4
UNROLL = 8
PARTS = 4


def place():
    row = lax.axis_index("row")
    return row // 2, row % 2, lax.axis_index("chan")


def normalise(x, gain):
    mean = jnp.mean(x, axis=-1, keepdims=True)
    centered = x - mean
    var = jnp.mean(centered * centered, axis=-1, keepdims=True)
    return (centered * lax.rsqrt(var + 1e-05) * gain).astype(BF16)


def gated(normed, chosen, valid, first, held):
    _, rows, toks = valid.shape
    wide = chosen.shape[0] // 2
    proj = lax.dot_general(chosen[...], normed, NT, preferred_element_type=F32)
    for g in range(normed.shape[0] // toks):
        mine = proj[:, g * toks : (g + 1) * toks]
        value = (jnp.tanh(mine[:wide]) + 1.0) * (valid[0, pl.ds(first + g, 1), :] * mine[wide:])
        for m in range(toks // LANES):
            spot = pl.ds(first + g, wide, stride=rows + 1)
            held[m, spot, :] = value[:, m * LANES : (m + 1) * LANES]


def write_pieces(outs, held, base):
    row = 0
    for out in outs:
        count, rows, _ = out.shape
        for c in range(count):
            for m in range(held.shape[0]):
                lanes = slice(base + m * LANES, base + (m + 1) * LANES)
                out[c, :, lanes] = held[m, row : row + rows, :].astype(BF16)
            row += rows + 1


def right_rows(pair, valid, gain, chosen, normed_out, held, start=0, rows=None):
    toks = pair.shape[1]
    rows = rows or pair.shape[0]

    @pl.loop(0, rows // GROUP, unroll=UNROLL)
    def _(at):
        first = start + at * GROUP
        x = pair[pl.ds(first, GROUP)].astype(F32).reshape(GROUP * toks, -1)
        normed = normalise(x, gain[...])
        normed_out[pl.ds(first * toks, GROUP * toks), :] = normed
        gated(normed, chosen, valid, first, held)


def right_own_kernel(pair, mask, gain, weight, *rest):
    out, normed_out, first, second, chosen_left, valid, gain_out, turned, held, arrived, sems = rest
    step = arrived.shape[0] // PARTS
    copies = []
    for n in range(PARTS):
        span = pl.ds(n * step, step)
        copies.append(pltpu.make_async_copy(pair.at[span], arrived.at[span], sems.at[n]))
        copies[n].start()
    gain_out[...] = gain[...]
    hidden = weight.shape[1] // 4
    part = hidden // 4
    _, y, core = place()
    turned[...] = weight[...].T
    valid[0] = mask[...].astype(F32) * 0.5
    for n in range(4):
        half = 0.5 if n % 2 == 0 else 1.0
        for p in range(2):
            start = pl.multiple_of(n * hidden + ((2 * y + core) ^ (2 * p)) * part, part)
            columns = turned[pl.ds(start, part), :] * half
            if n < 2:
                at = (2 * n + p) * part
                chosen_left[at : at + part, :] = columns
            else:
                chosen = second if p else first
                chosen[(n - 2) * part : (n - 1) * part, :] = columns
    for n in range(PARTS):
        copies[n].wait()
        right_rows(arrived, valid, gain, first, normed_out, held, n * step, step)
    write_pieces([out], held, 0)


def right_twin_kernel(pair, mask, gain, chosen, before, out, normed_out, valid, held):
    out[:, :, : before.shape[2]] = before[...]
    valid[0] = mask[...].astype(F32) * 0.5
    right_rows(pair, valid, gain, chosen, normed_out, held)
    write_pieces([out], held, pair.shape[1])


def rows_kernel(normed0, normed1, valid0, valid1, chosen, *rest):
    *outs, held = rest
    _, rows, toks = valid0.shape
    for n, (normed, valid) in enumerate(((normed0, valid0), (normed1, valid1))):

        @pl.loop(0, rows // GROUP, unroll=UNROLL)
        def _(at):
            first = at * GROUP
            gated(normed[pl.ds(first * toks, GROUP * toks), :], chosen, valid, first, held)

        write_pieces(outs, held, n * toks)


def gate_kernel(normed, weight, out):
    rows, toks, _ = out.shape

    @pl.loop(0, rows // GROUP, unroll=UNROLL)
    def _(at):
        x = normed[pl.ds(at * GROUP * toks, GROUP * toks), :]
        logits = jnp.dot(x, weight[...], preferred_element_type=F32)
        out[pl.ds(at * GROUP, GROUP)] = (0.5 * jnp.tanh(0.5 * logits) + 0.5).reshape(GROUP, toks, -1)


def product_kernel(mirror, instead, first, n_left, n_right, *rest):
    *refs, held = rest
    planes = [refs[2 * n : 2 * n + 2] for n in range(n_left + n_right)]
    lefts, rights = planes[:n_left], planes[n_left:]
    refs = refs[2 * (n_left + n_right) :]
    other, outs = refs[0], refs[1 if instead else 0 :]
    count, span, toks = outs[0].shape
    rows = span // 2
    z, y, _ = place()
    at_end = (z == 0) | (z == 2 * n_right - 1)
    z = 2 * n_right - 1 - z if mirror else z
    for s in range(n_right):
        for p in range(2):
            start = pl.multiple_of((z + n_right - s) % n_right * span + (y ^ p) * rows, rows)
            at = 0 if p else first
            held[:, pl.ds(start, rows), :] = rights[s][p][at : at + count]
    for c in range(count):
        left = jnp.concatenate([x for own, other in lefts for x in (own[first + c], other[c])], axis=0)
        out = lax.dot_general(left, held[c], NT, preferred_element_type=F32).astype(BF16)
        outs[0][c] = out[:span]
        if n_left == 2:
            outs[1][c, :, :toks] = out[span : span + rows]
            outs[1][c, :, toks:] = out[span + rows :]
    if instead:

        @pl.when(at_end)
        def _():
            outs[1][: other.shape[0]] = other[...]


def hand_out_kernel(planes, near, far, end, *outs):
    _, rows, toks = outs[0].shape
    z, _, core = place()
    at_end = (z == 0) | (z == planes - 1)
    for r in range(4):
        is_near = (core ^ (r % 2)) == z // (planes // 2)
        span = slice((r // 2) * rows, (r // 2 + 1) * rows)
        lanes = slice((r // 2) * toks, (r // 2 + 1) * toks)

        @pl.when(is_near)
        def _():
            outs[r][...] = near[:, span, :]

        @pl.when(jnp.logical_not(is_near | at_end))
        def _():
            outs[r][...] = far[:, span, :]

        @pl.when(jnp.logical_not(is_near) & at_end)
        def _():
            outs[r][...] = end[:, :, lanes]


def update_kernel(gain, weight, gate, *rest):
    pieces, out, turned = rest[:-2], rest[-2], rest[-1]
    part = sum(x.shape[0] for x in pieces[::4])
    _, rows, toks = pieces[0].shape
    hidden = 4 * part
    pitch = hidden + 1
    _, y, core = place()
    scale = jnp.broadcast_to(gain[...], (toks, hidden)).T
    for r in range(4):
        base = ((2 * y + core) ^ r) * part
        for piece in pieces[r::4]:
            for c in range(piece.shape[0]):
                value = piece[c].astype(F32)
                for m in range(toks // LANES):
                    turned[m, pl.ds(base + c, rows, stride=pitch), :] = value[
                        :, m * LANES : (m + 1) * LANES
                    ]
            base = base + piece.shape[0]

    @pl.loop(0, rows, unroll=32)
    def _(i):
        x = jnp.concatenate(
            [turned[m, pl.ds(i * pitch, hidden), :] for m in range(toks // LANES)], axis=1
        )
        mean = jnp.mean(x, axis=0, keepdims=True)
        centered = x - mean
        var = jnp.mean(centered * centered, axis=0, keepdims=True)
        pnorm = (centered * lax.rsqrt(var + 1e-05) * scale).astype(BF16)
        mapped = lax.dot_general(pnorm, weight[...], TN, preferred_element_type=F32)
        out[i] = (gate[i] * mapped).astype(BF16)


def kernel(body, name, out_shape, in_specs, scratch=(), limit=None):
    outs = jax.tree.map(lambda _: VMEM, out_shape)

    def call(*args):
        arrays = [*args, *jax.tree.leaves(out_shape), *scratch]
        arrays = [x for x in arrays if hasattr(x.dtype, "itemsize")]
        size = sum(x.dtype.itemsize * math.prod(x.shape) for x in arrays)
        return pl.pallas_call(
            body,
            out_shape=out_shape,
            in_specs=in_specs,
            out_specs=outs,
            scratch_shapes=list(scratch),
            compiler_params=pltpu.CompilerParams(
                vmem_limit_bytes=limit or size + SPARE, fuse_transposed_lhs_in_matmul=True
            ),
            name=name,
        )(*args)

    return call


def local(pair, pair_mask, in_gain, proj_weight, gate_weight, out_gain, out_weight, *, n_row):
    rows, toks, channels = pair.shape
    hidden = proj_weight.shape[1] // 4
    part = hidden // 4
    planes = n_row // 2
    half = planes // 2
    counts = [part * share // sum(SHARES) for share in SHARES]
    groups = range(len(counts))
    def send(x, target, name):
        pairs = []
        for source in range(2 * n_row):
            to = target(source // 4, source // 2 % 2, source % 2)
            if to is not None:
                pairs.append((source, 4 * to[0] + 2 * to[1] + to[2]))
        with jax.named_scope(name):
            return lax.ppermute(x, ("row", "chan"), pairs)

    def after(x, *earlier):
        return lax.optimization_barrier((x, *earlier))[0]

    def in_plane(r):
        return lambda p, b, k: (p, b ^ (r // 2), k ^ (r % 2))

    def shifted(s):
        return lambda p, b, k: (p // half * half + (p + s) % half, b, k)

    def mirrored(p, b, k):
        return (p, b, 1 - k) if p in (0, planes - 1) else (planes - 1 - p, b, k)

    def edge(p, b, k):
        swap = {0: 1, 1: 0, planes - 1: planes - 2, planes - 2: planes - 1}
        return (swap[p], b, k) if p in swap else (p, b, 1 - k)

    def outward(p, b, k):
        return {1: (0, b, k), planes - 2: (planes - 1, b, k)}.get(p)

    gains = in_gain.reshape(1, -1)
    twin, twin_mask = send(pair, in_plane(1), "pair"), send(pair_mask, in_plane(1), "mask")

    def piece(count, height, depth):
        return jax.ShapeDtypeStruct((count, height, depth), BF16)

    def columns(count):
        return pltpu.VMEM((toks // LANES, count * (rows + 1), LANES), F32)

    rows_all = jax.ShapeDtypeStruct((rows * toks, channels), BF16)
    valid_shape = jax.ShapeDtypeStruct((1, rows, toks), F32)
    weights = [jax.ShapeDtypeStruct((n * part, channels), BF16) for n in (2, 2, 4)]
    before, normed0, first, second, chosen_left, valid, gains = kernel(
        right_own_kernel,
        "right_own",
        [piece(part, rows, toks), rows_all, *weights, valid_shape, gains],
        [pl.BlockSpec(memory_space=pl.ANY)] + [VMEM] * 3,
        [
            pltpu.VMEM((4 * hidden, channels), BF16),
            columns(part),
            pltpu.VMEM(pair.shape, BF16),
            pltpu.SemaphoreType.DMA((PARTS,)),
        ],
        GRANT,
    )(pair, pair_mask, gains, proj_weight)
    right0, normed1, twin_valid = kernel(
        right_twin_kernel,
        "right_twin",
        [piece(part, rows, 2 * toks), rows_all, valid_shape],
        [VMEM] * 5,
        [columns(part)],
    )(twin, twin_mask, gains, first, before)

    def operand(chosen, shares, name):
        return kernel(
            rows_kernel,
            name,
            [piece(count, rows, 2 * toks) for count in shares],
            [VMEM] * 5,
            [columns(sum(shares))],
        )(normed0, normed1, valid, twin_valid, chosen)

    right1 = list(operand(second, counts, "right_neighbour"))

    def mid(name, x, *earlier):
        return send(after(x, *earlier), mirrored, f"mid_{name}")

    def end_right(name, x, *earlier):
        x = after(x, *earlier)
        return [send(x, shifted(s), f"end_right_{name}") for s in range(1, half)]

    def end_left(name, x, *earlier):
        return send(after(x, *earlier), edge, f"end_left_{name}")

    def cross(name, x, *earlier):
        return send(after(x, *earlier), in_plane(2), f"cross_{name}")

    own0 = mid("own_0", right0)
    crossed = cross("right_0", right1[0])
    near0 = end_right("0", right0)
    left0, *left1 = operand(chosen_left, (part, *counts), "left")
    gate = kernel(
        gate_kernel, "gate", jax.ShapeDtypeStruct((rows, toks, channels), F32), [VMEM] * 2
    )(normed0, gate_weight)
    right1[0] = after(crossed, left0)
    own1 = [mid("own_10", right1[0])]
    near1 = [end_right("10", right1[0])]
    left1[0] = cross("left_0", left1[0], crossed, near0[-1])
    next0 = [mid("next_0", x, own0) for x in near0]
    outer0 = end_left("0", left0, own0)
    right1[1] = cross("right_1", right1[1], left1[0], own1[0], near1[0][-1])
    next1 = [[mid("next_10", x, own1[0], gate) for x in near1[0]]]
    outer1 = [end_left("10", left1[0], near1[0][-1])]
    left1[1] = cross("left_1", left1[1], right1[1], next0[-1])
    own1.append(mid("own_11", right1[1], own1[0]))
    near1.append(end_right("11", right1[1], outer0))
    def products(mirror, first, lefts, rights, name, instead=()):
        span = 2 * rows * len(rights)
        count = lefts[0][1].shape[0]
        args = [x for arrays in (*lefts, *rights) for x in arrays] + [*instead]
        shapes = [piece(count, 2 * rows, span), piece(count, rows, 2 * span)]
        return kernel(
            functools.partial(
                product_kernel, mirror, bool(instead), first, len(lefts), len(rights)
            ),
            name,
            shapes[: len(lefts)],
            [VMEM] * len(args),
            [pltpu.VMEM((count, span, 2 * toks), BF16)],
        )(*args)

    def near_planes(g):
        return list(zip([right0, *near0], [right1[g], *near1[g]]))

    def far_planes(g):
        return list(zip([own0, *next0], [own1[g], *next1[g]]))

    def hand_out(g, close, away, ends):
        handed = kernel(
            functools.partial(hand_out_kernel, planes),
            "hand_out",
            [piece(counts[g], rows, toks)] * 4,
            [VMEM] * 3,
        )(close, away, ends)
        return [handed[0]] + [
            send(handed[r], in_plane(r), f"return_{g}{r}") for r in range(1, 4)
        ]

    close, mine, first = [], [(left0, x) for x in left1], [0, counts[0]]
    for g in groups:
        close += products(False, first[g], [mine[g]], near_planes(g), "near")
    sides = [mine[0], (outer0, outer1[0])]
    away0, swapped = products(True, first[0], sides, far_planes(0), "away", [left1[1]])
    next1.append([mid("next_11", x, next1[0][-1], own1[1], away0) for x in near1[1]])
    swapped = send(swapped, edge, "left_11_and_products_back_0")
    pieces = hand_out(0, close[0], away0, swapped)
    sides = [(after(left0, pieces[0], close[1]), left1[1]), (outer0, swapped)]
    away1, ends = products(True, first[1], sides, far_planes(1), "away")
    ends = send(ends, edge, "products_back_1")
    pieces += hand_out(1, close[1], away1, ends)

    return kernel(
        update_kernel,
        "update",
        jax.ShapeDtypeStruct((rows, toks, channels), BF16),
        [VMEM] * (3 + len(pieces)),
        [pltpu.VMEM((toks // LANES, rows * (hidden + 1), LANES), F32)],
    )(out_gain.reshape(1, -1), out_weight, gate, *pieces)


def solution(mesh):
    placed = (
        P(("groups", "row"), "chan", None),
        P(("groups", "row"), "chan"),
        P(),
        P(),
        P(),
        P(),
        P(),
    )
    return jax.shard_map(
        functools.partial(local, n_row=mesh.shape["row"]),
        mesh=mesh,
        in_specs=placed,
        out_specs=P(("groups", "row"), "chan", None),
        check_vma=False,
    )
```

```python
import functools
import math

import jax
import jax.numpy as jnp
from jax import lax
from jax.experimental import pallas as pl
from jax.experimental.pallas import tpu as pltpu
from jax.sharding import PartitionSpec as P

F32, BF16 = jnp.float32, jnp.bfloat16
LANES = 128
SPARE = 6 * 1024 * 1024
SHARES = (9, 7)
NT = (((1,), (1,)), ((), ()))
TN = (((0,), (0,)), ((), ()))
VMEM = pl.BlockSpec(memory_space=pltpu.VMEM)
GROUP = 4
UNROLL = 8


def place():
    row = lax.axis_index("row")
    return row // 2, row % 2, lax.axis_index("chan")


def normalise(x, gain):
    mean = jnp.mean(x, axis=-1, keepdims=True)
    centered = x - mean
    var = jnp.mean(centered * centered, axis=-1, keepdims=True)
    return (centered * lax.rsqrt(var + 1e-05) * gain).astype(BF16)


def gated(normed, chosen, valid, first, held):
    _, rows, toks = valid.shape
    wide = chosen.shape[0] // 2
    proj = lax.dot_general(chosen[...], normed, NT, preferred_element_type=F32)
    for g in range(normed.shape[0] // toks):
        mine = proj[:, g * toks : (g + 1) * toks]
        value = (jnp.tanh(mine[:wide]) + 1.0) * (valid[0, pl.ds(first + g, 1), :] * mine[wide:])
        for m in range(toks // LANES):
            spot = pl.ds(first + g, wide, stride=rows + 1)
            held[m, spot, :] = value[:, m * LANES : (m + 1) * LANES]


def write_pieces(outs, held, base):
    row = 0
    for out in outs:
        count, rows, _ = out.shape
        for c in range(count):
            for m in range(held.shape[0]):
                lanes = slice(base + m * LANES, base + (m + 1) * LANES)
                out[c, :, lanes] = held[m, row : row + rows, :].astype(BF16)
            row += rows + 1


def right_rows(pair, valid, gain, chosen, normed_out, held):
    rows, toks, _ = pair.shape

    @pl.loop(0, rows // GROUP, unroll=UNROLL)
    def _(at):
        first = at * GROUP
        x = pair[pl.ds(first, GROUP)].astype(F32).reshape(GROUP * toks, -1)
        normed = normalise(x, gain[...])
        normed_out[pl.ds(first * toks, GROUP * toks), :] = normed
        gated(normed, chosen, valid, first, held)


def right_own_kernel(pair, mask, gain, weight, *rest):
    out, normed_out, first, second, chosen_left, valid, gain_out, turned, held = rest
    gain_out[...] = gain[...]
    hidden = weight.shape[1] // 4
    part = hidden // 4
    _, y, core = place()
    turned[...] = weight[...].T
    valid[0] = mask[...].astype(F32) * 0.5
    for n in range(4):
        half = 0.5 if n % 2 == 0 else 1.0
        for p in range(2):
            start = pl.multiple_of(n * hidden + ((2 * y + core) ^ (2 * p)) * part, part)
            columns = turned[pl.ds(start, part), :] * half
            if n < 2:
                at = (2 * n + p) * part
                chosen_left[at : at + part, :] = columns
            else:
                chosen = second if p else first
                chosen[(n - 2) * part : (n - 1) * part, :] = columns
    right_rows(pair, valid, gain, first, normed_out, held)
    write_pieces([out], held, 0)


def right_twin_kernel(pair, mask, gain, chosen, before, out, normed_out, valid, held):
    out[:, :, : before.shape[2]] = before[...]
    valid[0] = mask[...].astype(F32) * 0.5
    right_rows(pair, valid, gain, chosen, normed_out, held)
    write_pieces([out], held, pair.shape[1])


def rows_kernel(normed0, normed1, valid0, valid1, chosen, *rest):
    *outs, held = rest
    _, rows, toks = valid0.shape
    for n, (normed, valid) in enumerate(((normed0, valid0), (normed1, valid1))):

        @pl.loop(0, rows // GROUP, unroll=UNROLL)
        def _(at):
            first = at * GROUP
            gated(normed[pl.ds(first * toks, GROUP * toks), :], chosen, valid, first, held)

        write_pieces(outs, held, n * toks)


def gate_kernel(normed, weight, out):
    rows, toks, _ = out.shape

    @pl.loop(0, rows // GROUP, unroll=UNROLL)
    def _(at):
        x = normed[pl.ds(at * GROUP * toks, GROUP * toks), :]
        logits = jnp.dot(x, weight[...], preferred_element_type=F32)
        out[pl.ds(at * GROUP, GROUP)] = (0.5 * jnp.tanh(0.5 * logits) + 0.5).reshape(GROUP, toks, -1)


def product_kernel(mirror, instead, first, n_left, n_right, *rest):
    *refs, held = rest
    planes = [refs[2 * n : 2 * n + 2] for n in range(n_left + n_right)]
    lefts, rights = planes[:n_left], planes[n_left:]
    refs = refs[2 * (n_left + n_right) :]
    other, outs = refs[0], refs[1 if instead else 0 :]
    count, span, toks = outs[0].shape
    rows = span // 2
    z, y, _ = place()
    at_end = (z == 0) | (z == 2 * n_right - 1)
    z = 2 * n_right - 1 - z if mirror else z
    for s in range(n_right):
        for p in range(2):
            start = pl.multiple_of((z + n_right - s) % n_right * span + (y ^ p) * rows, rows)
            at = 0 if p else first
            held[:, pl.ds(start, rows), :] = rights[s][p][at : at + count]
    for c in range(count):
        left = jnp.concatenate([x for own, other in lefts for x in (own[first + c], other[c])], axis=0)
        out = lax.dot_general(left, held[c], NT, preferred_element_type=F32).astype(BF16)
        outs[0][c] = out[:span]
        if n_left == 2:
            outs[1][c, :, :toks] = out[span : span + rows]
            outs[1][c, :, toks:] = out[span + rows :]
    if instead:

        @pl.when(at_end)
        def _():
            outs[1][: other.shape[0]] = other[...]


def hand_out_kernel(planes, near, far, end, *outs):
    _, rows, toks = outs[0].shape
    z, _, core = place()
    at_end = (z == 0) | (z == planes - 1)
    for r in range(4):
        is_near = (core ^ (r % 2)) == z // (planes // 2)
        span = slice((r // 2) * rows, (r // 2 + 1) * rows)
        lanes = slice((r // 2) * toks, (r // 2 + 1) * toks)

        @pl.when(is_near)
        def _():
            outs[r][...] = near[:, span, :]

        @pl.when(jnp.logical_not(is_near | at_end))
        def _():
            outs[r][...] = far[:, span, :]

        @pl.when(jnp.logical_not(is_near) & at_end)
        def _():
            outs[r][...] = end[:, :, lanes]


def update_kernel(gain, weight, gate, *rest):
    pieces, out, turned = rest[:-2], rest[-2], rest[-1]
    part = sum(x.shape[0] for x in pieces[::4])
    _, rows, toks = pieces[0].shape
    hidden = 4 * part
    pitch = hidden + 1
    _, y, core = place()
    scale = jnp.broadcast_to(gain[...], (toks, hidden)).T
    for r in range(4):
        base = ((2 * y + core) ^ r) * part
        for piece in pieces[r::4]:
            for c in range(piece.shape[0]):
                value = piece[c].astype(F32)
                for m in range(toks // LANES):
                    turned[m, pl.ds(base + c, rows, stride=pitch), :] = value[
                        :, m * LANES : (m + 1) * LANES
                    ]
            base = base + piece.shape[0]

    @pl.loop(0, rows, unroll=32)
    def _(i):
        x = jnp.concatenate(
            [turned[m, pl.ds(i * pitch, hidden), :] for m in range(toks // LANES)], axis=1
        )
        mean = jnp.mean(x, axis=0, keepdims=True)
        centered = x - mean
        var = jnp.mean(centered * centered, axis=0, keepdims=True)
        pnorm = (centered * lax.rsqrt(var + 1e-05) * scale).astype(BF16)
        mapped = lax.dot_general(pnorm, weight[...], TN, preferred_element_type=F32)
        out[i] = (gate[i] * mapped).astype(BF16)


def kernel(body, name, out_shape, in_specs, scratch=()):
    outs = jax.tree.map(lambda _: VMEM, out_shape)

    def call(*args):
        arrays = [*args, *jax.tree.leaves(out_shape), *scratch]
        size = sum(x.dtype.itemsize * math.prod(x.shape) for x in arrays)
        return pl.pallas_call(
            body,
            out_shape=out_shape,
            in_specs=in_specs,
            out_specs=outs,
            scratch_shapes=list(scratch),
            compiler_params=pltpu.CompilerParams(vmem_limit_bytes=size + SPARE),
            name=name,
        )(*args)

    return call


def local(pair, pair_mask, in_gain, proj_weight, gate_weight, out_gain, out_weight, *, n_row):
    rows, toks, channels = pair.shape
    hidden = proj_weight.shape[1] // 4
    part = hidden // 4
    planes = n_row // 2
    half = planes // 2
    counts = [part * share // sum(SHARES) for share in SHARES]
    groups = range(len(counts))
    def send(x, target, name):
        pairs = []
        for source in range(2 * n_row):
            to = target(source // 4, source // 2 % 2, source % 2)
            if to is not None:
                pairs.append((source, 4 * to[0] + 2 * to[1] + to[2]))
        with jax.named_scope(name):
            return lax.ppermute(x, ("row", "chan"), pairs)

    def after(x, *earlier):
        return lax.optimization_barrier((x, *earlier))[0]

    def in_plane(r):
        return lambda p, b, k: (p, b ^ (r // 2), k ^ (r % 2))

    def shifted(s):
        return lambda p, b, k: (p // half * half + (p + s) % half, b, k)

    def mirrored(p, b, k):
        return (p, b, 1 - k) if p in (0, planes - 1) else (planes - 1 - p, b, k)

    def edge(p, b, k):
        swap = {0: 1, 1: 0, planes - 1: planes - 2, planes - 2: planes - 1}
        return (swap[p], b, k) if p in swap else (p, b, 1 - k)

    def outward(p, b, k):
        return {1: (0, b, k), planes - 2: (planes - 1, b, k)}.get(p)

    gains = in_gain.reshape(1, -1)
    twin, twin_mask = send(pair, in_plane(1), "pair"), send(pair_mask, in_plane(1), "mask")

    def piece(count, height, depth):
        return jax.ShapeDtypeStruct((count, height, depth), BF16)

    def columns(count):
        return pltpu.VMEM((toks // LANES, count * (rows + 1), LANES), F32)

    rows_all = jax.ShapeDtypeStruct((rows * toks, channels), BF16)
    valid_shape = jax.ShapeDtypeStruct((1, rows, toks), F32)
    weights = [jax.ShapeDtypeStruct((n * part, channels), BF16) for n in (2, 2, 4)]
    before, normed0, first, second, chosen_left, valid, gains = kernel(
        right_own_kernel,
        "right_own",
        [piece(part, rows, toks), rows_all, *weights, valid_shape, gains],
        [VMEM] * 4,
        [pltpu.VMEM((4 * hidden, channels), BF16), columns(part)],
    )(pair, pair_mask, gains, proj_weight)
    right0, normed1, twin_valid = kernel(
        right_twin_kernel,
        "right_twin",
        [piece(part, rows, 2 * toks), rows_all, valid_shape],
        [VMEM] * 5,
        [columns(part)],
    )(twin, twin_mask, gains, first, before)

    def operand(chosen, shares, name):
        return kernel(
            rows_kernel,
            name,
            [piece(count, rows, 2 * toks) for count in shares],
            [VMEM] * 5,
            [columns(sum(shares))],
        )(normed0, normed1, valid, twin_valid, chosen)

    right1 = list(operand(second, counts, "right_neighbour"))

    def mid(name, x, *earlier):
        return send(after(x, *earlier), mirrored, f"mid_{name}")

    def end_right(name, x, *earlier):
        x = after(x, *earlier)
        return [send(x, shifted(s), f"end_right_{name}") for s in range(1, half)]

    def end_left(name, x, *earlier):
        return send(after(x, *earlier), edge, f"end_left_{name}")

    def cross(name, x, *earlier):
        return send(after(x, *earlier), in_plane(2), f"cross_{name}")

    own0 = mid("own_0", right0)
    crossed = cross("right_0", right1[0])
    near0 = end_right("0", right0)
    left0, *left1 = operand(chosen_left, (part, *counts), "left")
    gate = kernel(
        gate_kernel, "gate", jax.ShapeDtypeStruct((rows, toks, channels), F32), [VMEM] * 2
    )(normed0, gate_weight)
    right1[0] = after(crossed, left0)
    own1 = [mid("own_10", right1[0])]
    near1 = [end_right("10", right1[0])]
    left1[0] = cross("left_0", left1[0], crossed, near0[-1])
    next0 = [mid("next_0", x, own0) for x in near0]
    outer0 = end_left("0", left0, own0)
    right1[1] = cross("right_1", right1[1], left1[0], own1[0], near1[0][-1])
    next1 = [[mid("next_10", x, own1[0], gate) for x in near1[0]]]
    outer1 = [end_left("10", left1[0], near1[0][-1])]
    left1[1] = cross("left_1", left1[1], right1[1], next0[-1])
    own1.append(mid("own_11", right1[1], own1[0]))
    near1.append(end_right("11", right1[1], outer0))
    def products(mirror, first, lefts, rights, name, instead=()):
        span = 2 * rows * len(rights)
        count = lefts[0][1].shape[0]
        args = [x for arrays in (*lefts, *rights) for x in arrays] + [*instead]
        shapes = [piece(count, 2 * rows, span), piece(count, rows, 2 * span)]
        return kernel(
            functools.partial(
                product_kernel, mirror, bool(instead), first, len(lefts), len(rights)
            ),
            name,
            shapes[: len(lefts)],
            [VMEM] * len(args),
            [pltpu.VMEM((count, span, 2 * toks), BF16)],
        )(*args)

    def near_planes(g):
        return list(zip([right0, *near0], [right1[g], *near1[g]]))

    def far_planes(g):
        return list(zip([own0, *next0], [own1[g], *next1[g]]))

    def hand_out(g, close, away, ends):
        handed = kernel(
            functools.partial(hand_out_kernel, planes),
            "hand_out",
            [piece(counts[g], rows, toks)] * 4,
            [VMEM] * 3,
        )(close, away, ends)
        return [handed[0]] + [
            send(handed[r], in_plane(r), f"return_{g}{r}") for r in range(1, 4)
        ]

    close, mine, first = [], [(left0, x) for x in left1], [0, counts[0]]
    for g in groups:
        close += products(False, first[g], [mine[g]], near_planes(g), "near")
    sides = [mine[0], (outer0, outer1[0])]
    away0, swapped = products(True, first[0], sides, far_planes(0), "away", [left1[1]])
    next1.append([mid("next_11", x, next1[0][-1], own1[1], away0) for x in near1[1]])
    swapped = send(swapped, edge, "left_11_and_products_back_0")
    pieces = hand_out(0, close[0], away0, swapped)
    sides = [(after(left0, pieces[0], close[1]), left1[1]), (outer0, swapped)]
    away1, ends = products(True, first[1], sides, far_planes(1), "away")
    ends = send(ends, edge, "products_back_1")
    pieces += hand_out(1, close[1], away1, ends)

    return kernel(
        update_kernel,
        "update",
        jax.ShapeDtypeStruct((rows, toks, channels), BF16),
        [VMEM] * (3 + len(pieces)),
        [pltpu.VMEM((toks // LANES, rows * (hidden + 1), LANES), F32)],
    )(out_gain.reshape(1, -1), out_weight, gate, *pieces)


def solution(mesh):
    placed = (
        P(("groups", "row"), "chan", None),
        P(("groups", "row"), "chan"),
        P(),
        P(),
        P(),
        P(),
        P(),
    )
    return jax.shard_map(
        functools.partial(local, n_row=mesh.shape["row"]),
        mesh=mesh,
        in_specs=placed,
        out_specs=P(("groups", "row"), "chan", None),
        check_vma=False,
    )
```

```python
import functools
import math

import jax
import jax.numpy as jnp
from jax import lax
from jax.experimental import pallas as pl
from jax.experimental.pallas import tpu as pltpu
from jax.sharding import PartitionSpec as P

F32, BF16 = jnp.float32, jnp.bfloat16
LANES = 128
SPARE = 6 * 1024 * 1024
SHARES = (9, 7)
NT = (((1,), (1,)), ((), ()))
TN = (((0,), (0,)), ((), ()))
VMEM = pl.BlockSpec(memory_space=pltpu.VMEM)
GROUP = 16
UNROLL = 2


def place():
    row = lax.axis_index("row")
    return row // 2, row % 2, lax.axis_index("chan")


def normalise(x, gain):
    mean = jnp.mean(x, axis=-1, keepdims=True)
    centered = x - mean
    var = jnp.mean(centered * centered, axis=-1, keepdims=True)
    return (centered * lax.rsqrt(var + 1e-05) * gain).astype(BF16)


def gated(normed, chosen, valid, first, held):
    _, rows, toks = valid.shape
    wide = chosen.shape[0] // 2
    proj = lax.dot_general(chosen[...], normed, NT, preferred_element_type=F32)
    for g in range(normed.shape[0] // toks):
        mine = proj[:, g * toks : (g + 1) * toks]
        value = (jnp.tanh(mine[:wide]) + 1.0) * (valid[0, pl.ds(first + g, 1), :] * mine[wide:])
        for m in range(toks // LANES):
            spot = pl.ds(first + g, wide, stride=rows + 1)
            held[m, spot, :] = value[:, m * LANES : (m + 1) * LANES]


def write_pieces(outs, held, base):
    row = 0
    for out in outs:
        count, rows, _ = out.shape
        for c in range(count):
            for m in range(held.shape[0]):
                lanes = slice(base + m * LANES, base + (m + 1) * LANES)
                out[c, :, lanes] = held[m, row : row + rows, :].astype(BF16)
            row += rows + 1


def right_rows(pair, valid, gain, chosen, normed_out, held):
    rows, toks, _ = pair.shape

    @pl.loop(0, rows // GROUP, unroll=UNROLL)
    def _(at):
        first = at * GROUP
        x = pair[pl.ds(first, GROUP)].astype(F32).reshape(GROUP * toks, -1)
        normed = normalise(x, gain[...])
        normed_out[pl.ds(first * toks, GROUP * toks), :] = normed
        gated(normed, chosen, valid, first, held)


def right_own_kernel(pair, mask, gain, weight, *rest):
    out, normed_out, first, second, chosen_left, valid, gain_out, turned, held = rest
    gain_out[...] = gain[...]
    hidden = weight.shape[1] // 4
    part = hidden // 4
    _, y, core = place()
    turned[...] = weight[...].T
    valid[0] = mask[...].astype(F32) * 0.5
    for n in range(4):
        half = 0.5 if n % 2 == 0 else 1.0
        for p in range(2):
            start = pl.multiple_of(n * hidden + ((2 * y + core) ^ (2 * p)) * part, part)
            columns = turned[pl.ds(start, part), :] * half
            if n < 2:
                at = (2 * n + p) * part
                chosen_left[at : at + part, :] = columns
            else:
                chosen = second if p else first
                chosen[(n - 2) * part : (n - 1) * part, :] = columns
    right_rows(pair, valid, gain, first, normed_out, held)
    write_pieces([out], held, 0)


def right_twin_kernel(pair, mask, gain, chosen, before, out, normed_out, valid, held):
    out[:, :, : before.shape[2]] = before[...]
    valid[0] = mask[...].astype(F32) * 0.5
    right_rows(pair, valid, gain, chosen, normed_out, held)
    write_pieces([out], held, pair.shape[1])


def rows_kernel(normed0, normed1, valid0, valid1, chosen, *rest):
    *outs, held = rest
    _, rows, toks = valid0.shape
    for n, (normed, valid) in enumerate(((normed0, valid0), (normed1, valid1))):

        @pl.loop(0, rows // GROUP, unroll=UNROLL)
        def _(at):
            first = at * GROUP
            gated(normed[pl.ds(first * toks, GROUP * toks), :], chosen, valid, first, held)

        write_pieces(outs, held, n * toks)


def gate_kernel(normed, weight, out):
    rows, toks, _ = out.shape

    @pl.loop(0, rows // GROUP, unroll=UNROLL)
    def _(at):
        x = normed[pl.ds(at * GROUP * toks, GROUP * toks), :]
        logits = jnp.dot(x, weight[...], preferred_element_type=F32)
        out[pl.ds(at * GROUP, GROUP)] = (0.5 * jnp.tanh(0.5 * logits) + 0.5).reshape(GROUP, toks, -1)


def product_kernel(mirror, instead, first, n_left, n_right, *rest):
    *refs, held = rest
    planes = [refs[2 * n : 2 * n + 2] for n in range(n_left + n_right)]
    lefts, rights = planes[:n_left], planes[n_left:]
    refs = refs[2 * (n_left + n_right) :]
    other, outs = refs[0], refs[1 if instead else 0 :]
    count, span, toks = outs[0].shape
    rows = span // 2
    z, y, _ = place()
    at_end = (z == 0) | (z == 2 * n_right - 1)
    z = 2 * n_right - 1 - z if mirror else z
    for s in range(n_right):
        for p in range(2):
            start = pl.multiple_of((z + n_right - s) % n_right * span + (y ^ p) * rows, rows)
            at = 0 if p else first
            held[:, pl.ds(start, rows), :] = rights[s][p][at : at + count]
    for c in range(count):
        left = jnp.concatenate([x for own, other in lefts for x in (own[first + c], other[c])], axis=0)
        out = lax.dot_general(left, held[c], NT, preferred_element_type=F32).astype(BF16)
        outs[0][c] = out[:span]
        if n_left == 2:
            outs[1][c, :, :toks] = out[span : span + rows]
            outs[1][c, :, toks:] = out[span + rows :]
    if instead:

        @pl.when(at_end)
        def _():
            outs[1][: other.shape[0]] = other[...]


def hand_out_kernel(planes, near, far, end, *outs):
    _, rows, toks = outs[0].shape
    z, _, core = place()
    at_end = (z == 0) | (z == planes - 1)
    for r in range(4):
        is_near = (core ^ (r % 2)) == z // (planes // 2)
        span = slice((r // 2) * rows, (r // 2 + 1) * rows)
        lanes = slice((r // 2) * toks, (r // 2 + 1) * toks)

        @pl.when(is_near)
        def _():
            outs[r][...] = near[:, span, :]

        @pl.when(jnp.logical_not(is_near | at_end))
        def _():
            outs[r][...] = far[:, span, :]

        @pl.when(jnp.logical_not(is_near) & at_end)
        def _():
            outs[r][...] = end[:, :, lanes]


def update_kernel(gain, weight, gate, *rest):
    pieces, out, turned = rest[:-2], rest[-2], rest[-1]
    part = sum(x.shape[0] for x in pieces[::4])
    _, rows, toks = pieces[0].shape
    hidden = 4 * part
    pitch = hidden + 1
    _, y, core = place()
    scale = jnp.broadcast_to(gain[...], (toks, hidden)).T
    for r in range(4):
        base = ((2 * y + core) ^ r) * part
        for piece in pieces[r::4]:
            for c in range(piece.shape[0]):
                value = piece[c].astype(F32)
                for m in range(toks // LANES):
                    turned[m, pl.ds(base + c, rows, stride=pitch), :] = value[
                        :, m * LANES : (m + 1) * LANES
                    ]
            base = base + piece.shape[0]

    @pl.loop(0, rows, unroll=32)
    def _(i):
        x = jnp.concatenate(
            [turned[m, pl.ds(i * pitch, hidden), :] for m in range(toks // LANES)], axis=1
        )
        mean = jnp.mean(x, axis=0, keepdims=True)
        centered = x - mean
        var = jnp.mean(centered * centered, axis=0, keepdims=True)
        pnorm = (centered * lax.rsqrt(var + 1e-05) * scale).astype(BF16)
        mapped = lax.dot_general(pnorm, weight[...], TN, preferred_element_type=F32)
        out[i] = (gate[i] * mapped).astype(BF16)


def kernel(body, name, out_shape, in_specs, scratch=()):
    outs = jax.tree.map(lambda _: VMEM, out_shape)

    def call(*args):
        arrays = [*args, *jax.tree.leaves(out_shape), *scratch]
        size = sum(x.dtype.itemsize * math.prod(x.shape) for x in arrays)
        return pl.pallas_call(
            body,
            out_shape=out_shape,
            in_specs=in_specs,
            out_specs=outs,
            scratch_shapes=list(scratch),
            compiler_params=pltpu.CompilerParams(vmem_limit_bytes=size + SPARE),
            name=name,
        )(*args)

    return call


def local(pair, pair_mask, in_gain, proj_weight, gate_weight, out_gain, out_weight, *, n_row):
    rows, toks, channels = pair.shape
    hidden = proj_weight.shape[1] // 4
    part = hidden // 4
    planes = n_row // 2
    half = planes // 2
    counts = [part * share // sum(SHARES) for share in SHARES]
    groups = range(len(counts))
    def send(x, target, name):
        pairs = []
        for source in range(2 * n_row):
            to = target(source // 4, source // 2 % 2, source % 2)
            if to is not None:
                pairs.append((source, 4 * to[0] + 2 * to[1] + to[2]))
        with jax.named_scope(name):
            return lax.ppermute(x, ("row", "chan"), pairs)

    def after(x, *earlier):
        return lax.optimization_barrier((x, *earlier))[0]

    def in_plane(r):
        return lambda p, b, k: (p, b ^ (r // 2), k ^ (r % 2))

    def shifted(s):
        return lambda p, b, k: (p // half * half + (p + s) % half, b, k)

    def mirrored(p, b, k):
        return (p, b, 1 - k) if p in (0, planes - 1) else (planes - 1 - p, b, k)

    def edge(p, b, k):
        swap = {0: 1, 1: 0, planes - 1: planes - 2, planes - 2: planes - 1}
        return (swap[p], b, k) if p in swap else (p, b, 1 - k)

    def outward(p, b, k):
        return {1: (0, b, k), planes - 2: (planes - 1, b, k)}.get(p)

    gains = in_gain.reshape(1, -1)
    twin, twin_mask = send(pair, in_plane(1), "pair"), send(pair_mask, in_plane(1), "mask")

    def piece(count, height, depth):
        return jax.ShapeDtypeStruct((count, height, depth), BF16)

    def columns(count):
        return pltpu.VMEM((toks // LANES, count * (rows + 1), LANES), F32)

    rows_all = jax.ShapeDtypeStruct((rows * toks, channels), BF16)
    valid_shape = jax.ShapeDtypeStruct((1, rows, toks), F32)
    weights = [jax.ShapeDtypeStruct((n * part, channels), BF16) for n in (2, 2, 4)]
    before, normed0, first, second, chosen_left, valid, gains = kernel(
        right_own_kernel,
        "right_own",
        [piece(part, rows, toks), rows_all, *weights, valid_shape, gains],
        [VMEM] * 4,
        [pltpu.VMEM((4 * hidden, channels), BF16), columns(part)],
    )(pair, pair_mask, gains, proj_weight)
    right0, normed1, twin_valid = kernel(
        right_twin_kernel,
        "right_twin",
        [piece(part, rows, 2 * toks), rows_all, valid_shape],
        [VMEM] * 5,
        [columns(part)],
    )(twin, twin_mask, gains, first, before)

    def operand(chosen, shares, name):
        return kernel(
            rows_kernel,
            name,
            [piece(count, rows, 2 * toks) for count in shares],
            [VMEM] * 5,
            [columns(sum(shares))],
        )(normed0, normed1, valid, twin_valid, chosen)

    right1 = list(operand(second, counts, "right_neighbour"))

    def mid(name, x, *earlier):
        return send(after(x, *earlier), mirrored, f"mid_{name}")

    def end_right(name, x, *earlier):
        x = after(x, *earlier)
        return [send(x, shifted(s), f"end_right_{name}") for s in range(1, half)]

    def end_left(name, x, *earlier):
        return send(after(x, *earlier), edge, f"end_left_{name}")

    def cross(name, x, *earlier):
        return send(after(x, *earlier), in_plane(2), f"cross_{name}")

    own0 = mid("own_0", right0)
    crossed = cross("right_0", right1[0])
    near0 = end_right("0", right0)
    left0, *left1 = operand(chosen_left, (part, *counts), "left")
    gate = kernel(
        gate_kernel, "gate", jax.ShapeDtypeStruct((rows, toks, channels), F32), [VMEM] * 2
    )(normed0, gate_weight)
    right1[0] = after(crossed, left0)
    own1 = [mid("own_10", right1[0])]
    near1 = [end_right("10", right1[0])]
    left1[0] = cross("left_0", left1[0], crossed, near0[-1])
    next0 = [mid("next_0", x, own0) for x in near0]
    outer0 = end_left("0", left0, own0)
    right1[1] = cross("right_1", right1[1], left1[0], own1[0], near1[0][-1])
    next1 = [[mid("next_10", x, own1[0], gate) for x in near1[0]]]
    outer1 = [end_left("10", left1[0], near1[0][-1])]
    left1[1] = cross("left_1", left1[1], right1[1], next0[-1])
    own1.append(mid("own_11", right1[1], own1[0]))
    near1.append(end_right("11", right1[1], outer0))
    def products(mirror, first, lefts, rights, name, instead=()):
        span = 2 * rows * len(rights)
        count = lefts[0][1].shape[0]
        args = [x for arrays in (*lefts, *rights) for x in arrays] + [*instead]
        shapes = [piece(count, 2 * rows, span), piece(count, rows, 2 * span)]
        return kernel(
            functools.partial(
                product_kernel, mirror, bool(instead), first, len(lefts), len(rights)
            ),
            name,
            shapes[: len(lefts)],
            [VMEM] * len(args),
            [pltpu.VMEM((count, span, 2 * toks), BF16)],
        )(*args)

    def near_planes(g):
        return list(zip([right0, *near0], [right1[g], *near1[g]]))

    def far_planes(g):
        return list(zip([own0, *next0], [own1[g], *next1[g]]))

    def hand_out(g, close, away, ends):
        handed = kernel(
            functools.partial(hand_out_kernel, planes),
            "hand_out",
            [piece(counts[g], rows, toks)] * 4,
            [VMEM] * 3,
        )(close, away, ends)
        return [handed[0]] + [
            send(handed[r], in_plane(r), f"return_{g}{r}") for r in range(1, 4)
        ]

    close, mine, first = [], [(left0, x) for x in left1], [0, counts[0]]
    for g in groups:
        close += products(False, first[g], [mine[g]], near_planes(g), "near")
    sides = [mine[0], (outer0, outer1[0])]
    away0, swapped = products(True, first[0], sides, far_planes(0), "away", [left1[1]])
    next1.append([mid("next_11", x, next1[0][-1], own1[1], away0) for x in near1[1]])
    swapped = send(swapped, edge, "left_11_and_products_back_0")
    pieces = hand_out(0, close[0], away0, swapped)
    sides = [(after(left0, pieces[0], close[1]), left1[1]), (outer0, swapped)]
    away1, ends = products(True, first[1], sides, far_planes(1), "away")
    ends = send(ends, edge, "products_back_1")
    pieces += hand_out(1, close[1], away1, ends)

    return kernel(
        update_kernel,
        "update",
        jax.ShapeDtypeStruct((rows, toks, channels), BF16),
        [VMEM] * (3 + len(pieces)),
        [pltpu.VMEM((toks // LANES, rows * (hidden + 1), LANES), F32)],
    )(out_gain.reshape(1, -1), out_weight, gate, *pieces)


def solution(mesh):
    placed = (
        P(("groups", "row"), "chan", None),
        P(("groups", "row"), "chan"),
        P(),
        P(),
        P(),
        P(),
        P(),
    )
    return jax.shard_map(
        functools.partial(local, n_row=mesh.shape["row"]),
        mesh=mesh,
        in_specs=placed,
        out_specs=P(("groups", "row"), "chan", None),
        check_vma=False,
    )
```

```python
import functools
import math

import jax
import jax.numpy as jnp
from jax import lax
from jax.experimental import pallas as pl
from jax.experimental.pallas import tpu as pltpu
from jax.sharding import PartitionSpec as P

F32, BF16 = jnp.float32, jnp.bfloat16
LANES = 128
SPARE = 6 * 1024 * 1024
SHARES = (9, 7)
NT = (((1,), (1,)), ((), ()))
TN = (((0,), (0,)), ((), ()))
VMEM = pl.BlockSpec(memory_space=pltpu.VMEM)
GROUP = 4
UNROLL = 8


def place():
    row = lax.axis_index("row")
    return row // 2, row % 2, lax.axis_index("chan")


def normalise(x, gain):
    mean = jnp.mean(x, axis=-1, keepdims=True)
    centered = x - mean
    var = jnp.mean(centered * centered, axis=-1, keepdims=True)
    return (centered * lax.rsqrt(var + 1e-05) * gain).astype(BF16)


def gated(normed, chosen, valid, first, held):
    _, rows, toks = valid.shape
    wide = chosen.shape[0] // 2
    proj = lax.dot_general(chosen[...], normed, NT, preferred_element_type=F32)
    for g in range(normed.shape[0] // toks):
        mine = proj[:, g * toks : (g + 1) * toks]
        value = (jnp.tanh(mine[:wide]) + 1.0) * (valid[0, pl.ds(first + g, 1), :] * mine[wide:])
        for m in range(toks // LANES):
            spot = pl.ds(first + g, wide, stride=rows + 1)
            held[m, spot, :] = value[:, m * LANES : (m + 1) * LANES]


def write_pieces(outs, held, base):
    row = 0
    for out in outs:
        count, rows, _ = out.shape
        for c in range(count):
            for m in range(held.shape[0]):
                lanes = slice(base + m * LANES, base + (m + 1) * LANES)
                out[c, :, lanes] = held[m, row : row + rows, :].astype(BF16)
            row += rows + 1


def right_rows(pair, valid, gain, chosen, normed_out, held):
    rows, toks, _ = pair.shape

    @pl.loop(0, rows // GROUP, unroll=UNROLL)
    def _(at):
        first = at * GROUP
        x = pair[pl.ds(first, GROUP)].astype(F32).reshape(GROUP * toks, -1)
        normed = normalise(x, gain[...])
        normed_out[pl.ds(first * toks, GROUP * toks), :] = normed
        gated(normed, chosen, valid, first, held)


def right_own_kernel(pair, mask, gain, weight, *rest):
    out, normed_out, first, second, chosen_left, valid, gain_out, turned, held = rest
    gain_out[...] = gain[...]
    hidden = weight.shape[1] // 4
    part = hidden // 4
    _, y, core = place()
    turned[...] = weight[...].T
    valid[0] = mask[...].astype(F32) * 0.5
    for n in range(4):
        half = 0.5 if n % 2 == 0 else 1.0
        for p in range(2):
            start = pl.multiple_of(n * hidden + ((2 * y + core) ^ (2 * p)) * part, part)
            columns = turned[pl.ds(start, part), :] * half
            if n < 2:
                at = (2 * n + p) * part
                chosen_left[at : at + part, :] = columns
            else:
                chosen = second if p else first
                chosen[(n - 2) * part : (n - 1) * part, :] = columns
    right_rows(pair, valid, gain, first, normed_out, held)
    write_pieces([out], held, 0)


def right_twin_kernel(pair, mask, gain, chosen, before, out, normed_out, valid, held):
    out[:, :, : before.shape[2]] = before[...]
    valid[0] = mask[...].astype(F32) * 0.5
    right_rows(pair, valid, gain, chosen, normed_out, held)
    write_pieces([out], held, pair.shape[1])


def rows_kernel(normed0, normed1, valid0, valid1, chosen, *rest):
    *outs, held = rest
    _, rows, toks = valid0.shape
    for n, (normed, valid) in enumerate(((normed0, valid0), (normed1, valid1))):

        @pl.loop(0, rows // GROUP, unroll=UNROLL)
        def _(at):
            first = at * GROUP
            gated(normed[pl.ds(first * toks, GROUP * toks), :], chosen, valid, first, held)

        write_pieces(outs, held, n * toks)


def gate_kernel(normed, weight, out):
    rows, toks, _ = out.shape

    @pl.loop(0, rows // GROUP, unroll=UNROLL)
    def _(at):
        x = normed[pl.ds(at * GROUP * toks, GROUP * toks), :]
        logits = jnp.dot(x, weight[...], preferred_element_type=F32)
        out[pl.ds(at * GROUP, GROUP)] = (0.5 * jnp.tanh(0.5 * logits) + 0.5).reshape(GROUP, toks, -1)


def product_kernel(mirror, instead, first, n_left, n_right, *rest):
    *refs, held = rest
    planes = [refs[2 * n : 2 * n + 2] for n in range(n_left + n_right)]
    lefts, rights = planes[:n_left], planes[n_left:]
    refs = refs[2 * (n_left + n_right) :]
    other, outs = refs[0], refs[1 if instead else 0 :]
    count, span, toks = outs[0].shape
    rows = span // 2
    z, y, _ = place()
    at_end = (z == 0) | (z == 2 * n_right - 1)
    z = 2 * n_right - 1 - z if mirror else z
    for s in range(n_right):
        for p in range(2):
            start = pl.multiple_of((z + n_right - s) % n_right * span + (y ^ p) * rows, rows)
            at = 0 if p else first
            held[:, pl.ds(start, rows), :] = rights[s][p][at : at + count]
    for c in range(count):
        left = jnp.concatenate([x for own, other in lefts for x in (own[first + c], other[c])], axis=0)
        out = lax.dot_general(left, held[c], NT, preferred_element_type=F32).astype(BF16)
        outs[0][c] = out[:span]
        if n_left == 2:
            outs[1][c, :, :toks] = out[span : span + rows]
            outs[1][c, :, toks:] = out[span + rows :]
    if instead:

        @pl.when(at_end)
        def _():
            outs[1][: other.shape[0]] = other[...]


def hand_out_kernel(planes, near, far, end, *outs):
    _, rows, toks = outs[0].shape
    z, _, core = place()
    at_end = (z == 0) | (z == planes - 1)
    for r in range(4):
        is_near = (core ^ (r % 2)) == z // (planes // 2)
        span = slice((r // 2) * rows, (r // 2 + 1) * rows)
        lanes = slice((r // 2) * toks, (r // 2 + 1) * toks)

        @pl.when(is_near)
        def _():
            outs[r][...] = near[:, span, :]

        @pl.when(jnp.logical_not(is_near | at_end))
        def _():
            outs[r][...] = far[:, span, :]

        @pl.when(jnp.logical_not(is_near) & at_end)
        def _():
            outs[r][...] = end[:, :, lanes]


def update_kernel(gain, weight, gate, *rest):
    pieces, out, turned = rest[:-2], rest[-2], rest[-1]
    part = sum(x.shape[0] for x in pieces[::4])
    _, rows, toks = pieces[0].shape
    hidden = 4 * part
    pitch = hidden + 1
    _, y, core = place()
    scale = jnp.broadcast_to(gain[...], (toks, hidden)).T
    for r in range(4):
        base = ((2 * y + core) ^ r) * part
        for piece in pieces[r::4]:
            for c in range(piece.shape[0]):
                value = piece[c].astype(F32)
                for m in range(toks // LANES):
                    turned[m, pl.ds(base + c, rows, stride=pitch), :] = value[
                        :, m * LANES : (m + 1) * LANES
                    ]
            base = base + piece.shape[0]

    @pl.loop(0, rows, unroll=32)
    def _(i):
        x = jnp.concatenate(
            [turned[m, pl.ds(i * pitch, hidden), :] for m in range(toks // LANES)], axis=1
        )
        mean = jnp.mean(x, axis=0, keepdims=True)
        centered = x - mean
        var = jnp.mean(centered * centered, axis=0, keepdims=True)
        pnorm = (centered * lax.rsqrt(var + 1e-05) * scale).astype(BF16)
        mapped = lax.dot_general(pnorm, weight[...], TN, preferred_element_type=F32)
        out[i] = (gate[i] * mapped).astype(BF16)


def kernel(body, name, out_shape, in_specs, scratch=()):
    outs = jax.tree.map(lambda _: VMEM, out_shape)

    def call(*args):
        arrays = [*args, *jax.tree.leaves(out_shape), *scratch]
        size = sum(x.dtype.itemsize * math.prod(x.shape) for x in arrays)
        return pl.pallas_call(
            body,
            out_shape=out_shape,
            in_specs=in_specs,
            out_specs=outs,
            scratch_shapes=list(scratch),
            compiler_params=pltpu.CompilerParams(vmem_limit_bytes=size + SPARE),
            name=name,
        )(*args)

    return call


def local(pair, pair_mask, in_gain, proj_weight, gate_weight, out_gain, out_weight, *, n_row):
    rows, toks, channels = pair.shape
    hidden = proj_weight.shape[1] // 4
    part = hidden // 4
    planes = n_row // 2
    half = planes // 2
    counts = [part * share // sum(SHARES) for share in SHARES]
    groups = range(len(counts))
    def send(x, target, name):
        pairs = []
        for source in range(2 * n_row):
            to = target(source // 4, source // 2 % 2, source % 2)
            if to is not None:
                pairs.append((source, 4 * to[0] + 2 * to[1] + to[2]))
        with jax.named_scope(name):
            return lax.ppermute(x, ("row", "chan"), pairs)

    def after(x, *earlier):
        return lax.optimization_barrier((x, *earlier))[0]

    def in_plane(r):
        return lambda p, b, k: (p, b ^ (r // 2), k ^ (r % 2))

    def shifted(s):
        return lambda p, b, k: (p // half * half + (p + s) % half, b, k)

    def mirrored(p, b, k):
        return (p, b, 1 - k) if p in (0, planes - 1) else (planes - 1 - p, b, k)

    def edge(p, b, k):
        swap = {0: 1, 1: 0, planes - 1: planes - 2, planes - 2: planes - 1}
        return (swap[p], b, k) if p in swap else (p, b, 1 - k)

    def outward(p, b, k):
        return {1: (0, b, k), planes - 2: (planes - 1, b, k)}.get(p)

    gains = in_gain.reshape(1, -1)
    twin, twin_mask = send(pair, in_plane(1), "pair"), send(pair_mask, in_plane(1), "mask")

    def piece(count, height, depth):
        return jax.ShapeDtypeStruct((count, height, depth), BF16)

    def columns(count):
        return pltpu.VMEM((toks // LANES, (count + 1) * (rows + 1), LANES), F32)

    rows_all = jax.ShapeDtypeStruct((rows * toks, channels), BF16)
    valid_shape = jax.ShapeDtypeStruct((1, rows, toks), F32)
    weights = [jax.ShapeDtypeStruct((n * part, channels), BF16) for n in (2, 2, 4)]
    before, normed0, first, second, chosen_left, valid, gains = kernel(
        right_own_kernel,
        "right_own",
        [piece(part, rows, toks), rows_all, *weights, valid_shape, gains],
        [VMEM] * 4,
        [pltpu.VMEM((4 * hidden, channels), BF16), columns(part)],
    )(pair, pair_mask, gains, proj_weight)
    right0, normed1, twin_valid = kernel(
        right_twin_kernel,
        "right_twin",
        [piece(part, rows, 2 * toks), rows_all, valid_shape],
        [VMEM] * 5,
        [columns(part)],
    )(twin, twin_mask, gains, first, before)

    def operand(chosen, shares, name):
        return kernel(
            rows_kernel,
            name,
            [piece(count, rows, 2 * toks) for count in shares],
            [VMEM] * 5,
            [columns(sum(shares))],
        )(normed0, normed1, valid, twin_valid, chosen)

    right1 = list(operand(second, counts, "right_neighbour"))

    def mid(name, x, *earlier):
        return send(after(x, *earlier), mirrored, f"mid_{name}")

    def end_right(name, x, *earlier):
        x = after(x, *earlier)
        return [send(x, shifted(s), f"end_right_{name}") for s in range(1, half)]

    def end_left(name, x, *earlier):
        return send(after(x, *earlier), edge, f"end_left_{name}")

    def cross(name, x, *earlier):
        return send(after(x, *earlier), in_plane(2), f"cross_{name}")

    own0 = mid("own_0", right0)
    crossed = cross("right_0", right1[0])
    near0 = end_right("0", right0)
    left0, *left1 = operand(chosen_left, (part, *counts), "left")
    gate = kernel(
        gate_kernel, "gate", jax.ShapeDtypeStruct((rows, toks, channels), F32), [VMEM] * 2
    )(normed0, gate_weight)
    right1[0] = after(crossed, left0)
    own1 = [mid("own_10", right1[0])]
    near1 = [end_right("10", right1[0])]
    left1[0] = cross("left_0", left1[0], crossed, near0[-1])
    next0 = [mid("next_0", x, own0) for x in near0]
    outer0 = end_left("0", left0, own0)
    right1[1] = cross("right_1", right1[1], left1[0], own1[0], near1[0][-1])
    next1 = [[mid("next_10", x, own1[0], gate) for x in near1[0]]]
    outer1 = [end_left("10", left1[0], near1[0][-1])]
    left1[1] = cross("left_1", left1[1], right1[1], next0[-1])
    own1.append(mid("own_11", right1[1], own1[0]))
    near1.append(end_right("11", right1[1], outer0))
    def products(mirror, first, lefts, rights, name, instead=()):
        span = 2 * rows * len(rights)
        count = lefts[0][1].shape[0]
        args = [x for arrays in (*lefts, *rights) for x in arrays] + [*instead]
        shapes = [piece(count, 2 * rows, span), piece(count, rows, 2 * span)]
        return kernel(
            functools.partial(
                product_kernel, mirror, bool(instead), first, len(lefts), len(rights)
            ),
            name,
            shapes[: len(lefts)],
            [VMEM] * len(args),
            [pltpu.VMEM((count, span, 2 * toks), BF16)],
        )(*args)

    def near_planes(g):
        return list(zip([right0, *near0], [right1[g], *near1[g]]))

    def far_planes(g):
        return list(zip([own0, *next0], [own1[g], *next1[g]]))

    def hand_out(g, close, away, ends):
        handed = kernel(
            functools.partial(hand_out_kernel, planes),
            "hand_out",
            [piece(counts[g], rows, toks)] * 4,
            [VMEM] * 3,
        )(close, away, ends)
        return [handed[0]] + [
            send(handed[r], in_plane(r), f"return_{g}{r}") for r in range(1, 4)
        ]

    close, mine, first = [], [(left0, x) for x in left1], [0, counts[0]]
    for g in groups:
        close += products(False, first[g], [mine[g]], near_planes(g), "near")
    sides = [mine[0], (outer0, outer1[0])]
    away0, swapped = products(True, first[0], sides, far_planes(0), "away", [left1[1]])
    next1.append([mid("next_11", x, next1[0][-1], own1[1], away0) for x in near1[1]])
    swapped = send(swapped, edge, "left_11_and_products_back_0")
    pieces = hand_out(0, close[0], away0, swapped)
    sides = [(after(left0, pieces[0], close[1]), left1[1]), (outer0, swapped)]
    away1, ends = products(True, first[1], sides, far_planes(1), "away")
    ends = send(ends, edge, "products_back_1")
    pieces += hand_out(1, close[1], away1, ends)

    return kernel(
        update_kernel,
        "update",
        jax.ShapeDtypeStruct((rows, toks, channels), BF16),
        [VMEM] * (3 + len(pieces)),
        [pltpu.VMEM((toks // LANES, (rows + 1) * (hidden + 1), LANES), F32)],
    )(out_gain.reshape(1, -1), out_weight, gate, *pieces)


def solution(mesh):
    placed = (
        P(("groups", "row"), "chan", None),
        P(("groups", "row"), "chan"),
        P(),
        P(),
        P(),
        P(),
        P(),
    )
    return jax.shard_map(
        functools.partial(local, n_row=mesh.shape["row"]),
        mesh=mesh,
        in_specs=placed,
        out_specs=P(("groups", "row"), "chan", None),
        check_vma=False,
    )
```

```python
import functools
import math

import jax
import jax.numpy as jnp
from jax import lax
from jax.experimental import pallas as pl
from jax.experimental.pallas import tpu as pltpu
from jax.sharding import PartitionSpec as P

F32, BF16 = jnp.float32, jnp.bfloat16
LANES = 128
SPARE = 6 * 1024 * 1024
SHARES = (9, 7)
NT = (((1,), (1,)), ((), ()))
TN = (((0,), (0,)), ((), ()))
VMEM = pl.BlockSpec(memory_space=pltpu.VMEM)
GROUP = 4
UNROLL = 8


def place():
    row = lax.axis_index("row")
    return row // 2, row % 2, lax.axis_index("chan")


def normalise(x, gain):
    mean = jnp.mean(x, axis=-1, keepdims=True)
    centered = x - mean
    var = jnp.mean(centered * centered, axis=-1, keepdims=True)
    return (centered * lax.rsqrt(var + 1e-05) * gain).astype(BF16)


def gated(normed, chosen, valid, first, held):
    _, rows, toks = valid.shape
    wide = chosen.shape[0] // 2
    proj = lax.dot_general(chosen[...], normed, NT, preferred_element_type=F32)
    for g in range(normed.shape[0] // toks):
        mine = proj[:, g * toks : (g + 1) * toks]
        value = (jnp.tanh(mine[:wide]) + 1.0) * (valid[0, pl.ds(first + g, 1), :] * mine[wide:])
        for m in range(toks // LANES):
            spot = pl.ds(first + g, wide, stride=rows + 1)
            held[m, spot, :] = value[:, m * LANES : (m + 1) * LANES]


def write_pieces(outs, held, base):
    row = 0
    for out in outs:
        count, rows, _ = out.shape
        for c in range(count):
            for m in range(held.shape[0]):
                lanes = slice(base + m * LANES, base + (m + 1) * LANES)
                out[c, :, lanes] = held[m, row : row + rows, :].astype(BF16)
            row += rows + 1


def right_rows(pair, valid, gain, chosen, normed_out, held):
    rows, toks, _ = pair.shape

    @pl.loop(0, rows // GROUP, unroll=UNROLL)
    def _(at):
        first = at * GROUP
        x = pair[pl.ds(first, GROUP)].astype(F32).reshape(GROUP * toks, -1)
        normed = normalise(x, gain[...])
        normed_out[pl.ds(first * toks, GROUP * toks), :] = normed
        gated(normed, chosen, valid, first, held)


def right_own_kernel(pair, mask, gain, weight, *rest):
    out, normed_out, first, second, chosen_left, valid, gain_out, turned, held = rest
    gain_out[...] = gain[...]
    hidden = weight.shape[1] // 4
    part = hidden // 4
    _, y, core = place()
    turned[...] = weight[...].T
    valid[0] = mask[...].astype(F32) * 0.5
    for n in range(4):
        half = 0.5 if n % 2 == 0 else 1.0
        for p in range(2):
            start = pl.multiple_of(n * hidden + ((2 * y + core) ^ (2 * p)) * part, part)
            columns = turned[pl.ds(start, part), :] * half
            if n < 2:
                at = (2 * n + p) * part
                chosen_left[at : at + part, :] = columns
            else:
                chosen = second if p else first
                chosen[(n - 2) * part : (n - 1) * part, :] = columns
    right_rows(pair, valid, gain, first, normed_out, held)
    write_pieces([out], held, 0)


def right_twin_kernel(pair, mask, gain, chosen, before, out, normed_out, valid, held):
    out[:, :, : before.shape[2]] = before[...]
    valid[0] = mask[...].astype(F32) * 0.5
    right_rows(pair, valid, gain, chosen, normed_out, held)
    write_pieces([out], held, pair.shape[1])


def rows_kernel(normed0, normed1, valid0, valid1, chosen, *rest):
    *outs, held = rest
    _, rows, toks = valid0.shape
    for n, (normed, valid) in enumerate(((normed0, valid0), (normed1, valid1))):

        @pl.loop(0, rows // GROUP, unroll=UNROLL)
        def _(at):
            first = at * GROUP
            gated(normed[pl.ds(first * toks, GROUP * toks), :], chosen, valid, first, held)

        write_pieces(outs, held, n * toks)


def gate_kernel(normed, weight, out):
    rows, toks, _ = out.shape

    @pl.loop(0, rows // GROUP, unroll=UNROLL)
    def _(at):
        x = normed[pl.ds(at * GROUP * toks, GROUP * toks), :]
        logits = jnp.dot(x, weight[...], preferred_element_type=F32)
        out[pl.ds(at * GROUP, GROUP)] = (0.5 * jnp.tanh(0.5 * logits) + 0.5).reshape(GROUP, toks, -1)


def product_kernel(mirror, instead, first, n_left, n_right, *rest):
    *refs, held = rest
    planes = [refs[2 * n : 2 * n + 2] for n in range(n_left + n_right)]
    lefts, rights = planes[:n_left], planes[n_left:]
    refs = refs[2 * (n_left + n_right) :]
    other, outs = refs[0], refs[1 if instead else 0 :]
    count, span, toks = outs[0].shape
    rows = span // 2
    z, y, _ = place()
    at_end = (z == 0) | (z == 2 * n_right - 1)
    z = 2 * n_right - 1 - z if mirror else z
    for s in range(n_right):
        for p in range(2):
            start = pl.multiple_of((z + n_right - s) % n_right * span + (y ^ p) * rows, rows)
            at = 0 if p else first
            held[:, pl.ds(start, rows), :] = rights[s][p][at : at + count]
    for c in range(count):
        left = jnp.concatenate([x for own, other in lefts for x in (own[first + c], other[c])], axis=0)
        out = lax.dot_general(left, held[c], NT, preferred_element_type=F32).astype(BF16)
        outs[0][c] = out[:span]
        if n_left == 2:
            outs[1][c, :, :toks] = out[span : span + rows]
            outs[1][c, :, toks:] = out[span + rows :]
    if instead:

        @pl.when(at_end)
        def _():
            outs[1][: other.shape[0]] = other[...]


def hand_out_kernel(planes, near, far, end, *outs):
    _, rows, toks = outs[0].shape
    z, _, core = place()
    at_end = (z == 0) | (z == planes - 1)
    for r in range(4):
        is_near = (core ^ (r % 2)) == z // (planes // 2)
        span = slice((r // 2) * rows, (r // 2 + 1) * rows)
        lanes = slice((r // 2) * toks, (r // 2 + 1) * toks)

        @pl.when(is_near)
        def _():
            outs[r][...] = near[:, span, :]

        @pl.when(jnp.logical_not(is_near | at_end))
        def _():
            outs[r][...] = far[:, span, :]

        @pl.when(jnp.logical_not(is_near) & at_end)
        def _():
            outs[r][...] = end[:, :, lanes]


def update_kernel(gain, weight, gate, *rest):
    pieces, out, turned = rest[:-2], rest[-2], rest[-1]
    part = sum(x.shape[0] for x in pieces[::4])
    _, rows, toks = pieces[0].shape
    hidden = 4 * part
    pitch = hidden + 1
    _, y, core = place()
    scale = jnp.broadcast_to(gain[...], (toks, hidden)).T
    for r in range(4):
        base = ((2 * y + core) ^ r) * part
        for piece in pieces[r::4]:
            for c in range(piece.shape[0]):
                value = piece[c].astype(F32)
                for m in range(toks // LANES):
                    turned[m, pl.ds(base + c, rows, stride=pitch), :] = value[
                        :, m * LANES : (m + 1) * LANES
                    ]
            base = base + piece.shape[0]

    @pl.loop(0, rows, unroll=32)
    def _(i):
        x = jnp.concatenate(
            [turned[m, pl.ds(i * pitch, hidden), :] for m in range(toks // LANES)], axis=1
        )
        mean = jnp.mean(x, axis=0, keepdims=True)
        centered = x - mean
        var = jnp.mean(centered * centered, axis=0, keepdims=True)
        pnorm = (centered * lax.rsqrt(var + 1e-05) * scale).astype(BF16)
        mapped = lax.dot_general(pnorm, weight[...], TN, preferred_element_type=F32)
        out[i] = (gate[i] * mapped).astype(BF16)


def kernel(body, name, out_shape, in_specs, scratch=()):
    outs = jax.tree.map(lambda _: VMEM, out_shape)

    def call(*args):
        arrays = [*args, *jax.tree.leaves(out_shape), *scratch]
        size = sum(x.dtype.itemsize * math.prod(x.shape) for x in arrays)
        return pl.pallas_call(
            body,
            out_shape=out_shape,
            in_specs=in_specs,
            out_specs=outs,
            scratch_shapes=list(scratch),
            compiler_params=pltpu.CompilerParams(vmem_limit_bytes=size + SPARE),
            name=name,
        )(*args)

    return call


def local(pair, pair_mask, in_gain, proj_weight, gate_weight, out_gain, out_weight, *, n_row):
    rows, toks, channels = pair.shape
    hidden = proj_weight.shape[1] // 4
    part = hidden // 4
    planes = n_row // 2
    half = planes // 2
    counts = [part * share // sum(SHARES) for share in SHARES]
    groups = range(len(counts))
    def send(x, target, name):
        pairs = []
        for source in range(2 * n_row):
            to = target(source // 4, source // 2 % 2, source % 2)
            if to is not None:
                pairs.append((source, 4 * to[0] + 2 * to[1] + to[2]))
        with jax.named_scope(name):
            return lax.ppermute(x, ("row", "chan"), pairs)

    def after(x, *earlier):
        return lax.optimization_barrier((x, *earlier))[0]

    def in_plane(r):
        return lambda p, b, k: (p, b ^ (r // 2), k ^ (r % 2))

    def shifted(s):
        return lambda p, b, k: (p // half * half + (p + s) % half, b, k)

    def mirrored(p, b, k):
        return (p, b, 1 - k) if p in (0, planes - 1) else (planes - 1 - p, b, k)

    def edge(p, b, k):
        swap = {0: 1, 1: 0, planes - 1: planes - 2, planes - 2: planes - 1}
        return (swap[p], b, k) if p in swap else (p, b, 1 - k)

    def outward(p, b, k):
        return {1: (0, b, k), planes - 2: (planes - 1, b, k)}.get(p)

    gains = in_gain.reshape(1, -1)
    twin, twin_mask = send(pair, in_plane(1), "pair"), send(pair_mask, in_plane(1), "mask")

    def piece(count, height, depth):
        return jax.ShapeDtypeStruct((count, height, depth), BF16)

    def columns(count):
        return pltpu.VMEM((toks // LANES, (count + 1) * (rows + 1), LANES), F32)

    rows_all = jax.ShapeDtypeStruct((rows * toks, channels), BF16)
    valid_shape = jax.ShapeDtypeStruct((1, rows, toks), F32)
    weights = [jax.ShapeDtypeStruct((n * part, channels), BF16) for n in (2, 2, 4)]
    before, normed0, first, second, chosen_left, valid, gains = kernel(
        right_own_kernel,
        "right_own",
        [piece(part, rows, toks), rows_all, *weights, valid_shape, gains],
        [VMEM] * 4,
        [pltpu.VMEM((4 * hidden, channels), BF16), columns(part)],
    )(pair, pair_mask, gains, proj_weight)
    right0, normed1, twin_valid = kernel(
        right_twin_kernel,
        "right_twin",
        [piece(part, rows, 2 * toks), rows_all, valid_shape],
        [VMEM] * 5,
        [columns(part)],
    )(twin, twin_mask, gains, first, before)

    def operand(chosen, shares, name):
        return kernel(
            rows_kernel,
            name,
            [piece(count, rows, 2 * toks) for count in shares],
            [VMEM] * 5,
            [columns(sum(shares))],
        )(normed0, normed1, valid, twin_valid, chosen)

    right1 = list(operand(second, counts, "right_neighbour"))

    def mid(name, x, *earlier):
        return send(after(x, *earlier), mirrored, f"mid_{name}")

    def end_right(name, x, *earlier):
        x = after(x, *earlier)
        return [send(x, shifted(s), f"end_right_{name}") for s in range(1, half)]

    def end_left(name, x, *earlier):
        return send(after(x, *earlier), edge, f"end_left_{name}")

    def cross(name, x, *earlier):
        return send(after(x, *earlier), in_plane(2), f"cross_{name}")

    own0 = mid("own_0", right0)
    crossed = cross("right_0", right1[0])
    near0 = end_right("0", right0)
    left0, *left1 = operand(chosen_left, (part, *counts), "left")
    gate = kernel(
        gate_kernel, "gate", jax.ShapeDtypeStruct((rows, toks, channels), F32), [VMEM] * 2
    )(normed0, gate_weight)
    right1[0] = after(crossed, left0)
    own1 = [mid("own_10", right1[0])]
    near1 = [end_right("10", right1[0])]
    left1[0] = cross("left_0", left1[0], crossed, own0)
    next0 = [mid("next_0", x, own0) for x in near0]
    outer0 = end_left("0", left0, own0)
    right1[1] = cross("right_1", right1[1], left1[0], own1[0], near1[0][-1])
    next1 = [[mid("next_10", x, own1[0], gate) for x in near1[0]]]
    outer1 = [end_left("10", left1[0], near1[0][-1])]
    left1[1] = cross("left_1", left1[1], right1[1], next0[-1])
    own1.append(mid("own_11", right1[1], own1[0]))
    near1.append(end_right("11", right1[1], outer0))
    def products(mirror, first, lefts, rights, name, instead=()):
        span = 2 * rows * len(rights)
        count = lefts[0][1].shape[0]
        args = [x for arrays in (*lefts, *rights) for x in arrays] + [*instead]
        shapes = [piece(count, 2 * rows, span), piece(count, rows, 2 * span)]
        return kernel(
            functools.partial(
                product_kernel, mirror, bool(instead), first, len(lefts), len(rights)
            ),
            name,
            shapes[: len(lefts)],
            [VMEM] * len(args),
            [pltpu.VMEM((count, span, 2 * toks), BF16)],
        )(*args)

    def near_planes(g):
        return list(zip([right0, *near0], [right1[g], *near1[g]]))

    def far_planes(g):
        return list(zip([own0, *next0], [own1[g], *next1[g]]))

    def hand_out(g, close, away, ends):
        handed = kernel(
            functools.partial(hand_out_kernel, planes),
            "hand_out",
            [piece(counts[g], rows, toks)] * 4,
            [VMEM] * 3,
        )(close, away, ends)
        return [handed[0]] + [
            send(handed[r], in_plane(r), f"return_{g}{r}") for r in range(1, 4)
        ]

    close, mine, first = [], [(left0, x) for x in left1], [0, counts[0]]
    for g in groups:
        close += products(False, first[g], [mine[g]], near_planes(g), "near")
    sides = [mine[0], (outer0, outer1[0])]
    away0, swapped = products(True, first[0], sides, far_planes(0), "away", [left1[1]])
    next1.append([mid("next_11", x, next1[0][-1], own1[1], away0) for x in near1[1]])
    swapped = send(swapped, edge, "left_11_and_products_back_0")
    pieces = hand_out(0, close[0], away0, swapped)
    sides = [(after(left0, pieces[0], close[1]), left1[1]), (outer0, swapped)]
    away1, ends = products(True, first[1], sides, far_planes(1), "away")
    ends = send(ends, edge, "products_back_1")
    pieces += hand_out(1, close[1], away1, ends)

    return kernel(
        update_kernel,
        "update",
        jax.ShapeDtypeStruct((rows, toks, channels), BF16),
        [VMEM] * (3 + len(pieces)),
        [pltpu.VMEM((toks // LANES, (rows + 1) * (hidden + 1), LANES), F32)],
    )(out_gain.reshape(1, -1), out_weight, gate, *pieces)


def solution(mesh):
    placed = (
        P(("groups", "row"), "chan", None),
        P(("groups", "row"), "chan"),
        P(),
        P(),
        P(),
        P(),
        P(),
    )
    return jax.shard_map(
        functools.partial(local, n_row=mesh.shape["row"]),
        mesh=mesh,
        in_specs=placed,
        out_specs=P(("groups", "row"), "chan", None),
        check_vma=False,
    )
```

```python
import functools
import math

import jax
import jax.numpy as jnp
from jax import lax
from jax.experimental import pallas as pl
from jax.experimental.pallas import tpu as pltpu
from jax.sharding import PartitionSpec as P

F32, BF16 = jnp.float32, jnp.bfloat16
LANES = 128
SPARE = 6 * 1024 * 1024
SHARES = (9, 7)
NT = (((1,), (1,)), ((), ()))
TN = (((0,), (0,)), ((), ()))
VMEM = pl.BlockSpec(memory_space=pltpu.VMEM)
GROUP = 4
UNROLL = 8


def place():
    row = lax.axis_index("row")
    return row // 2, row % 2, lax.axis_index("chan")


def normalise(x, gain):
    mean = jnp.mean(x, axis=-1, keepdims=True)
    centered = x - mean
    var = jnp.mean(centered * centered, axis=-1, keepdims=True)
    return (centered * lax.rsqrt(var + 1e-05) * gain).astype(BF16)


def gated(normed, chosen, valid, first, held):
    _, rows, toks = valid.shape
    wide = chosen.shape[0] // 2
    proj = lax.dot_general(chosen[...], normed, NT, preferred_element_type=F32)
    for g in range(normed.shape[0] // toks):
        mine = proj[:, g * toks : (g + 1) * toks]
        value = (jnp.tanh(mine[:wide]) + 1.0) * (valid[0, pl.ds(first + g, 1), :] * mine[wide:])
        for m in range(toks // LANES):
            spot = pl.ds(first + g, wide, stride=rows + 1)
            held[m, spot, :] = value[:, m * LANES : (m + 1) * LANES]


def write_pieces(outs, held, base):
    row = 0
    for out in outs:
        count, rows, _ = out.shape
        for c in range(count):
            for m in range(held.shape[0]):
                lanes = slice(base + m * LANES, base + (m + 1) * LANES)
                out[c, :, lanes] = held[m, row : row + rows, :].astype(BF16)
            row += rows + 1


def right_rows(pair, valid, gain, chosen, normed_out, held):
    rows, toks, _ = pair.shape

    @pl.loop(0, rows // GROUP, unroll=UNROLL)
    def _(at):
        first = at * GROUP
        x = pair[pl.ds(first, GROUP)].astype(F32).reshape(GROUP * toks, -1)
        normed = normalise(x, gain[...])
        normed_out[pl.ds(first * toks, GROUP * toks), :] = normed
        gated(normed, chosen, valid, first, held)


def right_own_kernel(pair, mask, gain, weight, *rest):
    out, normed_out, first, second, chosen_left, valid, gain_out, turned, held = rest
    gain_out[...] = gain[...]
    hidden = weight.shape[1] // 4
    part = hidden // 4
    _, y, core = place()
    turned[...] = weight[...].T
    valid[0] = mask[...].astype(F32) * 0.5
    for n in range(4):
        half = 0.5 if n % 2 == 0 else 1.0
        for p in range(2):
            start = pl.multiple_of(n * hidden + ((2 * y + core) ^ (2 * p)) * part, part)
            columns = turned[pl.ds(start, part), :] * half
            if n < 2:
                at = (2 * n + p) * part
                chosen_left[at : at + part, :] = columns
            else:
                chosen = second if p else first
                chosen[(n - 2) * part : (n - 1) * part, :] = columns
    right_rows(pair, valid, gain, first, normed_out, held)
    write_pieces([out], held, 0)


def right_twin_kernel(pair, mask, gain, chosen, before, out, normed_out, valid, held):
    out[:, :, : before.shape[2]] = before[...]
    valid[0] = mask[...].astype(F32) * 0.5
    right_rows(pair, valid, gain, chosen, normed_out, held)
    write_pieces([out], held, pair.shape[1])


def rows_kernel(normed0, normed1, valid0, valid1, chosen, *rest):
    *outs, held = rest
    _, rows, toks = valid0.shape
    for n, (normed, valid) in enumerate(((normed0, valid0), (normed1, valid1))):

        @pl.loop(0, rows // GROUP, unroll=UNROLL)
        def _(at):
            first = at * GROUP
            gated(normed[pl.ds(first * toks, GROUP * toks), :], chosen, valid, first, held)

        write_pieces(outs, held, n * toks)


def gate_kernel(normed, weight, out):
    rows, toks, _ = out.shape

    @pl.loop(0, rows // GROUP, unroll=UNROLL)
    def _(at):
        x = normed[pl.ds(at * GROUP * toks, GROUP * toks), :]
        logits = jnp.dot(x, weight[...], preferred_element_type=F32)
        out[pl.ds(at * GROUP, GROUP)] = (0.5 * jnp.tanh(0.5 * logits) + 0.5).reshape(GROUP, toks, -1)


def product_kernel(mirror, instead, first, n_left, n_right, *rest):
    *refs, held = rest
    planes = [refs[2 * n : 2 * n + 2] for n in range(n_left + n_right)]
    lefts, rights = planes[:n_left], planes[n_left:]
    refs = refs[2 * (n_left + n_right) :]
    other, outs = refs[0], refs[1 if instead else 0 :]
    count, span, toks = outs[0].shape
    rows = span // 2
    z, y, _ = place()
    at_end = (z == 0) | (z == 2 * n_right - 1)
    z = 2 * n_right - 1 - z if mirror else z
    for s in range(n_right):
        for p in range(2):
            start = pl.multiple_of((z + n_right - s) % n_right * span + (y ^ p) * rows, rows)
            at = 0 if p else first
            held[:, pl.ds(start, rows), :] = rights[s][p][at : at + count]
    for c in range(count):
        left = jnp.concatenate([x for own, other in lefts for x in (own[first + c], other[c])], axis=0)
        out = lax.dot_general(left, held[c], NT, preferred_element_type=F32).astype(BF16)
        outs[0][c] = out[:span]
        if n_left == 2:
            outs[1][c, :, :toks] = out[span : span + rows]
            outs[1][c, :, toks:] = out[span + rows :]
    if instead:

        @pl.when(at_end)
        def _():
            outs[1][: other.shape[0]] = other[...]


def hand_out_kernel(planes, beside, near, far, end, *outs):
    _, rows, toks = outs[0].shape
    z, _, core = place()
    at_end = (z == 0) | (z == planes - 1)
    for r in range(4):
        is_near = (core ^ (r % 2)) == z // (planes // 2)
        span = slice((r // 2) * rows, (r // 2 + 1) * rows)
        lanes = slice((r // 2) * toks, (r // 2 + 1) * toks)

        @pl.when(is_near)
        def _():
            outs[r][...] = near[:, span, :]

        @pl.when(jnp.logical_not(is_near | at_end))
        def _():
            outs[r][...] = far[:, span, :]

        @pl.when(jnp.logical_not(is_near) & at_end)
        def _():
            outs[r][...] = end[:, :, lanes] if beside else end[:, span, :]


def update_kernel(gain, weight, gate, *rest):
    pieces, out, turned = rest[:-2], rest[-2], rest[-1]
    part = sum(x.shape[0] for x in pieces[::4])
    _, rows, toks = pieces[0].shape
    hidden = 4 * part
    pitch = hidden + 1
    _, y, core = place()
    scale = jnp.broadcast_to(gain[...], (toks, hidden)).T
    for r in range(4):
        base = ((2 * y + core) ^ r) * part
        for piece in pieces[r::4]:
            for c in range(piece.shape[0]):
                value = piece[c].astype(F32)
                for m in range(toks // LANES):
                    turned[m, pl.ds(base + c, rows, stride=pitch), :] = value[
                        :, m * LANES : (m + 1) * LANES
                    ]
            base = base + piece.shape[0]

    @pl.loop(0, rows, unroll=32)
    def _(i):
        x = jnp.concatenate(
            [turned[m, pl.ds(i * pitch, hidden), :] for m in range(toks // LANES)], axis=1
        )
        mean = jnp.mean(x, axis=0, keepdims=True)
        centered = x - mean
        var = jnp.mean(centered * centered, axis=0, keepdims=True)
        pnorm = (centered * lax.rsqrt(var + 1e-05) * scale).astype(BF16)
        mapped = lax.dot_general(pnorm, weight[...], TN, preferred_element_type=F32)
        out[i] = (gate[i] * mapped).astype(BF16)


def kernel(body, name, out_shape, in_specs, scratch=()):
    outs = jax.tree.map(lambda _: VMEM, out_shape)

    def call(*args):
        arrays = [*args, *jax.tree.leaves(out_shape), *scratch]
        size = sum(x.dtype.itemsize * math.prod(x.shape) for x in arrays)
        return pl.pallas_call(
            body,
            out_shape=out_shape,
            in_specs=in_specs,
            out_specs=outs,
            scratch_shapes=list(scratch),
            compiler_params=pltpu.CompilerParams(vmem_limit_bytes=size + SPARE),
            name=name,
        )(*args)

    return call


def local(pair, pair_mask, in_gain, proj_weight, gate_weight, out_gain, out_weight, *, n_row):
    rows, toks, channels = pair.shape
    hidden = proj_weight.shape[1] // 4
    part = hidden // 4
    planes = n_row // 2
    half = planes // 2
    counts = [part * share // sum(SHARES) for share in SHARES]
    groups = range(len(counts))
    def send(x, target, name):
        pairs = []
        for source in range(2 * n_row):
            to = target(source // 4, source // 2 % 2, source % 2)
            if to is not None:
                pairs.append((source, 4 * to[0] + 2 * to[1] + to[2]))
        with jax.named_scope(name):
            return lax.ppermute(x, ("row", "chan"), pairs)

    def after(x, *earlier):
        return lax.optimization_barrier((x, *earlier))[0]

    def in_plane(r):
        return lambda p, b, k: (p, b ^ (r // 2), k ^ (r % 2))

    def shifted(s):
        return lambda p, b, k: (p // half * half + (p + s) % half, b, k)

    def mirrored(p, b, k):
        return (p, b, 1 - k) if p in (0, planes - 1) else (planes - 1 - p, b, k)

    def edge(p, b, k):
        swap = {0: 1, 1: 0, planes - 1: planes - 2, planes - 2: planes - 1}
        return (swap[p], b, k) if p in swap else (p, b, 1 - k)

    def outward(p, b, k):
        return {1: (0, b, k), planes - 2: (planes - 1, b, k)}.get(p)

    gains = in_gain.reshape(1, -1)
    twin, twin_mask = send(pair, in_plane(1), "pair"), send(pair_mask, in_plane(1), "mask")

    def piece(count, height, depth):
        return jax.ShapeDtypeStruct((count, height, depth), BF16)

    def columns(count):
        return pltpu.VMEM((toks // LANES, (count + 1) * (rows + 1), LANES), F32)

    rows_all = jax.ShapeDtypeStruct((rows * toks, channels), BF16)
    valid_shape = jax.ShapeDtypeStruct((1, rows, toks), F32)
    weights = [jax.ShapeDtypeStruct((n * part, channels), BF16) for n in (2, 2, 4)]
    before, normed0, first, second, chosen_left, valid, gains = kernel(
        right_own_kernel,
        "right_own",
        [piece(part, rows, toks), rows_all, *weights, valid_shape, gains],
        [VMEM] * 4,
        [pltpu.VMEM((4 * hidden, channels), BF16), columns(part)],
    )(pair, pair_mask, gains, proj_weight)
    right0, normed1, twin_valid = kernel(
        right_twin_kernel,
        "right_twin",
        [piece(part, rows, 2 * toks), rows_all, valid_shape],
        [VMEM] * 5,
        [columns(part)],
    )(twin, twin_mask, gains, first, before)

    def operand(chosen, shares, name):
        return kernel(
            rows_kernel,
            name,
            [piece(count, rows, 2 * toks) for count in shares],
            [VMEM] * 5,
            [columns(sum(shares))],
        )(normed0, normed1, valid, twin_valid, chosen)

    right1 = list(operand(second, counts, "right_neighbour"))

    def mid(name, x, *earlier):
        return send(after(x, *earlier), mirrored, f"mid_{name}")

    def end_right(name, x, *earlier):
        x = after(x, *earlier)
        return [send(x, shifted(s), f"end_right_{name}") for s in range(1, half)]

    def end_left(name, x, *earlier):
        return send(after(x, *earlier), edge, f"end_left_{name}")

    def cross(name, x, *earlier):
        return send(after(x, *earlier), in_plane(2), f"cross_{name}")

    own0 = mid("own_0", right0)
    crossed = cross("right_0", right1[0])
    near0 = end_right("0", right0)
    left0, *left1 = operand(chosen_left, (part, *counts), "left")
    gate = kernel(
        gate_kernel, "gate", jax.ShapeDtypeStruct((rows, toks, channels), F32), [VMEM] * 2
    )(normed0, gate_weight)
    right1[0] = after(crossed, left0)
    own1 = [mid("own_10", right1[0])]
    near1 = [end_right("10", right1[0])]
    left1[0] = cross("left_0", left1[0], crossed, near0[-1])
    next0 = [mid("next_0", x, own0) for x in near0]
    outer0 = end_left("0", left0, own0)
    right1[1] = cross("right_1", right1[1], left1[0], own1[0], near1[0][-1])
    next1 = [[mid("next_10", x, own1[0], gate) for x in near1[0]]]
    outer1 = [end_left("10", left1[0], near1[0][-1])]
    left1[1] = cross("left_1", left1[1], right1[1], next0[-1])
    own1.append(mid("own_11", right1[1], own1[0]))
    near1.append(end_right("11", right1[1], outer0))
    def products(mirror, first, lefts, rights, name, instead=()):
        span = 2 * rows * len(rights)
        count = rights[0][1].shape[0]
        args = [x for arrays in (*lefts, *rights) for x in arrays] + [*instead]
        shapes = [piece(count, 2 * rows, span), piece(count, rows, 2 * span)]
        return kernel(
            functools.partial(
                product_kernel, mirror, bool(instead), first, len(lefts), len(rights)
            ),
            name,
            shapes[: len(lefts)],
            [VMEM] * len(args),
            [pltpu.VMEM((count, span, 2 * toks), BF16)],
        )(*args)

    def near_planes(g):
        return list(zip([right0, *near0], [right1[g], *near1[g]]))

    def far_planes(g):
        return list(zip([own0, *next0], [own1[g], *next1[g]]))

    def hand_out(g, close, away, ends):
        handed = kernel(
            functools.partial(hand_out_kernel, planes, g == 0),
            "hand_out",
            [piece(counts[g], rows, toks)] * 4,
            [VMEM] * 3,
        )(close, away, ends)
        return [handed[0]] + [
            send(handed[r], in_plane(r), f"return_{g}{r}") for r in range(1, 4)
        ]

    close, mine, first = [], [(left0, x) for x in left1], [0, counts[0]]
    for g in groups:
        close += products(False, first[g], [mine[g]], near_planes(g), "near")
    sides = [mine[0], (outer0, outer1[0])]
    away0, swapped = products(True, first[0], sides, far_planes(0), "away", [left1[1]])
    next1.append([mid("next_11", x, next1[0][-1], own1[1], away0) for x in near1[1]])
    swapped = send(swapped, edge, "left_11_and_products_back_0")
    pieces = hand_out(0, close[0], away0, swapped)
    side = (after(outer0, pieces[0], close[1]), swapped)
    (ends,) = products(True, first[1], [side], far_planes(1), "away_for_ends")
    (away1,) = products(True, first[1], [(after(left0, ends), left1[1])], far_planes(1), "away")
    ends = send(ends, edge, "products_back_1")
    pieces += hand_out(1, close[1], away1, ends)

    return kernel(
        update_kernel,
        "update",
        jax.ShapeDtypeStruct((rows, toks, channels), BF16),
        [VMEM] * (3 + len(pieces)),
        [pltpu.VMEM((toks // LANES, (rows + 1) * (hidden + 1), LANES), F32)],
    )(out_gain.reshape(1, -1), out_weight, gate, *pieces)


def solution(mesh):
    placed = (
        P(("groups", "row"), "chan", None),
        P(("groups", "row"), "chan"),
        P(),
        P(),
        P(),
        P(),
        P(),
    )
    return jax.shard_map(
        functools.partial(local, n_row=mesh.shape["row"]),
        mesh=mesh,
        in_specs=placed,
        out_specs=P(("groups", "row"), "chan", None),
        check_vma=False,
    )
```

```python
import functools
import math

import jax
import jax.numpy as jnp
from jax import lax
from jax.experimental import pallas as pl
from jax.experimental.pallas import tpu as pltpu
from jax.sharding import PartitionSpec as P

F32, BF16 = jnp.float32, jnp.bfloat16
LANES = 128
SPARE = 6 * 1024 * 1024
SHARES = (17, 15)
NT = (((1,), (1,)), ((), ()))
TN = (((0,), (0,)), ((), ()))
VMEM = pl.BlockSpec(memory_space=pltpu.VMEM)
GROUP = 4
UNROLL = 8


def place():
    row = lax.axis_index("row")
    return row // 2, row % 2, lax.axis_index("chan")


def normalise(x, gain):
    mean = jnp.mean(x, axis=-1, keepdims=True)
    centered = x - mean
    var = jnp.mean(centered * centered, axis=-1, keepdims=True)
    return (centered * lax.rsqrt(var + 1e-05) * gain).astype(BF16)


def gated(normed, chosen, valid, first, held):
    _, rows, toks = valid.shape
    wide = chosen.shape[0] // 2
    proj = lax.dot_general(chosen[...], normed, NT, preferred_element_type=F32)
    for g in range(normed.shape[0] // toks):
        mine = proj[:, g * toks : (g + 1) * toks]
        value = (jnp.tanh(mine[:wide]) + 1.0) * (valid[0, pl.ds(first + g, 1), :] * mine[wide:])
        for m in range(toks // LANES):
            spot = pl.ds(first + g, wide, stride=rows + 1)
            held[m, spot, :] = value[:, m * LANES : (m + 1) * LANES]


def write_pieces(outs, held, base):
    row = 0
    for out in outs:
        count, rows, _ = out.shape
        for c in range(count):
            for m in range(held.shape[0]):
                lanes = slice(base + m * LANES, base + (m + 1) * LANES)
                out[c, :, lanes] = held[m, row : row + rows, :].astype(BF16)
            row += rows + 1


def right_rows(pair, valid, gain, chosen, normed_out, held):
    rows, toks, _ = pair.shape

    @pl.loop(0, rows // GROUP, unroll=UNROLL)
    def _(at):
        first = at * GROUP
        x = pair[pl.ds(first, GROUP)].astype(F32).reshape(GROUP * toks, -1)
        normed = normalise(x, gain[...])
        normed_out[pl.ds(first * toks, GROUP * toks), :] = normed
        gated(normed, chosen, valid, first, held)


def right_own_kernel(pair, mask, gain, weight, *rest):
    out, normed_out, first, second, chosen_left, valid, gain_out, turned, held = rest
    gain_out[...] = gain[...]
    hidden = weight.shape[1] // 4
    part = hidden // 4
    _, y, core = place()
    turned[...] = weight[...].T
    valid[0] = mask[...].astype(F32) * 0.5
    for n in range(4):
        half = 0.5 if n % 2 == 0 else 1.0
        for p in range(2):
            start = pl.multiple_of(n * hidden + ((2 * y + core) ^ (2 * p)) * part, part)
            columns = turned[pl.ds(start, part), :] * half
            if n < 2:
                at = (2 * n + p) * part
                chosen_left[at : at + part, :] = columns
            else:
                chosen = second if p else first
                chosen[(n - 2) * part : (n - 1) * part, :] = columns
    right_rows(pair, valid, gain, first, normed_out, held)
    write_pieces([out], held, 0)


def right_twin_kernel(pair, mask, gain, chosen, before, out, normed_out, valid, held):
    out[:, :, : before.shape[2]] = before[...]
    valid[0] = mask[...].astype(F32) * 0.5
    right_rows(pair, valid, gain, chosen, normed_out, held)
    write_pieces([out], held, pair.shape[1])


def rows_kernel(normed0, normed1, valid0, valid1, chosen, *rest):
    *outs, held = rest
    _, rows, toks = valid0.shape
    for n, (normed, valid) in enumerate(((normed0, valid0), (normed1, valid1))):

        @pl.loop(0, rows // GROUP, unroll=UNROLL)
        def _(at):
            first = at * GROUP
            gated(normed[pl.ds(first * toks, GROUP * toks), :], chosen, valid, first, held)

        write_pieces(outs, held, n * toks)


def gate_kernel(normed, weight, out):
    rows, toks, _ = out.shape

    @pl.loop(0, rows // GROUP, unroll=UNROLL)
    def _(at):
        x = normed[pl.ds(at * GROUP * toks, GROUP * toks), :]
        logits = jnp.dot(x, weight[...], preferred_element_type=F32)
        out[pl.ds(at * GROUP, GROUP)] = (0.5 * jnp.tanh(0.5 * logits) + 0.5).reshape(GROUP, toks, -1)


def product_kernel(mirror, instead, first, n_left, n_right, *rest):
    *refs, held = rest
    planes = [refs[2 * n : 2 * n + 2] for n in range(n_left + n_right)]
    lefts, rights = planes[:n_left], planes[n_left:]
    refs = refs[2 * (n_left + n_right) :]
    other, outs = refs[0], refs[1 if instead else 0 :]
    count, span, toks = outs[0].shape
    rows = span // 2
    z, y, _ = place()
    at_end = (z == 0) | (z == 2 * n_right - 1)
    z = 2 * n_right - 1 - z if mirror else z
    for s in range(n_right):
        for p in range(2):
            start = pl.multiple_of((z + n_right - s) % n_right * span + (y ^ p) * rows, rows)
            at = 0 if p else first
            held[:, pl.ds(start, rows), :] = rights[s][p][at : at + count]
    for c in range(count):
        left = jnp.concatenate([x for own, other in lefts for x in (own[first + c], other[c])], axis=0)
        out = lax.dot_general(left, held[c], NT, preferred_element_type=F32).astype(BF16)
        outs[0][c] = out[:span]
        if n_left == 2:
            outs[1][c, :, :toks] = out[span : span + rows]
            outs[1][c, :, toks:] = out[span + rows :]
    if instead:

        @pl.when(at_end)
        def _():
            outs[1][: other.shape[0]] = other[...]


def hand_out_kernel(planes, beside, near, far, end, *outs):
    _, rows, toks = outs[0].shape
    z, _, core = place()
    at_end = (z == 0) | (z == planes - 1)
    for r in range(4):
        is_near = (core ^ (r % 2)) == z // (planes // 2)
        span = slice((r // 2) * rows, (r // 2 + 1) * rows)
        lanes = slice((r // 2) * toks, (r // 2 + 1) * toks)

        @pl.when(is_near)
        def _():
            outs[r][...] = near[:, span, :]

        @pl.when(jnp.logical_not(is_near | at_end))
        def _():
            outs[r][...] = far[:, span, :]

        @pl.when(jnp.logical_not(is_near) & at_end)
        def _():
            outs[r][...] = end[:, :, lanes] if beside else end[:, span, :]


def update_kernel(gain, weight, gate, *rest):
    pieces, out, turned = rest[:-2], rest[-2], rest[-1]
    part = sum(x.shape[0] for x in pieces[::4])
    _, rows, toks = pieces[0].shape
    hidden = 4 * part
    pitch = hidden + 1
    _, y, core = place()
    scale = jnp.broadcast_to(gain[...], (toks, hidden)).T
    for r in range(4):
        base = ((2 * y + core) ^ r) * part
        for piece in pieces[r::4]:
            for c in range(piece.shape[0]):
                value = piece[c].astype(F32)
                for m in range(toks // LANES):
                    turned[m, pl.ds(base + c, rows, stride=pitch), :] = value[
                        :, m * LANES : (m + 1) * LANES
                    ]
            base = base + piece.shape[0]

    @pl.loop(0, rows, unroll=32)
    def _(i):
        x = jnp.concatenate(
            [turned[m, pl.ds(i * pitch, hidden), :] for m in range(toks // LANES)], axis=1
        )
        mean = jnp.mean(x, axis=0, keepdims=True)
        centered = x - mean
        var = jnp.mean(centered * centered, axis=0, keepdims=True)
        pnorm = (centered * lax.rsqrt(var + 1e-05) * scale).astype(BF16)
        mapped = lax.dot_general(pnorm, weight[...], TN, preferred_element_type=F32)
        out[i] = (gate[i] * mapped).astype(BF16)


def kernel(body, name, out_shape, in_specs, scratch=()):
    outs = jax.tree.map(lambda _: VMEM, out_shape)

    def call(*args):
        arrays = [*args, *jax.tree.leaves(out_shape), *scratch]
        size = sum(x.dtype.itemsize * math.prod(x.shape) for x in arrays)
        return pl.pallas_call(
            body,
            out_shape=out_shape,
            in_specs=in_specs,
            out_specs=outs,
            scratch_shapes=list(scratch),
            compiler_params=pltpu.CompilerParams(vmem_limit_bytes=size + SPARE),
            name=name,
        )(*args)

    return call


def local(pair, pair_mask, in_gain, proj_weight, gate_weight, out_gain, out_weight, *, n_row):
    rows, toks, channels = pair.shape
    hidden = proj_weight.shape[1] // 4
    part = hidden // 4
    planes = n_row // 2
    half = planes // 2
    counts = [part * share // sum(SHARES) for share in SHARES]
    groups = range(len(counts))
    def send(x, target, name):
        pairs = []
        for source in range(2 * n_row):
            to = target(source // 4, source // 2 % 2, source % 2)
            if to is not None:
                pairs.append((source, 4 * to[0] + 2 * to[1] + to[2]))
        with jax.named_scope(name):
            return lax.ppermute(x, ("row", "chan"), pairs)

    def after(x, *earlier):
        return lax.optimization_barrier((x, *earlier))[0]

    def in_plane(r):
        return lambda p, b, k: (p, b ^ (r // 2), k ^ (r % 2))

    def shifted(s):
        return lambda p, b, k: (p // half * half + (p + s) % half, b, k)

    def mirrored(p, b, k):
        return (p, b, 1 - k) if p in (0, planes - 1) else (planes - 1 - p, b, k)

    def edge(p, b, k):
        swap = {0: 1, 1: 0, planes - 1: planes - 2, planes - 2: planes - 1}
        return (swap[p], b, k) if p in swap else (p, b, 1 - k)

    def outward(p, b, k):
        return {1: (0, b, k), planes - 2: (planes - 1, b, k)}.get(p)

    gains = in_gain.reshape(1, -1)
    twin, twin_mask = send(pair, in_plane(1), "pair"), send(pair_mask, in_plane(1), "mask")

    def piece(count, height, depth):
        return jax.ShapeDtypeStruct((count, height, depth), BF16)

    def columns(count):
        return pltpu.VMEM((toks // LANES, (count + 1) * (rows + 1), LANES), F32)

    rows_all = jax.ShapeDtypeStruct((rows * toks, channels), BF16)
    valid_shape = jax.ShapeDtypeStruct((1, rows, toks), F32)
    weights = [jax.ShapeDtypeStruct((n * part, channels), BF16) for n in (2, 2, 4)]
    before, normed0, first, second, chosen_left, valid, gains = kernel(
        right_own_kernel,
        "right_own",
        [piece(part, rows, toks), rows_all, *weights, valid_shape, gains],
        [VMEM] * 4,
        [pltpu.VMEM((4 * hidden, channels), BF16), columns(part)],
    )(pair, pair_mask, gains, proj_weight)
    right0, normed1, twin_valid = kernel(
        right_twin_kernel,
        "right_twin",
        [piece(part, rows, 2 * toks), rows_all, valid_shape],
        [VMEM] * 5,
        [columns(part)],
    )(twin, twin_mask, gains, first, before)

    def operand(chosen, shares, name):
        return kernel(
            rows_kernel,
            name,
            [piece(count, rows, 2 * toks) for count in shares],
            [VMEM] * 5,
            [columns(sum(shares))],
        )(normed0, normed1, valid, twin_valid, chosen)

    right1 = list(operand(second, counts, "right_neighbour"))

    def mid(name, x, *earlier):
        return send(after(x, *earlier), mirrored, f"mid_{name}")

    def end_right(name, x, *earlier):
        x = after(x, *earlier)
        return [send(x, shifted(s), f"end_right_{name}") for s in range(1, half)]

    def end_left(name, x, *earlier):
        return send(after(x, *earlier), edge, f"end_left_{name}")

    def cross(name, x, *earlier):
        return send(after(x, *earlier), in_plane(2), f"cross_{name}")

    own0 = mid("own_0", right0)
    crossed = cross("right_0", right1[0])
    near0 = end_right("0", right0)
    left0, *left1 = operand(chosen_left, (part, *counts), "left")
    gate = kernel(
        gate_kernel, "gate", jax.ShapeDtypeStruct((rows, toks, channels), F32), [VMEM] * 2
    )(normed0, gate_weight)
    right1[0] = after(crossed, left0)
    own1 = [mid("own_10", right1[0])]
    near1 = [end_right("10", right1[0])]
    left1[0] = cross("left_0", left1[0], crossed, near0[-1])
    next0 = [mid("next_0", x, own0) for x in near0]
    outer0 = end_left("0", left0, own0)
    right1[1] = cross("right_1", right1[1], left1[0], own1[0], near1[0][-1])
    next1 = [[mid("next_10", x, own1[0], gate) for x in near1[0]]]
    outer1 = [end_left("10", left1[0], near1[0][-1])]
    left1[1] = cross("left_1", left1[1], right1[1], next0[-1])
    own1.append(mid("own_11", right1[1], own1[0]))
    near1.append(end_right("11", right1[1], outer0))
    def products(mirror, first, lefts, rights, name, instead=()):
        span = 2 * rows * len(rights)
        count = rights[0][1].shape[0]
        args = [x for arrays in (*lefts, *rights) for x in arrays] + [*instead]
        shapes = [piece(count, 2 * rows, span), piece(count, rows, 2 * span)]
        return kernel(
            functools.partial(
                product_kernel, mirror, bool(instead), first, len(lefts), len(rights)
            ),
            name,
            shapes[: len(lefts)],
            [VMEM] * len(args),
            [pltpu.VMEM((count, span, 2 * toks), BF16)],
        )(*args)

    def near_planes(g):
        return list(zip([right0, *near0], [right1[g], *near1[g]]))

    def far_planes(g):
        return list(zip([own0, *next0], [own1[g], *next1[g]]))

    def hand_out(g, close, away, ends):
        handed = kernel(
            functools.partial(hand_out_kernel, planes, g == 0),
            "hand_out",
            [piece(counts[g], rows, toks)] * 4,
            [VMEM] * 3,
        )(close, away, ends)
        return [handed[0]] + [
            send(handed[r], in_plane(r), f"return_{g}{r}") for r in range(1, 4)
        ]

    close, mine, first = [], [(left0, x) for x in left1], [0, counts[0]]
    for g in groups:
        close += products(False, first[g], [mine[g]], near_planes(g), "near")
    sides = [mine[0], (outer0, outer1[0])]
    away0, swapped = products(True, first[0], sides, far_planes(0), "away", [left1[1]])
    next1.append([mid("next_11", x, next1[0][-1], own1[1], away0) for x in near1[1]])
    swapped = send(swapped, edge, "left_11_and_products_back_0")
    pieces = hand_out(0, close[0], away0, swapped)
    side = (after(outer0, pieces[0], close[1]), swapped)
    (ends,) = products(True, first[1], [side], far_planes(1), "away_for_ends")
    (away1,) = products(True, first[1], [(after(left0, ends), left1[1])], far_planes(1), "away")
    ends = send(ends, edge, "products_back_1")
    pieces += hand_out(1, close[1], away1, ends)

    return kernel(
        update_kernel,
        "update",
        jax.ShapeDtypeStruct((rows, toks, channels), BF16),
        [VMEM] * (3 + len(pieces)),
        [pltpu.VMEM((toks // LANES, (rows + 1) * (hidden + 1), LANES), F32)],
    )(out_gain.reshape(1, -1), out_weight, gate, *pieces)


def solution(mesh):
    placed = (
        P(("groups", "row"), "chan", None),
        P(("groups", "row"), "chan"),
        P(),
        P(),
        P(),
        P(),
        P(),
    )
    return jax.shard_map(
        functools.partial(local, n_row=mesh.shape["row"]),
        mesh=mesh,
        in_specs=placed,
        out_specs=P(("groups", "row"), "chan", None),
        check_vma=False,
    )
```
